256 devices in a mesh: row: 4 (over y), col: 16 (over z, core), head: 4 (over x).
Axes of the slice: x: 4, y: 4, z: 8, core: 2. Of those that a mesh axis runs over, the one named last changes fastest.
Arguments:
- queries: bfloat16 [192, 512, 1024], P('row', 'col', 'head'), may hold values from -16 to 16
- keys: bfloat16 [192, 512, 1024], P('row', 'col', 'head'), may hold values from -16 to 16
- values: bfloat16 [192, 512, 1024], P('row', 'col', 'head'), may hold values from -16 to 16
- positions: int32 [2, 192, 512], P(None, 'row', 'col'), may hold values from 0 to 512, as said below
- conv_weight: float32 [9, 1024], P(None, 'head'), may hold values from -2 to 2
- norm_gain: float32 [1024], P('head'), may hold values from 0.5 to 1.5
- norm_bias: float32 [1024], P('head'), may hold values from -3 to 3
Outputs:
- normed: bfloat16 [192, 512, 1024], P('row', 'col', 'head')
The draws below stay inside these ranges and needn't reach their ends.
Inputs may be any that keep to these rules, and one draw needn't show every extreme that they name: positions[0] depends only on the grid row and positions[1] only on the grid column; each starts at 0 on the first grid line, rises by 0, 1 or 2 from one line to the next, and ends at 192 (rows) or 512 (columns).
All inputs are finite; a program needn't handle non-finite values.
Results may differ from the reference program's by a relative error of at most 0.0055.
Values may be sent and summed in bfloat16 or wider, within the bound.
No kernel may reach another device: no remote copies, remote signals or barrier semaphores. Data moves between devices by JAX's collectives and lax.ppermute only.
A program may use at most 128 MiB of HBM per device.

```python
import math
import jax
import jax.numpy as jnp
from jax import lax

HEADS = 16
HD = 64
D = 1024
AGR = 4
AGC = 1
PR = 12
PC = 32
TR = 48
TC = 32
NR = 192
NC = 512
AGENTS = 256
N_ROW = 4
N_COL = 16


def position_grid(key):
    row_jitter = jax.random.randint(jax.random.fold_in(key, 101), (NR,), 0, 2)
    col_jitter = jax.random.randint(jax.random.fold_in(key, 102), (NC,), 0, 2)
    row_line = jnp.arange(NR, dtype=jnp.int32)
    col_line = jnp.arange(NC, dtype=jnp.int32)
    row_jitter = jnp.where(row_line == 0, 0, jnp.where(row_line == NR - 1, 1, row_jitter))
    col_jitter = jnp.where(col_line == 0, 0, jnp.where(col_line == NC - 1, 1, col_jitter))
    row_index = (row_line + row_jitter).astype(jnp.int32)
    col_index = (col_line + col_jitter).astype(jnp.int32)
    return jnp.stack([jnp.broadcast_to(row_index[:, None], (NR, NC)), jnp.broadcast_to(col_index[None, :], (NR, NC))]).astype(jnp.int32)


def draw_positions(key, part):
    return position_grid(key)


def smooth_field(key, channels, amplitude):
    wave_key = jax.random.fold_in(key, 201)
    key_rows, key_cols, key_phase = jax.random.split(wave_key, 3)
    freq_rows = jax.random.uniform(key_rows, (8,), jnp.float32, -4.0, 4.0)
    freq_cols = jax.random.uniform(key_cols, (8,), jnp.float32, -4.0, 4.0)
    phases = jax.random.uniform(key_phase, (8,), jnp.float32, 0.0, 2.0 * math.pi)
    row_pos = jnp.arange(NR, dtype=jnp.float32) / NR
    col_pos = jnp.arange(NC, dtype=jnp.float32) / NC
    wave_arg = 2.0 * math.pi * (row_pos[:, None, None] * freq_rows + col_pos[None, :, None] * freq_cols) + phases
    wave_basis = jnp.cos(wave_arg)
    return amplitude * jnp.einsum('ijw,wc->ijc', wave_basis, channels) / math.sqrt(8.0)


def query_channels(key):
    return jax.random.normal(jax.random.fold_in(key, 301), (8, D), jnp.float32)


def key_channels(key):
    return 0.7 * query_channels(key) + 0.7 * jax.random.normal(jax.random.fold_in(key, 302), (8, D), jnp.float32)


def value_channels(key):
    return jax.random.normal(jax.random.fold_in(key, 303), (8, D), jnp.float32)


def draw_queries(key, part):
    field = smooth_field(key, query_channels(key), 1.7)
    rough_key = jax.random.fold_in(key, 401)
    result = field + jax.random.normal(rough_key, (NR, NC, D), jnp.float32)
    return jnp.clip(result, -16.0, 16.0).astype(jnp.bfloat16)


def draw_keys(key, part):
    field = smooth_field(key, key_channels(key), 1.7)
    rough_key = jax.random.fold_in(key, 411)
    result = field + jax.random.normal(rough_key, (NR, NC, D), jnp.float32)
    return jnp.clip(result, -16.0, 16.0).astype(jnp.bfloat16)


def draw_values(key, part):
    field = smooth_field(key, value_channels(key), 1.7)
    rough_key = jax.random.fold_in(key, 421)
    channel_ramp = jnp.arange(D, dtype=jnp.float32) / (D - 1)
    rough_part = jax.random.normal(rough_key, (NR, NC, D), jnp.float32)
    result = (field + rough_part) * (0.5 * jnp.power(jnp.float32(4.0), channel_ramp))
    return jnp.clip(result, -16.0, 16.0).astype(jnp.bfloat16)


def levels(stream_key, dims, cuts, least, top_value):
    loudness = 1.0
    for position, blocks in cuts:
        heights = jax.random.uniform(jax.random.fold_in(jax.random.fold_in(stream_key, 6), position), (blocks,), jnp.float32, least / len(cuts), top_value / len(cuts))
        loudness = loudness * jnp.repeat(jnp.exp(heights), dims[position] // blocks).reshape((-1,) + (1,) * (len(dims) - 1 - position))
    return loudness


def bell_draw(stream_key, shape, spread, reach, cuts=(), held_as=jnp.bfloat16):
    level = levels(stream_key, shape, cuts, -0.22, 0.18) if cuts else 1.0
    values = jax.random.normal(stream_key, shape, jnp.float32) * spread * level
    return jnp.minimum(jnp.maximum(values, -reach), reach).astype(held_as)


def setup_inputs(seed: int = 0) -> dict:
    key_list = jax.random.split(jax.random.key(seed), 8)
    queries = draw_queries(jax.random.fold_in(key_list[7], 71), 0)
    keys = draw_keys(jax.random.fold_in(key_list[7], 71), 0)
    values = draw_values(jax.random.fold_in(key_list[7], 71), 0)
    positions = draw_positions(jax.random.fold_in(key_list[7], 71), 0)
    conv_weight = bell_draw(key_list[4], (9, D), 9 ** -0.5, 2.0, ((1, 4),), jnp.float32)
    norm_gain = jnp.clip(1.0 + 0.1 * jax.random.normal(key_list[5], (D,), jnp.float32), 0.5, 1.5)
    norm_bias = bell_draw(key_list[6], (D,), 0.5, 3.0, ((0, 4),), jnp.float32)
    return dict(queries=queries, keys=keys, values=values, positions=positions, conv_weight=conv_weight, norm_gain=norm_gain, norm_bias=norm_bias)


epsilon = 1e-05

def rotate_pairs(segment, angles):
    quarter = segment.shape[-1] // 2
    cosine = jnp.cos(angles)[..., None, :]
    sines = jnp.sin(angles)[..., None, :]
    lower = segment[..., :quarter]
    upper = segment[..., quarter:]
    return jnp.concatenate([lower * cosine - upper * sines, lower * sines + upper * cosine], -1)

def rotary(inputs, positions, head_size):
    full_shape = inputs.shape
    head_count = full_shape[-1] // head_size
    quarter = head_size // 4
    half_size = head_size // 2
    frequency = jnp.power(jnp.float32(100.0), -jnp.arange(quarter, dtype=jnp.float32) / quarter)
    row_angles = positions[0].astype(jnp.float32)[..., None] * frequency
    col_angles = positions[1].astype(jnp.float32)[..., None] * frequency
    unpacked = inputs.astype(jnp.float32).reshape(full_shape[:-1] + (head_count, head_size))
    turned = jnp.concatenate([rotate_pairs(unpacked[..., :half_size], row_angles), rotate_pairs(unpacked[..., half_size:], col_angles)], -1)
    return turned.reshape(full_shape).astype(jnp.bfloat16)

def reference(queries, keys, values, positions, conv_weight, norm_gain, norm_bias):
    score_scale = 1.0 / math.sqrt(HD)
    zero = jnp.zeros((), jnp.int32)
    tile_ids = jnp.arange(N_ROW * N_COL, dtype=jnp.int32)
    padded = jnp.pad(values, ((1, 1), (1, 1), (0, 0)))

    def take_tile(array, tile_index, extra):
        tile_row = (tile_index // N_COL).astype(jnp.int32)
        tile_col = (tile_index % N_COL).astype(jnp.int32)
        return lax.dynamic_slice(array, (tile_row * TR, tile_col * TC, zero), (TR + extra, TC + extra, array.shape[-1]))

    def take_positions(tile_index):
        tile_row = (tile_index // N_COL).astype(jnp.int32)
        tile_col = (tile_index % N_COL).astype(jnp.int32)
        return lax.dynamic_slice(positions, (zero, tile_row * TR, tile_col * TC), (2, TR, TC))

    def pool_tile(tile_index):
        turned = rotary(take_tile(queries, tile_index, 0), take_positions(tile_index), HD)
        cells = turned.astype(jnp.float32).reshape(AGR, PR, AGC, PC, D).mean(axis=(1, 3))
        return cells.reshape(AGR * AGC, D).astype(jnp.bfloat16)
    agents = lax.map(pool_tile, tile_ids).reshape(AGENTS, D)
    agent_heads = agents.astype(jnp.float32).reshape(AGENTS, HEADS, HD)

    def agent_partials(tile_index):
        turned = rotary(take_tile(keys, tile_index, 0), take_positions(tile_index), HD)
        turned = turned.astype(jnp.float32).reshape(TR * TC, HEADS, HD)
        tile_values = take_tile(values, tile_index, 0).astype(jnp.float32).reshape(TR * TC, HEADS, HD)
        scores = jnp.einsum('ahd,thd->hat', agent_heads, turned) * score_scale
        highest = scores.max(-1)
        exponent = jnp.exp(scores - highest[..., None])
        totals = exponent.sum(-1)
        weights = exponent.astype(jnp.bfloat16).astype(jnp.float32)
        numerator = jnp.einsum('hat,thd->had', weights, tile_values)
        return (highest, totals, numerator)
    tile_peaks, tile_totals, tile_numers = lax.map(agent_partials, tile_ids)
    overall = tile_peaks.max(0)
    factor = jnp.exp(tile_peaks - overall)
    totals = (factor * tile_totals).sum(0)
    numerator = (factor[..., None] * tile_numers).sum(0)
    agent_values = (numerator / totals[..., None]).astype(jnp.bfloat16).astype(jnp.float32)

    def output_tile(tile_index):
        turned = rotary(take_tile(queries, tile_index, 0), take_positions(tile_index), HD)
        turned = turned.astype(jnp.float32).reshape(TR * TC, HEADS, HD)
        scores = jnp.einsum('thd,ahd->hta', turned, agent_heads) * score_scale
        probabilities = jax.nn.softmax(scores, -1).astype(jnp.bfloat16).astype(jnp.float32)
        attended = jnp.einsum('hta,had->thd', probabilities, agent_values).reshape(TR, TC, D)
        window = take_tile(padded, tile_index, 2).astype(jnp.float32)
        convolved = jnp.zeros((TR, TC, D), jnp.float32)
        for step_row in range(3):
            for step_col in range(3):
                convolved = convolved + window[step_row:step_row + TR, step_col:step_col + TC] * conv_weight[3 * step_row + step_col]
        summed = attended + convolved
        average = summed.mean(-1, keepdims=True)
        centered = summed - average
        variance = (centered * centered).mean(-1, keepdims=True)
        return (centered * lax.rsqrt(variance + epsilon) * norm_gain + norm_bias).astype(jnp.bfloat16)
    tiles_out = lax.map(output_tile, tile_ids)
    return tiles_out.reshape(N_ROW, N_COL, TR, TC, D).transpose(0, 2, 1, 3, 4).reshape(NR, NC, D)
```

```python
import math

import jax
import jax.numpy as jnp
from jax import lax
from jax.experimental import pallas as pl
from jax.experimental.pallas import tpu as pltpu
from jax.sharding import PartitionSpec as P

HD = 64
D = 1024
AGR = 4
TR = 48
TC = 32
CH = 256
N = TR * TC
AGENTS = 256
TILES = 64
LOCAL_HEADS = 4
ROWS = LOCAL_HEADS * AGENTS // TILES
BLOCKS = N // 128

f32 = jnp.float32
bf16 = jnp.bfloat16
epsilon = 1e-05

VMEM_SPEC = pl.BlockSpec(memory_space=pltpu.VMEM)


def call(kernel, out_shape, n_in, scratch=(), flops=0, nbytes=0, name=None):
    outs = jax.tree.map(lambda s: VMEM_SPEC, out_shape)
    return pl.pallas_call(
        kernel,
        out_shape=out_shape,
        in_specs=[VMEM_SPEC] * n_in,
        out_specs=outs,
        scratch_shapes=list(scratch),
        compiler_params=pltpu.CompilerParams(vmem_limit_bytes=32 * 1024 * 1024),
        cost_estimate=pl.CostEstimate(flops=flops, bytes_accessed=nbytes, transcendentals=0),
        name=name,
    )


def shape(dims, dtype):
    return jax.ShapeDtypeStruct(dims, dtype)


def lanes(dims):
    return lax.broadcasted_iota(jnp.int32, dims, len(dims) - 1)


def turn_matrix():
    source = lax.broadcasted_iota(jnp.int32, (CH, CH), 0)
    target = lax.broadcasted_iota(jnp.int32, (CH, CH), 1)
    low = (target & 31) < 16
    minus = jnp.where(low & (source == target + 16), -1.0, 0.0)
    plus = jnp.where((~low) & (source == target - 16), 1.0, 0.0)
    return (minus + plus).astype(bf16)


def sin_cos(angle):
    return jnp.sin(angle), jnp.cos(angle)


def turned(x, matrix, cosine, sine):
    swapped = jnp.dot(x, matrix, preferred_element_type=f32)
    return (x.astype(f32) * cosine + swapped * sine).astype(bf16)


def cell_tables(cos_r, sin_r, cos_c, sin_c, first, rows):
    cosine = jnp.concatenate(
        [cos_r[first + i : first + i + 1, :] * cos_c for i in range(rows)], axis=0
    )
    sine = jnp.concatenate(
        [sin_r[first + i : first + i + 1, :] + sin_c for i in range(rows)], axis=0
    )
    return cosine, sine


def query_kernel(pos_ref, freq_ref, q_ref, tq_ref, agents_ref, tab_r_ref, tab_c_ref, turn_ref):
    freq = freq_ref[...]
    row_pos = pos_ref[0][:, 0:1].astype(f32)
    col_line = pos_ref[1][0:1, :].astype(f32)
    eye = lax.broadcasted_iota(jnp.int32, (TC, TC), 0) == lax.broadcasted_iota(
        jnp.int32, (TC, TC), 1
    )
    col_pos = jnp.sum(jnp.where(eye, jnp.broadcast_to(col_line, (TC, TC)), 0.0), 1, keepdims=True)
    angles = jnp.concatenate([row_pos * freq[0:1, :], col_pos * freq[1:2, :]], axis=0)
    sines, cosines = sin_cos(angles)
    sines = jnp.concatenate([sines, sines], axis=1)
    cosines = jnp.concatenate([cosines, cosines], axis=1)
    tab_r_ref[0] = cosines[:TR]
    tab_r_ref[1] = sines[:TR]
    tab_c_ref[0] = cosines[TR:]
    tab_c_ref[1] = sines[TR:]
    matrix = turn_matrix()
    turn_ref[...] = matrix
    step = N // AGR
    means = []
    for cell in range(AGR):
        cosine, sine = cell_tables(
            cosines[:TR], sines[:TR], cosines[TR:], sines[TR:], cell * (TR // AGR), TR // AGR
        )
        rotated = turned(q_ref[pl.ds(cell * step, step), :], matrix, cosine, sine)
        tq_ref[pl.ds(cell * step, step), :] = rotated
        mean = jnp.sum(rotated.astype(f32), 0, keepdims=True) / step
        means.append(mean.astype(bf16).astype(f32))
    packed = jnp.concatenate([m[:, :128] for m in means] + [m[:, 128:] for m in means], axis=0)
    agents_ref[...] = jnp.broadcast_to(packed[None], (TILES, 8, 128))


def key_kernel(tab_r_ref, tab_c_ref, turn_ref, k_ref, tk_ref):
    matrix = turn_ref[...]
    step = N // AGR
    for cell in range(AGR):
        cosine, sine = cell_tables(
            tab_r_ref[0], tab_r_ref[1], tab_c_ref[0], tab_c_ref[1], cell * (TR // AGR), TR // AGR
        )
        tk_ref[pl.ds(cell * step, step), :] = turned(
            k_ref[pl.ds(cell * step, step), :], matrix, cosine, sine
        )


def agent_pairs(agents_ref, scale):
    pairs = []
    for pair in range(2):
        parts = [agents_ref[pl.ds(4 * pair + k, TILES, stride=8), :] for k in range(AGR)]
        pairs.append((jnp.concatenate(parts, axis=0) * scale).astype(bf16))
    return pairs


def half_mask(dims, parity):
    return (lanes(dims) // HD) == parity


def partial_kernel(agents_ref, tk_ref, v_ref, out_ref, score_ref):
    pairs = agent_pairs(agents_ref, 1.0 / math.sqrt(HD))
    chunk = 512
    for head in range(LOCAL_HEADS):
        pair, parity = head // 2, head % 2
        cols = pl.ds(pair * 128, 128)
        own = pairs[pair]
        own = jnp.where(half_mask(own.shape, parity), own, jnp.zeros_like(own))
        peak = None
        for c in range(N // chunk):
            scores = lax.dot_general(
                own,
                tk_ref[pl.ds(c * chunk, chunk), cols],
                (((1,), (1,)), ((), ())),
                preferred_element_type=f32,
            )
            score_ref[:, pl.ds(c * chunk, chunk)] = scores
            for s in range(chunk // 128):
                piece = scores[:, s * 128 : (s + 1) * 128]
                peak = piece if peak is None else jnp.maximum(peak, piece)
        peak = jnp.max(peak, 1, keepdims=True)
        acc = jnp.zeros((AGENTS, 128), f32)
        for c in range(N // chunk):
            weights = jnp.exp(score_ref[:, pl.ds(c * chunk, chunk)] - peak).astype(bf16)
            block = v_ref[pl.ds(c * chunk, chunk), cols]
            block = jnp.where(half_mask(block.shape, parity), block, jnp.ones_like(block))
            acc = acc + jnp.dot(weights, block, preferred_element_type=f32)
        other = pltpu.roll(acc, HD, 1)
        numer, total = (acc, other) if parity == 0 else (other, acc)
        logs = peak + jnp.log(total)
        values = numer / total
        logs = jnp.max(jnp.where(half_mask(logs.shape, 0), logs, -3e38), 1, keepdims=True)
        first = logs.astype(bf16).astype(f32)
        second = (logs - first).astype(bf16).astype(f32)
        third = logs - first - second
        lane = lanes((AGENTS, 128))
        packed = jnp.where(
            lane < HD,
            values,
            jnp.where(
                lane == HD,
                first,
                jnp.where(lane == HD + 1, second, jnp.where(lane == HD + 2, third, 0.0)),
            ),
        )
        out_ref[pl.ds(head * AGENTS, AGENTS), :] = packed.astype(bf16)


def merge_kernel(parts_ref, out_ref):
    source = lax.broadcasted_iota(jnp.int32, (128, 128), 0)
    picker = jnp.where((source >= HD) & (source < HD + 3), 1.0, 0.0).astype(bf16)
    parts = parts_ref[...]
    logs = jnp.dot(parts, picker, preferred_element_type=f32).reshape(TILES, ROWS, 128)
    values = parts.astype(f32).reshape(TILES, ROWS, 128)
    peak = jnp.max(logs, 0)
    weights = jnp.exp(logs - peak[None])
    merged = jnp.sum(weights * values, 0) / jnp.sum(weights, 0)
    merged = jnp.where(lanes(merged.shape) < HD, merged, 0.0)
    merged = (merged + pltpu.roll(merged, HD, 1)).astype(bf16)
    out_ref[...] = jnp.broadcast_to(merged[None], (TILES, ROWS, 128))


def probability_kernel(agents_ref, tq_ref, prob_ref, recip_ref):
    pairs = agent_pairs(agents_ref, 1.0 / math.sqrt(HD))
    target = [
        jnp.where(half_mask((AGENTS, 128), parity), 1.0, 0.0).astype(bf16) for parity in range(2)
    ]
    owns = []
    for head in range(LOCAL_HEADS):
        own = pairs[head // 2]
        owns.append(jnp.where(half_mask(own.shape, head % 2), own, jnp.zeros_like(own)))
    chunk = 256

    def body(c, carry):
        rows = pl.ds(pl.multiple_of(c * chunk, chunk), chunk)
        for pair in range(2):
            cols = pl.ds(pair * 128, 128)
            queries = tq_ref[rows, cols]
            total = jnp.zeros((chunk, 128), f32)
            for parity in range(2):
                head = 2 * pair + parity
                scores = lax.dot_general(
                    queries, owns[head], (((1,), (1,)), ((), ())), preferred_element_type=f32
                )
                weights = jnp.exp(scores - jnp.max(scores, 1, keepdims=True)).astype(bf16)
                prob_ref[rows, pl.ds(head * AGENTS, AGENTS)] = weights
                total = total + jnp.dot(weights, target[parity], preferred_element_type=f32)
            recip_ref[rows, cols] = 1.0 / total
        return carry

    lax.fori_loop(0, N // chunk, body, 0)


def edge_kernel(left_ref, right_ref, first_ref, last_ref):
    first_ref[...] = left_ref[:, 0, :]
    last_ref[...] = right_ref[:, 15, :]


def line_kernel(v_top_ref, v_bottom_ref, left_ref, right_ref, up_ref, down_ref):
    for v_ref, row, out_ref in ((v_top_ref, 0, up_ref), (v_bottom_ref, TR - 1, down_ref)):
        out_ref[pl.ds(0, TC), :] = v_ref[0]
        left = left_ref[row : row + 1, :].astype(f32)
        right = right_ref[row : row + 1, :].astype(f32)
        tail = jnp.concatenate([left, right, jnp.zeros((14, CH), f32)], axis=0)
        out_ref[pl.ds(TC, 16), :] = tail.astype(bf16)


def conv_kernel(v_ref, left_ref, right_ref, above_ref, below_ref, w_ref, out_ref, l_ref, r_ref):
    l_ref[...] = left_ref[...].astype(f32)
    r_ref[...] = right_ref[...].astype(f32)
    for half in range(2):
        cols = pl.ds(half * 128, 128)
        w = [jnp.broadcast_to(w_ref[t : t + 1, cols], (TC, 128)) for t in range(9)]
        column = lax.broadcasted_iota(jnp.int32, (TC, 128), 0)

        def taps(row, left, right):
            row = row.astype(f32)
            before = jnp.where(column == 0, left, pltpu.roll(row, 1, 0))
            after = jnp.where(column == TC - 1, right, pltpu.roll(row, TC - 1, 0))
            return [before * w[3 * d] + row * w[3 * d + 1] + after * w[3 * d + 2] for d in range(3)]

        tail = above_ref[pl.ds(TC, 16), cols].astype(f32)
        t0 = taps(above_ref[pl.ds(0, TC), cols], tail[0:1], tail[1:2])

        def group(start, carry):
            a, b = carry
            lefts, rights = l_ref[pl.ds(start, 8), cols], r_ref[pl.ds(start, 8), cols]
            for k in range(8):
                t = taps(v_ref[start + k, :, cols], lefts[k : k + 1], rights[k : k + 1])
                if a is not None:
                    at = (start + k - 1) * TC
                    if not isinstance(at, int):
                        at = pl.multiple_of(at, TC)
                    out_ref[pl.ds(at, TC), cols] = a + t[2]
                a, b = b + t[1], t[0]
            return a, b

        carry = group(0, (None, t0[0]))
        a, b = lax.fori_loop(
            1, TR // 8, lambda g, c: group(pl.multiple_of(g * 8, 8), c), carry
        )
        tail = below_ref[pl.ds(TC, 16), cols].astype(f32)
        t = taps(below_ref[pl.ds(0, TC), cols], tail[0:1], tail[1:2])
        out_ref[pl.ds((TR - 1) * TC, TC), cols] = a + t[2]


def attend_kernel(av_ref, prob_ref, recip_ref, conv_ref, sum_ref, stat_ref):
    halves = []
    for pair in range(2):
        pieces = []
        for parity in range(2):
            part = av_ref[pl.ds((2 * pair + parity) * AGENTS, AGENTS), :]
            pieces.append(jnp.where(half_mask(part.shape, parity), part, jnp.zeros_like(part)))
        halves.append(jnp.concatenate(pieces, axis=0))
    eye = lax.broadcasted_iota(jnp.int32, (128, 128), 0) == lanes((128, 128))

    for b in range(BLOCKS):
        rows = pl.ds(b * 128, 128)
        xs = []
        for pair in range(2):
            cols = pl.ds(pair * 128, 128)
            attended = jnp.dot(
                prob_ref[rows, pl.ds(pair * 2 * AGENTS, 2 * AGENTS)],
                halves[pair],
                preferred_element_type=f32,
            )
            x = attended * recip_ref[rows, cols] + conv_ref[rows, cols]
            sum_ref[rows, cols] = x
            xs.append(x)
        mean = jnp.sum(xs[0] + xs[1], 1, keepdims=True) * (1.0 / CH)
        c0, c1 = xs[0] - mean, xs[1] - mean
        squares = jnp.sum(c0 * c0 + c1 * c1, 1, keepdims=True)
        stat_ref[b : b + 1, :] = jnp.sum(jnp.where(eye, mean, 0.0), 0, keepdims=True)
        stat_ref[BLOCKS + b : BLOCKS + b + 1, :] = jnp.sum(
            jnp.where(eye, squares, 0.0), 0, keepdims=True
        )


def norm_kernel(s0_ref, s1_ref, s2_ref, s3_ref, sum_ref, gain_ref, bias_ref, out_ref):
    stats = [s[...] for s in (s0_ref, s1_ref, s2_ref, s3_ref)]
    means = [s[:BLOCKS] for s in stats]
    mean = (means[0] + means[1] + means[2] + means[3]) * 0.25
    squares = sum(s[BLOCKS:] for s in stats)
    for m in means:
        squares = squares + CH * (m - mean) * (m - mean)
    scale = lax.rsqrt(squares * (1.0 / D) + epsilon)
    for b in range(BLOCKS):
        rows = pl.ds(b * 128, 128)
        m = jnp.broadcast_to(mean[b : b + 1], (128, 128)).T
        s = jnp.broadcast_to(scale[b : b + 1], (128, 128)).T
        for half in range(2):
            cols = pl.ds(half * 128, 128)
            out_ref[rows, cols] = (
                (sum_ref[rows, cols] - m) * s * gain_ref[0:1, cols] + bias_ref[0:1, cols]
            ).astype(bf16)


def frequencies():
    lane = jnp.arange(128) % HD
    power = jnp.power(f32(100.0), -(lane % 16).astype(f32) / 16)
    return jnp.stack([jnp.where(lane < 32, power, 0.0), jnp.where(lane < 32, 0.0, power)])


def spread(x):
    return lax.all_to_all(x, ("row", "col"), 0, 0)


def shift(x, axis, step):
    count = lax.axis_size(axis)
    pairs = [(i, i + step) for i in range(count) if 0 <= i + step < count]
    return lax.ppermute(x, axis, pairs)


def shards(queries, keys, values, positions, conv_weight, norm_gain, norm_bias):
    q = queries.reshape(N, CH)
    k = keys.reshape(N, CH)
    v = values.reshape(N, CH)
    mb = 1 << 20
    tq, packed, tab_r, tab_c, turn = call(
        query_kernel,
        (
            shape((N, CH), bf16),
            shape((TILES, 8, 128), f32),
            shape((2, TR, CH), f32),
            shape((2, TC, CH), f32),
            shape((CH, CH), bf16),
        ),
        3,
        nbytes=8 * mb,
        name="turn_queries",
    )(positions, frequencies(), q)
    agents = spread(packed).reshape(TILES * 8, 128)
    tk = call(key_kernel, shape((N, CH), bf16), 4, nbytes=6 * mb, name="turn_keys")(
        tab_r, tab_c, turn, k
    )
    parts = call(
        partial_kernel,
        shape((LOCAL_HEADS * AGENTS, 128), bf16),
        3,
        scratch=[pltpu.VMEM((AGENTS, N), f32)],
        nbytes=20 * mb,
        name="partials",
    )(agents, tk, v)
    received = spread(parts.reshape(TILES, ROWS, 128)).reshape(TILES * ROWS, 128)
    prob, recip = call(
        probability_kernel,
        (shape((N, LOCAL_HEADS * AGENTS), bf16), shape((N, CH), f32)),
        2,
        nbytes=20 * mb,
        name="probabilities",
    )(agents, tq)
    merged = call(merge_kernel, shape((TILES, ROWS, 128), bf16), 1, nbytes=2 * mb, name="merge")(
        received
    )
    agent_values = spread(merged).reshape(TILES * ROWS, 128)

    first, last = pl.pallas_call(
        edge_kernel,
        out_shape=(shape((TR, CH), bf16),) * 2,
        grid=(1,),
        in_specs=[
            pl.BlockSpec((TR, 16, CH), lambda i: (0, 0, 0)),
            pl.BlockSpec((TR, 16, CH), lambda i: (0, 1, 0)),
        ],
        out_specs=(pl.BlockSpec((TR, CH), lambda i: (0, 0)),) * 2,
        name="edges",
    )(values, values)
    left = shift(last, "col", 1)
    right = shift(first, "col", -1)
    up, down = pl.pallas_call(
        line_kernel,
        out_shape=(shape((TC + 16, CH), bf16),) * 2,
        grid=(1,),
        in_specs=[
            pl.BlockSpec((1, TC, CH), lambda i: (0, 0, 0)),
            pl.BlockSpec((1, TC, CH), lambda i: (TR - 1, 0, 0)),
            pl.BlockSpec((TR, CH), lambda i: (0, 0)),
            pl.BlockSpec((TR, CH), lambda i: (0, 0)),
        ],
        out_specs=(pl.BlockSpec((TC + 16, CH), lambda i: (0, 0)),) * 2,
        name="lines",
    )(values, values, left, right)
    above = shift(down, "row", 1)
    below = shift(up, "row", -1)
    convolved = call(
        conv_kernel,
        shape((N, CH), f32),
        6,
        scratch=[pltpu.VMEM((TR, CH), f32), pltpu.VMEM((TR, CH), f32)],
        nbytes=8 * mb,
        name="conv",
    )(values, left, right, above, below, conv_weight)

    summed, stats = call(
        attend_kernel,
        (shape((N, CH), f32), shape((2 * BLOCKS, 128), f32)),
        4,
        nbytes=8 * mb,
        name="attend",
    )(agent_values, prob, recip, convolved)
    heads = lax.axis_size("head")
    others = [
        lax.ppermute(stats, "head", [(i, (i + d) % heads) for i in range(heads)])
        for d in range(1, heads)
    ]
    normed = call(norm_kernel, shape((N, CH), bf16), 7, nbytes=4 * mb, name="norm")(
        stats, *others, summed, norm_gain.reshape(1, CH), norm_bias.reshape(1, CH)
    )
    return normed.reshape(TR, TC, CH)


def solution(mesh):
    in_specs = (
        P("row", "col", "head"),
        P("row", "col", "head"),
        P("row", "col", "head"),
        P(None, "row", "col"),
        P(None, "head"),
        P("head"),
        P("head"),
    )
    out_specs = P("row", "col", "head")
    return jax.shard_map(shards, mesh=mesh, in_specs=in_specs, out_specs=out_specs, check_vma=False)
```

```python
import math

import jax
import jax.numpy as jnp
from jax import lax
from jax.experimental import pallas as pl
from jax.experimental.pallas import tpu as pltpu
from jax.sharding import PartitionSpec as P

HD = 64
D = 1024
AGR = 4
TR = 48
TC = 32
CH = 256
N = TR * TC
AGENTS = 256
TILES = 64
LOCAL_HEADS = 4
ROWS = LOCAL_HEADS * AGENTS // TILES
BLOCKS = N // 128

f32 = jnp.float32
bf16 = jnp.bfloat16
epsilon = 1e-05

VMEM_SPEC = pl.BlockSpec(memory_space=pltpu.VMEM)


def call(kernel, out_shape, n_in, scratch=(), flops=0, nbytes=0, name=None):
    outs = jax.tree.map(lambda s: VMEM_SPEC, out_shape)
    return pl.pallas_call(
        kernel,
        out_shape=out_shape,
        in_specs=[VMEM_SPEC] * n_in,
        out_specs=outs,
        scratch_shapes=list(scratch),
        compiler_params=pltpu.CompilerParams(vmem_limit_bytes=12 * 1024 * 1024),
        cost_estimate=pl.CostEstimate(flops=flops, bytes_accessed=nbytes, transcendentals=0),
        name=name,
    )


def shape(dims, dtype):
    return jax.ShapeDtypeStruct(dims, dtype)


def lanes(dims):
    return lax.broadcasted_iota(jnp.int32, dims, len(dims) - 1)


def turn_matrix():
    source = lax.broadcasted_iota(jnp.int32, (CH, CH), 0)
    target = lax.broadcasted_iota(jnp.int32, (CH, CH), 1)
    low = (target & 31) < 16
    minus = jnp.where(low & (source == target + 16), -1.0, 0.0)
    plus = jnp.where((~low) & (source == target - 16), 1.0, 0.0)
    return (minus + plus).astype(bf16)


def sin_cos(angle):
    return jnp.sin(angle), jnp.cos(angle)


def turned(x, matrix, cosine, sine):
    swapped = jnp.dot(x, matrix, preferred_element_type=f32)
    return (x.astype(f32) * cosine + swapped * sine).astype(bf16)


def cell_tables(cos_r, sin_r, cos_c, sin_c, first, rows):
    cosine = jnp.concatenate(
        [cos_r[first + i : first + i + 1, :] * cos_c for i in range(rows)], axis=0
    )
    sine = jnp.concatenate(
        [sin_r[first + i : first + i + 1, :] + sin_c for i in range(rows)], axis=0
    )
    return cosine, sine


def query_kernel(
    pos_ref, freq_ref, q_ref, tq_ref, agents_ref, tab_r_ref, tab_c_ref, turn_ref, held_ref, sems
):
    step = N // AGR
    copies = []
    for cell in range(AGR):
        part = pl.ds(cell * step, step)
        copy = pltpu.make_async_copy(q_ref.at[part, :], held_ref.at[part, :], sems.at[cell])
        copy.start()
        copies.append(copy)
    freq = freq_ref[...]
    row_line = pos_ref[0][0:1, :].astype(f32)
    col_pos = pos_ref[1][:, 0:1].astype(f32)
    eye = lax.broadcasted_iota(jnp.int32, (TR, TR), 0) == lax.broadcasted_iota(
        jnp.int32, (TR, TR), 1
    )
    row_pos = jnp.sum(jnp.where(eye, jnp.broadcast_to(row_line, (TR, TR)), 0.0), 1, keepdims=True)
    angles = jnp.concatenate([row_pos * freq[0:1, :], col_pos * freq[1:2, :]], axis=0)
    sines, cosines = sin_cos(angles)
    sines = jnp.concatenate([sines, sines], axis=1)
    cosines = jnp.concatenate([cosines, cosines], axis=1)
    tab_r_ref[0] = cosines[:TR]
    tab_r_ref[1] = sines[:TR]
    tab_c_ref[0] = cosines[TR:]
    tab_c_ref[1] = sines[TR:]
    matrix = turn_matrix()
    turn_ref[...] = matrix
    means = []
    for cell in range(AGR):
        cosine, sine = cell_tables(
            cosines[:TR], sines[:TR], cosines[TR:], sines[TR:], cell * (TR // AGR), TR // AGR
        )
        copies[cell].wait()
        rotated = turned(held_ref[pl.ds(cell * step, step), :], matrix, cosine, sine)
        tq_ref[pl.ds(cell * step, step), :] = rotated
        mean = jnp.sum(rotated.astype(f32), 0, keepdims=True) / step
        means.append(mean.astype(bf16).astype(f32))
    packed = jnp.concatenate([m[:, :128] for m in means] + [m[:, 128:] for m in means], axis=0)
    agents_ref[...] = jnp.broadcast_to(packed.astype(bf16)[None], (TILES, 8, 128))


def key_kernel(tab_r_ref, tab_c_ref, turn_ref, k_ref, v_ref, tk_ref, first_ref, last_ref):
    first_ref[...] = v_ref[:, 0, :]
    last_ref[...] = v_ref[:, TC - 1, :]
    matrix = turn_ref[...]
    step = N // AGR
    for cell in range(AGR):
        cosine, sine = cell_tables(
            tab_r_ref[0], tab_r_ref[1], tab_c_ref[0], tab_c_ref[1], cell * (TR // AGR), TR // AGR
        )
        tk_ref[pl.ds(cell * step, step), :] = turned(
            k_ref[pl.ds(cell * step, step), :], matrix, cosine, sine
        )


def agent_pairs(agents_ref, wide_ref, scale):
    wide_ref[...] = agents_ref[...].astype(f32).reshape(TILES * 8, 128) * scale
    pairs = []
    for pair in range(2):
        parts = [wide_ref[pl.ds(4 * pair + k, TILES, stride=8), :] for k in range(AGR)]
        pairs.append(jnp.concatenate(parts, axis=0).astype(bf16))
    return pairs


def half_mask(dims, parity):
    return (lanes(dims) // HD) == parity


def partial_kernel(agents_ref, tk_ref, v_ref, out_ref, score_ref, wide_ref):
    pairs = agent_pairs(agents_ref, wide_ref, 1.0 / math.sqrt(HD))
    chunk = 512
    for head in range(LOCAL_HEADS):
        pair, parity = head // 2, head % 2
        cols = pl.ds(pair * 128, 128)
        own = pairs[pair]
        own = jnp.where(half_mask(own.shape, parity), own, jnp.zeros_like(own))
        peak = None
        for c in range(N // chunk):
            scores = lax.dot_general(
                own,
                tk_ref[pl.ds(c * chunk, chunk), cols],
                (((1,), (1,)), ((), ())),
                preferred_element_type=f32,
            )
            score_ref[:, pl.ds(c * chunk, chunk)] = scores
            for s in range(chunk // 128):
                piece = scores[:, s * 128 : (s + 1) * 128]
                peak = piece if peak is None else jnp.maximum(peak, piece)
        peak = jnp.max(peak, 1, keepdims=True)
        acc = jnp.zeros((AGENTS, 128), f32)
        for c in range(N // chunk):
            weights = jnp.exp(score_ref[:, pl.ds(c * chunk, chunk)] - peak).astype(bf16)
            block = v_ref[pl.ds(c * chunk, chunk), cols]
            block = jnp.where(half_mask(block.shape, parity), block, jnp.ones_like(block))
            acc = acc + jnp.dot(weights, block, preferred_element_type=f32)
        other = pltpu.roll(acc, HD, 1)
        numer, total = (acc, other) if parity == 0 else (other, acc)
        logs = peak + jnp.log(total)
        values = numer / total
        logs = jnp.max(jnp.where(half_mask(logs.shape, 0), logs, -3e38), 1, keepdims=True)
        first = logs.astype(bf16).astype(f32)
        second = (logs - first).astype(bf16).astype(f32)
        third = logs - first - second
        lane = lanes((AGENTS, 128))
        packed = jnp.where(
            lane < HD,
            values,
            jnp.where(
                lane == HD,
                first,
                jnp.where(lane == HD + 1, second, jnp.where(lane == HD + 2, third, 0.0)),
            ),
        )
        groups = packed.reshape(2, ROWS, 8, 128)
        out_ref[pl.ds(head * ROWS, ROWS)] = jnp.concatenate([groups[0], groups[1]], 1).astype(bf16)


def merge_kernel(parts_ref, out_ref):
    source = lax.broadcasted_iota(jnp.int32, (128, 128), 0)
    picker = jnp.where((source >= HD) & (source < HD + 3), 1.0, 0.0).astype(bf16)
    parts = parts_ref[...].reshape(TILES * ROWS, 128)
    logs = jnp.dot(parts, picker, preferred_element_type=f32).reshape(TILES, ROWS, 128)
    values = parts.astype(f32).reshape(TILES, ROWS, 128)
    peak = jnp.max(logs, 0)
    weights = jnp.exp(logs - peak[None])
    merged = jnp.sum(weights * values, 0) / jnp.sum(weights, 0)
    merged = jnp.where(lanes((8, 128)) < HD, merged[:8], pltpu.roll(merged[8:], HD, 1))
    out_ref[...] = jnp.broadcast_to(merged.astype(bf16)[None], (TILES, 8, 128))


def probability_kernel(agents_ref, tq_ref, prob_ref, wide_ref):
    pairs = agent_pairs(agents_ref, wide_ref, 1.0 / math.sqrt(HD))
    ones = jnp.ones((AGENTS, 128), bf16)
    owns = []
    for head in range(LOCAL_HEADS):
        own = pairs[head // 2]
        owns.append(jnp.where(half_mask(own.shape, head % 2), own, jnp.zeros_like(own)))
    chunk = 256

    def body(c, carry):
        rows = pl.ds(pl.multiple_of(c * chunk, chunk), chunk)
        for head in range(LOCAL_HEADS):
            scores = lax.dot_general(
                tq_ref[rows, pl.ds(head // 2 * 128, 128)],
                owns[head],
                (((1,), (1,)), ((), ())),
                preferred_element_type=f32,
            )
            weights = jnp.exp(scores - jnp.max(scores, 1, keepdims=True))
            total = jnp.dot(weights.astype(bf16), ones, preferred_element_type=f32)
            scale = 1.0 / total
            scale = jnp.concatenate([scale, scale], axis=1)
            prob_ref[rows, pl.ds(head * AGENTS, AGENTS)] = (weights * scale).astype(bf16)
        return carry

    lax.fori_loop(0, N // chunk, body, 0)


def line_kernel(v_top_ref, v_bottom_ref, left_ref, right_ref, up_ref, down_ref):
    for v_ref, row, out_ref in ((v_top_ref, 0, up_ref), (v_bottom_ref, TR - 1, down_ref)):
        out_ref[pl.ds(0, TC), :] = v_ref[0]
        left = left_ref[row : row + 1, :].astype(f32)
        right = right_ref[row : row + 1, :].astype(f32)
        tail = jnp.concatenate([left, right, jnp.zeros((14, CH), f32)], axis=0)
        out_ref[pl.ds(TC, 16), :] = tail.astype(bf16)


def conv_kernel(v_ref, left_ref, right_ref, above_ref, below_ref, w_ref, out_ref, l_ref, r_ref):
    l_ref[...] = left_ref[...].astype(f32)
    r_ref[...] = right_ref[...].astype(f32)
    for half in range(2):
        cols = pl.ds(half * 128, 128)
        w = [jnp.broadcast_to(w_ref[t : t + 1, cols], (TC, 128)) for t in range(9)]
        column = lax.broadcasted_iota(jnp.int32, (TC, 128), 0)

        def taps(row, left, right):
            row = row.astype(f32)
            before = jnp.where(column == 0, left, pltpu.roll(row, 1, 0))
            after = jnp.where(column == TC - 1, right, pltpu.roll(row, TC - 1, 0))
            return [before * w[3 * d] + row * w[3 * d + 1] + after * w[3 * d + 2] for d in range(3)]

        tail = above_ref[pl.ds(TC, 16), cols].astype(f32)
        t0 = taps(above_ref[pl.ds(0, TC), cols], tail[0:1], tail[1:2])

        def group(start, carry):
            a, b = carry
            lefts, rights = l_ref[pl.ds(start, 8), cols], r_ref[pl.ds(start, 8), cols]
            for k in range(8):
                t = taps(v_ref[start + k, :, cols], lefts[k : k + 1], rights[k : k + 1])
                if a is not None:
                    at = (start + k - 1) * TC
                    if not isinstance(at, int):
                        at = pl.multiple_of(at, TC)
                    out_ref[pl.ds(at, TC), cols] = a + t[2]
                a, b = b + t[1], t[0]
            return a, b

        carry = group(0, (None, t0[0]))
        a, b = lax.fori_loop(
            1, TR // 8, lambda g, c: group(pl.multiple_of(g * 8, 8), c), carry
        )
        tail = below_ref[pl.ds(TC, 16), cols].astype(f32)
        t = taps(below_ref[pl.ds(0, TC), cols], tail[0:1], tail[1:2])
        out_ref[pl.ds((TR - 1) * TC, TC), cols] = a + t[2]


def attend_kernel(av_ref, prob_ref, conv_ref, sum_ref, stat_ref):
    halves = []
    for pair in range(2):
        pieces = []
        for parity in range(2):
            part = av_ref[pl.ds((2 * pair + parity) * ROWS, ROWS)].astype(f32).reshape(128, 128)
            other = pltpu.roll(part, HD, 1)
            own = half_mask(part.shape, parity)
            for piece in (part, other) if parity == 0 else (other, part):
                pieces.append(jnp.where(own, piece, 0.0))
        halves.append(jnp.concatenate(pieces, axis=0).astype(bf16))
    eye = lax.broadcasted_iota(jnp.int32, (128, 128), 0) == lanes((128, 128))

    for b in range(BLOCKS):
        rows = pl.ds(b * 128, 128)
        xs = []
        for pair in range(2):
            cols = pl.ds(pair * 128, 128)
            attended = jnp.dot(
                prob_ref[rows, pl.ds(pair * 2 * AGENTS, 2 * AGENTS)],
                halves[pair],
                preferred_element_type=f32,
            )
            x = attended + conv_ref[rows, cols]
            sum_ref[rows, cols] = x
            xs.append(x)
        mean = jnp.sum(xs[0] + xs[1], 1, keepdims=True) * (1.0 / CH)
        c0, c1 = xs[0] - mean, xs[1] - mean
        squares = jnp.sum(c0 * c0 + c1 * c1, 1, keepdims=True)
        stat_ref[b : b + 1, :] = jnp.sum(jnp.where(eye, mean, 0.0), 0, keepdims=True)
        stat_ref[BLOCKS + b : BLOCKS + b + 1, :] = jnp.sum(
            jnp.where(eye, squares, 0.0), 0, keepdims=True
        )


def norm_kernel(s0_ref, s1_ref, s2_ref, s3_ref, sum_ref, gain_ref, bias_ref, out_ref):
    stats = [s[...] for s in (s0_ref, s1_ref, s2_ref, s3_ref)]
    means = [s[:BLOCKS] for s in stats]
    mean = (means[0] + means[1] + means[2] + means[3]) * 0.25
    squares = sum(s[BLOCKS:] for s in stats)
    for m in means:
        squares = squares + CH * (m - mean) * (m - mean)
    scale = lax.rsqrt(squares * (1.0 / D) + epsilon)
    for b in range(BLOCKS):
        rows = pl.ds(b * 128, 128)
        m = jnp.broadcast_to(mean[b : b + 1], (128, 128)).T
        s = jnp.broadcast_to(scale[b : b + 1], (128, 128)).T
        for half in range(2):
            cols = pl.ds(half * 128, 128)
            out_ref[rows, cols] = (
                (sum_ref[rows, cols] - m) * s * gain_ref[0:1, cols] + bias_ref[0:1, cols]
            ).astype(bf16)


def frequencies():
    lane = jnp.arange(128) % HD
    power = jnp.power(f32(100.0), -(lane % 16).astype(f32) / 16)
    return jnp.stack([jnp.where(lane < 32, power, 0.0), jnp.where(lane < 32, 0.0, power)])


def spread(x):
    return lax.all_to_all(x, ("row", "col"), 0, 0)


def shift(x, axis, step):
    count = lax.axis_size(axis)
    pairs = [(i, i + step) for i in range(count) if 0 <= i + step < count]
    return lax.ppermute(x, axis, pairs)


def after(x, *others):
    return lax.optimization_barrier((x, *others))[0]


def shards(queries, keys, values, positions, conv_weight, norm_gain, norm_bias):
    q = queries.reshape(N, CH)
    k = keys.reshape(N, CH)
    v = values.reshape(N, CH)
    mb = 1 << 20
    wide = pltpu.VMEM((TILES * 8, 128), f32)
    tq, packed, tab_r, tab_c, turn = pl.pallas_call(
        query_kernel,
        out_shape=(
            shape((N, CH), bf16),
            shape((TILES, 8, 128), bf16),
            shape((2, TR, CH), f32),
            shape((2, TC, CH), f32),
            shape((CH, CH), bf16),
        ),
        in_specs=[VMEM_SPEC, VMEM_SPEC, pl.BlockSpec(memory_space=pltpu.HBM)],
        out_specs=(VMEM_SPEC,) * 5,
        scratch_shapes=[pltpu.VMEM((N, CH), bf16), pltpu.SemaphoreType.DMA((AGR,))],
        compiler_params=pltpu.CompilerParams(vmem_limit_bytes=12 * 1024 * 1024),
        cost_estimate=pl.CostEstimate(flops=0, bytes_accessed=8 * mb, transcendentals=0),
        name="turn_queries",
    )(jnp.swapaxes(positions, 1, 2), frequencies(), q)
    agents = spread(packed)
    tk, first, last = call(
        key_kernel,
        (shape((N, CH), bf16), shape((TR, CH), bf16), shape((TR, CH), bf16)),
        5,
        nbytes=4 * mb,
        name="turn_keys",
    )(tab_r, tab_c, turn, k, values)
    left = shift(last, "col", 1)
    right = shift(first, "col", -1)
    agents = after(agents, left, right)
    parts = call(
        partial_kernel,
        shape((TILES, ROWS, 128), bf16),
        3,
        scratch=[pltpu.VMEM((AGENTS, N), f32), wide],
        nbytes=10 * mb,
        name="partials",
    )(agents, tk, v)
    received = spread(parts)
    up, down = pl.pallas_call(
        line_kernel,
        out_shape=(shape((TC + 16, CH), bf16),) * 2,
        grid=(1,),
        in_specs=[
            pl.BlockSpec((1, TC, CH), lambda i: (0, 0, 0)),
            pl.BlockSpec((1, TC, CH), lambda i: (TR - 1, 0, 0)),
            pl.BlockSpec((TR, CH), lambda i: (0, 0)),
            pl.BlockSpec((TR, CH), lambda i: (0, 0)),
        ],
        out_specs=(pl.BlockSpec((TC + 16, CH), lambda i: (0, 0)),) * 2,
        name="lines",
    )(values, values, left, right)
    above = shift(down, "row", 1)
    below = shift(up, "row", -1)
    received = after(received, above, below)
    merged = call(merge_kernel, shape((TILES, 8, 128), bf16), 1, nbytes=2 * mb, name="merge")(
        received
    )
    agent_values = spread(merged)
    prob = call(
        probability_kernel,
        shape((N, LOCAL_HEADS * AGENTS), bf16),
        2,
        scratch=[wide],
        nbytes=15 * mb,
        name="probabilities",
    )(agents, tq)
    convolved = call(
        conv_kernel,
        shape((N, CH), f32),
        6,
        scratch=[pltpu.VMEM((TR, CH), f32), pltpu.VMEM((TR, CH), f32)],
        nbytes=4 * mb,
        name="conv",
    )(values, left, right, above, below, conv_weight)
    summed, stats = call(
        attend_kernel,
        (shape((N, CH), f32), shape((2 * BLOCKS, 128), f32)),
        3,
        nbytes=4 * mb,
        name="attend",
    )(agent_values, prob, convolved)
    heads = lax.axis_size("head")
    others = [
        lax.ppermute(stats, "head", [(i, (i + d) % heads) for i in range(heads)])
        for d in range(1, heads)
    ]
    normed = call(norm_kernel, shape((N, CH), bf16), 7, nbytes=4 * mb, name="norm")(
        stats, *others, summed, norm_gain.reshape(1, CH), norm_bias.reshape(1, CH)
    )
    return normed.reshape(TR, TC, CH)


def solution(mesh):
    in_specs = (
        P("row", "col", "head"),
        P("row", "col", "head"),
        P("row", "col", "head"),
        P(None, "row", "col"),
        P(None, "head"),
        P("head"),
        P("head"),
    )
    out_specs = P("row", "col", "head")
    return jax.shard_map(shards, mesh=mesh, in_specs=in_specs, out_specs=out_specs, check_vma=False)
```

```python
import math

import jax
import jax.numpy as jnp
from jax import lax
from jax.experimental import pallas as pl
from jax.experimental.pallas import tpu as pltpu
from jax.sharding import PartitionSpec as P

HD = 64
D = 1024
AGR = 4
TR = 48
TC = 32
CH = 256
N = TR * TC
AGENTS = 256
TILES = 64
LOCAL_HEADS = 4
ROWS = LOCAL_HEADS * AGENTS // TILES
BLOCKS = N // 128

f32 = jnp.float32
bf16 = jnp.bfloat16
epsilon = 1e-05

VMEM_SPEC = pl.BlockSpec(memory_space=pltpu.VMEM)
HBM_SPEC = pl.BlockSpec(memory_space=pltpu.HBM)


def call(kernel, outs, in_spaces, scratch=(), nbytes=0, name=None, out_spaces=None):
    fn = pl.pallas_call(
        kernel,
        out_shape=outs,
        in_specs=[HBM_SPEC if c == "h" else VMEM_SPEC for c in in_spaces],
        out_specs=(
            tuple(HBM_SPEC if c == "h" else VMEM_SPEC for c in out_spaces or " " * len(outs))
            if isinstance(outs, tuple)
            else VMEM_SPEC
        ),
        scratch_shapes=list(scratch),
        compiler_params=pltpu.CompilerParams(vmem_limit_bytes=12 * 1024 * 1024),
        cost_estimate=pl.CostEstimate(flops=0, bytes_accessed=nbytes, transcendentals=0),
        name=name,
    )

    def run(*args):
        spaces = {"h": pltpu.HBM, "v": pltpu.VMEM}
        return fn(
            *[
                pltpu.with_memory_space_constraint(x, spaces[c]) if c in spaces else x
                for x, c in zip(args, in_spaces, strict=True)
            ]
        )

    return run


def shape(dims, dtype):
    return jax.ShapeDtypeStruct(dims, dtype)


def near(dims, dtype):
    return pltpu.VMEM(dims, dtype)


def far(dims, dtype):
    return pltpu.HBM(dims, dtype)


def lanes(dims):
    return lax.broadcasted_iota(jnp.int32, dims, len(dims) - 1)


def turn_matrix():
    source = lax.broadcasted_iota(jnp.int32, (CH, CH), 0)
    target = lax.broadcasted_iota(jnp.int32, (CH, CH), 1)
    low = (target & 31) < 16
    minus = jnp.where(low & (source == target + 16), -1.0, 0.0)
    plus = jnp.where((~low) & (source == target - 16), 1.0, 0.0)
    return (minus + plus).astype(bf16)


def sin_cos(angle):
    return jnp.sin(angle), jnp.cos(angle)


def turned(x, matrix, cosine, sine):
    swapped = jnp.dot(x, matrix, preferred_element_type=f32)
    return (x.astype(f32) * cosine + swapped * sine).astype(bf16)


def cell_tables(cos_r, sin_r, cos_c, sin_c, first, rows):
    cosine = jnp.concatenate(
        [cos_r[first + i : first + i + 1, :] * cos_c for i in range(rows)], axis=0
    )
    sine = jnp.concatenate(
        [sin_r[first + i : first + i + 1, :] + sin_c for i in range(rows)], axis=0
    )
    return cosine, sine


def slots(block):
    twice = jnp.concatenate([block, block], axis=0).astype(bf16)
    return jnp.broadcast_to(twice[None], (TILES // 2, 16, 128)).reshape(TILES * 8, 128)


def query_kernel(
    pos_ref,
    q_ref,
    tq_ref,
    agents_ref,
    tab_r_ref,
    tab_c_ref,
    turn_ref,
    held_ref,
    done_ref,
    spot_ref,
    sems,
):
    step = N // AGR
    place = pltpu.make_async_copy(pos_ref, spot_ref, sems.at[AGR])
    place.start()
    copies = []
    for cell in range(AGR):
        part = pl.ds(cell * step, step)
        copy = pltpu.make_async_copy(q_ref.at[part, :], held_ref.at[part, :], sems.at[cell])
        copy.start()
        copies.append(copy)
    matrix = turn_matrix()
    turn_ref[...] = matrix
    lane = lanes((1, 128)) % HD
    power = jnp.exp((lane % 16).astype(f32) * f32(-math.log(100.0) / 16))
    freq_r = jnp.where(lane < 32, power, 0.0)
    freq_c = jnp.where(lane < 32, 0.0, power)
    place.wait()
    row_line = spot_ref[0][0:1, :].astype(f32)
    col_pos = spot_ref[1][:, 0:1].astype(f32)
    eye = lax.broadcasted_iota(jnp.int32, (TR, TR), 0) == lax.broadcasted_iota(
        jnp.int32, (TR, TR), 1
    )
    row_pos = jnp.sum(jnp.where(eye, jnp.broadcast_to(row_line, (TR, TR)), 0.0), 1, keepdims=True)
    angles = jnp.concatenate([row_pos * freq_r, col_pos * freq_c], axis=0)
    sines, cosines = sin_cos(angles)
    sines = jnp.concatenate([sines, sines], axis=1)
    cosines = jnp.concatenate([cosines, cosines], axis=1)
    tab_r_ref[0] = cosines[:TR]
    tab_r_ref[1] = sines[:TR]
    tab_c_ref[0] = cosines[TR:]
    tab_c_ref[1] = sines[TR:]
    means = []
    for cell in range(AGR):
        cosine, sine = cell_tables(
            cosines[:TR], sines[:TR], cosines[TR:], sines[TR:], cell * (TR // AGR), TR // AGR
        )
        copies[cell].wait()
        rotated = turned(held_ref[pl.ds(cell * step, step), :], matrix, cosine, sine)
        part = pl.ds(cell * step, step)
        done_ref[part, :] = rotated
        copies[cell] = pltpu.make_async_copy(
            done_ref.at[part, :], tq_ref.at[part, :], sems.at[AGR + 1 + cell]
        )
        copies[cell].start()
        mean = jnp.sum(rotated.astype(f32), 0, keepdims=True) / step
        means.append(mean.astype(bf16).astype(f32))
    packed = jnp.concatenate([m[:, :128] for m in means] + [m[:, 128:] for m in means], axis=0)
    agents_ref[...] = slots(packed)
    for copy in copies:
        copy.wait()


def key_kernel(
    tab_r_ref,
    tab_c_ref,
    turn_ref,
    k_ref,
    v_ref,
    tk_ref,
    first_ref,
    last_ref,
    top_ref,
    bottom_ref,
):
    top_ref[...] = v_ref[0]
    bottom_ref[...] = v_ref[TR - 1]
    first_ref[...] = v_ref[:, 0, :]
    last_ref[...] = v_ref[:, TC - 1, :]
    matrix = turn_ref[...]
    step = N // AGR
    for cell in range(AGR):
        cosine, sine = cell_tables(
            tab_r_ref[0], tab_r_ref[1], tab_c_ref[0], tab_c_ref[1], cell * (TR // AGR), TR // AGR
        )
        tk_ref[pl.ds(cell * step, step), :] = turned(
            k_ref[pl.ds(cell * step, step), :], matrix, cosine, sine
        )


def agent_pairs(agents_ref, scale):
    target = lax.broadcasted_iota(jnp.int32, (AGENTS, TILES * 8), 0)
    source = lax.broadcasted_iota(jnp.int32, (AGENTS, TILES * 8), 1)
    agents = agents_ref[...]
    pairs = []
    for pair in range(2):
        wanted = (target & (TILES - 1)) * 8 + (target // TILES) + 4 * pair
        pick = jnp.where(source == wanted, scale, 0.0).astype(bf16)
        pairs.append(jnp.dot(pick, agents, preferred_element_type=f32).astype(bf16))
    return pairs


def half_mask(dims, parity):
    return (lanes(dims) // HD) == parity


def partial_kernel(agents_ref, tk_ref, v_ref, out_ref, score_ref):
    pairs = agent_pairs(agents_ref, 1.0 / math.sqrt(HD))
    chunk = 512
    for head in range(LOCAL_HEADS):
        pair, parity = head // 2, head % 2
        cols = pl.ds(pair * 128, 128)
        own = pairs[pair]
        own = jnp.where(half_mask(own.shape, parity), own, jnp.zeros_like(own))
        peak = None
        for c in range(N // chunk):
            scores = lax.dot_general(
                own,
                tk_ref[pl.ds(c * chunk, chunk), cols],
                (((1,), (1,)), ((), ())),
                preferred_element_type=f32,
            )
            score_ref[:, pl.ds(c * chunk, chunk)] = scores
            for s in range(chunk // 128):
                piece = scores[:, s * 128 : (s + 1) * 128]
                peak = piece if peak is None else jnp.maximum(peak, piece)
        peak = jnp.max(peak, 1, keepdims=True)
        acc = jnp.zeros((AGENTS, 128), f32)
        for c in range(N // chunk):
            weights = jnp.exp(score_ref[:, pl.ds(c * chunk, chunk)] - peak).astype(bf16)
            block = v_ref[pl.ds(c * chunk, chunk), cols]
            block = jnp.where(half_mask(block.shape, parity), block, jnp.ones_like(block))
            acc = acc + jnp.dot(weights, block, preferred_element_type=f32)
        other = pltpu.roll(acc, HD, 1)
        numer, total = (acc, other) if parity == 0 else (other, acc)
        logs = peak + jnp.log(total)
        values = numer / total
        logs = jnp.max(jnp.where(half_mask(logs.shape, 0), logs, -3e38), 1, keepdims=True)
        first = logs.astype(bf16).astype(f32)
        second = (logs - first).astype(bf16).astype(f32)
        third = logs - first - second
        lane = lanes((AGENTS, 128))
        packed = jnp.where(
            lane < HD,
            values,
            jnp.where(
                lane == HD,
                first,
                jnp.where(lane == HD + 1, second, jnp.where(lane == HD + 2, third, 0.0)),
            ),
        )
        groups = packed.reshape(2, ROWS, 8, 128)
        groups = jnp.concatenate([groups[0], groups[1]], 1).reshape(AGENTS, 128)
        out_ref[pl.ds(head * AGENTS, AGENTS), :] = groups.astype(bf16)


def merge_kernel(parts_ref, out_ref):
    source = lax.broadcasted_iota(jnp.int32, (128, 128), 0)
    picker = jnp.where((source >= HD) & (source < HD + 3), 1.0, 0.0).astype(bf16)
    parts = parts_ref[...]
    logs = jnp.dot(parts, picker, preferred_element_type=f32).reshape(TILES, ROWS, 128)
    values = parts.astype(f32).reshape(TILES, ROWS, 128)
    peak = jnp.max(logs, 0)
    weights = jnp.exp(logs - peak[None])
    merged = jnp.sum(weights * values, 0) / jnp.sum(weights, 0)
    merged = jnp.where(lanes((8, 128)) < HD, merged[:8], pltpu.roll(merged[8:], HD, 1))
    out_ref[...] = slots(merged)


def probability_kernel(agents_ref, tq_ref, prob_ref, held_ref, sems):
    chunk = 256

    def fetch(c):
        rows = pl.ds(pl.multiple_of(c * chunk, chunk), chunk)
        return pltpu.make_async_copy(tq_ref.at[rows, :], held_ref.at[rows, :], sems.at[c])

    for c in range(N // chunk):
        fetch(c).start()
    pairs = agent_pairs(agents_ref, 1.0 / math.sqrt(HD))
    ones = jnp.ones((AGENTS, 128), bf16)
    owns = []
    for head in range(LOCAL_HEADS):
        own = pairs[head // 2]
        owns.append(jnp.where(half_mask(own.shape, head % 2), own, jnp.zeros_like(own)))

    def body(c, carry):
        fetch(c).wait()
        rows = pl.ds(pl.multiple_of(c * chunk, chunk), chunk)
        for head in range(LOCAL_HEADS):
            scores = lax.dot_general(
                held_ref[rows, pl.ds(head // 2 * 128, 128)],
                owns[head],
                (((1,), (1,)), ((), ())),
                preferred_element_type=f32,
            )
            weights = jnp.exp(scores - jnp.max(scores, 1, keepdims=True))
            total = jnp.dot(weights.astype(bf16), ones, preferred_element_type=f32)
            scale = 1.0 / total
            scale = jnp.concatenate([scale, scale], axis=1)
            prob_ref[rows, pl.ds(head * AGENTS, AGENTS)] = (weights * scale).astype(bf16)
        return carry

    lax.fori_loop(0, N // chunk, body, 0)


def line_kernel(top_ref, bottom_ref, left_ref, right_ref, up_ref, down_ref):
    for line_ref, row, out_ref in ((top_ref, 0, up_ref), (bottom_ref, TR - 1, down_ref)):
        out_ref[pl.ds(0, TC), :] = line_ref[...]
        left = left_ref[row : row + 1, :].astype(f32)
        right = right_ref[row : row + 1, :].astype(f32)
        tail = jnp.concatenate([left, right, jnp.zeros((14, CH), f32)], axis=0)
        out_ref[pl.ds(TC, 16), :] = tail.astype(bf16)


def conv_kernel(v_ref, left_ref, right_ref, above_ref, below_ref, w_ref, out_ref, l_ref, r_ref):
    l_ref[...] = left_ref[...].astype(f32)
    r_ref[...] = right_ref[...].astype(f32)
    for half in range(2):
        cols = pl.ds(half * 128, 128)
        w = [jnp.broadcast_to(w_ref[t : t + 1, cols], (TC, 128)) for t in range(9)]
        column = lax.broadcasted_iota(jnp.int32, (TC, 128), 0)

        def taps(row, left, right):
            row = row.astype(f32)
            before = jnp.where(column == 0, left, pltpu.roll(row, 1, 0))
            after = jnp.where(column == TC - 1, right, pltpu.roll(row, TC - 1, 0))
            return [before * w[3 * d] + row * w[3 * d + 1] + after * w[3 * d + 2] for d in range(3)]

        tail = above_ref[pl.ds(TC, 16), cols].astype(f32)
        t0 = taps(above_ref[pl.ds(0, TC), cols], tail[0:1], tail[1:2])

        def group(start, carry):
            a, b = carry
            lefts, rights = l_ref[pl.ds(start, 8), cols], r_ref[pl.ds(start, 8), cols]
            for k in range(8):
                t = taps(v_ref[start + k, :, cols], lefts[k : k + 1], rights[k : k + 1])
                if a is not None:
                    at = (start + k - 1) * TC
                    if not isinstance(at, int):
                        at = pl.multiple_of(at, TC)
                    out_ref[pl.ds(at, TC), cols] = a + t[2]
                a, b = b + t[1], t[0]
            return a, b

        carry = group(0, (None, t0[0]))
        a, b = lax.fori_loop(
            1, TR // 8, lambda g, c: group(pl.multiple_of(g * 8, 8), c), carry
        )
        tail = below_ref[pl.ds(TC, 16), cols].astype(f32)
        t = taps(below_ref[pl.ds(0, TC), cols], tail[0:1], tail[1:2])
        out_ref[pl.ds((TR - 1) * TC, TC), cols] = a + t[2]


def attend_kernel(av_ref, prob_ref, conv_hbm_ref, sum_ref, stat_ref, conv_ref, sems):
    step = N // AGR
    copies = []
    for c in range(AGR):
        part = pl.ds(c * step, step)
        copies.append(
            pltpu.make_async_copy(conv_hbm_ref.at[part, :], conv_ref.at[part, :], sems.at[c])
        )
        copies[c].start()
    halves = []
    for pair in range(2):
        pieces = []
        for parity in range(2):
            part = av_ref[pl.ds((2 * pair + parity) * 128, 128), :].astype(f32)
            other = pltpu.roll(part, HD, 1)
            own = half_mask(part.shape, parity)
            for piece in (part, other) if parity == 0 else (other, part):
                pieces.append(jnp.where(own, piece, 0.0))
        halves.append(jnp.concatenate(pieces, axis=0).astype(bf16))
    eye = lax.broadcasted_iota(jnp.int32, (128, 128), 0) == lanes((128, 128))

    for b in range(BLOCKS):
        if b * 128 % step == 0:
            copies[b * 128 // step].wait()
        rows = pl.ds(b * 128, 128)
        xs = []
        for pair in range(2):
            cols = pl.ds(pair * 128, 128)
            attended = jnp.dot(
                prob_ref[rows, pl.ds(pair * 2 * AGENTS, 2 * AGENTS)],
                halves[pair],
                preferred_element_type=f32,
            )
            x = attended + conv_ref[rows, cols]
            sum_ref[rows, cols] = x
            xs.append(x)
        mean = jnp.sum(xs[0] + xs[1], 1, keepdims=True) * (1.0 / CH)
        c0, c1 = xs[0] - mean, xs[1] - mean
        squares = jnp.sum(c0 * c0 + c1 * c1, 1, keepdims=True)
        stat_ref[b : b + 1, :] = jnp.sum(jnp.where(eye, mean, 0.0), 0, keepdims=True)
        stat_ref[BLOCKS + b : BLOCKS + b + 1, :] = jnp.sum(
            jnp.where(eye, squares, 0.0), 0, keepdims=True
        )


def norm_kernel(s0_ref, s1_ref, s2_ref, s3_ref, sum_ref, gain_ref, bias_ref, out_ref):
    stats = [s[...] for s in (s0_ref, s1_ref, s2_ref, s3_ref)]
    means = [s[:BLOCKS] for s in stats]
    mean = (means[0] + means[1] + means[2] + means[3]) * 0.25
    squares = sum(s[BLOCKS:] for s in stats)
    for m in means:
        squares = squares + CH * (m - mean) * (m - mean)
    scale = lax.rsqrt(squares * (1.0 / D) + epsilon)
    for b in range(BLOCKS):
        rows = pl.ds(b * 128, 128)
        m = jnp.broadcast_to(mean[b : b + 1], (128, 128)).T
        s = jnp.broadcast_to(scale[b : b + 1], (128, 128)).T
        for half in range(2):
            cols = pl.ds(half * 128, 128)
            out_ref[rows, cols] = (
                (sum_ref[rows, cols] - m) * s * gain_ref[0:1, cols] + bias_ref[0:1, cols]
            ).astype(bf16)


def spread(x):
    slot = x.reshape(TILES, x.shape[0] // TILES, 128)
    return lax.all_to_all(slot, ("row", "col"), 0, 0).reshape(x.shape)


def shift(x, axis, step):
    count = lax.axis_size(axis)
    pairs = [(i, i + step) for i in range(count) if 0 <= i + step < count]
    return lax.ppermute(x, axis, pairs)


def after(x, *others):
    return lax.optimization_barrier((x, *others))[0]


def shards(queries, keys, values, positions, conv_weight, norm_gain, norm_bias):
    q = queries.reshape(N, CH)
    k = keys.reshape(N, CH)
    v = values.reshape(N, CH)
    mb = 1 << 20
    tq, packed, tab_r, tab_c, turn = call(
        query_kernel,
        (
            far((N, CH), bf16),
            shape((TILES * 8, 128), bf16),
            near((2, TR, CH), f32),
            near((2, TC, CH), f32),
            near((CH, CH), bf16),
        ),
        "hh",
        scratch=[
            pltpu.VMEM((N, CH), bf16),
            pltpu.VMEM((N, CH), bf16),
            pltpu.VMEM((2, TC, TR), jnp.int32),
            pltpu.SemaphoreType.DMA((2 * AGR + 1,)),
        ],
        out_spaces="h    ",
        nbytes=8 * mb,
        name="turn_queries",
    )(jnp.swapaxes(positions, 1, 2), q)
    agents = spread(packed)
    tk, first, last, top, bottom = call(
        key_kernel,
        (near((N, CH), bf16),) + (near((TR, CH), bf16),) * 2 + (near((TC, CH), bf16),) * 2,
        "vvv  ",
        nbytes=4 * mb,
        name="turn_keys",
    )(tab_r, tab_c, turn, k, values)
    left = shift(last, "col", 1)
    right = shift(first, "col", -1)
    parts = call(
        partial_kernel,
        shape((TILES * ROWS, 128), bf16),
        " v ",
        scratch=[pltpu.VMEM((AGENTS, N), f32)],
        nbytes=10 * mb,
        name="partials",
    )(agents, tk, v)
    parts = after(parts, left, right)
    received = spread(parts)
    up, down = call(
        line_kernel, (near((TC + 16, CH), bf16),) * 2, "vvvv", nbytes=mb // 4, name="lines"
    )(top, bottom, left, right)
    above = shift(down, "row", 1)
    below = shift(up, "row", -1)
    received = after(received, up, down)
    merged = call(merge_kernel, shape((TILES * 8, 128), bf16), " ", nbytes=2 * mb, name="merge")(
        received
    )
    merged = after(merged, above, below)
    agent_values = spread(merged)
    prob = call(
        probability_kernel,
        near((N, LOCAL_HEADS * AGENTS), bf16),
        " h",
        scratch=[pltpu.VMEM((N, CH), bf16), pltpu.SemaphoreType.DMA((N // 256,))],
        nbytes=15 * mb,
        name="probabilities",
    )(agents, tq)
    convolved = call(
        conv_kernel,
        far((N, CH), f32),
        " vvvv ",
        scratch=[pltpu.VMEM((TR, CH), f32), pltpu.VMEM((TR, CH), f32)],
        nbytes=4 * mb,
        name="conv",
    )(values, left, right, above, below, conv_weight)
    summed, stats = call(
        attend_kernel,
        (near((N, CH), f32), near((2 * BLOCKS, 128), f32)),
        " vh",
        scratch=[pltpu.VMEM((N, CH), f32), pltpu.SemaphoreType.DMA((AGR,))],
        nbytes=4 * mb,
        name="attend",
    )(agent_values, prob, convolved)
    heads = lax.axis_size("head")
    others = [
        lax.ppermute(stats, "head", [(i, (i + d) % heads) for i in range(heads)])
        for d in range(1, heads)
    ]
    normed = call(norm_kernel, shape((N, CH), bf16), "v   v  ", nbytes=4 * mb, name="norm")(
        stats, *others, summed, norm_gain.reshape(1, CH), norm_bias.reshape(1, CH)
    )
    return normed.reshape(TR, TC, CH)


def solution(mesh):
    in_specs = (
        P("row", "col", "head"),
        P("row", "col", "head"),
        P("row", "col", "head"),
        P(None, "row", "col"),
        P(None, "head"),
        P("head"),
        P("head"),
    )
    out_specs = P("row", "col", "head")
    return jax.shard_map(shards, mesh=mesh, in_specs=in_specs, out_specs=out_specs, check_vma=False)
```

```python
import math

import jax
import jax.numpy as jnp
from jax import lax
from jax.experimental import pallas as pl
from jax.experimental.pallas import tpu as pltpu
from jax.sharding import PartitionSpec as P

HD = 64
D = 1024
AGR = 4
TR = 48
TC = 32
CH = 256
N = TR * TC
AGENTS = 256
TILES = 64
LOCAL_HEADS = 4
ROWS = LOCAL_HEADS * AGENTS // TILES
BLOCKS = N // 128

f32 = jnp.float32
bf16 = jnp.bfloat16
epsilon = 1e-05

VMEM_SPEC = pl.BlockSpec(memory_space=pltpu.VMEM)
HBM_SPEC = pl.BlockSpec(memory_space=pltpu.HBM)


def call(kernel, outs, in_spaces, scratch=(), nbytes=0, name=None, out_spaces=None):
    fn = pl.pallas_call(
        kernel,
        out_shape=outs,
        in_specs=[HBM_SPEC if c == "h" else VMEM_SPEC for c in in_spaces],
        out_specs=(
            tuple(HBM_SPEC if c == "h" else VMEM_SPEC for c in out_spaces or " " * len(outs))
            if isinstance(outs, tuple)
            else VMEM_SPEC
        ),
        scratch_shapes=list(scratch),
        compiler_params=pltpu.CompilerParams(vmem_limit_bytes=20 * 1024 * 1024),
        cost_estimate=pl.CostEstimate(flops=0, bytes_accessed=nbytes, transcendentals=0),
        name=name,
    )

    def run(*args):
        spaces = {"h": pltpu.HBM, "v": pltpu.VMEM}
        return fn(
            *[
                pltpu.with_memory_space_constraint(x, spaces[c]) if c in spaces else x
                for x, c in zip(args, in_spaces, strict=True)
            ]
        )

    return run


def shape(dims, dtype):
    return jax.ShapeDtypeStruct(dims, dtype)


def near(dims, dtype):
    return pltpu.VMEM(dims, dtype)


def far(dims, dtype):
    return pltpu.HBM(dims, dtype)


def lanes(dims):
    return lax.broadcasted_iota(jnp.int32, dims, len(dims) - 1)


def turn_matrix():
    source = lax.broadcasted_iota(jnp.int32, (CH, CH), 0)
    target = lax.broadcasted_iota(jnp.int32, (CH, CH), 1)
    low = (target & 31) < 16
    minus = jnp.where(low & (source == target + 16), -1.0, 0.0)
    plus = jnp.where((~low) & (source == target - 16), 1.0, 0.0)
    return (minus + plus).astype(bf16)


def sin_cos(angle):
    return jnp.sin(angle), jnp.cos(angle)


def turned(x, matrix, cosine, sine):
    swapped = jnp.dot(x, matrix, preferred_element_type=f32)
    return (x.astype(f32) * cosine + swapped * sine).astype(bf16)


def cell_tables(cos_r, sin_r, cos_c, sin_c, first, rows):
    cosine = jnp.concatenate(
        [cos_r[first + i : first + i + 1, :] * cos_c for i in range(rows)], axis=0
    )
    sine = jnp.concatenate(
        [sin_r[first + i : first + i + 1, :] + sin_c for i in range(rows)], axis=0
    )
    return cosine, sine


def slots(block):
    twice = jnp.concatenate([block, block], axis=0).astype(bf16)
    return jnp.broadcast_to(twice[None], (TILES // 2, 16, 128)).reshape(TILES * 8, 128)


def query_kernel(
    pos_ref,
    q_ref,
    agents_ref,
    tab_r_ref,
    tab_c_ref,
    turn_ref,
    held_ref,
    spot_ref,
    sems,
):
    step = N // AGR
    place = pltpu.make_async_copy(pos_ref, spot_ref, sems.at[AGR])
    place.start()
    copies = []
    for cell in range(AGR):
        part = pl.ds(cell * step, step)
        copy = pltpu.make_async_copy(q_ref.at[part, :], held_ref.at[part, :], sems.at[cell])
        copy.start()
        copies.append(copy)
    matrix = turn_matrix()
    turn_ref[...] = matrix
    lane = lanes((1, 128)) % HD
    power = jnp.exp((lane % 16).astype(f32) * f32(-math.log(100.0) / 16))
    freq_r = jnp.where(lane < 32, power, 0.0)
    freq_c = jnp.where(lane < 32, 0.0, power)
    place.wait()
    row_line = spot_ref[0][0:1, :].astype(f32)
    col_pos = spot_ref[1][:, 0:1].astype(f32)
    eye = lax.broadcasted_iota(jnp.int32, (TR, TR), 0) == lax.broadcasted_iota(
        jnp.int32, (TR, TR), 1
    )
    row_pos = jnp.sum(jnp.where(eye, jnp.broadcast_to(row_line, (TR, TR)), 0.0), 1, keepdims=True)
    angles = jnp.concatenate([row_pos * freq_r, col_pos * freq_c], axis=0)
    sines, cosines = sin_cos(angles)
    sines = jnp.concatenate([sines, sines], axis=1)
    cosines = jnp.concatenate([cosines, cosines], axis=1)
    tab_r_ref[0] = cosines[:TR]
    tab_r_ref[1] = sines[:TR]
    tab_c_ref[0] = cosines[TR:]
    tab_c_ref[1] = sines[TR:]
    means = []
    for cell in range(AGR):
        cosine, sine = cell_tables(
            cosines[:TR], sines[:TR], cosines[TR:], sines[TR:], cell * (TR // AGR), TR // AGR
        )
        copies[cell].wait()
        rotated = turned(held_ref[pl.ds(cell * step, step), :], matrix, cosine, sine)
        mean = jnp.sum(rotated.astype(f32), 0, keepdims=True) / step
        means.append(mean.astype(bf16).astype(f32))
    packed = jnp.concatenate([m[:, :128] for m in means] + [m[:, 128:] for m in means], axis=0)
    agents_ref[...] = slots(packed)


def key_kernel(
    tab_r_ref,
    tab_c_ref,
    turn_ref,
    v_ref,
    k_ref,
    q_ref,
    tk_ref,
    tq_ref,
    first_ref,
    last_ref,
    top_ref,
    bottom_ref,
    k_held_ref,
    q_held_ref,
    done_ref,
    v_held_ref,
    sems,
):
    step = N // AGR
    parts = [pl.ds(cell * step, step) for cell in range(AGR)]

    def moves(source, target, first):
        return [
            pltpu.make_async_copy(source.at[part, :], target.at[part, :], sems.at[first + i])
            for i, part in enumerate(parts)
        ]

    k_in, q_in = moves(k_ref, k_held_ref, 0), moves(q_ref, q_held_ref, AGR)
    q_out = moves(done_ref, tq_ref, 2 * AGR)
    v_in = pltpu.make_async_copy(v_ref, v_held_ref, sems.at[3 * AGR])
    for copy in q_in + k_in + [v_in]:
        copy.start()
    matrix = turn_ref[...]
    for cell, part in enumerate(parts):
        cosine, sine = cell_tables(
            tab_r_ref[0], tab_r_ref[1], tab_c_ref[0], tab_c_ref[1], cell * (TR // AGR), TR // AGR
        )
        q_in[cell].wait()
        done_ref[part, :] = turned(q_held_ref[part, :], matrix, cosine, sine)
        q_out[cell].start()
        k_in[cell].wait()
        tk_ref[part, :] = turned(k_held_ref[part, :], matrix, cosine, sine)
    v_in.wait()
    top_ref[...] = v_held_ref[0]
    bottom_ref[...] = v_held_ref[TR - 1]
    first_ref[...] = v_held_ref[:, 0, :]
    last_ref[...] = v_held_ref[:, TC - 1, :]
    for copy in q_out:
        copy.wait()


def agent_pairs(agents_ref, scale):
    target = lax.broadcasted_iota(jnp.int32, (AGENTS, TILES * 8), 0)
    source = lax.broadcasted_iota(jnp.int32, (AGENTS, TILES * 8), 1)
    agents = agents_ref[...]
    pairs = []
    for pair in range(2):
        wanted = (target & (TILES - 1)) * 8 + (target // TILES) + 4 * pair
        pick = jnp.where(source == wanted, scale, 0.0).astype(bf16)
        pairs.append(jnp.dot(pick, agents, preferred_element_type=f32).astype(bf16))
    return pairs


def half_mask(dims, parity):
    return (lanes(dims) // HD) == parity


def partial_kernel(agents_ref, tk_ref, v_hbm_ref, out_ref, score_ref, v_ref, sem):
    fetch = pltpu.make_async_copy(v_hbm_ref, v_ref, sem)
    fetch.start()
    pairs = agent_pairs(agents_ref, 1.0 / math.sqrt(HD))
    chunk = 512
    for head in range(LOCAL_HEADS):
        pair, parity = head // 2, head % 2
        cols = pl.ds(pair * 128, 128)
        own = pairs[pair]
        own = jnp.where(half_mask(own.shape, parity), own, jnp.zeros_like(own))
        peak = None
        for c in range(N // chunk):
            scores = lax.dot_general(
                own,
                tk_ref[pl.ds(c * chunk, chunk), cols],
                (((1,), (1,)), ((), ())),
                preferred_element_type=f32,
            )
            score_ref[:, pl.ds(c * chunk, chunk)] = scores
            for s in range(chunk // 128):
                piece = scores[:, s * 128 : (s + 1) * 128]
                peak = piece if peak is None else jnp.maximum(peak, piece)
        peak = jnp.max(peak, 1, keepdims=True)
        acc = jnp.zeros((AGENTS, 128), f32)
        if head == 0:
            fetch.wait()
        for c in range(N // chunk):
            weights = jnp.exp(score_ref[:, pl.ds(c * chunk, chunk)] - peak).astype(bf16)
            block = v_ref[pl.ds(c * chunk, chunk), cols]
            block = jnp.where(half_mask(block.shape, parity), block, jnp.ones_like(block))
            acc = acc + jnp.dot(weights, block, preferred_element_type=f32)
        other = pltpu.roll(acc, HD, 1)
        numer, total = (acc, other) if parity == 0 else (other, acc)
        logs = peak + jnp.log(total)
        values = numer / total
        logs = jnp.max(jnp.where(half_mask(logs.shape, 0), logs, -3e38), 1, keepdims=True)
        first = logs.astype(bf16).astype(f32)
        second = (logs - first).astype(bf16).astype(f32)
        third = logs - first - second
        lane = lanes((AGENTS, 128))
        packed = jnp.where(
            lane < HD,
            values,
            jnp.where(
                lane == HD,
                first,
                jnp.where(lane == HD + 1, second, jnp.where(lane == HD + 2, third, 0.0)),
            ),
        )
        groups = packed.reshape(2, ROWS, 8, 128)
        groups = jnp.concatenate([groups[0], groups[1]], 1).reshape(AGENTS, 128)
        out_ref[pl.ds(head * AGENTS, AGENTS), :] = groups.astype(bf16)


def merge_kernel(parts_ref, out_ref):
    source = lax.broadcasted_iota(jnp.int32, (128, 128), 0)
    picker = jnp.where((source >= HD) & (source < HD + 3), 1.0, 0.0).astype(bf16)
    parts = parts_ref[...]
    logs = jnp.dot(parts, picker, preferred_element_type=f32).reshape(TILES, ROWS, 128)
    values = parts.astype(f32).reshape(TILES, ROWS, 128)
    peak = jnp.max(logs, 0)
    weights = jnp.exp(logs - peak[None])
    merged = jnp.sum(weights * values, 0) / jnp.sum(weights, 0)
    merged = jnp.where(lanes((8, 128)) < HD, merged[:8], pltpu.roll(merged[8:], HD, 1))
    out_ref[...] = slots(merged)


def probability_kernel(
    agents_ref,
    tq_ref,
    v_ref,
    left_ref,
    right_ref,
    above_ref,
    below_ref,
    w_ref,
    prob_ref,
    conv_ref,
    held_ref,
    v_held_ref,
    total_ref,
    l_ref,
    r_ref,
    sems,
):
    chunk = 256

    def fetch(c):
        rows = pl.ds(pl.multiple_of(c * chunk, chunk), chunk)
        return pltpu.make_async_copy(tq_ref.at[rows, :], held_ref.at[rows, :], sems.at[c])

    for c in range(N // chunk):
        fetch(c).start()
    v_in = pltpu.make_async_copy(v_ref, v_held_ref, sems.at[N // chunk])
    conv_out = pltpu.make_async_copy(total_ref, conv_ref, sems.at[N // chunk + 1])
    v_in.start()
    pairs = agent_pairs(agents_ref, 1.0 / math.sqrt(HD))
    v_in.wait()
    convolve(
        v_held_ref, left_ref, right_ref, above_ref, below_ref, w_ref, total_ref, l_ref, r_ref
    )
    conv_out.start()
    ones = jnp.ones((AGENTS, 128), bf16)
    owns = []
    for head in range(LOCAL_HEADS):
        own = pairs[head // 2]
        owns.append(jnp.where(half_mask(own.shape, head % 2), own, jnp.zeros_like(own)))

    def body(c, carry):
        fetch(c).wait()
        rows = pl.ds(pl.multiple_of(c * chunk, chunk), chunk)
        for head in range(LOCAL_HEADS):
            scores = lax.dot_general(
                held_ref[rows, pl.ds(head // 2 * 128, 128)],
                owns[head],
                (((1,), (1,)), ((), ())),
                preferred_element_type=f32,
            )
            weights = jnp.exp(scores - jnp.max(scores, 1, keepdims=True))
            total = jnp.dot(weights.astype(bf16), ones, preferred_element_type=f32)
            scale = 1.0 / total
            scale = jnp.concatenate([scale, scale], axis=1)
            prob_ref[rows, pl.ds(head * AGENTS, AGENTS)] = (weights * scale).astype(bf16)
        return carry

    lax.fori_loop(0, N // chunk, body, 0)
    conv_out.wait()


def line_kernel(top_ref, bottom_ref, left_ref, right_ref, up_ref, down_ref):
    for line_ref, row, out_ref in ((top_ref, 0, up_ref), (bottom_ref, TR - 1, down_ref)):
        out_ref[pl.ds(0, TC), :] = line_ref[...]
        left = left_ref[row : row + 1, :].astype(f32)
        right = right_ref[row : row + 1, :].astype(f32)
        tail = jnp.concatenate([left, right, jnp.zeros((14, CH), f32)], axis=0)
        out_ref[pl.ds(TC, 16), :] = tail.astype(bf16)


def convolve(v_ref, left_ref, right_ref, above_ref, below_ref, w_ref, out_ref, l_ref, r_ref):
    l_ref[...] = left_ref[...].astype(f32)
    r_ref[...] = right_ref[...].astype(f32)
    for half in range(2):
        cols = pl.ds(half * 128, 128)

        def put(at, total):
            out_ref[pl.ds(at, TC), cols] = total

        w = [jnp.broadcast_to(w_ref[t : t + 1, cols], (TC, 128)) for t in range(9)]
        column = lax.broadcasted_iota(jnp.int32, (TC, 128), 0)

        def taps(row, left, right):
            row = row.astype(f32)
            before = jnp.where(column == 0, left, pltpu.roll(row, 1, 0))
            after = jnp.where(column == TC - 1, right, pltpu.roll(row, TC - 1, 0))
            return [before * w[3 * d] + row * w[3 * d + 1] + after * w[3 * d + 2] for d in range(3)]

        tail = above_ref[pl.ds(TC, 16), cols].astype(f32)
        t0 = taps(above_ref[pl.ds(0, TC), cols], tail[0:1], tail[1:2])

        def group(start, carry):
            a, b = carry
            lefts, rights = l_ref[pl.ds(start, 8), cols], r_ref[pl.ds(start, 8), cols]
            for k in range(8):
                t = taps(v_ref[start + k, :, cols], lefts[k : k + 1], rights[k : k + 1])
                if a is not None:
                    at = (start + k - 1) * TC
                    if not isinstance(at, int):
                        at = pl.multiple_of(at, TC)
                    put(at, a + t[2])
                a, b = b + t[1], t[0]
            return a, b

        carry = group(0, (None, t0[0]))
        a, b = lax.fori_loop(
            1, TR // 8, lambda g, c: group(pl.multiple_of(g * 8, 8), c), carry
        )
        tail = below_ref[pl.ds(TC, 16), cols].astype(f32)
        t = taps(below_ref[pl.ds(0, TC), cols], tail[0:1], tail[1:2])
        put((TR - 1) * TC, a + t[2])


def attend_kernel(av_ref, prob_ref, conv_hbm_ref, sum_ref, stat_ref, conv_ref, sem):
    fetch = pltpu.make_async_copy(conv_hbm_ref, conv_ref, sem)
    fetch.start()
    eye = lax.broadcasted_iota(jnp.int32, (128, 128), 0) == lanes((128, 128))
    for pair in range(2):
        pieces = []
        for parity in range(2):
            part = av_ref[pl.ds((2 * pair + parity) * 128, 128), :].astype(f32)
            other = pltpu.roll(part, HD, 1)
            own = half_mask(part.shape, parity)
            for piece in (part, other) if parity == 0 else (other, part):
                pieces.append(jnp.where(own, piece, 0.0))
        agent_values = jnp.concatenate(pieces, axis=0).astype(bf16)
        for b in range(N // 512):
            rows = pl.ds(b * 512, 512)
            sum_ref[rows, pl.ds(pair * 128, 128)] = jnp.dot(
                prob_ref[rows, pl.ds(pair * 2 * AGENTS, 2 * AGENTS)],
                agent_values,
                preferred_element_type=f32,
            )
    fetch.wait()
    for b in range(BLOCKS):
        rows = pl.ds(b * 128, 128)
        x = sum_ref[rows, :] + conv_ref[rows, :]
        sum_ref[rows, :] = x
        mean = jnp.sum(x[:, :128] + x[:, 128:], 1, keepdims=True) * (1.0 / CH)
        x = x - mean
        x = x * x
        squares = jnp.sum(x[:, :128] + x[:, 128:], 1, keepdims=True)
        stat_ref[b : b + 1, :] = jnp.sum(jnp.where(eye, mean, 0.0), 0, keepdims=True)
        stat_ref[BLOCKS + b : BLOCKS + b + 1, :] = jnp.sum(
            jnp.where(eye, squares, 0.0), 0, keepdims=True
        )


def norm_kernel(s0_ref, s1_ref, s2_ref, s3_ref, sum_ref, gain_ref, bias_ref, out_ref, done_ref, sems):
    stats = [s[...] for s in (s0_ref, s1_ref, s2_ref, s3_ref)]
    means = [s[:BLOCKS] for s in stats]
    mean = (means[0] + means[1] + means[2] + means[3]) * 0.25
    squares = sum(s[BLOCKS:] for s in stats)
    for m in means:
        squares = squares + CH * (m - mean) * (m - mean)
    scale = lax.rsqrt(squares * (1.0 / D) + epsilon)
    step = N // AGR
    copies = []
    for b in range(BLOCKS):
        rows = pl.ds(b * 128, 128)
        m = jnp.broadcast_to(mean[b : b + 1], (128, 128)).T
        s = jnp.broadcast_to(scale[b : b + 1], (128, 128)).T
        for half in range(2):
            cols = pl.ds(half * 128, 128)
            done_ref[rows, cols] = (
                (sum_ref[rows, cols] - m) * s * gain_ref[0:1, cols] + bias_ref[0:1, cols]
            ).astype(bf16)
        if (b + 1) * 128 % step == 0:
            part = pl.ds((b + 1) * 128 - step, step)
            copy = pltpu.make_async_copy(
                done_ref.at[part, :], out_ref.at[part, :], sems.at[len(copies)]
            )
            copy.start()
            copies.append(copy)
    for copy in copies:
        copy.wait()


def spread(x):
    slot = x.reshape(TILES, x.shape[0] // TILES, 128)
    return lax.all_to_all(slot, ("row", "col"), 0, 0).reshape(x.shape)


def shift(x, axis, step):
    count = lax.axis_size(axis)
    pairs = [(i, i + step) for i in range(count) if 0 <= i + step < count]
    return lax.ppermute(x, axis, pairs)


def after(x, *others):
    return lax.optimization_barrier((x, *others))[0]


def shards(queries, keys, values, positions, conv_weight, norm_gain, norm_bias):
    q = queries.reshape(N, CH)
    k = keys.reshape(N, CH)
    v = values.reshape(N, CH)
    mb = 1 << 20
    packed, tab_r, tab_c, turn = call(
        query_kernel,
        (
            shape((TILES * 8, 128), bf16),
            near((2, TR, CH), f32),
            near((2, TC, CH), f32),
            near((CH, CH), bf16),
        ),
        "hh",
        scratch=[
            pltpu.VMEM((N, CH), bf16),
            pltpu.VMEM((2, TC, TR), jnp.int32),
            pltpu.SemaphoreType.DMA((AGR + 1,)),
        ],
        nbytes=8 * mb,
        name="pool_queries",
    )(jnp.swapaxes(positions, 1, 2), q)
    agents = spread(packed)
    tk, tq, first, last, top, bottom = call(
        key_kernel,
        (near((N, CH), bf16), far((N, CH), bf16))
        + (near((TR, CH), bf16),) * 2
        + (near((TC, CH), bf16),) * 2,
        "vvvhhh",
        scratch=[pltpu.VMEM((N, CH), bf16)] * 3
        + [pltpu.VMEM((TR, TC, CH), bf16), pltpu.SemaphoreType.DMA((3 * AGR + 1,))],
        nbytes=4 * mb,
        out_spaces=" h    ",
        name="turn_keys",
    )(tab_r, tab_c, turn, values, k, q)
    left = shift(last, "col", 1)
    right = shift(first, "col", -1)
    parts = call(
        partial_kernel,
        shape((TILES * ROWS, 128), bf16),
        " vh",
        scratch=[
            pltpu.VMEM((AGENTS, N), f32),
            pltpu.VMEM((N, CH), bf16),
            pltpu.SemaphoreType.DMA(()),
        ],
        nbytes=10 * mb,
        name="partials",
    )(agents, tk, v)
    parts = after(parts, left, right)
    received = spread(parts)
    up, down = call(
        line_kernel, (near((TC + 16, CH), bf16),) * 2, "vvvv", nbytes=mb // 4, name="lines"
    )(top, bottom, left, right)
    above = shift(down, "row", 1)
    below = shift(up, "row", -1)
    received = after(received, up, down)
    merged = call(merge_kernel, shape((TILES * 8, 128), bf16), " ", nbytes=2 * mb, name="merge")(
        received
    )
    merged = after(merged, above, below)
    agent_values = spread(merged)
    prob, convolved = call(
        probability_kernel,
        (near((N, LOCAL_HEADS * AGENTS), bf16), far((N, CH), f32)),
        " hhvvvv ",
        scratch=[
            pltpu.VMEM((N, CH), bf16),
            pltpu.VMEM((TR, TC, CH), bf16),
            pltpu.VMEM((N, CH), f32),
            pltpu.VMEM((TR, CH), f32),
            pltpu.VMEM((TR, CH), f32),
            pltpu.SemaphoreType.DMA((N // 256 + 2,)),
        ],
        nbytes=20 * mb,
        out_spaces=" h",
        name="probabilities",
    )(agents, tq, values, left, right, above, below, conv_weight)
    summed, stats = call(
        attend_kernel,
        (near((N, CH), f32), near((2 * BLOCKS, 128), f32)),
        " vh",
        scratch=[pltpu.VMEM((N, CH), f32), pltpu.SemaphoreType.DMA(())],
        nbytes=4 * mb,
        name="attend",
    )(agent_values, prob, convolved)
    heads = lax.axis_size("head")
    others = [
        lax.ppermute(stats, "head", [(i, (i + d) % heads) for i in range(heads)])
        for d in range(1, heads)
    ]
    normed = call(
        norm_kernel,
        (shape((N, CH), bf16),),
        "v   v  ",
        scratch=[pltpu.VMEM((N, CH), bf16), pltpu.SemaphoreType.DMA((AGR,))],
        nbytes=4 * mb,
        out_spaces="h",
        name="norm",
    )(
        stats, *others, summed, norm_gain.reshape(1, CH), norm_bias.reshape(1, CH)
    )[0]
    return normed.reshape(TR, TC, CH)


def solution(mesh):
    in_specs = (
        P("row", "col", "head"),
        P("row", "col", "head"),
        P("row", "col", "head"),
        P(None, "row", "col"),
        P(None, "head"),
        P("head"),
        P("head"),
    )
    out_specs = P("row", "col", "head")
    return jax.shard_map(shards, mesh=mesh, in_specs=in_specs, out_specs=out_specs, check_vma=False)
```

```python
import math

import jax
import jax.numpy as jnp
from jax import lax
from jax.experimental import pallas as pl
from jax.experimental.pallas import tpu as pltpu
from jax.sharding import PartitionSpec as P

HD = 64
D = 1024
AGR = 4
TR = 48
TC = 32
CH = 256
N = TR * TC
AGENTS = 256
TILES = 64
LOCAL_HEADS = 4
ROWS = LOCAL_HEADS * AGENTS // TILES
BLOCKS = N // 128

f32 = jnp.float32
bf16 = jnp.bfloat16
epsilon = 1e-05

VMEM_SPEC = pl.BlockSpec(memory_space=pltpu.VMEM)
HBM_SPEC = pl.BlockSpec(memory_space=pltpu.HBM)


def call(kernel, outs, in_spaces, scratch=(), nbytes=0, name=None, out_spaces=None):
    fn = pl.pallas_call(
        kernel,
        out_shape=outs,
        in_specs=[HBM_SPEC if c == "h" else VMEM_SPEC for c in in_spaces],
        out_specs=(
            tuple(HBM_SPEC if c == "h" else VMEM_SPEC for c in out_spaces or " " * len(outs))
            if isinstance(outs, tuple)
            else VMEM_SPEC
        ),
        scratch_shapes=list(scratch),
        compiler_params=pltpu.CompilerParams(vmem_limit_bytes=20 * 1024 * 1024),
        cost_estimate=pl.CostEstimate(flops=0, bytes_accessed=nbytes, transcendentals=0),
        name=name,
    )

    def run(*args):
        spaces = {"h": pltpu.HBM, "v": pltpu.VMEM}
        return fn(
            *[
                pltpu.with_memory_space_constraint(x, spaces[c]) if c in spaces else x
                for x, c in zip(args, in_spaces, strict=True)
            ]
        )

    return run


def shape(dims, dtype):
    return jax.ShapeDtypeStruct(dims, dtype)


def near(dims, dtype):
    return pltpu.VMEM(dims, dtype)


def far(dims, dtype):
    return pltpu.HBM(dims, dtype)


def lanes(dims):
    return lax.broadcasted_iota(jnp.int32, dims, len(dims) - 1)


def turn_matrix():
    source = lax.broadcasted_iota(jnp.int32, (CH, CH), 0)
    target = lax.broadcasted_iota(jnp.int32, (CH, CH), 1)
    low = (target & 31) < 16
    minus = jnp.where(low & (source == target + 16), -1.0, 0.0)
    plus = jnp.where((~low) & (source == target - 16), 1.0, 0.0)
    return (minus + plus).astype(bf16)


def sin_cos(angle):
    return jnp.sin(angle), jnp.cos(angle)


def turned(x, matrix, cosine, sine):
    swapped = jnp.dot(x, matrix, preferred_element_type=f32)
    return (x.astype(f32) * cosine + swapped * sine).astype(bf16)


def split_tables(cosines, sines):
    cosines = jnp.concatenate([cosines, cosines], axis=1)
    sines = jnp.concatenate([sines, sines], axis=1)
    return cosines[:TR], sines[:TR], cosines[TR:], sines[TR:]


def cell_tables(tables, first, rows):
    cos_r, sin_r, cos_c, sin_c = tables
    cosine = jnp.concatenate(
        [cos_r[first + i : first + i + 1, :] * cos_c for i in range(rows)], axis=0
    )
    sine = jnp.concatenate(
        [sin_r[first + i : first + i + 1, :] + sin_c for i in range(rows)], axis=0
    )
    return cosine, sine


def slots(block):
    twice = jnp.concatenate([block, block], axis=0).astype(bf16)
    return jnp.broadcast_to(twice[None], (TILES // 2, 16, 128)).reshape(TILES * 8, 128)


def query_kernel(
    pos_ref,
    q_ref,
    agents_ref,
    tab_ref,
    held_ref,
    spot_ref,
    sems,
):
    step = N // AGR
    place = pltpu.make_async_copy(pos_ref, spot_ref, sems.at[AGR])
    place.start()
    copies = []
    for cell in range(AGR):
        part = pl.ds(cell * step, step)
        copy = pltpu.make_async_copy(q_ref.at[part, :], held_ref.at[part, :], sems.at[cell])
        copy.start()
        copies.append(copy)
    matrix = turn_matrix()
    lane = lanes((1, 128)) % HD
    power = jnp.exp((lane % 16).astype(f32) * f32(-math.log(100.0) / 16))
    freq_r = jnp.where(lane < 32, power, 0.0)
    freq_c = jnp.where(lane < 32, 0.0, power)
    place.wait()
    row_line = spot_ref[0][0:1, :].astype(f32)
    col_pos = spot_ref[1][:, 0:1].astype(f32)
    eye = lax.broadcasted_iota(jnp.int32, (TR, TR), 0) == lax.broadcasted_iota(
        jnp.int32, (TR, TR), 1
    )
    row_pos = jnp.sum(jnp.where(eye, jnp.broadcast_to(row_line, (TR, TR)), 0.0), 1, keepdims=True)
    angles = jnp.concatenate([row_pos * freq_r, col_pos * freq_c], axis=0)
    sines, cosines = sin_cos(angles)
    tab_ref[0] = cosines
    tab_ref[1] = sines
    tables = split_tables(cosines, sines)
    means = []
    for cell in range(AGR):
        cosine, sine = cell_tables(tables, cell * (TR // AGR), TR // AGR)
        copies[cell].wait()
        rotated = turned(held_ref[pl.ds(cell * step, step), :], matrix, cosine, sine)
        mean = jnp.sum(rotated.astype(f32), 0, keepdims=True) / step
        means.append(mean.astype(bf16).astype(f32))
    packed = jnp.concatenate([m[:, :128] for m in means] + [m[:, 128:] for m in means], axis=0)
    agents_ref[...] = slots(packed)


def key_kernel(
    tab_hbm_ref,
    v_ref,
    k_ref,
    tk_ref,
    first_ref,
    last_ref,
    top_ref,
    bottom_ref,
    tab_ref,
    held_ref,
    sems,
):
    step = N // AGR
    table = pltpu.make_async_copy(tab_hbm_ref, tab_ref, sems.at[AGR])
    table.start()
    copies = []
    for cell in range(AGR):
        part = pl.ds(cell * step, step)
        copies.append(
            pltpu.make_async_copy(k_ref.at[part, :], held_ref.at[part, :], sems.at[cell])
        )
        copies[cell].start()
    top_ref[...] = v_ref[0]
    bottom_ref[...] = v_ref[TR - 1]
    first_ref[...] = v_ref[:, 0, :]
    last_ref[...] = v_ref[:, TC - 1, :]
    matrix = turn_matrix()
    table.wait()
    tables = split_tables(tab_ref[0], tab_ref[1])
    for cell in range(AGR):
        part = pl.ds(cell * step, step)
        cosine, sine = cell_tables(tables, cell * (TR // AGR), TR // AGR)
        copies[cell].wait()
        tk_ref[part, :] = turned(held_ref[part, :], matrix, cosine, sine)


def agent_pairs(agents_ref, scale):
    target = lax.broadcasted_iota(jnp.int32, (AGENTS, TILES * 8), 0)
    source = lax.broadcasted_iota(jnp.int32, (AGENTS, TILES * 8), 1)
    agents = agents_ref[...]
    pairs = []
    for pair in range(2):
        wanted = (target & (TILES - 1)) * 8 + (target // TILES) + 4 * pair
        pick = jnp.where(source == wanted, scale, 0.0).astype(bf16)
        pairs.append(jnp.dot(pick, agents, preferred_element_type=f32).astype(bf16))
    return pairs


def half_mask(dims, parity):
    return (lanes(dims) // HD) == parity


def partial_kernel(agents_ref, tk_ref, v_ref, out_ref, score_ref):
    pairs = agent_pairs(agents_ref, 1.0 / math.sqrt(HD))
    chunk = 512
    for head in range(LOCAL_HEADS):
        pair, parity = head // 2, head % 2
        cols = pl.ds(pair * 128, 128)
        own = pairs[pair]
        own = jnp.where(half_mask(own.shape, parity), own, jnp.zeros_like(own))
        peak = None
        for c in range(N // chunk):
            scores = lax.dot_general(
                own,
                tk_ref[pl.ds(c * chunk, chunk), cols],
                (((1,), (1,)), ((), ())),
                preferred_element_type=f32,
            )
            score_ref[:, pl.ds(c * chunk, chunk)] = scores
            for s in range(chunk // 128):
                piece = scores[:, s * 128 : (s + 1) * 128]
                peak = piece if peak is None else jnp.maximum(peak, piece)
        peak = jnp.max(peak, 1, keepdims=True)
        acc = jnp.zeros((AGENTS, 128), f32)
        for c in range(N // chunk):
            weights = jnp.exp(score_ref[:, pl.ds(c * chunk, chunk)] - peak).astype(bf16)
            block = v_ref[pl.ds(c * chunk, chunk), cols]
            block = jnp.where(half_mask(block.shape, parity), block, jnp.ones_like(block))
            acc = acc + jnp.dot(weights, block, preferred_element_type=f32)
        other = pltpu.roll(acc, HD, 1)
        numer, total = (acc, other) if parity == 0 else (other, acc)
        logs = peak + jnp.log(total)
        values = numer / total
        logs = jnp.max(jnp.where(half_mask(logs.shape, 0), logs, -3e38), 1, keepdims=True)
        first = logs.astype(bf16).astype(f32)
        second = (logs - first).astype(bf16).astype(f32)
        third = logs - first - second
        lane = lanes((AGENTS, 128))
        packed = jnp.where(
            lane < HD,
            values,
            jnp.where(
                lane == HD,
                first,
                jnp.where(lane == HD + 1, second, jnp.where(lane == HD + 2, third, 0.0)),
            ),
        )
        groups = packed.reshape(2, ROWS, 8, 128)
        groups = jnp.concatenate([groups[0], groups[1]], 1).reshape(AGENTS, 128)
        out_ref[pl.ds(head * AGENTS, AGENTS), :] = groups.astype(bf16)


def merge_kernel(parts_ref, out_ref):
    source = lax.broadcasted_iota(jnp.int32, (128, 128), 0)
    picker = jnp.where((source >= HD) & (source < HD + 3), 1.0, 0.0).astype(bf16)
    parts = parts_ref[...]
    logs = jnp.dot(parts, picker, preferred_element_type=f32).reshape(TILES, ROWS, 128)
    values = parts.astype(f32).reshape(TILES, ROWS, 128)
    peak = jnp.max(logs, 0)
    weights = jnp.exp(logs - peak[None])
    merged = jnp.sum(weights * values, 0) / jnp.sum(weights, 0)
    merged = jnp.where(lanes((8, 128)) < HD, merged[:8], pltpu.roll(merged[8:], HD, 1))
    out_ref[...] = slots(merged)


def probability_kernel(agents_ref, tab_hbm_ref, q_ref, prob_ref, tab_ref, held_ref, sems):
    chunk = 256
    table = pltpu.make_async_copy(tab_hbm_ref, tab_ref, sems.at[N // chunk])
    table.start()

    def fetch(c):
        rows = pl.ds(pl.multiple_of(c * chunk, chunk), chunk)
        return pltpu.make_async_copy(q_ref.at[rows, :], held_ref.at[rows, :], sems.at[c])

    for c in range(N // chunk):
        fetch(c).start()
    pairs = agent_pairs(agents_ref, 1.0 / math.sqrt(HD))
    matrix = turn_matrix()
    table.wait()
    ones = jnp.ones((AGENTS, 128), bf16)
    owns = []
    for head in range(LOCAL_HEADS):
        own = pairs[head // 2]
        owns.append(jnp.where(half_mask(own.shape, head % 2), own, jnp.zeros_like(own)))

    def body(c, carry):
        fetch(c).wait()
        rows = pl.ds(pl.multiple_of(c * chunk, chunk), chunk)
        lines = pl.ds(pl.multiple_of(c * (chunk // TC), chunk // TC), chunk // TC)
        near_rows = [tab_ref[i, lines, :] for i in range(2)]
        near_cols = [tab_ref[i, pl.ds(TR, TC), :] for i in range(2)]
        tables = [jnp.concatenate([t, t], axis=1) for t in near_rows + near_cols]
        cosine, sine = cell_tables(tables, 0, chunk // TC)
        queries = turned(held_ref[rows, :], matrix, cosine, sine)
        for head in range(LOCAL_HEADS):
            scores = lax.dot_general(
                queries[:, head // 2 * 128 : head // 2 * 128 + 128],
                owns[head],
                (((1,), (1,)), ((), ())),
                preferred_element_type=f32,
            )
            weights = jnp.exp(scores - jnp.max(scores, 1, keepdims=True))
            total = jnp.dot(weights.astype(bf16), ones, preferred_element_type=f32)
            scale = 1.0 / total
            scale = jnp.concatenate([scale, scale], axis=1)
            prob_ref[rows, pl.ds(head * AGENTS, AGENTS)] = (weights * scale).astype(bf16)
        return carry

    lax.fori_loop(0, N // chunk, body, 0)


def line_kernel(top_ref, bottom_ref, left_ref, right_ref, up_ref, down_ref):
    for line_ref, row, out_ref in ((top_ref, 0, up_ref), (bottom_ref, TR - 1, down_ref)):
        out_ref[pl.ds(0, TC), :] = line_ref[...]
        left = left_ref[row : row + 1, :].astype(f32)
        right = right_ref[row : row + 1, :].astype(f32)
        tail = jnp.concatenate([left, right, jnp.zeros((14, CH), f32)], axis=0)
        out_ref[pl.ds(TC, 16), :] = tail.astype(bf16)


def conv_kernel(
    v_hbm_ref,
    left_ref,
    right_ref,
    above_ref,
    below_ref,
    w_ref,
    out_ref,
    v_ref,
    l_ref,
    r_ref,
    sem,
):
    fetch = pltpu.make_async_copy(v_hbm_ref, v_ref, sem)
    fetch.start()
    fetch.wait()
    l_ref[...] = left_ref[...].astype(f32)
    r_ref[...] = right_ref[...].astype(f32)
    for half in range(2):
        cols = pl.ds(half * 128, 128)

        def put(at, total):
            out_ref[pl.ds(at, TC), cols] = total

        w = [jnp.broadcast_to(w_ref[t : t + 1, cols], (TC, 128)) for t in range(9)]
        column = lax.broadcasted_iota(jnp.int32, (TC, 128), 0)

        def taps(row, left, right):
            row = row.astype(f32)
            before = jnp.where(column == 0, left, pltpu.roll(row, 1, 0))
            after = jnp.where(column == TC - 1, right, pltpu.roll(row, TC - 1, 0))
            return [before * w[3 * d] + row * w[3 * d + 1] + after * w[3 * d + 2] for d in range(3)]

        tail = above_ref[pl.ds(TC, 16), cols].astype(f32)
        t0 = taps(above_ref[pl.ds(0, TC), cols], tail[0:1], tail[1:2])

        def group(start, carry):
            a, b = carry
            lefts, rights = l_ref[pl.ds(start, 8), cols], r_ref[pl.ds(start, 8), cols]
            for k in range(8):
                t = taps(v_ref[start + k, :, cols], lefts[k : k + 1], rights[k : k + 1])
                if a is not None:
                    at = (start + k - 1) * TC
                    if not isinstance(at, int):
                        at = pl.multiple_of(at, TC)
                    put(at, a + t[2])
                a, b = b + t[1], t[0]
            return a, b

        carry = group(0, (None, t0[0]))
        a, b = lax.fori_loop(
            1, TR // 8, lambda g, c: group(pl.multiple_of(g * 8, 8), c), carry
        )
        tail = below_ref[pl.ds(TC, 16), cols].astype(f32)
        t = taps(below_ref[pl.ds(0, TC), cols], tail[0:1], tail[1:2])
        put((TR - 1) * TC, a + t[2])


def attend_kernel(av_ref, prob_ref, conv_hbm_ref, sum_ref, stat_ref, conv_ref, sem):
    fetch = pltpu.make_async_copy(conv_hbm_ref, conv_ref, sem)
    fetch.start()
    eye = lax.broadcasted_iota(jnp.int32, (128, 128), 0) == lanes((128, 128))
    for pair in range(2):
        pieces = []
        for parity in range(2):
            part = av_ref[pl.ds((2 * pair + parity) * 128, 128), :].astype(f32)
            other = pltpu.roll(part, HD, 1)
            own = half_mask(part.shape, parity)
            for piece in (part, other) if parity == 0 else (other, part):
                pieces.append(jnp.where(own, piece, 0.0))
        agent_values = jnp.concatenate(pieces, axis=0).astype(bf16)
        for b in range(N // 512):
            rows = pl.ds(b * 512, 512)
            sum_ref[rows, pl.ds(pair * 128, 128)] = jnp.dot(
                prob_ref[rows, pl.ds(pair * 2 * AGENTS, 2 * AGENTS)],
                agent_values,
                preferred_element_type=f32,
            )
    fetch.wait()
    for b in range(BLOCKS):
        rows = pl.ds(b * 128, 128)
        x = sum_ref[rows, :] + conv_ref[rows, :]
        sum_ref[rows, :] = x
        mean = jnp.sum(x[:, :128] + x[:, 128:], 1, keepdims=True) * (1.0 / CH)
        x = x - mean
        x = x * x
        squares = jnp.sum(x[:, :128] + x[:, 128:], 1, keepdims=True)
        stat_ref[b : b + 1, :] = jnp.sum(jnp.where(eye, mean, 0.0), 0, keepdims=True)
        stat_ref[BLOCKS + b : BLOCKS + b + 1, :] = jnp.sum(
            jnp.where(eye, squares, 0.0), 0, keepdims=True
        )


def norm_kernel(s0_ref, s1_ref, s2_ref, s3_ref, sum_ref, gain_ref, bias_ref, out_ref, done_ref, sems):
    stats = [s[...] for s in (s0_ref, s1_ref, s2_ref, s3_ref)]
    means = [s[:BLOCKS] for s in stats]
    mean = (means[0] + means[1] + means[2] + means[3]) * 0.25
    squares = sum(s[BLOCKS:] for s in stats)
    for m in means:
        squares = squares + CH * (m - mean) * (m - mean)
    scale = lax.rsqrt(squares * (1.0 / D) + epsilon)
    step = N // AGR
    copies = []
    for b in range(BLOCKS):
        rows = pl.ds(b * 128, 128)
        m = jnp.broadcast_to(mean[b : b + 1], (128, 128)).T
        s = jnp.broadcast_to(scale[b : b + 1], (128, 128)).T
        for half in range(2):
            cols = pl.ds(half * 128, 128)
            done_ref[rows, cols] = (
                (sum_ref[rows, cols] - m) * s * gain_ref[0:1, cols] + bias_ref[0:1, cols]
            ).astype(bf16)
        if (b + 1) * 128 % step == 0:
            part = pl.ds((b + 1) * 128 - step, step)
            copy = pltpu.make_async_copy(
                done_ref.at[part, :], out_ref.at[part, :], sems.at[len(copies)]
            )
            copy.start()
            copies.append(copy)
    for copy in copies:
        copy.wait()


def spread(x):
    slot = x.reshape(TILES, x.shape[0] // TILES, 128)
    return lax.all_to_all(slot, ("row", "col"), 0, 0).reshape(x.shape)


def shift(x, axis, step):
    count = lax.axis_size(axis)
    pairs = [(i, i + step) for i in range(count) if 0 <= i + step < count]
    return lax.ppermute(x, axis, pairs)


def after(x, *others):
    return lax.optimization_barrier((x, *others))[0]


def shards(queries, keys, values, positions, conv_weight, norm_gain, norm_bias):
    q = queries.reshape(N, CH)
    k = keys.reshape(N, CH)
    v = values.reshape(N, CH)
    mb = 1 << 20
    packed, table = call(
        query_kernel,
        (far((TILES * 8, 128), bf16), far((2, TR + TC, 128), f32)),
        "hh",
        scratch=[
            pltpu.VMEM((N, CH), bf16),
            pltpu.VMEM((2, TC, TR), jnp.int32),
            pltpu.SemaphoreType.DMA((AGR + 1,)),
        ],
        nbytes=8 * mb,
        name="pool_queries",
    )(jnp.swapaxes(positions, 1, 2), q)
    agents = spread(packed)
    held_table = pltpu.VMEM((2, TR + TC, 128), f32)
    tk, first, last, top, bottom = call(
        key_kernel,
        (near((N, CH), bf16),)
        + (near((TR, CH), bf16),) * 2
        + (near((TC, CH), bf16),) * 2,
        "h h",
        scratch=[held_table, pltpu.VMEM((N, CH), bf16), pltpu.SemaphoreType.DMA((AGR + 1,))],
        nbytes=4 * mb,
        name="turn_keys",
    )(table, values, k)
    left = shift(last, "col", 1)
    right = shift(first, "col", -1)
    parts = call(
        partial_kernel,
        far((TILES * ROWS, 128), bf16),
        " v ",
        scratch=[pltpu.VMEM((AGENTS, N), f32)],
        nbytes=10 * mb,
        name="partials",
    )(agents, tk, v)
    up, down = call(
        line_kernel,
        (near((TC + 16, CH), bf16),) * 2,
        "vv  ",
        nbytes=mb // 4,
        name="lines",
    )(top, bottom, *lax.optimization_barrier((left, right, agents))[:2])
    above = shift(down, "row", 1)
    below = shift(up, "row", -1)
    parts = after(parts, above, below)
    received = spread(parts)
    prob = call(
        probability_kernel,
        near((N, LOCAL_HEADS * AGENTS), bf16),
        " hh",
        scratch=[
            held_table,
            pltpu.VMEM((N, CH), bf16),
            pltpu.SemaphoreType.DMA((N // 256 + 1,)),
        ],
        nbytes=20 * mb,
        name="probabilities",
    )(agents, table, q)
    received = after(received, prob)
    merged = call(merge_kernel, far((TILES * 8, 128), bf16), " ", nbytes=2 * mb, name="merge")(
        received
    )
    agent_values = spread(merged)
    convolved = call(
        conv_kernel,
        far((N, CH), f32),
        "h     ",
        scratch=[pltpu.VMEM((TR, TC, CH), bf16)]
        + [pltpu.VMEM((TR, CH), f32)] * 2
        + [pltpu.SemaphoreType.DMA(())],
        nbytes=6 * mb,
        name="conv",
    )(values, left, right, above, below, conv_weight)
    summed, stats = call(
        attend_kernel,
        (near((N, CH), f32), near((2 * BLOCKS, 128), f32)),
        " vh",
        scratch=[pltpu.VMEM((N, CH), f32), pltpu.SemaphoreType.DMA(())],
        nbytes=4 * mb,
        name="attend",
    )(agent_values, prob, convolved)
    heads = lax.axis_size("head")
    others = [
        lax.ppermute(stats, "head", [(i, (i + d) % heads) for i in range(heads)])
        for d in range(1, heads)
    ]
    normed = call(
        norm_kernel,
        (shape((N, CH), bf16),),
        "v   v  ",
        scratch=[pltpu.VMEM((N, CH), bf16), pltpu.SemaphoreType.DMA((AGR,))],
        nbytes=4 * mb,
        out_spaces="h",
        name="norm",
    )(
        stats, *others, summed, norm_gain.reshape(1, CH), norm_bias.reshape(1, CH)
    )[0]
    return normed.reshape(TR, TC, CH)


def solution(mesh):
    in_specs = (
        P("row", "col", "head"),
        P("row", "col", "head"),
        P("row", "col", "head"),
        P(None, "row", "col"),
        P(None, "head"),
        P("head"),
        P("head"),
    )
    out_specs = P("row", "col", "head")
    return jax.shard_map(shards, mesh=mesh, in_specs=in_specs, out_specs=out_specs, check_vma=False)
```

```python
import math

import jax
import jax.numpy as jnp
from jax import lax
from jax.experimental import pallas as pl
from jax.experimental.pallas import tpu as pltpu
from jax.sharding import PartitionSpec as P

HD = 64
D = 1024
AGR = 4
TR = 48
TC = 32
CH = 256
N = TR * TC
AGENTS = 256
TILES = 64
LOCAL_HEADS = 4
ROWS = LOCAL_HEADS * AGENTS // TILES
BLOCKS = N // 128

f32 = jnp.float32
bf16 = jnp.bfloat16
epsilon = 1e-05

VMEM_SPEC = pl.BlockSpec(memory_space=pltpu.VMEM)
HBM_SPEC = pl.BlockSpec(memory_space=pltpu.HBM)


def call(kernel, outs, in_spaces, scratch=(), nbytes=0, name=None, out_spaces=None):
    fn = pl.pallas_call(
        kernel,
        out_shape=outs,
        in_specs=[HBM_SPEC if c == "h" else VMEM_SPEC for c in in_spaces],
        out_specs=(
            tuple(HBM_SPEC if c == "h" else VMEM_SPEC for c in out_spaces or " " * len(outs))
            if isinstance(outs, tuple)
            else VMEM_SPEC
        ),
        scratch_shapes=list(scratch),
        compiler_params=pltpu.CompilerParams(vmem_limit_bytes=20 * 1024 * 1024),
        cost_estimate=pl.CostEstimate(flops=0, bytes_accessed=nbytes, transcendentals=0),
        name=name,
    )

    def run(*args):
        spaces = {"h": pltpu.HBM, "v": pltpu.VMEM}
        return fn(
            *[
                pltpu.with_memory_space_constraint(x, spaces[c]) if c in spaces else x
                for x, c in zip(args, in_spaces, strict=True)
            ]
        )

    return run


def shape(dims, dtype):
    return jax.ShapeDtypeStruct(dims, dtype)


def near(dims, dtype):
    return pltpu.VMEM(dims, dtype)


def far(dims, dtype):
    return pltpu.HBM(dims, dtype)


def lanes(dims):
    return lax.broadcasted_iota(jnp.int32, dims, len(dims) - 1)


def turn_matrix():
    source = lax.broadcasted_iota(jnp.int32, (CH, CH), 0)
    target = lax.broadcasted_iota(jnp.int32, (CH, CH), 1)
    low = (target & 31) < 16
    minus = jnp.where(low & (source == target + 16), -1.0, 0.0)
    plus = jnp.where((~low) & (source == target - 16), 1.0, 0.0)
    return (minus + plus).astype(bf16)


def sin_cos(angle):
    return jnp.sin(angle), jnp.cos(angle)


def turned(x, matrix, cosine, sine):
    swapped = jnp.dot(x, matrix, preferred_element_type=f32)
    return (x.astype(f32) * cosine + swapped * sine).astype(bf16)


def split_tables(cosines, sines):
    cosines = jnp.concatenate([cosines, cosines], axis=1)
    sines = jnp.concatenate([sines, sines], axis=1)
    return cosines[:TR], sines[:TR], cosines[TR:], sines[TR:]


def cell_tables(tables, first, rows):
    cos_r, sin_r, cos_c, sin_c = tables
    cosine = jnp.concatenate(
        [cos_r[first + i : first + i + 1, :] * cos_c for i in range(rows)], axis=0
    )
    sine = jnp.concatenate(
        [sin_r[first + i : first + i + 1, :] + sin_c for i in range(rows)], axis=0
    )
    return cosine, sine


def slots(block):
    twice = jnp.concatenate([block, block], axis=0).astype(bf16)
    return jnp.broadcast_to(twice[None], (TILES // 2, 16, 128)).reshape(TILES * 8, 128)


def query_kernel(
    pos_ref,
    q_ref,
    agents_ref,
    tab_ref,
    held_ref,
    spot_ref,
    sems,
):
    step = N // AGR
    place = pltpu.make_async_copy(pos_ref, spot_ref, sems.at[AGR])
    place.start()
    copies = []
    for cell in range(AGR):
        part = pl.ds(cell * step, step)
        copy = pltpu.make_async_copy(q_ref.at[part, :], held_ref.at[part, :], sems.at[cell])
        copy.start()
        copies.append(copy)
    matrix = turn_matrix()
    lane = lanes((1, 128)) % HD
    power = jnp.exp((lane % 16).astype(f32) * f32(-math.log(100.0) / 16))
    freq_r = jnp.where(lane < 32, power, 0.0)
    freq_c = jnp.where(lane < 32, 0.0, power)
    place.wait()
    row_line = spot_ref[0][0:1, :].astype(f32)
    col_pos = spot_ref[1][:, 0:1].astype(f32)
    eye = lax.broadcasted_iota(jnp.int32, (TR, TR), 0) == lax.broadcasted_iota(
        jnp.int32, (TR, TR), 1
    )
    row_pos = jnp.sum(jnp.where(eye, jnp.broadcast_to(row_line, (TR, TR)), 0.0), 1, keepdims=True)
    angles = jnp.concatenate([row_pos * freq_r, col_pos * freq_c], axis=0)
    sines, cosines = sin_cos(angles)
    tab_ref[0] = cosines
    tab_ref[1] = sines
    tables = split_tables(cosines, sines)
    means = []
    for cell in range(AGR):
        cosine, sine = cell_tables(tables, cell * (TR // AGR), TR // AGR)
        copies[cell].wait()
        rotated = turned(held_ref[pl.ds(cell * step, step), :], matrix, cosine, sine)
        mean = jnp.sum(rotated.astype(f32), 0, keepdims=True) / step
        means.append(mean.astype(bf16).astype(f32))
    packed = jnp.concatenate([m[:, :128] for m in means] + [m[:, 128:] for m in means], axis=0)
    agents_ref[...] = slots(packed)


def key_kernel(
    tab_hbm_ref,
    v_ref,
    k_ref,
    tk_ref,
    first_ref,
    last_ref,
    tab_ref,
    held_ref,
    sems,
):
    step = N // AGR
    table = pltpu.make_async_copy(tab_hbm_ref, tab_ref, sems.at[AGR])
    table.start()
    copies = []
    for cell in range(AGR):
        part = pl.ds(cell * step, step)
        copies.append(
            pltpu.make_async_copy(k_ref.at[part, :], held_ref.at[part, :], sems.at[cell])
        )
        copies[cell].start()
    first_ref[...] = v_ref[:, 0, :]
    last_ref[...] = v_ref[:, TC - 1, :]
    matrix = turn_matrix()
    table.wait()
    tables = split_tables(tab_ref[0], tab_ref[1])
    for cell in range(AGR):
        part = pl.ds(cell * step, step)
        cosine, sine = cell_tables(tables, cell * (TR // AGR), TR // AGR)
        copies[cell].wait()
        tk_ref[part, :] = turned(held_ref[part, :], matrix, cosine, sine)


def agent_pairs(agents_ref, scale):
    target = lax.broadcasted_iota(jnp.int32, (AGENTS, TILES * 8), 0)
    source = lax.broadcasted_iota(jnp.int32, (AGENTS, TILES * 8), 1)
    agents = agents_ref[...]
    pairs = []
    for pair in range(2):
        wanted = (target & (TILES - 1)) * 8 + (target // TILES) + 4 * pair
        pick = jnp.where(source == wanted, scale, 0.0).astype(bf16)
        pairs.append(jnp.dot(pick, agents, preferred_element_type=f32).astype(bf16))
    return pairs


def half_mask(dims, parity):
    return (lanes(dims) // HD) == parity


def partial_kernel(agents_ref, tk_ref, v_ref, out_ref, score_ref):
    pairs = agent_pairs(agents_ref, 1.0 / math.sqrt(HD))
    chunk = 512
    for head in range(LOCAL_HEADS):
        pair, parity = head // 2, head % 2
        cols = pl.ds(pair * 128, 128)
        own = pairs[pair]
        own = jnp.where(half_mask(own.shape, parity), own, jnp.zeros_like(own))
        peak = None
        for c in range(N // chunk):
            scores = lax.dot_general(
                own,
                tk_ref[pl.ds(c * chunk, chunk), cols],
                (((1,), (1,)), ((), ())),
                preferred_element_type=f32,
            )
            score_ref[:, pl.ds(c * chunk, chunk)] = scores
            for s in range(chunk // 128):
                piece = scores[:, s * 128 : (s + 1) * 128]
                peak = piece if peak is None else jnp.maximum(peak, piece)
        peak = jnp.max(peak, 1, keepdims=True)
        acc = jnp.zeros((AGENTS, 128), f32)
        for c in range(N // chunk):
            weights = jnp.exp(score_ref[:, pl.ds(c * chunk, chunk)] - peak).astype(bf16)
            block = v_ref[pl.ds(c * chunk, chunk), cols]
            block = jnp.where(half_mask(block.shape, parity), block, jnp.ones_like(block))
            acc = acc + jnp.dot(weights, block, preferred_element_type=f32)
        other = pltpu.roll(acc, HD, 1)
        numer, total = (acc, other) if parity == 0 else (other, acc)
        logs = peak + jnp.log(total)
        values = numer / total
        logs = jnp.max(jnp.where(half_mask(logs.shape, 0), logs, -3e38), 1, keepdims=True)
        first = logs.astype(bf16).astype(f32)
        second = (logs - first).astype(bf16).astype(f32)
        third = logs - first - second
        lane = lanes((AGENTS, 128))
        packed = jnp.where(
            lane < HD,
            values,
            jnp.where(
                lane == HD,
                first,
                jnp.where(lane == HD + 1, second, jnp.where(lane == HD + 2, third, 0.0)),
            ),
        )
        groups = packed.reshape(2, ROWS, 8, 128)
        groups = jnp.concatenate([groups[0], groups[1]], 1).reshape(AGENTS, 128)
        out_ref[pl.ds(head * AGENTS, AGENTS), :] = groups.astype(bf16)


def merge_kernel(parts_ref, out_ref):
    source = lax.broadcasted_iota(jnp.int32, (128, 128), 0)
    picker = jnp.where((source >= HD) & (source < HD + 3), 1.0, 0.0).astype(bf16)
    parts = parts_ref[...]
    logs = jnp.dot(parts, picker, preferred_element_type=f32).reshape(TILES, ROWS, 128)
    values = parts.astype(f32).reshape(TILES, ROWS, 128)
    peak = jnp.max(logs, 0)
    weights = jnp.exp(logs - peak[None])
    merged = jnp.sum(weights * values, 0) / jnp.sum(weights, 0)
    merged = jnp.where(lanes((8, 128)) < HD, merged[:8], pltpu.roll(merged[8:], HD, 1))
    out_ref[...] = slots(merged)


def probability_kernel(agents_ref, tab_hbm_ref, q_ref, prob_ref, tab_ref, held_ref, sems):
    chunk = 256
    table = pltpu.make_async_copy(tab_hbm_ref, tab_ref, sems.at[N // chunk])
    table.start()

    def fetch(c):
        rows = pl.ds(pl.multiple_of(c * chunk, chunk), chunk)
        return pltpu.make_async_copy(q_ref.at[rows, :], held_ref.at[rows, :], sems.at[c])

    for c in range(N // chunk):
        fetch(c).start()
    pairs = agent_pairs(agents_ref, 1.0 / math.sqrt(HD))
    matrix = turn_matrix()
    table.wait()
    ones = jnp.ones((AGENTS, 128), bf16)
    owns = []
    for head in range(LOCAL_HEADS):
        own = pairs[head // 2]
        owns.append(jnp.where(half_mask(own.shape, head % 2), own, jnp.zeros_like(own)))

    def body(c, carry):
        fetch(c).wait()
        rows = pl.ds(pl.multiple_of(c * chunk, chunk), chunk)
        lines = pl.ds(pl.multiple_of(c * (chunk // TC), chunk // TC), chunk // TC)
        near_rows = [tab_ref[i, lines, :] for i in range(2)]
        near_cols = [tab_ref[i, pl.ds(TR, TC), :] for i in range(2)]
        tables = [jnp.concatenate([t, t], axis=1) for t in near_rows + near_cols]
        cosine, sine = cell_tables(tables, 0, chunk // TC)
        queries = turned(held_ref[rows, :], matrix, cosine, sine)
        for head in range(LOCAL_HEADS):
            scores = lax.dot_general(
                queries[:, head // 2 * 128 : head // 2 * 128 + 128],
                owns[head],
                (((1,), (1,)), ((), ())),
                preferred_element_type=f32,
            )
            weights = jnp.exp(scores - jnp.max(scores, 1, keepdims=True))
            total = jnp.dot(weights.astype(bf16), ones, preferred_element_type=f32)
            scale = 1.0 / total
            scale = jnp.concatenate([scale, scale], axis=1)
            prob_ref[rows, pl.ds(head * AGENTS, AGENTS)] = (weights * scale).astype(bf16)
        return carry

    lax.fori_loop(0, N // chunk, body, 0)


def line_kernel(v_ref, left_hbm_ref, right_hbm_ref, up_ref, down_ref, left_ref, right_ref, sems):
    copies = [
        pltpu.make_async_copy(source, target, sems.at[i])
        for i, (source, target) in enumerate(
            (
                (v_ref.at[0], up_ref.at[pl.ds(0, TC), :]),
                (v_ref.at[TR - 1], down_ref.at[pl.ds(0, TC), :]),
                (left_hbm_ref, left_ref),
                (right_hbm_ref, right_ref),
            )
        )
    ]
    for copy in copies:
        copy.start()
    for copy in copies:
        copy.wait()
    for row, out_ref in ((0, up_ref), (TR - 1, down_ref)):
        left = left_ref[row : row + 1, :].astype(f32)
        right = right_ref[row : row + 1, :].astype(f32)
        tail = jnp.concatenate([left, right, jnp.zeros((14, CH), f32)], axis=0)
        out_ref[pl.ds(TC, 16), :] = tail.astype(bf16)


def conv_kernel(
    v_hbm_ref,
    left_hbm_ref,
    right_hbm_ref,
    above_ref,
    below_ref,
    w_ref,
    out_ref,
    v_ref,
    left_ref,
    right_ref,
    l_ref,
    r_ref,
    sems,
):
    copies = [
        pltpu.make_async_copy(source, target, sems.at[i])
        for i, (source, target) in enumerate(
            ((left_hbm_ref, left_ref), (right_hbm_ref, right_ref), (v_hbm_ref, v_ref))
        )
    ]
    for copy in copies:
        copy.start()
    for copy in copies:
        copy.wait()
    l_ref[...] = left_ref[...].astype(f32)
    r_ref[...] = right_ref[...].astype(f32)
    for half in range(2):
        cols = pl.ds(half * 128, 128)

        def put(at, total):
            out_ref[pl.ds(at, TC), cols] = total

        w = [jnp.broadcast_to(w_ref[t : t + 1, cols], (TC, 128)) for t in range(9)]
        column = lax.broadcasted_iota(jnp.int32, (TC, 128), 0)

        def taps(row, left, right):
            row = row.astype(f32)
            before = jnp.where(column == 0, left, pltpu.roll(row, 1, 0))
            after = jnp.where(column == TC - 1, right, pltpu.roll(row, TC - 1, 0))
            return [before * w[3 * d] + row * w[3 * d + 1] + after * w[3 * d + 2] for d in range(3)]

        tail = above_ref[pl.ds(TC, 16), cols].astype(f32)
        t0 = taps(above_ref[pl.ds(0, TC), cols], tail[0:1], tail[1:2])

        def group(start, carry):
            a, b = carry
            lefts, rights = l_ref[pl.ds(start, 8), cols], r_ref[pl.ds(start, 8), cols]
            for k in range(8):
                t = taps(v_ref[start + k, :, cols], lefts[k : k + 1], rights[k : k + 1])
                if a is not None:
                    at = (start + k - 1) * TC
                    if not isinstance(at, int):
                        at = pl.multiple_of(at, TC)
                    put(at, a + t[2])
                a, b = b + t[1], t[0]
            return a, b

        carry = group(0, (None, t0[0]))
        a, b = lax.fori_loop(
            1, TR // 8, lambda g, c: group(pl.multiple_of(g * 8, 8), c), carry
        )
        tail = below_ref[pl.ds(TC, 16), cols].astype(f32)
        t = taps(below_ref[pl.ds(0, TC), cols], tail[0:1], tail[1:2])
        put((TR - 1) * TC, a + t[2])


def attend_kernel(av_ref, prob_ref, conv_hbm_ref, sum_ref, stat_ref, conv_ref, sem):
    fetch = pltpu.make_async_copy(conv_hbm_ref, conv_ref, sem)
    fetch.start()
    eye = lax.broadcasted_iota(jnp.int32, (128, 128), 0) == lanes((128, 128))
    for pair in range(2):
        pieces = []
        for parity in range(2):
            part = av_ref[pl.ds((2 * pair + parity) * 128, 128), :].astype(f32)
            other = pltpu.roll(part, HD, 1)
            own = half_mask(part.shape, parity)
            for piece in (part, other) if parity == 0 else (other, part):
                pieces.append(jnp.where(own, piece, 0.0))
        agent_values = jnp.concatenate(pieces, axis=0).astype(bf16)
        for b in range(N // 512):
            rows = pl.ds(b * 512, 512)
            sum_ref[rows, pl.ds(pair * 128, 128)] = jnp.dot(
                prob_ref[rows, pl.ds(pair * 2 * AGENTS, 2 * AGENTS)],
                agent_values,
                preferred_element_type=f32,
            )
    fetch.wait()
    for b in range(BLOCKS):
        rows = pl.ds(b * 128, 128)
        x = sum_ref[rows, :] + conv_ref[rows, :]
        sum_ref[rows, :] = x
        mean = jnp.sum(x[:, :128] + x[:, 128:], 1, keepdims=True) * (1.0 / CH)
        x = x - mean
        x = x * x
        squares = jnp.sum(x[:, :128] + x[:, 128:], 1, keepdims=True)
        stat_ref[b : b + 1, :] = jnp.sum(jnp.where(eye, mean, 0.0), 0, keepdims=True)
        stat_ref[BLOCKS + b : BLOCKS + b + 1, :] = jnp.sum(
            jnp.where(eye, squares, 0.0), 0, keepdims=True
        )


def norm_kernel(s0_ref, s1_ref, s2_ref, s3_ref, sum_ref, gain_ref, bias_ref, out_ref, done_ref, sems):
    stats = [s[...] for s in (s0_ref, s1_ref, s2_ref, s3_ref)]
    means = [s[:BLOCKS] for s in stats]
    mean = (means[0] + means[1] + means[2] + means[3]) * 0.25
    squares = sum(s[BLOCKS:] for s in stats)
    for m in means:
        squares = squares + CH * (m - mean) * (m - mean)
    scale = lax.rsqrt(squares * (1.0 / D) + epsilon)
    step = N // AGR
    copies = []
    for b in range(BLOCKS):
        rows = pl.ds(b * 128, 128)
        m = jnp.broadcast_to(mean[b : b + 1], (128, 128)).T
        s = jnp.broadcast_to(scale[b : b + 1], (128, 128)).T
        for half in range(2):
            cols = pl.ds(half * 128, 128)
            done_ref[rows, cols] = (
                (sum_ref[rows, cols] - m) * s * gain_ref[0:1, cols] + bias_ref[0:1, cols]
            ).astype(bf16)
        if (b + 1) * 128 % step == 0:
            part = pl.ds((b + 1) * 128 - step, step)
            copy = pltpu.make_async_copy(
                done_ref.at[part, :], out_ref.at[part, :], sems.at[len(copies)]
            )
            copy.start()
            copies.append(copy)
    for copy in copies:
        copy.wait()


def spread(x):
    slot = x.reshape(TILES, x.shape[0] // TILES, 128)
    return lax.all_to_all(slot, ("row", "col"), 0, 0).reshape(x.shape)


def shift(x, axis, step):
    count = lax.axis_size(axis)
    pairs = [(i, i + step) for i in range(count) if 0 <= i + step < count]
    return lax.ppermute(x, axis, pairs)


def after(x, *others):
    return lax.optimization_barrier((x, *others))[0]


def shards(queries, keys, values, positions, conv_weight, norm_gain, norm_bias):
    q = queries.reshape(N, CH)
    k = keys.reshape(N, CH)
    v = values.reshape(N, CH)
    mb = 1 << 20
    packed, table = call(
        query_kernel,
        (far((TILES * 8, 128), bf16), far((2, TR + TC, 128), f32)),
        "hh",
        scratch=[
            pltpu.VMEM((N, CH), bf16),
            pltpu.VMEM((2, TC, TR), jnp.int32),
            pltpu.SemaphoreType.DMA((AGR + 1,)),
        ],
        nbytes=8 * mb,
        name="pool_queries",
    )(jnp.swapaxes(positions, 1, 2), q)
    agents = spread(packed)
    held_table = pltpu.VMEM((2, TR + TC, 128), f32)
    tk, first, last = call(
        key_kernel,
        (near((N, CH), bf16),) + (far((TR, CH), bf16),) * 2,
        "h h",
        scratch=[held_table, pltpu.VMEM((N, CH), bf16), pltpu.SemaphoreType.DMA((AGR + 1,))],
        nbytes=4 * mb,
        name="turn_keys",
    )(table, values, k)
    parts = call(
        partial_kernel,
        far((TILES * ROWS, 128), bf16),
        " v ",
        scratch=[pltpu.VMEM((AGENTS, N), f32)],
        nbytes=10 * mb,
        name="partials",
    )(agents, tk, v)
    last, first, parts = lax.optimization_barrier((last, first, parts))
    left = shift(last, "col", 1)
    right = shift(first, "col", -1)
    received = spread(parts)
    prob = call(
        probability_kernel,
        near((N, LOCAL_HEADS * AGENTS), bf16),
        " hh",
        scratch=[
            held_table,
            pltpu.VMEM((N, CH), bf16),
            pltpu.SemaphoreType.DMA((N // 256 + 1,)),
        ],
        nbytes=20 * mb,
        name="probabilities",
    )(agents, table, q)
    received = after(received, prob, left, right)
    merged = call(merge_kernel, far((TILES * 8, 128), bf16), " ", nbytes=2 * mb, name="merge")(
        received
    )
    left, right, merged = lax.optimization_barrier((left, right, merged))
    up, down = call(
        line_kernel,
        (near((TC + 16, CH), bf16),) * 2,
        "hhh",
        scratch=[pltpu.VMEM((TR, CH), bf16)] * 2 + [pltpu.SemaphoreType.DMA((4,))],
        nbytes=mb // 4,
        name="lines",
    )(values, left, right)
    above = shift(down, "row", 1)
    below = shift(up, "row", -1)
    agent_values = spread(merged)
    convolved = call(
        conv_kernel,
        far((N, CH), f32),
        "hhh   ",
        scratch=[pltpu.VMEM((TR, TC, CH), bf16)]
        + [pltpu.VMEM((TR, CH), bf16)] * 2
        + [pltpu.VMEM((TR, CH), f32)] * 2
        + [pltpu.SemaphoreType.DMA((3,))],
        nbytes=6 * mb,
        name="conv",
    )(values, left, right, above, below, conv_weight)
    summed, stats = call(
        attend_kernel,
        (near((N, CH), f32), near((2 * BLOCKS, 128), f32)),
        " vh",
        scratch=[pltpu.VMEM((N, CH), f32), pltpu.SemaphoreType.DMA(())],
        nbytes=4 * mb,
        name="attend",
    )(agent_values, prob, convolved)
    heads = lax.axis_size("head")
    others = [
        lax.ppermute(stats, "head", [(i, (i + d) % heads) for i in range(heads)])
        for d in range(1, heads)
    ]
    normed = call(
        norm_kernel,
        (shape((N, CH), bf16),),
        "v   v  ",
        scratch=[pltpu.VMEM((N, CH), bf16), pltpu.SemaphoreType.DMA((AGR,))],
        nbytes=4 * mb,
        out_spaces="h",
        name="norm",
    )(
        stats, *others, summed, norm_gain.reshape(1, CH), norm_bias.reshape(1, CH)
    )[0]
    return normed.reshape(TR, TC, CH)


def solution(mesh):
    in_specs = (
        P("row", "col", "head"),
        P("row", "col", "head"),
        P("row", "col", "head"),
        P(None, "row", "col"),
        P(None, "head"),
        P("head"),
        P("head"),
    )
    out_specs = P("row", "col", "head")
    return jax.shard_map(shards, mesh=mesh, in_specs=in_specs, out_specs=out_specs, check_vma=False)
```

```python
import math

import jax
import jax.numpy as jnp
from jax import lax
from jax.experimental import pallas as pl
from jax.experimental.pallas import tpu as pltpu
from jax.sharding import PartitionSpec as P

HD = 64
D = 1024
AGR = 4
TR = 48
TC = 32
CH = 256
N = TR * TC
AGENTS = 256
TILES = 64
LOCAL_HEADS = 4
ROWS = LOCAL_HEADS * AGENTS // TILES
BLOCKS = N // 128

f32 = jnp.float32
bf16 = jnp.bfloat16
epsilon = 1e-05

VMEM_SPEC = pl.BlockSpec(memory_space=pltpu.VMEM)
HBM_SPEC = pl.BlockSpec(memory_space=pltpu.HBM)


def call(kernel, outs, in_spaces, scratch=(), nbytes=0, name=None, out_spaces=None):
    fn = pl.pallas_call(
        kernel,
        out_shape=outs,
        in_specs=[HBM_SPEC if c == "h" else VMEM_SPEC for c in in_spaces],
        out_specs=(
            tuple(HBM_SPEC if c == "h" else VMEM_SPEC for c in out_spaces or " " * len(outs))
            if isinstance(outs, tuple)
            else VMEM_SPEC
        ),
        scratch_shapes=list(scratch),
        compiler_params=pltpu.CompilerParams(vmem_limit_bytes=20 * 1024 * 1024),
        cost_estimate=pl.CostEstimate(flops=0, bytes_accessed=nbytes, transcendentals=0),
        name=name,
    )

    def run(*args):
        spaces = {"h": pltpu.HBM, "v": pltpu.VMEM}
        return fn(
            *[
                pltpu.with_memory_space_constraint(x, spaces[c]) if c in spaces else x
                for x, c in zip(args, in_spaces, strict=True)
            ]
        )

    return run


def shape(dims, dtype):
    return jax.ShapeDtypeStruct(dims, dtype)


def near(dims, dtype):
    return pltpu.VMEM(dims, dtype)


def far(dims, dtype):
    return pltpu.HBM(dims, dtype)


def lanes(dims):
    return lax.broadcasted_iota(jnp.int32, dims, len(dims) - 1)


def turn_matrix():
    source = lax.broadcasted_iota(jnp.int32, (CH, CH), 0)
    target = lax.broadcasted_iota(jnp.int32, (CH, CH), 1)
    low = (target & 31) < 16
    minus = jnp.where(low & (source == target + 16), -1.0, 0.0)
    plus = jnp.where((~low) & (source == target - 16), 1.0, 0.0)
    return (minus + plus).astype(bf16)


def sin_cos(angle):
    return jnp.sin(angle), jnp.cos(angle)


def turned(x, matrix, cosine, sine):
    swapped = jnp.dot(x, matrix, preferred_element_type=f32)
    return (x.astype(f32) * cosine + swapped * sine).astype(bf16)


def split_tables(cosines, sines):
    cosines = jnp.concatenate([cosines, cosines], axis=1)
    sines = jnp.concatenate([sines, sines], axis=1)
    return cosines[:TR], sines[:TR], cosines[TR:], sines[TR:]


def cell_tables(tables, first, rows):
    cos_r, sin_r, cos_c, sin_c = tables
    cosine = jnp.concatenate(
        [cos_r[first + i : first + i + 1, :] * cos_c for i in range(rows)], axis=0
    )
    sine = jnp.concatenate(
        [sin_r[first + i : first + i + 1, :] + sin_c for i in range(rows)], axis=0
    )
    return cosine, sine


def slots(block):
    twice = jnp.concatenate([block, block], axis=0).astype(bf16)
    return jnp.broadcast_to(twice[None], (TILES // 2, 16, 128)).reshape(TILES * 8, 128)


def query_kernel(
    pos_ref,
    q_ref,
    agents_ref,
    tab_ref,
    held_ref,
    spot_ref,
    sems,
):
    step = N // AGR
    place = pltpu.make_async_copy(pos_ref, spot_ref, sems.at[AGR])
    place.start()
    copies = []
    for cell in range(AGR):
        part = pl.ds(cell * step, step)
        copy = pltpu.make_async_copy(q_ref.at[part, :], held_ref.at[part, :], sems.at[cell])
        copy.start()
        copies.append(copy)
    matrix = turn_matrix()
    lane = lanes((1, 128)) % HD
    power = jnp.exp((lane % 16).astype(f32) * f32(-math.log(100.0) / 16))
    freq_r = jnp.where(lane < 32, power, 0.0)
    freq_c = jnp.where(lane < 32, 0.0, power)
    place.wait()
    row_line = spot_ref[0][0:1, :].astype(f32)
    col_pos = spot_ref[1][:, 0:1].astype(f32)
    eye = lax.broadcasted_iota(jnp.int32, (TR, TR), 0) == lax.broadcasted_iota(
        jnp.int32, (TR, TR), 1
    )
    row_pos = jnp.sum(jnp.where(eye, jnp.broadcast_to(row_line, (TR, TR)), 0.0), 1, keepdims=True)
    angles = jnp.concatenate([row_pos * freq_r, col_pos * freq_c], axis=0)
    sines, cosines = sin_cos(angles)
    tab_ref[0] = cosines
    tab_ref[1] = sines
    tables = split_tables(cosines, sines)
    means = []
    for cell in range(AGR):
        cosine, sine = cell_tables(tables, cell * (TR // AGR), TR // AGR)
        copies[cell].wait()
        rotated = turned(held_ref[pl.ds(cell * step, step), :], matrix, cosine, sine)
        mean = jnp.sum(rotated.astype(f32), 0, keepdims=True) / step
        means.append(mean.astype(bf16).astype(f32))
    packed = jnp.concatenate([m[:, :128] for m in means] + [m[:, 128:] for m in means], axis=0)
    agents_ref[...] = slots(packed)


def even_core():
    return lax.rem(lax.axis_index("col"), 2) == 0


def even_row():
    return lax.rem(lax.axis_index("row"), 2) == 0


def key_kernel(
    tab_hbm_ref,
    v_ref,
    k_ref,
    tk_ref,
    near_ref,
    far_ref,
    tab_ref,
    held_ref,
    sems,
):
    step = N // AGR
    table = pltpu.make_async_copy(tab_hbm_ref, tab_ref, sems.at[AGR])
    table.start()
    copies = []
    for cell in range(AGR):
        part = pl.ds(cell * step, step)
        copies.append(
            pltpu.make_async_copy(k_ref.at[part, :], held_ref.at[part, :], sems.at[cell])
        )
        copies[cell].start()
    first, last = v_ref[:, 0, :], v_ref[:, TC - 1, :]
    even = even_core()
    near_ref[...] = jnp.where(even, last, first)
    far_ref[...] = jnp.where(even, first, last)
    matrix = turn_matrix()
    table.wait()
    tables = split_tables(tab_ref[0], tab_ref[1])
    for cell in range(AGR):
        part = pl.ds(cell * step, step)
        cosine, sine = cell_tables(tables, cell * (TR // AGR), TR // AGR)
        copies[cell].wait()
        tk_ref[part, :] = turned(held_ref[part, :], matrix, cosine, sine)


def agent_pairs(agents_ref, scale):
    target = lax.broadcasted_iota(jnp.int32, (AGENTS, TILES * 8), 0)
    source = lax.broadcasted_iota(jnp.int32, (AGENTS, TILES * 8), 1)
    agents = agents_ref[...]
    pairs = []
    for pair in range(2):
        wanted = (target & (TILES - 1)) * 8 + (target // TILES) + 4 * pair
        pick = jnp.where(source == wanted, scale, 0.0).astype(bf16)
        pairs.append(jnp.dot(pick, agents, preferred_element_type=f32).astype(bf16))
    return pairs


def half_mask(dims, parity):
    return (lanes(dims) // HD) == parity


def partial_kernel(agents_ref, tk_ref, v_ref, out_ref, score_ref):
    pairs = agent_pairs(agents_ref, 1.0 / math.sqrt(HD))
    chunk = 512
    for head in range(LOCAL_HEADS):
        pair, parity = head // 2, head % 2
        cols = pl.ds(pair * 128, 128)
        own = pairs[pair]
        own = jnp.where(half_mask(own.shape, parity), own, jnp.zeros_like(own))
        peak = None
        for c in range(N // chunk):
            scores = lax.dot_general(
                own,
                tk_ref[pl.ds(c * chunk, chunk), cols],
                (((1,), (1,)), ((), ())),
                preferred_element_type=f32,
            )
            score_ref[:, pl.ds(c * chunk, chunk)] = scores
            for s in range(chunk // 128):
                piece = scores[:, s * 128 : (s + 1) * 128]
                peak = piece if peak is None else jnp.maximum(peak, piece)
        peak = jnp.max(peak, 1, keepdims=True)
        acc = jnp.zeros((AGENTS, 128), f32)
        for c in range(N // chunk):
            weights = jnp.exp(score_ref[:, pl.ds(c * chunk, chunk)] - peak).astype(bf16)
            block = v_ref[pl.ds(c * chunk, chunk), cols]
            block = jnp.where(half_mask(block.shape, parity), block, jnp.ones_like(block))
            acc = acc + jnp.dot(weights, block, preferred_element_type=f32)
        other = pltpu.roll(acc, HD, 1)
        numer, total = (acc, other) if parity == 0 else (other, acc)
        logs = peak + jnp.log(total)
        values = numer / total
        logs = jnp.max(jnp.where(half_mask(logs.shape, 0), logs, -3e38), 1, keepdims=True)
        first = logs.astype(bf16).astype(f32)
        second = (logs - first).astype(bf16).astype(f32)
        third = logs - first - second
        lane = lanes((AGENTS, 128))
        packed = jnp.where(
            lane < HD,
            values,
            jnp.where(
                lane == HD,
                first,
                jnp.where(lane == HD + 1, second, jnp.where(lane == HD + 2, third, 0.0)),
            ),
        )
        groups = packed.reshape(2, ROWS, 8, 128)
        groups = jnp.concatenate([groups[0], groups[1]], 1).reshape(AGENTS, 128)
        out_ref[pl.ds(head * AGENTS, AGENTS), :] = groups.astype(bf16)


def merge_kernel(parts_ref, out_ref):
    source = lax.broadcasted_iota(jnp.int32, (128, 128), 0)
    picker = jnp.where((source >= HD) & (source < HD + 3), 1.0, 0.0).astype(bf16)
    parts = parts_ref[...]
    logs = jnp.dot(parts, picker, preferred_element_type=f32).reshape(TILES, ROWS, 128)
    values = parts.astype(f32).reshape(TILES, ROWS, 128)
    peak = jnp.max(logs, 0)
    weights = jnp.exp(logs - peak[None])
    merged = jnp.sum(weights * values, 0) / jnp.sum(weights, 0)
    merged = jnp.where(lanes((8, 128)) < HD, merged[:8], pltpu.roll(merged[8:], HD, 1))
    out_ref[...] = slots(merged)


def probability_kernel(agents_ref, tab_hbm_ref, q_ref, prob_ref, tab_ref, held_ref, sems):
    chunk = 256
    table = pltpu.make_async_copy(tab_hbm_ref, tab_ref, sems.at[N // chunk])
    table.start()

    def fetch(c):
        rows = pl.ds(pl.multiple_of(c * chunk, chunk), chunk)
        return pltpu.make_async_copy(q_ref.at[rows, :], held_ref.at[rows, :], sems.at[c])

    for c in range(N // chunk):
        fetch(c).start()
    pairs = agent_pairs(agents_ref, 1.0 / math.sqrt(HD))
    matrix = turn_matrix()
    table.wait()
    ones = jnp.ones((AGENTS, 128), bf16)
    owns = []
    for head in range(LOCAL_HEADS):
        own = pairs[head // 2]
        owns.append(jnp.where(half_mask(own.shape, head % 2), own, jnp.zeros_like(own)))

    def body(c, carry):
        fetch(c).wait()
        rows = pl.ds(pl.multiple_of(c * chunk, chunk), chunk)
        lines = pl.ds(pl.multiple_of(c * (chunk // TC), chunk // TC), chunk // TC)
        near_rows = [tab_ref[i, lines, :] for i in range(2)]
        near_cols = [tab_ref[i, pl.ds(TR, TC), :] for i in range(2)]
        tables = [jnp.concatenate([t, t], axis=1) for t in near_rows + near_cols]
        cosine, sine = cell_tables(tables, 0, chunk // TC)
        queries = turned(held_ref[rows, :], matrix, cosine, sine)
        for head in range(LOCAL_HEADS):
            scores = lax.dot_general(
                queries[:, head // 2 * 128 : head // 2 * 128 + 128],
                owns[head],
                (((1,), (1,)), ((), ())),
                preferred_element_type=f32,
            )
            weights = jnp.exp(scores - jnp.max(scores, 1, keepdims=True))
            total = jnp.dot(weights.astype(bf16), ones, preferred_element_type=f32)
            scale = 1.0 / total
            scale = jnp.concatenate([scale, scale], axis=1)
            prob_ref[rows, pl.ds(head * AGENTS, AGENTS)] = (weights * scale).astype(bf16)
        return carry

    lax.fori_loop(0, N // chunk, body, 0)


def line_kernel(
    v_ref,
    near_hbm_ref,
    far_hbm_ref,
    mate_ref,
    rest_ref,
    top_ref,
    bottom_ref,
    near_ref,
    far_ref,
    sems,
):
    copies = [
        pltpu.make_async_copy(source, target, sems.at[i])
        for i, (source, target) in enumerate(
            (
                (v_ref.at[0], top_ref),
                (v_ref.at[TR - 1], bottom_ref),
                (near_hbm_ref, near_ref),
                (far_hbm_ref, far_ref),
            )
        )
    ]
    for copy in copies:
        copy.start()
    for copy in copies:
        copy.wait()
    lines = []
    for row, line_ref in ((0, top_ref), (TR - 1, bottom_ref)):
        mate = near_ref[row : row + 1, :].astype(f32)
        rest = far_ref[row : row + 1, :].astype(f32)
        left = jnp.where(even_core(), rest, mate)
        right = jnp.where(even_core(), mate, rest)
        tail = jnp.concatenate([left, right, jnp.zeros((14, CH), f32)], axis=0)
        lines.append(jnp.concatenate([line_ref[...].astype(f32), tail], axis=0))
    mate_ref[...] = jnp.where(even_row(), lines[1], lines[0]).astype(bf16)
    rest_ref[...] = jnp.where(even_row(), lines[0], lines[1]).astype(bf16)


def conv_kernel(
    v_hbm_ref,
    near_hbm_ref,
    far_hbm_ref,
    mate_ref,
    rest_ref,
    w_ref,
    out_hbm_ref,
    v_ref,
    near_ref,
    far_ref,
    above_ref,
    below_ref,
    l_ref,
    r_ref,
    out_ref,
    sems,
):
    copies = [
        pltpu.make_async_copy(near_hbm_ref, near_ref, sems.at[0]),
        pltpu.make_async_copy(far_hbm_ref, far_ref, sems.at[1]),
    ]
    for half in range(2):
        cols = pl.ds(half * 128, 128)
        copies.append(
            pltpu.make_async_copy(
                v_hbm_ref.at[:, :, cols], v_ref.at[:, :, cols], sems.at[2 + half]
            )
        )
    outs = []
    for half in range(2):
        cols = pl.ds(half * 128, 128)
        outs.append(
            pltpu.make_async_copy(
                out_ref.at[:, cols], out_hbm_ref.at[:, cols], sems.at[4 + half]
            )
        )
    for copy in copies:
        copy.start()
    mate, rest = mate_ref[...].astype(f32), rest_ref[...].astype(f32)
    above_ref[...] = jnp.where(even_row(), rest, mate)
    below_ref[...] = jnp.where(even_row(), mate, rest)
    copies[0].wait()
    copies[1].wait()
    mate, rest = near_ref[...].astype(f32), far_ref[...].astype(f32)
    l_ref[...] = jnp.where(even_core(), rest, mate)
    r_ref[...] = jnp.where(even_core(), mate, rest)
    for half in range(2):
        cols = pl.ds(half * 128, 128)
        copies[2 + half].wait()

        def put(at, total):
            out_ref[pl.ds(at, TC), cols] = total

        w = [jnp.broadcast_to(w_ref[t : t + 1, cols], (TC, 128)) for t in range(9)]
        column = lax.broadcasted_iota(jnp.int32, (TC, 128), 0)

        def taps(row, left, right):
            row = row.astype(f32)
            before = jnp.where(column == 0, left, pltpu.roll(row, 1, 0))
            after = jnp.where(column == TC - 1, right, pltpu.roll(row, TC - 1, 0))
            return [before * w[3 * d] + row * w[3 * d + 1] + after * w[3 * d + 2] for d in range(3)]

        tail = above_ref[pl.ds(TC, 8), cols]
        t0 = taps(above_ref[pl.ds(0, TC), cols], tail[0:1], tail[1:2])

        def group(start, carry):
            a, b = carry
            lefts, rights = l_ref[pl.ds(start, 8), cols], r_ref[pl.ds(start, 8), cols]
            for k in range(8):
                t = taps(v_ref[start + k, :, cols], lefts[k : k + 1], rights[k : k + 1])
                if a is not None:
                    at = (start + k - 1) * TC
                    if not isinstance(at, int):
                        at = pl.multiple_of(at, TC)
                    put(at, a + t[2])
                a, b = b + t[1], t[0]
            return a, b

        carry = group(0, (None, t0[0]))
        a, b = lax.fori_loop(
            1, TR // 8, lambda g, c: group(pl.multiple_of(g * 8, 8), c), carry
        )
        tail = below_ref[pl.ds(TC, 8), cols]
        t = taps(below_ref[pl.ds(0, TC), cols], tail[0:1], tail[1:2])
        put((TR - 1) * TC, a + t[2])
        outs[half].start()
    for copy in outs:
        copy.wait()


def attend_kernel(av_ref, prob_ref, conv_hbm_ref, sum_ref, stat_ref, conv_ref, sem):
    fetch = pltpu.make_async_copy(conv_hbm_ref, conv_ref, sem)
    fetch.start()
    eye = lax.broadcasted_iota(jnp.int32, (128, 128), 0) == lanes((128, 128))
    for pair in range(2):
        pieces = []
        for parity in range(2):
            part = av_ref[pl.ds((2 * pair + parity) * 128, 128), :].astype(f32)
            other = pltpu.roll(part, HD, 1)
            own = half_mask(part.shape, parity)
            for piece in (part, other) if parity == 0 else (other, part):
                pieces.append(jnp.where(own, piece, 0.0))
        agent_values = jnp.concatenate(pieces, axis=0).astype(bf16)
        for b in range(N // 512):
            rows = pl.ds(b * 512, 512)
            sum_ref[rows, pl.ds(pair * 128, 128)] = jnp.dot(
                prob_ref[rows, pl.ds(pair * 2 * AGENTS, 2 * AGENTS)],
                agent_values,
                preferred_element_type=f32,
            )
    fetch.wait()
    for b in range(BLOCKS):
        rows = pl.ds(b * 128, 128)
        x = sum_ref[rows, :] + conv_ref[rows, :]
        sum_ref[rows, :] = x
        mean = jnp.sum(x[:, :128] + x[:, 128:], 1, keepdims=True) * (1.0 / CH)
        x = x - mean
        x = x * x
        squares = jnp.sum(x[:, :128] + x[:, 128:], 1, keepdims=True)
        stat_ref[b : b + 1, :] = jnp.sum(jnp.where(eye, mean, 0.0), 0, keepdims=True)
        stat_ref[BLOCKS + b : BLOCKS + b + 1, :] = jnp.sum(
            jnp.where(eye, squares, 0.0), 0, keepdims=True
        )


def norm_kernel(s0_ref, s1_ref, s2_ref, s3_ref, sum_ref, gain_ref, bias_ref, out_ref, done_ref, sems):
    stats = [s[...] for s in (s0_ref, s1_ref, s2_ref, s3_ref)]
    means = [s[:BLOCKS] for s in stats]
    mean = (means[0] + means[1] + means[2] + means[3]) * 0.25
    squares = sum(s[BLOCKS:] for s in stats)
    for m in means:
        squares = squares + CH * (m - mean) * (m - mean)
    scale = lax.rsqrt(squares * (1.0 / D) + epsilon)
    step = N // AGR
    copies = []
    for b in range(BLOCKS):
        rows = pl.ds(b * 128, 128)
        m = jnp.broadcast_to(mean[b : b + 1], (128, 128)).T
        s = jnp.broadcast_to(scale[b : b + 1], (128, 128)).T
        for half in range(2):
            cols = pl.ds(half * 128, 128)
            done_ref[rows, cols] = (
                (sum_ref[rows, cols] - m) * s * gain_ref[0:1, cols] + bias_ref[0:1, cols]
            ).astype(bf16)
        if (b + 1) * 128 % step == 0:
            part = pl.ds((b + 1) * 128 - step, step)
            copy = pltpu.make_async_copy(
                done_ref.at[part, :], out_ref.at[part, :], sems.at[len(copies)]
            )
            copy.start()
            copies.append(copy)
    for copy in copies:
        copy.wait()


def spread(x):
    slot = x.reshape(TILES, x.shape[0] // TILES, 128)
    return lax.all_to_all(slot, ("row", "col"), 0, 0).reshape(x.shape)


def swap(x, axis, pairs):
    return lax.ppermute(x, axis, [p for i, j in pairs for p in ((i, j), (j, i))])


def chain(axis, first):
    return [(i, i + 1) for i in range(first, lax.axis_size(axis) - 1, 2)]


def after(x, *others):
    return lax.optimization_barrier((x, *others))[0]


def shards(queries, keys, values, positions, conv_weight, norm_gain, norm_bias):
    q = queries.reshape(N, CH)
    k = keys.reshape(N, CH)
    v = values.reshape(N, CH)
    mb = 1 << 20
    packed, table = call(
        query_kernel,
        (far((TILES * 8, 128), bf16), far((2, TR + TC, 128), f32)),
        "hh",
        scratch=[
            pltpu.VMEM((N, CH), bf16),
            pltpu.VMEM((2, TC, TR), jnp.int32),
            pltpu.SemaphoreType.DMA((AGR + 1,)),
        ],
        nbytes=8 * mb,
        name="pool_queries",
    )(jnp.swapaxes(positions, 1, 2), q)
    agents = spread(packed)
    held_table = pltpu.VMEM((2, TR + TC, 128), f32)
    tk, inner, outer = call(
        key_kernel,
        (near((N, CH), bf16),) + (far((TR, CH), bf16),) * 2,
        "h h",
        scratch=[held_table, pltpu.VMEM((N, CH), bf16), pltpu.SemaphoreType.DMA((AGR + 1,))],
        nbytes=4 * mb,
        name="turn_keys",
    )(table, values, k)
    parts = call(
        partial_kernel,
        far((TILES * ROWS, 128), bf16),
        " v ",
        scratch=[pltpu.VMEM((AGENTS, N), f32)],
        nbytes=10 * mb,
        name="partials",
    )(agents, tk, v)
    inner, outer, parts = lax.optimization_barrier((inner, outer, parts))
    inner = swap(inner, "col", chain("col", 0))
    outer = swap(outer, "col", chain("col", 1))
    received = spread(parts)
    mate, rest = call(
        line_kernel,
        (near((TC + 16, CH), bf16),) * 2,
        "hhh",
        scratch=[pltpu.VMEM((TC, CH), bf16)] * 2
        + [pltpu.VMEM((TR, CH), bf16)] * 2
        + [pltpu.SemaphoreType.DMA((4,))],
        nbytes=mb // 4,
        name="lines",
    )(values, inner, outer)
    received = after(received, mate, rest)
    mate = swap(mate, "row", chain("row", 0))
    rest = swap(rest, "row", chain("row", 1))
    merged = call(merge_kernel, far((TILES * 8, 128), bf16), " ", nbytes=2 * mb, name="merge")(
        received
    )
    merged = after(merged, mate, rest)
    agent_values = spread(merged)
    prob = call(
        probability_kernel,
        near((N, LOCAL_HEADS * AGENTS), bf16),
        " hh",
        scratch=[
            held_table,
            pltpu.VMEM((N, CH), bf16),
            pltpu.SemaphoreType.DMA((N // 256 + 1,)),
        ],
        nbytes=20 * mb,
        name="probabilities",
    )(after(agents, merged), table, q)
    convolved = call(
        conv_kernel,
        (far((N, CH), f32),),
        "hhh   ",
        scratch=[pltpu.VMEM((TR, TC, CH), bf16)]
        + [pltpu.VMEM((TR, CH), bf16)] * 2
        + [pltpu.VMEM((TC + 16, CH), f32)] * 2
        + [pltpu.VMEM((TR, CH), f32)] * 2
        + [pltpu.VMEM((N, CH), f32), pltpu.SemaphoreType.DMA((6,))],
        nbytes=6 * mb,
        out_spaces="h",
        name="conv",
    )(values, inner, outer, mate, rest, conv_weight)[0]
    summed, stats = call(
        attend_kernel,
        (near((N, CH), f32), near((2 * BLOCKS, 128), f32)),
        " vh",
        scratch=[pltpu.VMEM((N, CH), f32), pltpu.SemaphoreType.DMA(())],
        nbytes=4 * mb,
        name="attend",
    )(agent_values, prob, convolved)
    heads = lax.axis_size("head")
    others = [
        lax.ppermute(stats, "head", [(i, i ^ d) for i in range(heads)]) for d in range(1, heads)
    ]
    normed = call(
        norm_kernel,
        (shape((N, CH), bf16),),
        "v   v  ",
        scratch=[pltpu.VMEM((N, CH), bf16), pltpu.SemaphoreType.DMA((AGR,))],
        nbytes=4 * mb,
        out_spaces="h",
        name="norm",
    )(
        stats, *others, summed, norm_gain.reshape(1, CH), norm_bias.reshape(1, CH)
    )[0]
    return normed.reshape(TR, TC, CH)


def solution(mesh):
    in_specs = (
        P("row", "col", "head"),
        P("row", "col", "head"),
        P("row", "col", "head"),
        P(None, "row", "col"),
        P(None, "head"),
        P("head"),
        P("head"),
    )
    out_specs = P("row", "col", "head")
    return jax.shard_map(shards, mesh=mesh, in_specs=in_specs, out_specs=out_specs, check_vma=False)
```

```python
import math

import jax
import jax.numpy as jnp
from jax import lax
from jax.experimental import pallas as pl
from jax.experimental.pallas import tpu as pltpu
from jax.sharding import PartitionSpec as P

HD = 64
D = 1024
AGR = 4
TR = 48
TC = 32
CH = 256
N = TR * TC
AGENTS = 256
TILES = 64
LOCAL_HEADS = 4
ROWS = LOCAL_HEADS * AGENTS // TILES
BLOCKS = N // 128

f32 = jnp.float32
bf16 = jnp.bfloat16
epsilon = 1e-05

VMEM_SPEC = pl.BlockSpec(memory_space=pltpu.VMEM)
HBM_SPEC = pl.BlockSpec(memory_space=pltpu.HBM)


def call(kernel, outs, in_spaces, scratch=(), nbytes=0, name=None, out_spaces=None):
    fn = pl.pallas_call(
        kernel,
        out_shape=outs,
        in_specs=[HBM_SPEC if c == "h" else VMEM_SPEC for c in in_spaces],
        out_specs=(
            tuple(HBM_SPEC if c == "h" else VMEM_SPEC for c in out_spaces or " " * len(outs))
            if isinstance(outs, tuple)
            else VMEM_SPEC
        ),
        scratch_shapes=list(scratch),
        compiler_params=pltpu.CompilerParams(vmem_limit_bytes=20 * 1024 * 1024),
        cost_estimate=pl.CostEstimate(flops=0, bytes_accessed=nbytes, transcendentals=0),
        name=name,
    )

    def run(*args):
        spaces = {"h": pltpu.HBM, "v": pltpu.VMEM}
        return fn(
            *[
                pltpu.with_memory_space_constraint(x, spaces[c]) if c in spaces else x
                for x, c in zip(args, in_spaces, strict=True)
            ]
        )

    return run


def shape(dims, dtype):
    return jax.ShapeDtypeStruct(dims, dtype)


def near(dims, dtype):
    return pltpu.VMEM(dims, dtype)


def far(dims, dtype):
    return pltpu.HBM(dims, dtype)


def lanes(dims):
    return lax.broadcasted_iota(jnp.int32, dims, len(dims) - 1)


def turn_matrix():
    source = lax.broadcasted_iota(jnp.int32, (CH, CH), 0)
    target = lax.broadcasted_iota(jnp.int32, (CH, CH), 1)
    low = (target & 31) < 16
    minus = jnp.where(low & (source == target + 16), -1.0, 0.0)
    plus = jnp.where((~low) & (source == target - 16), 1.0, 0.0)
    return (minus + plus).astype(bf16)


def sin_cos(angle):
    return jnp.sin(angle), jnp.cos(angle)


def turned(x, matrix, cosine, sine):
    swapped = jnp.dot(x, matrix, preferred_element_type=f32)
    return (x.astype(f32) * cosine + swapped * sine).astype(bf16)


def split_tables(cosines, sines):
    cosines = jnp.concatenate([cosines, cosines], axis=1)
    sines = jnp.concatenate([sines, sines], axis=1)
    return cosines[:TR], sines[:TR], cosines[TR:], sines[TR:]


def cell_tables(tables, first, rows):
    cos_r, sin_r, cos_c, sin_c = tables
    cosine = jnp.concatenate(
        [cos_r[first + i : first + i + 1, :] * cos_c for i in range(rows)], axis=0
    )
    sine = jnp.concatenate(
        [sin_r[first + i : first + i + 1, :] + sin_c for i in range(rows)], axis=0
    )
    return cosine, sine


def slots(block):
    twice = jnp.concatenate([block, block], axis=0).astype(bf16)
    return jnp.broadcast_to(twice[None], (TILES // 2, 16, 128)).reshape(TILES * 8, 128)


def query_kernel(
    pos_ref,
    q_ref,
    agents_ref,
    tab_ref,
    held_ref,
    spot_ref,
    sems,
):
    step = N // AGR
    place = pltpu.make_async_copy(pos_ref, spot_ref, sems.at[AGR])
    place.start()
    copies = []
    for cell in range(AGR):
        part = pl.ds(cell * step, step)
        copy = pltpu.make_async_copy(q_ref.at[part, :], held_ref.at[part, :], sems.at[cell])
        copy.start()
        copies.append(copy)
    matrix = turn_matrix()
    lane = lanes((1, 128)) % HD
    power = jnp.exp((lane % 16).astype(f32) * f32(-math.log(100.0) / 16))
    freq_r = jnp.where(lane < 32, power, 0.0)
    freq_c = jnp.where(lane < 32, 0.0, power)
    place.wait()
    row_line = spot_ref[0][0:1, :].astype(f32)
    col_pos = spot_ref[1][:, 0:1].astype(f32)
    eye = lax.broadcasted_iota(jnp.int32, (TR, TR), 0) == lax.broadcasted_iota(
        jnp.int32, (TR, TR), 1
    )
    row_pos = jnp.sum(jnp.where(eye, jnp.broadcast_to(row_line, (TR, TR)), 0.0), 1, keepdims=True)
    angles = jnp.concatenate([row_pos * freq_r, col_pos * freq_c], axis=0)
    sines, cosines = sin_cos(angles)
    tab_ref[0] = cosines
    tab_ref[1] = sines
    tables = split_tables(cosines, sines)
    means = []
    for cell in range(AGR):
        cosine, sine = cell_tables(tables, cell * (TR // AGR), TR // AGR)
        copies[cell].wait()
        rotated = turned(held_ref[pl.ds(cell * step, step), :], matrix, cosine, sine)
        mean = jnp.sum(rotated.astype(f32), 0, keepdims=True) / step
        means.append(mean.astype(bf16).astype(f32))
    packed = jnp.concatenate([m[:, :128] for m in means] + [m[:, 128:] for m in means], axis=0)
    agents_ref[...] = slots(packed)


def even_core():
    return lax.rem(lax.axis_index("col"), 2) == 0


def even_row():
    return lax.rem(lax.axis_index("row"), 2) == 0


def key_kernel(
    tab_hbm_ref,
    v_ref,
    k_ref,
    tk_ref,
    near_ref,
    far_ref,
    tab_ref,
    held_ref,
    sems,
):
    step = N // AGR
    table = pltpu.make_async_copy(tab_hbm_ref, tab_ref, sems.at[AGR])
    table.start()
    copies = []
    for cell in range(AGR):
        part = pl.ds(cell * step, step)
        copies.append(
            pltpu.make_async_copy(k_ref.at[part, :], held_ref.at[part, :], sems.at[cell])
        )
        copies[cell].start()
    first, last = v_ref[:, 0, :], v_ref[:, TC - 1, :]
    even = even_core()
    near_ref[...] = jnp.where(even, last, first)
    far_ref[...] = jnp.where(even, first, last)
    matrix = turn_matrix()
    table.wait()
    tables = split_tables(tab_ref[0], tab_ref[1])
    for cell in range(AGR):
        part = pl.ds(cell * step, step)
        cosine, sine = cell_tables(tables, cell * (TR // AGR), TR // AGR)
        copies[cell].wait()
        tk_ref[part, :] = turned(held_ref[part, :], matrix, cosine, sine)


def agent_pairs(agents_ref, scale):
    target = lax.broadcasted_iota(jnp.int32, (AGENTS, TILES * 8), 0)
    source = lax.broadcasted_iota(jnp.int32, (AGENTS, TILES * 8), 1)
    agents = agents_ref[...]
    pairs = []
    for pair in range(2):
        wanted = (target & (TILES - 1)) * 8 + (target // TILES) + 4 * pair
        pick = jnp.where(source == wanted, scale, 0.0).astype(bf16)
        pairs.append(jnp.dot(pick, agents, preferred_element_type=f32).astype(bf16))
    return pairs


def half_mask(dims, parity):
    return (lanes(dims) // HD) == parity


def partial_kernel(agents_ref, tk_ref, v_ref, out_ref, score_ref):
    pairs = agent_pairs(agents_ref, 1.0 / math.sqrt(HD))
    chunk = 512
    for head in range(LOCAL_HEADS):
        pair, parity = head // 2, head % 2
        cols = pl.ds(pair * 128, 128)
        own = pairs[pair]
        own = jnp.where(half_mask(own.shape, parity), own, jnp.zeros_like(own))
        peak = None
        for c in range(N // chunk):
            scores = lax.dot_general(
                own,
                tk_ref[pl.ds(c * chunk, chunk), cols],
                (((1,), (1,)), ((), ())),
                preferred_element_type=f32,
            )
            score_ref[:, pl.ds(c * chunk, chunk)] = scores
            for s in range(chunk // 128):
                piece = scores[:, s * 128 : (s + 1) * 128]
                peak = piece if peak is None else jnp.maximum(peak, piece)
        peak = jnp.max(peak, 1, keepdims=True)
        acc = jnp.zeros((AGENTS, 128), f32)
        for c in range(N // chunk):
            weights = jnp.exp(score_ref[:, pl.ds(c * chunk, chunk)] - peak).astype(bf16)
            block = v_ref[pl.ds(c * chunk, chunk), cols]
            block = jnp.where(half_mask(block.shape, parity), block, jnp.ones_like(block))
            acc = acc + jnp.dot(weights, block, preferred_element_type=f32)
        other = pltpu.roll(acc, HD, 1)
        numer, total = (acc, other) if parity == 0 else (other, acc)
        logs = peak + jnp.log(total)
        values = numer / total
        logs = jnp.max(jnp.where(half_mask(logs.shape, 0), logs, -3e38), 1, keepdims=True)
        first = logs.astype(bf16).astype(f32)
        second = (logs - first).astype(bf16).astype(f32)
        third = logs - first - second
        lane = lanes((AGENTS, 128))
        packed = jnp.where(
            lane < HD,
            values,
            jnp.where(
                lane == HD,
                first,
                jnp.where(lane == HD + 1, second, jnp.where(lane == HD + 2, third, 0.0)),
            ),
        )
        groups = packed.reshape(2, ROWS, 8, 128)
        groups = jnp.concatenate([groups[0], groups[1]], 1).reshape(AGENTS, 128)
        out_ref[pl.ds(head * AGENTS, AGENTS), :] = groups.astype(bf16)


def merge_kernel(parts_ref, out_ref):
    source = lax.broadcasted_iota(jnp.int32, (128, 128), 0)
    picker = jnp.where((source >= HD) & (source < HD + 3), 1.0, 0.0).astype(bf16)
    parts = parts_ref[...]
    logs = jnp.dot(parts, picker, preferred_element_type=f32).reshape(TILES, ROWS, 128)
    values = parts.astype(f32).reshape(TILES, ROWS, 128)
    peak = jnp.max(logs, 0)
    weights = jnp.exp(logs - peak[None])
    merged = jnp.sum(weights * values, 0) / jnp.sum(weights, 0)
    merged = jnp.where(lanes((8, 128)) < HD, merged[:8], pltpu.roll(merged[8:], HD, 1))
    out_ref[...] = slots(merged)


def probability_kernel(agents_ref, tab_hbm_ref, q_ref, prob_ref, tab_ref, held_ref, sems):
    chunk = 256
    table = pltpu.make_async_copy(tab_hbm_ref, tab_ref, sems.at[N // chunk])
    table.start()

    def fetch(c):
        rows = pl.ds(pl.multiple_of(c * chunk, chunk), chunk)
        return pltpu.make_async_copy(q_ref.at[rows, :], held_ref.at[rows, :], sems.at[c])

    for c in range(N // chunk):
        fetch(c).start()
    pairs = agent_pairs(agents_ref, 1.0 / math.sqrt(HD))
    matrix = turn_matrix()
    table.wait()
    ones = jnp.ones((AGENTS, 128), bf16)
    owns = []
    for head in range(LOCAL_HEADS):
        own = pairs[head // 2]
        owns.append(jnp.where(half_mask(own.shape, head % 2), own, jnp.zeros_like(own)))

    def body(c, carry):
        fetch(c).wait()
        rows = pl.ds(pl.multiple_of(c * chunk, chunk), chunk)
        lines = pl.ds(pl.multiple_of(c * (chunk // TC), chunk // TC), chunk // TC)
        near_rows = [tab_ref[i, lines, :] for i in range(2)]
        near_cols = [tab_ref[i, pl.ds(TR, TC), :] for i in range(2)]
        tables = [jnp.concatenate([t, t], axis=1) for t in near_rows + near_cols]
        cosine, sine = cell_tables(tables, 0, chunk // TC)
        queries = turned(held_ref[rows, :], matrix, cosine, sine)
        for head in range(LOCAL_HEADS):
            scores = lax.dot_general(
                queries[:, head // 2 * 128 : head // 2 * 128 + 128],
                owns[head],
                (((1,), (1,)), ((), ())),
                preferred_element_type=f32,
            )
            weights = jnp.exp(scores - jnp.max(scores, 1, keepdims=True))
            total = jnp.dot(weights.astype(bf16), ones, preferred_element_type=f32)
            scale = 1.0 / total
            scale = jnp.concatenate([scale, scale], axis=1)
            prob_ref[rows, pl.ds(head * AGENTS, AGENTS)] = (weights * scale).astype(bf16)
        return carry

    lax.fori_loop(0, N // chunk, body, 0)


def line_kernel(
    v_ref,
    near_hbm_ref,
    far_hbm_ref,
    mate_ref,
    rest_ref,
    top_ref,
    bottom_ref,
    near_ref,
    far_ref,
    sems,
):
    copies = [
        pltpu.make_async_copy(source, target, sems.at[i])
        for i, (source, target) in enumerate(
            (
                (v_ref.at[0], top_ref),
                (v_ref.at[TR - 1], bottom_ref),
                (near_hbm_ref, near_ref),
                (far_hbm_ref, far_ref),
            )
        )
    ]
    for copy in copies:
        copy.start()
    for copy in copies:
        copy.wait()
    lines = []
    for row, line_ref in ((0, top_ref), (TR - 1, bottom_ref)):
        mate = near_ref[row : row + 1, :].astype(f32)
        rest = far_ref[row : row + 1, :].astype(f32)
        left = jnp.where(even_core(), rest, mate)
        right = jnp.where(even_core(), mate, rest)
        tail = jnp.concatenate([left, right, jnp.zeros((14, CH), f32)], axis=0)
        lines.append(jnp.concatenate([line_ref[...].astype(f32), tail], axis=0))
    mate_ref[...] = jnp.where(even_row(), lines[1], lines[0]).astype(bf16)
    rest_ref[...] = jnp.where(even_row(), lines[0], lines[1]).astype(bf16)


def conv_kernel(
    v_hbm_ref,
    near_hbm_ref,
    far_hbm_ref,
    mate_ref,
    rest_ref,
    w_ref,
    out_hbm_ref,
    v_ref,
    near_ref,
    far_ref,
    above_ref,
    below_ref,
    l_ref,
    r_ref,
    out_ref,
    sems,
):
    copies = [
        pltpu.make_async_copy(near_hbm_ref, near_ref, sems.at[0]),
        pltpu.make_async_copy(far_hbm_ref, far_ref, sems.at[1]),
    ]
    for half in range(2):
        cols = pl.ds(half * 128, 128)
        copies.append(
            pltpu.make_async_copy(
                v_hbm_ref.at[:, :, cols], v_ref.at[:, :, cols], sems.at[2 + half]
            )
        )
    outs = []
    for half in range(2):
        cols = pl.ds(half * 128, 128)
        outs.append(
            pltpu.make_async_copy(
                out_ref.at[:, cols], out_hbm_ref.at[:, cols], sems.at[4 + half]
            )
        )
    for copy in copies:
        copy.start()
    mate, rest = mate_ref[...].astype(f32), rest_ref[...].astype(f32)
    above_ref[...] = jnp.where(even_row(), rest, mate)
    below_ref[...] = jnp.where(even_row(), mate, rest)
    copies[0].wait()
    copies[1].wait()
    mate, rest = near_ref[...].astype(f32), far_ref[...].astype(f32)
    l_ref[...] = jnp.where(even_core(), rest, mate)
    r_ref[...] = jnp.where(even_core(), mate, rest)
    for half in range(2):
        cols = pl.ds(half * 128, 128)
        copies[2 + half].wait()

        def put(at, total):
            out_ref[pl.ds(at, TC), cols] = total

        w = [jnp.broadcast_to(w_ref[t : t + 1, cols], (TC, 128)) for t in range(9)]
        column = lax.broadcasted_iota(jnp.int32, (TC, 128), 0)

        def taps(row, left, right):
            row = row.astype(f32)
            before = jnp.where(column == 0, left, pltpu.roll(row, 1, 0))
            after = jnp.where(column == TC - 1, right, pltpu.roll(row, TC - 1, 0))
            return [before * w[3 * d] + row * w[3 * d + 1] + after * w[3 * d + 2] for d in range(3)]

        tail = above_ref[pl.ds(TC, 8), cols]
        t0 = taps(above_ref[pl.ds(0, TC), cols], tail[0:1], tail[1:2])

        def group(start, carry):
            a, b = carry
            lefts, rights = l_ref[pl.ds(start, 8), cols], r_ref[pl.ds(start, 8), cols]
            for k in range(8):
                t = taps(v_ref[start + k, :, cols], lefts[k : k + 1], rights[k : k + 1])
                if a is not None:
                    at = (start + k - 1) * TC
                    if not isinstance(at, int):
                        at = pl.multiple_of(at, TC)
                    put(at, a + t[2])
                a, b = b + t[1], t[0]
            return a, b

        carry = group(0, (None, t0[0]))
        a, b = lax.fori_loop(
            1, TR // 8, lambda g, c: group(pl.multiple_of(g * 8, 8), c), carry
        )
        tail = below_ref[pl.ds(TC, 8), cols]
        t = taps(below_ref[pl.ds(0, TC), cols], tail[0:1], tail[1:2])
        put((TR - 1) * TC, a + t[2])
        outs[half].start()
    for copy in outs:
        copy.wait()


def attend_kernel(av_ref, prob_ref, conv_hbm_ref, sum_ref, stat_ref, conv_ref, sems):
    step = N // AGR
    copies = []
    for c in range(AGR):
        part = pl.ds(c * step, step)
        copies.append(
            pltpu.make_async_copy(conv_hbm_ref.at[part, :], conv_ref.at[part, :], sems.at[c])
        )
        copies[c].start()
    eye = lax.broadcasted_iota(jnp.int32, (128, 128), 0) == lanes((128, 128))
    for pair in range(2):
        pieces = []
        for parity in range(2):
            part = av_ref[pl.ds((2 * pair + parity) * 128, 128), :].astype(f32)
            other = pltpu.roll(part, HD, 1)
            own = half_mask(part.shape, parity)
            for piece in (part, other) if parity == 0 else (other, part):
                pieces.append(jnp.where(own, piece, 0.0))
        agent_values = jnp.concatenate(pieces, axis=0).astype(bf16)
        for b in range(N // 512):
            rows = pl.ds(b * 512, 512)
            sum_ref[rows, pl.ds(pair * 128, 128)] = jnp.dot(
                prob_ref[rows, pl.ds(pair * 2 * AGENTS, 2 * AGENTS)],
                agent_values,
                preferred_element_type=f32,
            )
    for b in range(BLOCKS):
        if b * 128 % step == 0:
            copies[b * 128 // step].wait()
        rows = pl.ds(b * 128, 128)
        x = sum_ref[rows, :] + conv_ref[rows, :]
        sum_ref[rows, :] = x
        mean = jnp.sum(x[:, :128] + x[:, 128:], 1, keepdims=True) * (1.0 / CH)
        x = x - mean
        x = x * x
        squares = jnp.sum(x[:, :128] + x[:, 128:], 1, keepdims=True)
        stat_ref[b : b + 1, :] = jnp.sum(jnp.where(eye, mean, 0.0), 0, keepdims=True)
        stat_ref[BLOCKS + b : BLOCKS + b + 1, :] = jnp.sum(
            jnp.where(eye, squares, 0.0), 0, keepdims=True
        )


def norm_kernel(s0_ref, s1_ref, s2_ref, s3_ref, sum_ref, gain_ref, bias_ref, out_ref, done_ref, sems):
    stats = [s[...] for s in (s0_ref, s1_ref, s2_ref, s3_ref)]
    means = [s[:BLOCKS] for s in stats]
    mean = (means[0] + means[1] + means[2] + means[3]) * 0.25
    squares = sum(s[BLOCKS:] for s in stats)
    for m in means:
        squares = squares + CH * (m - mean) * (m - mean)
    scale = lax.rsqrt(squares * (1.0 / D) + epsilon)
    step = N // AGR
    copies = []
    for b in range(BLOCKS):
        rows = pl.ds(b * 128, 128)
        m = jnp.broadcast_to(mean[b : b + 1], (128, 128)).T
        s = jnp.broadcast_to(scale[b : b + 1], (128, 128)).T
        for half in range(2):
            cols = pl.ds(half * 128, 128)
            done_ref[rows, cols] = (
                (sum_ref[rows, cols] - m) * s * gain_ref[0:1, cols] + bias_ref[0:1, cols]
            ).astype(bf16)
        if (b + 1) * 128 % step == 0:
            part = pl.ds((b + 1) * 128 - step, step)
            copy = pltpu.make_async_copy(
                done_ref.at[part, :], out_ref.at[part, :], sems.at[len(copies)]
            )
            copy.start()
            copies.append(copy)
    for copy in copies:
        copy.wait()


def spread(x):
    slot = x.reshape(TILES, x.shape[0] // TILES, 128)
    return lax.all_to_all(slot, ("row", "col"), 0, 0).reshape(x.shape)


def swap(x, axis, pairs):
    return lax.ppermute(x, axis, [p for i, j in pairs for p in ((i, j), (j, i))])


def chain(axis, first):
    return [(i, i + 1) for i in range(first, lax.axis_size(axis) - 1, 2)]


def after(x, *others):
    return lax.optimization_barrier((x, *others))[0]


def shards(queries, keys, values, positions, conv_weight, norm_gain, norm_bias):
    q = queries.reshape(N, CH)
    k = keys.reshape(N, CH)
    v = values.reshape(N, CH)
    mb = 1 << 20
    packed, table = call(
        query_kernel,
        (far((TILES * 8, 128), bf16), far((2, TR + TC, 128), f32)),
        "hh",
        scratch=[
            pltpu.VMEM((N, CH), bf16),
            pltpu.VMEM((2, TC, TR), jnp.int32),
            pltpu.SemaphoreType.DMA((AGR + 1,)),
        ],
        nbytes=8 * mb,
        name="pool_queries",
    )(jnp.swapaxes(positions, 1, 2), q)
    agents = spread(packed)
    held_table = pltpu.VMEM((2, TR + TC, 128), f32)
    tk, inner, outer = call(
        key_kernel,
        (near((N, CH), bf16),) + (far((TR, CH), bf16),) * 2,
        "h h",
        scratch=[held_table, pltpu.VMEM((N, CH), bf16), pltpu.SemaphoreType.DMA((AGR + 1,))],
        nbytes=4 * mb,
        name="turn_keys",
    )(table, values, k)
    parts = call(
        partial_kernel,
        far((TILES * ROWS, 128), bf16),
        " v ",
        scratch=[pltpu.VMEM((AGENTS, N), f32)],
        nbytes=10 * mb,
        name="partials",
    )(agents, tk, v)
    inner = swap(inner, "col", chain("col", 0))
    outer = swap(outer, "col", chain("col", 1))
    parts, inner, outer = lax.optimization_barrier((parts, inner, outer))
    received = spread(parts)
    mate, rest = call(
        line_kernel,
        (near((TC + 16, CH), bf16),) * 2,
        "hhh",
        scratch=[pltpu.VMEM((TC, CH), bf16)] * 2
        + [pltpu.VMEM((TR, CH), bf16)] * 2
        + [pltpu.SemaphoreType.DMA((4,))],
        nbytes=mb // 4,
        name="lines",
    )(values, inner, outer)
    received = after(received, mate, rest)
    mate = swap(mate, "row", chain("row", 0))
    rest = swap(rest, "row", chain("row", 1))
    merged = call(merge_kernel, far((TILES * 8, 128), bf16), " ", nbytes=2 * mb, name="merge")(
        received
    )
    merged = after(merged, mate, rest)
    agent_values = spread(merged)
    prob = call(
        probability_kernel,
        near((N, LOCAL_HEADS * AGENTS), bf16),
        " hh",
        scratch=[
            held_table,
            pltpu.VMEM((N, CH), bf16),
            pltpu.SemaphoreType.DMA((N // 256 + 1,)),
        ],
        nbytes=20 * mb,
        name="probabilities",
    )(after(agents, merged), table, q)
    convolved = call(
        conv_kernel,
        (far((N, CH), f32),),
        "hhh   ",
        scratch=[pltpu.VMEM((TR, TC, CH), bf16)]
        + [pltpu.VMEM((TR, CH), bf16)] * 2
        + [pltpu.VMEM((TC + 16, CH), f32)] * 2
        + [pltpu.VMEM((TR, CH), f32)] * 2
        + [pltpu.VMEM((N, CH), f32), pltpu.SemaphoreType.DMA((6,))],
        nbytes=6 * mb,
        out_spaces="h",
        name="conv",
    )(values, inner, outer, mate, rest, conv_weight)[0]
    summed, stats = call(
        attend_kernel,
        (near((N, CH), f32), near((2 * BLOCKS, 128), f32)),
        " vh",
        scratch=[pltpu.VMEM((N, CH), f32), pltpu.SemaphoreType.DMA((AGR,))],
        nbytes=4 * mb,
        name="attend",
    )(agent_values, prob, convolved)
    heads = lax.axis_size("head")
    others = [
        lax.ppermute(stats, "head", [(i, i ^ d) for i in range(heads)]) for d in range(1, heads)
    ]
    normed = call(
        norm_kernel,
        (shape((N, CH), bf16),),
        "v   v  ",
        scratch=[pltpu.VMEM((N, CH), bf16), pltpu.SemaphoreType.DMA((AGR,))],
        nbytes=4 * mb,
        out_spaces="h",
        name="norm",
    )(
        stats, *others, summed, norm_gain.reshape(1, CH), norm_bias.reshape(1, CH)
    )[0]
    return normed.reshape(TR, TC, CH)


def solution(mesh):
    in_specs = (
        P("row", "col", "head"),
        P("row", "col", "head"),
        P("row", "col", "head"),
        P(None, "row", "col"),
        P(None, "head"),
        P("head"),
        P("head"),
    )
    out_specs = P("row", "col", "head")
    return jax.shard_map(shards, mesh=mesh, in_specs=in_specs, out_specs=out_specs, check_vma=False)
```

```python
import math

import jax
import jax.numpy as jnp
from jax import lax
from jax.experimental import pallas as pl
from jax.experimental.pallas import tpu as pltpu
from jax.sharding import PartitionSpec as P

HD = 64
D = 1024
AGR = 4
TR = 48
TC = 32
CH = 256
N = TR * TC
AGENTS = 256
TILES = 64
LOCAL_HEADS = 4
ROWS = LOCAL_HEADS * AGENTS // TILES
BLOCKS = N // 128

f32 = jnp.float32
bf16 = jnp.bfloat16
epsilon = 1e-05

VMEM_SPEC = pl.BlockSpec(memory_space=pltpu.VMEM)
HBM_SPEC = pl.BlockSpec(memory_space=pltpu.HBM)


def call(kernel, outs, in_spaces, scratch=(), nbytes=0, name=None, out_spaces=None):
    fn = pl.pallas_call(
        kernel,
        out_shape=outs,
        in_specs=[HBM_SPEC if c == "h" else VMEM_SPEC for c in in_spaces],
        out_specs=(
            tuple(HBM_SPEC if c == "h" else VMEM_SPEC for c in out_spaces or " " * len(outs))
            if isinstance(outs, tuple)
            else VMEM_SPEC
        ),
        scratch_shapes=list(scratch),
        compiler_params=pltpu.CompilerParams(vmem_limit_bytes=20 * 1024 * 1024),
        cost_estimate=pl.CostEstimate(flops=0, bytes_accessed=nbytes, transcendentals=0),
        name=name,
    )

    def run(*args):
        spaces = {"h": pltpu.HBM, "v": pltpu.VMEM}
        return fn(
            *[
                pltpu.with_memory_space_constraint(x, spaces[c]) if c in spaces else x
                for x, c in zip(args, in_spaces, strict=True)
            ]
        )

    return run


def shape(dims, dtype):
    return jax.ShapeDtypeStruct(dims, dtype)


def near(dims, dtype):
    return pltpu.VMEM(dims, dtype)


def far(dims, dtype):
    return pltpu.HBM(dims, dtype)


def lanes(dims):
    return lax.broadcasted_iota(jnp.int32, dims, len(dims) - 1)


def turn_matrix():
    source = lax.broadcasted_iota(jnp.int32, (CH, CH), 0)
    target = lax.broadcasted_iota(jnp.int32, (CH, CH), 1)
    low = (target & 31) < 16
    minus = jnp.where(low & (source == target + 16), -1.0, 0.0)
    plus = jnp.where((~low) & (source == target - 16), 1.0, 0.0)
    return (minus + plus).astype(bf16)


def sin_cos(angle):
    return jnp.sin(angle), jnp.cos(angle)


def turned(x, matrix, cosine, sine):
    swapped = jnp.dot(x, matrix, preferred_element_type=f32)
    return (x.astype(f32) * cosine + swapped * sine).astype(bf16)


def split_tables(cosines, sines):
    cosines = jnp.concatenate([cosines, cosines], axis=1)
    sines = jnp.concatenate([sines, sines], axis=1)
    return cosines[:TR], sines[:TR], cosines[TR:], sines[TR:]


def cell_tables(tables, first, rows):
    cos_r, sin_r, cos_c, sin_c = tables
    cosine = jnp.concatenate(
        [cos_r[first + i : first + i + 1, :] * cos_c for i in range(rows)], axis=0
    )
    sine = jnp.concatenate(
        [sin_r[first + i : first + i + 1, :] + sin_c for i in range(rows)], axis=0
    )
    return cosine, sine


def slots(block):
    twice = jnp.concatenate([block, block], axis=0).astype(bf16)
    return jnp.broadcast_to(twice[None], (TILES // 2, 16, 128)).reshape(TILES * 8, 128)


def query_kernel(
    pos_ref,
    q_ref,
    agents_ref,
    tab_ref,
    held_ref,
    spot_ref,
    sems,
):
    step = N // AGR
    place = pltpu.make_async_copy(pos_ref, spot_ref, sems.at[AGR])
    place.start()
    copies = []
    for cell in range(AGR):
        part = pl.ds(cell * step, step)
        copy = pltpu.make_async_copy(q_ref.at[part, :], held_ref.at[part, :], sems.at[cell])
        copy.start()
        copies.append(copy)
    matrix = turn_matrix()
    lane = lanes((1, 128)) % HD
    power = jnp.exp((lane % 16).astype(f32) * f32(-math.log(100.0) / 16))
    freq_r = jnp.where(lane < 32, power, 0.0)
    freq_c = jnp.where(lane < 32, 0.0, power)
    place.wait()
    row_line = spot_ref[0][0:1, :].astype(f32)
    col_pos = spot_ref[1][:, 0:1].astype(f32)
    eye = lax.broadcasted_iota(jnp.int32, (TR, TR), 0) == lax.broadcasted_iota(
        jnp.int32, (TR, TR), 1
    )
    row_pos = jnp.sum(jnp.where(eye, jnp.broadcast_to(row_line, (TR, TR)), 0.0), 1, keepdims=True)
    angles = jnp.concatenate([row_pos * freq_r, col_pos * freq_c], axis=0)
    sines, cosines = sin_cos(angles)
    tab_ref[0] = cosines
    tab_ref[1] = sines
    tables = split_tables(cosines, sines)
    means = []
    for cell in range(AGR):
        cosine, sine = cell_tables(tables, cell * (TR // AGR), TR // AGR)
        copies[cell].wait()
        rotated = turned(held_ref[pl.ds(cell * step, step), :], matrix, cosine, sine)
        mean = jnp.sum(rotated.astype(f32), 0, keepdims=True) / step
        means.append(mean.astype(bf16).astype(f32))
    packed = jnp.concatenate([m[:, :128] for m in means] + [m[:, 128:] for m in means], axis=0)
    agents_ref[...] = slots(packed)


def even_core():
    return lax.rem(lax.axis_index("col"), 2) == 0


def even_row():
    return lax.rem(lax.axis_index("row"), 2) == 0


def key_kernel(
    tab_hbm_ref,
    v_ref,
    k_ref,
    tk_ref,
    near_ref,
    far_ref,
    tab_ref,
    held_ref,
    sems,
):
    step = N // AGR
    table = pltpu.make_async_copy(tab_hbm_ref, tab_ref, sems.at[AGR])
    table.start()
    copies = []
    for cell in range(AGR):
        part = pl.ds(cell * step, step)
        copies.append(
            pltpu.make_async_copy(k_ref.at[part, :], held_ref.at[part, :], sems.at[cell])
        )
        copies[cell].start()
    first, last = v_ref[:, 0, :], v_ref[:, TC - 1, :]
    even = even_core()
    near_ref[...] = jnp.where(even, last, first)
    far_ref[...] = jnp.where(even, first, last)
    matrix = turn_matrix()
    table.wait()
    tables = split_tables(tab_ref[0], tab_ref[1])
    for cell in range(AGR):
        part = pl.ds(cell * step, step)
        cosine, sine = cell_tables(tables, cell * (TR // AGR), TR // AGR)
        copies[cell].wait()
        tk_ref[part, :] = turned(held_ref[part, :], matrix, cosine, sine)


def agent_pairs(agents_ref, scale):
    target = lax.broadcasted_iota(jnp.int32, (AGENTS, TILES * 8), 0)
    source = lax.broadcasted_iota(jnp.int32, (AGENTS, TILES * 8), 1)
    agents = agents_ref[...]
    pairs = []
    for pair in range(2):
        wanted = (target & (TILES - 1)) * 8 + (target // TILES) + 4 * pair
        pick = jnp.where(source == wanted, scale, 0.0).astype(bf16)
        pairs.append(jnp.dot(pick, agents, preferred_element_type=f32).astype(bf16))
    return pairs


def half_mask(dims, parity):
    return (lanes(dims) // HD) == parity


def partial_kernel(agents_ref, tk_ref, v_ref, out_ref, score_ref):
    pairs = agent_pairs(agents_ref, 1.0 / math.sqrt(HD))
    chunk = 512
    for head in range(LOCAL_HEADS):
        pair, parity = head // 2, head % 2
        cols = pl.ds(pair * 128, 128)
        own = pairs[pair]
        own = jnp.where(half_mask(own.shape, parity), own, jnp.zeros_like(own))
        peak = None
        for c in range(N // chunk):
            scores = lax.dot_general(
                own,
                tk_ref[pl.ds(c * chunk, chunk), cols],
                (((1,), (1,)), ((), ())),
                preferred_element_type=f32,
            )
            score_ref[:, pl.ds(c * chunk, chunk)] = scores
            for s in range(chunk // 128):
                piece = scores[:, s * 128 : (s + 1) * 128]
                peak = piece if peak is None else jnp.maximum(peak, piece)
        peak = jnp.max(peak, 1, keepdims=True)
        acc = jnp.zeros((AGENTS, 128), f32)
        for c in range(N // chunk):
            weights = jnp.exp(score_ref[:, pl.ds(c * chunk, chunk)] - peak).astype(bf16)
            block = v_ref[pl.ds(c * chunk, chunk), cols]
            block = jnp.where(half_mask(block.shape, parity), block, jnp.ones_like(block))
            acc = acc + jnp.dot(weights, block, preferred_element_type=f32)
        other = pltpu.roll(acc, HD, 1)
        numer, total = (acc, other) if parity == 0 else (other, acc)
        logs = peak + jnp.log(total)
        values = numer / total
        logs = jnp.max(jnp.where(half_mask(logs.shape, 0), logs, -3e38), 1, keepdims=True)
        first = logs.astype(bf16).astype(f32)
        second = (logs - first).astype(bf16).astype(f32)
        third = logs - first - second
        lane = lanes((AGENTS, 128))
        packed = jnp.where(
            lane < HD,
            values,
            jnp.where(
                lane == HD,
                first,
                jnp.where(lane == HD + 1, second, jnp.where(lane == HD + 2, third, 0.0)),
            ),
        )
        groups = packed.reshape(2, ROWS, 8, 128)
        groups = jnp.concatenate([groups[0], groups[1]], 1).reshape(AGENTS, 128)
        out_ref[pl.ds(head * AGENTS, AGENTS), :] = groups.astype(bf16)


def merge_kernel(parts_ref, out_ref):
    source = lax.broadcasted_iota(jnp.int32, (128, 128), 0)
    picker = jnp.where((source >= HD) & (source < HD + 3), 1.0, 0.0).astype(bf16)
    parts = parts_ref[...]
    logs = jnp.dot(parts, picker, preferred_element_type=f32).reshape(TILES, ROWS, 128)
    values = parts.astype(f32).reshape(TILES, ROWS, 128)
    peak = jnp.max(logs, 0)
    weights = jnp.exp(logs - peak[None])
    merged = jnp.sum(weights * values, 0) / jnp.sum(weights, 0)
    merged = jnp.where(lanes((8, 128)) < HD, merged[:8], pltpu.roll(merged[8:], HD, 1))
    out_ref[...] = slots(merged)


def probability_kernel(agents_ref, tab_hbm_ref, q_ref, prob_ref, tab_ref, held_ref, sems):
    chunk = 256
    table = pltpu.make_async_copy(tab_hbm_ref, tab_ref, sems.at[N // chunk])
    table.start()

    def fetch(c):
        rows = pl.ds(pl.multiple_of(c * chunk, chunk), chunk)
        return pltpu.make_async_copy(q_ref.at[rows, :], held_ref.at[rows, :], sems.at[c])

    for c in range(N // chunk):
        fetch(c).start()
    pairs = agent_pairs(agents_ref, 1.0 / math.sqrt(HD))
    matrix = turn_matrix()
    table.wait()
    ones = jnp.ones((AGENTS, 128), bf16)
    owns = []
    for head in range(LOCAL_HEADS):
        own = pairs[head // 2]
        owns.append(jnp.where(half_mask(own.shape, head % 2), own, jnp.zeros_like(own)))

    def body(c, carry):
        fetch(c).wait()
        rows = pl.ds(pl.multiple_of(c * chunk, chunk), chunk)
        lines = pl.ds(pl.multiple_of(c * (chunk // TC), chunk // TC), chunk // TC)
        near_rows = [tab_ref[i, lines, :] for i in range(2)]
        near_cols = [tab_ref[i, pl.ds(TR, TC), :] for i in range(2)]
        tables = [jnp.concatenate([t, t], axis=1) for t in near_rows + near_cols]
        cosine, sine = cell_tables(tables, 0, chunk // TC)
        queries = turned(held_ref[rows, :], matrix, cosine, sine)
        for head in range(LOCAL_HEADS):
            scores = lax.dot_general(
                queries[:, head // 2 * 128 : head // 2 * 128 + 128],
                owns[head],
                (((1,), (1,)), ((), ())),
                preferred_element_type=f32,
            )
            weights = jnp.exp(scores - jnp.max(scores, 1, keepdims=True))
            total = jnp.dot(weights.astype(bf16), ones, preferred_element_type=f32)
            scale = 1.0 / total
            scale = jnp.concatenate([scale, scale], axis=1)
            prob_ref[rows, pl.ds(head * AGENTS, AGENTS)] = (weights * scale).astype(bf16)
        return carry

    lax.fori_loop(0, N // chunk, body, 0)


def line_kernel(v_ref, near_ref, far_ref, mate_ref, rest_ref, top_ref, bottom_ref, sems):
    copies = [
        pltpu.make_async_copy(v_ref.at[0], top_ref, sems.at[0]),
        pltpu.make_async_copy(v_ref.at[TR - 1], bottom_ref, sems.at[1]),
    ]
    for copy in copies:
        copy.start()
    for copy in copies:
        copy.wait()
    lines = []
    for row, line_ref in ((0, top_ref), (TR - 1, bottom_ref)):
        mate = near_ref[row : row + 1, :].astype(f32)
        rest = far_ref[row : row + 1, :].astype(f32)
        left = jnp.where(even_core(), rest, mate)
        right = jnp.where(even_core(), mate, rest)
        tail = jnp.concatenate([left, right, jnp.zeros((14, CH), f32)], axis=0)
        lines.append(jnp.concatenate([line_ref[...].astype(f32), tail], axis=0))
    mate_ref[...] = jnp.where(even_row(), lines[1], lines[0]).astype(bf16)
    rest_ref[...] = jnp.where(even_row(), lines[0], lines[1]).astype(bf16)


def conv_kernel(
    v_ref,
    near_ref,
    far_ref,
    mate_ref,
    rest_ref,
    w_ref,
    out_hbm_ref,
    above_ref,
    below_ref,
    l_ref,
    r_ref,
    out_ref,
    sems,
):
    outs = []
    for half in range(2):
        cols = pl.ds(half * 128, 128)
        outs.append(
            pltpu.make_async_copy(
                out_ref.at[:, cols], out_hbm_ref.at[:, cols], sems.at[half]
            )
        )
    mate, rest = mate_ref[...].astype(f32), rest_ref[...].astype(f32)
    above_ref[...] = jnp.where(even_row(), rest, mate)
    below_ref[...] = jnp.where(even_row(), mate, rest)
    mate, rest = near_ref[...].astype(f32), far_ref[...].astype(f32)
    l_ref[...] = jnp.where(even_core(), rest, mate)
    r_ref[...] = jnp.where(even_core(), mate, rest)
    for half in range(2):
        cols = pl.ds(half * 128, 128)

        def put(at, total):
            out_ref[pl.ds(at, TC), cols] = total

        w = [jnp.broadcast_to(w_ref[t : t + 1, cols], (TC, 128)) for t in range(9)]
        column = lax.broadcasted_iota(jnp.int32, (TC, 128), 0)

        def taps(row, left, right):
            row = row.astype(f32)
            before = jnp.where(column == 0, left, pltpu.roll(row, 1, 0))
            after = jnp.where(column == TC - 1, right, pltpu.roll(row, TC - 1, 0))
            return [before * w[3 * d] + row * w[3 * d + 1] + after * w[3 * d + 2] for d in range(3)]

        tail = above_ref[pl.ds(TC, 8), cols]
        t0 = taps(above_ref[pl.ds(0, TC), cols], tail[0:1], tail[1:2])

        def group(start, carry):
            a, b = carry
            lefts, rights = l_ref[pl.ds(start, 8), cols], r_ref[pl.ds(start, 8), cols]
            for k in range(8):
                t = taps(v_ref[start + k, :, cols], lefts[k : k + 1], rights[k : k + 1])
                if a is not None:
                    at = (start + k - 1) * TC
                    if not isinstance(at, int):
                        at = pl.multiple_of(at, TC)
                    put(at, a + t[2])
                a, b = b + t[1], t[0]
            return a, b

        carry = group(0, (None, t0[0]))
        a, b = lax.fori_loop(
            1, TR // 8, lambda g, c: group(pl.multiple_of(g * 8, 8), c), carry
        )
        tail = below_ref[pl.ds(TC, 8), cols]
        t = taps(below_ref[pl.ds(0, TC), cols], tail[0:1], tail[1:2])
        put((TR - 1) * TC, a + t[2])
        outs[half].start()
    for copy in outs:
        copy.wait()


def attend_kernel(av_ref, prob_ref, conv_hbm_ref, sum_ref, stat_ref, conv_ref, sems):
    step = N // AGR
    copies = []
    for c in range(AGR):
        part = pl.ds(c * step, step)
        copies.append(
            pltpu.make_async_copy(conv_hbm_ref.at[part, :], conv_ref.at[part, :], sems.at[c])
        )
        copies[c].start()
    eye = lax.broadcasted_iota(jnp.int32, (128, 128), 0) == lanes((128, 128))
    for pair in range(2):
        pieces = []
        for parity in range(2):
            part = av_ref[pl.ds((2 * pair + parity) * 128, 128), :].astype(f32)
            other = pltpu.roll(part, HD, 1)
            own = half_mask(part.shape, parity)
            for piece in (part, other) if parity == 0 else (other, part):
                pieces.append(jnp.where(own, piece, 0.0))
        agent_values = jnp.concatenate(pieces, axis=0).astype(bf16)
        for b in range(N // 512):
            rows = pl.ds(b * 512, 512)
            sum_ref[rows, pl.ds(pair * 128, 128)] = jnp.dot(
                prob_ref[rows, pl.ds(pair * 2 * AGENTS, 2 * AGENTS)],
                agent_values,
                preferred_element_type=f32,
            )
    for b in range(BLOCKS):
        if b * 128 % step == 0:
            copies[b * 128 // step].wait()
        rows = pl.ds(b * 128, 128)
        x = sum_ref[rows, :] + conv_ref[rows, :]
        sum_ref[rows, :] = x
        mean = jnp.sum(x[:, :128] + x[:, 128:], 1, keepdims=True) * (1.0 / CH)
        x = x - mean
        x = x * x
        squares = jnp.sum(x[:, :128] + x[:, 128:], 1, keepdims=True)
        stat_ref[b : b + 1, :] = jnp.sum(jnp.where(eye, mean, 0.0), 0, keepdims=True)
        stat_ref[BLOCKS + b : BLOCKS + b + 1, :] = jnp.sum(
            jnp.where(eye, squares, 0.0), 0, keepdims=True
        )


def norm_kernel(s0_ref, s1_ref, s2_ref, s3_ref, sum_ref, gain_ref, bias_ref, out_ref, done_ref, sems):
    stats = [s[...] for s in (s0_ref, s1_ref, s2_ref, s3_ref)]
    means = [s[:BLOCKS] for s in stats]
    mean = (means[0] + means[1] + means[2] + means[3]) * 0.25
    squares = sum(s[BLOCKS:] for s in stats)
    for m in means:
        squares = squares + CH * (m - mean) * (m - mean)
    scale = lax.rsqrt(squares * (1.0 / D) + epsilon)
    step = N // AGR
    copies = []
    for b in range(BLOCKS):
        rows = pl.ds(b * 128, 128)
        m = jnp.broadcast_to(mean[b : b + 1], (128, 128)).T
        s = jnp.broadcast_to(scale[b : b + 1], (128, 128)).T
        for half in range(2):
            cols = pl.ds(half * 128, 128)
            done_ref[rows, cols] = (
                (sum_ref[rows, cols] - m) * s * gain_ref[0:1, cols] + bias_ref[0:1, cols]
            ).astype(bf16)
        if (b + 1) * 128 % step == 0:
            part = pl.ds((b + 1) * 128 - step, step)
            copy = pltpu.make_async_copy(
                done_ref.at[part, :], out_ref.at[part, :], sems.at[len(copies)]
            )
            copy.start()
            copies.append(copy)
    for copy in copies:
        copy.wait()


def spread(x):
    slot = x.reshape(TILES, x.shape[0] // TILES, 128)
    return lax.all_to_all(slot, ("row", "col"), 0, 0).reshape(x.shape)


def swap(x, axis, pairs):
    return lax.ppermute(x, axis, [p for i, j in pairs for p in ((i, j), (j, i))])


def chain(axis, first):
    return [(i, i + 1) for i in range(first, lax.axis_size(axis) - 1, 2)]


def after(x, *others):
    return lax.optimization_barrier((x, *others))[0]


def shards(queries, keys, values, positions, conv_weight, norm_gain, norm_bias):
    q = queries.reshape(N, CH)
    k = keys.reshape(N, CH)
    v = values.reshape(N, CH)
    mb = 1 << 20
    packed, table = call(
        query_kernel,
        (far((TILES * 8, 128), bf16), far((2, TR + TC, 128), f32)),
        "hh",
        scratch=[
            pltpu.VMEM((N, CH), bf16),
            pltpu.VMEM((2, TC, TR), jnp.int32),
            pltpu.SemaphoreType.DMA((AGR + 1,)),
        ],
        nbytes=8 * mb,
        name="pool_queries",
    )(jnp.swapaxes(positions, 1, 2), q)
    agents = spread(packed)
    held_table = pltpu.VMEM((2, TR + TC, 128), f32)
    tk, inner, outer = call(
        key_kernel,
        (near((N, CH), bf16),) + (far((TR, CH), bf16),) * 2,
        "h h",
        scratch=[held_table, pltpu.VMEM((N, CH), bf16), pltpu.SemaphoreType.DMA((AGR + 1,))],
        nbytes=4 * mb,
        name="turn_keys",
    )(table, values, k)
    parts = call(
        partial_kernel,
        far((TILES * ROWS, 128), bf16),
        " v ",
        scratch=[pltpu.VMEM((AGENTS, N), f32)],
        nbytes=10 * mb,
        name="partials",
    )(agents, tk, v)
    inner = swap(inner, "col", chain("col", 0))
    outer = swap(outer, "col", chain("col", 1))
    parts, inner, outer = lax.optimization_barrier((parts, inner, outer))
    received = spread(parts)
    mate, rest = call(
        line_kernel,
        (near((TC + 16, CH), bf16),) * 2,
        "hvv",
        scratch=[pltpu.VMEM((TC, CH), bf16)] * 2 + [pltpu.SemaphoreType.DMA((2,))],
        nbytes=mb // 4,
        name="lines",
    )(values, inner, outer)
    received = after(received, mate, rest)
    mate = swap(mate, "row", chain("row", 0))
    rest = swap(rest, "row", chain("row", 1))
    merged = call(merge_kernel, far((TILES * 8, 128), bf16), " ", nbytes=2 * mb, name="merge")(
        received
    )
    merged = after(merged, mate, rest)
    agent_values = spread(merged)
    prob = call(
        probability_kernel,
        near((N, LOCAL_HEADS * AGENTS), bf16),
        " hh",
        scratch=[
            held_table,
            pltpu.VMEM((N, CH), bf16),
            pltpu.SemaphoreType.DMA((N // 256 + 1,)),
        ],
        nbytes=20 * mb,
        name="probabilities",
    )(after(agents, merged), table, q)
    convolved = call(
        conv_kernel,
        (far((N, CH), f32),),
        " vvvv ",
        scratch=[pltpu.VMEM((TC + 16, CH), f32)] * 2
        + [pltpu.VMEM((TR, CH), f32)] * 2
        + [pltpu.VMEM((N, CH), f32), pltpu.SemaphoreType.DMA((2,))],
        nbytes=6 * mb,
        out_spaces="h",
        name="conv",
    )(values, inner, outer, mate, rest, conv_weight)[0]
    summed, stats = call(
        attend_kernel,
        (near((N, CH), f32), near((2 * BLOCKS, 128), f32)),
        " vh",
        scratch=[pltpu.VMEM((N, CH), f32), pltpu.SemaphoreType.DMA((AGR,))],
        nbytes=4 * mb,
        name="attend",
    )(agent_values, prob, convolved)
    heads = lax.axis_size("head")
    others = [
        lax.ppermute(stats, "head", [(i, i ^ d) for i in range(heads)]) for d in range(1, heads)
    ]
    normed = call(
        norm_kernel,
        (shape((N, CH), bf16),),
        "v   v  ",
        scratch=[pltpu.VMEM((N, CH), bf16), pltpu.SemaphoreType.DMA((AGR,))],
        nbytes=4 * mb,
        out_spaces="h",
        name="norm",
    )(
        stats, *others, summed, norm_gain.reshape(1, CH), norm_bias.reshape(1, CH)
    )[0]
    return normed.reshape(TR, TC, CH)


def solution(mesh):
    in_specs = (
        P("row", "col", "head"),
        P("row", "col", "head"),
        P("row", "col", "head"),
        P(None, "row", "col"),
        P(None, "head"),
        P("head"),
        P("head"),
    )
    out_specs = P("row", "col", "head")
    return jax.shard_map(shards, mesh=mesh, in_specs=in_specs, out_specs=out_specs, check_vma=False)
```

```python
import math

import jax
import jax.numpy as jnp
from jax import lax
from jax.experimental import pallas as pl
from jax.experimental.pallas import tpu as pltpu
from jax.sharding import PartitionSpec as P

HD = 64
D = 1024
AGR = 4
TR = 48
TC = 32
CH = 256
N = TR * TC
AGENTS = 256
TILES = 64
LOCAL_HEADS = 4
ROWS = LOCAL_HEADS * AGENTS // TILES
BLOCKS = N // 128

f32 = jnp.float32
bf16 = jnp.bfloat16
epsilon = 1e-05

VMEM_SPEC = pl.BlockSpec(memory_space=pltpu.VMEM)
HBM_SPEC = pl.BlockSpec(memory_space=pltpu.HBM)


def call(kernel, outs, in_spaces, scratch=(), nbytes=0, name=None, out_spaces=None):
    fn = pl.pallas_call(
        kernel,
        out_shape=outs,
        in_specs=[HBM_SPEC if c == "h" else VMEM_SPEC for c in in_spaces],
        out_specs=(
            tuple(HBM_SPEC if c == "h" else VMEM_SPEC for c in out_spaces or " " * len(outs))
            if isinstance(outs, tuple)
            else VMEM_SPEC
        ),
        scratch_shapes=list(scratch),
        compiler_params=pltpu.CompilerParams(vmem_limit_bytes=20 * 1024 * 1024),
        cost_estimate=pl.CostEstimate(flops=0, bytes_accessed=nbytes, transcendentals=0),
        name=name,
    )

    def run(*args):
        spaces = {"h": pltpu.HBM, "v": pltpu.VMEM}
        return fn(
            *[
                pltpu.with_memory_space_constraint(x, spaces[c]) if c in spaces else x
                for x, c in zip(args, in_spaces, strict=True)
            ]
        )

    return run


def shape(dims, dtype):
    return jax.ShapeDtypeStruct(dims, dtype)


def near(dims, dtype):
    return pltpu.VMEM(dims, dtype)


def far(dims, dtype):
    return pltpu.HBM(dims, dtype)


def lanes(dims):
    return lax.broadcasted_iota(jnp.int32, dims, len(dims) - 1)


def turn_matrix():
    source = lax.broadcasted_iota(jnp.int32, (CH, CH), 0)
    target = lax.broadcasted_iota(jnp.int32, (CH, CH), 1)
    low = (target & 31) < 16
    minus = jnp.where(low & (source == target + 16), -1.0, 0.0)
    plus = jnp.where((~low) & (source == target - 16), 1.0, 0.0)
    return (minus + plus).astype(bf16)


def sin_cos(angle):
    return jnp.sin(angle), jnp.cos(angle)


def turned(x, matrix, cosine, sine):
    swapped = jnp.dot(x, matrix, preferred_element_type=f32)
    return (x.astype(f32) * cosine + swapped * sine).astype(bf16)


def split_tables(cosines, sines):
    cosines = jnp.concatenate([cosines, cosines], axis=1)
    sines = jnp.concatenate([sines, sines], axis=1)
    return cosines[:TR], sines[:TR], cosines[TR:], sines[TR:]


def cell_tables(tables, first, rows):
    cos_r, sin_r, cos_c, sin_c = tables
    cosine = jnp.concatenate(
        [cos_r[first + i : first + i + 1, :] * cos_c for i in range(rows)], axis=0
    )
    sine = jnp.concatenate(
        [sin_r[first + i : first + i + 1, :] + sin_c for i in range(rows)], axis=0
    )
    return cosine, sine


def slots(block):
    twice = jnp.concatenate([block, block], axis=0).astype(bf16)
    return jnp.broadcast_to(twice[None], (TILES // 2, 16, 128)).reshape(TILES * 8, 128)


def query_kernel(
    pos_ref,
    q_ref,
    agents_ref,
    tab_ref,
    held_ref,
    spot_ref,
    sems,
):
    step = N // AGR
    place = pltpu.make_async_copy(pos_ref, spot_ref, sems.at[AGR])
    place.start()
    copies = []
    for cell in range(AGR):
        part = pl.ds(cell * step, step)
        copy = pltpu.make_async_copy(q_ref.at[part, :], held_ref.at[part, :], sems.at[cell])
        copy.start()
        copies.append(copy)
    matrix = turn_matrix()
    lane = lanes((1, 128)) % HD
    power = jnp.exp((lane % 16).astype(f32) * f32(-math.log(100.0) / 16))
    freq_r = jnp.where(lane < 32, power, 0.0)
    freq_c = jnp.where(lane < 32, 0.0, power)
    place.wait()
    row_line = spot_ref[0][0:1, :].astype(f32)
    col_pos = spot_ref[1][:, 0:1].astype(f32)
    eye = lax.broadcasted_iota(jnp.int32, (TR, TR), 0) == lax.broadcasted_iota(
        jnp.int32, (TR, TR), 1
    )
    row_pos = jnp.sum(jnp.where(eye, jnp.broadcast_to(row_line, (TR, TR)), 0.0), 1, keepdims=True)
    angles = jnp.concatenate([row_pos * freq_r, col_pos * freq_c], axis=0)
    sines, cosines = sin_cos(angles)
    tab_ref[0] = cosines
    tab_ref[1] = sines
    tables = split_tables(cosines, sines)
    means = []
    for cell in range(AGR):
        cosine, sine = cell_tables(tables, cell * (TR // AGR), TR // AGR)
        copies[cell].wait()
        rotated = turned(held_ref[pl.ds(cell * step, step), :], matrix, cosine, sine)
        mean = jnp.sum(rotated.astype(f32), 0, keepdims=True) / step
        means.append(mean.astype(bf16).astype(f32))
    packed = jnp.concatenate([m[:, :128] for m in means] + [m[:, 128:] for m in means], axis=0)
    agents_ref[...] = slots(packed)


def even_core():
    return lax.rem(lax.axis_index("col"), 2) == 0


def even_row():
    return lax.rem(lax.axis_index("row"), 2) == 0


def key_kernel(
    tab_hbm_ref,
    v_ref,
    k_ref,
    tk_ref,
    near_ref,
    far_ref,
    tab_ref,
    held_ref,
    sems,
):
    step = N // AGR
    table = pltpu.make_async_copy(tab_hbm_ref, tab_ref, sems.at[AGR])
    table.start()
    copies = []
    for cell in range(AGR):
        part = pl.ds(cell * step, step)
        copies.append(
            pltpu.make_async_copy(k_ref.at[part, :], held_ref.at[part, :], sems.at[cell])
        )
        copies[cell].start()
    first, last = v_ref[:, 0, :], v_ref[:, TC - 1, :]
    even = even_core()
    near_ref[...] = jnp.where(even, last, first)
    far_ref[...] = jnp.where(even, first, last)
    matrix = turn_matrix()
    table.wait()
    tables = split_tables(tab_ref[0], tab_ref[1])
    for cell in range(AGR):
        part = pl.ds(cell * step, step)
        cosine, sine = cell_tables(tables, cell * (TR // AGR), TR // AGR)
        copies[cell].wait()
        tk_ref[part, :] = turned(held_ref[part, :], matrix, cosine, sine)


def agent_pairs(agents_ref, wide_ref, scale):
    wide_ref[...] = agents_ref[...].astype(f32) * scale
    pairs = []
    for pair in range(2):
        parts = [wide_ref[pl.ds(4 * pair + k, TILES, stride=8), :] for k in range(AGR)]
        pairs.append(jnp.concatenate(parts, axis=0).astype(bf16))
    return pairs


def half_mask(dims, parity):
    return (lanes(dims) // HD) == parity


def partial_kernel(agents_ref, tk_ref, v_ref, out_ref, score_ref, wide_ref):
    pairs = agent_pairs(agents_ref, wide_ref, 1.0 / math.sqrt(HD))
    chunk = 512
    for head in range(LOCAL_HEADS):
        pair, parity = head // 2, head % 2
        cols = pl.ds(pair * 128, 128)
        own = pairs[pair]
        own = jnp.where(half_mask(own.shape, parity), own, jnp.zeros_like(own))
        peak = None
        for c in range(N // chunk):
            scores = lax.dot_general(
                own,
                tk_ref[pl.ds(c * chunk, chunk), cols],
                (((1,), (1,)), ((), ())),
                preferred_element_type=f32,
            )
            score_ref[:, pl.ds(c * chunk, chunk)] = scores
            for s in range(chunk // 128):
                piece = scores[:, s * 128 : (s + 1) * 128]
                peak = piece if peak is None else jnp.maximum(peak, piece)
        peak = jnp.max(peak, 1, keepdims=True)
        acc = jnp.zeros((AGENTS, 128), f32)
        for c in range(N // chunk):
            weights = jnp.exp(score_ref[:, pl.ds(c * chunk, chunk)] - peak).astype(bf16)
            block = v_ref[pl.ds(c * chunk, chunk), cols]
            block = jnp.where(half_mask(block.shape, parity), block, jnp.ones_like(block))
            acc = acc + jnp.dot(weights, block, preferred_element_type=f32)
        other = pltpu.roll(acc, HD, 1)
        numer, total = (acc, other) if parity == 0 else (other, acc)
        logs = peak + jnp.log(total)
        values = numer / total
        logs = jnp.max(jnp.where(half_mask(logs.shape, 0), logs, -3e38), 1, keepdims=True)
        first = logs.astype(bf16).astype(f32)
        second = (logs - first).astype(bf16).astype(f32)
        third = logs - first - second
        lane = lanes((AGENTS, 128))
        packed = jnp.where(
            lane < HD,
            values,
            jnp.where(
                lane == HD,
                first,
                jnp.where(lane == HD + 1, second, jnp.where(lane == HD + 2, third, 0.0)),
            ),
        )
        groups = packed.reshape(2, ROWS, 8, 128)
        groups = jnp.concatenate([groups[0], groups[1]], 1).reshape(AGENTS, 128)
        out_ref[pl.ds(head * AGENTS, AGENTS), :] = groups.astype(bf16)


def merge_kernel(parts_ref, out_ref):
    source = lax.broadcasted_iota(jnp.int32, (128, 128), 0)
    picker = jnp.where((source >= HD) & (source < HD + 3), 1.0, 0.0).astype(bf16)
    parts = parts_ref[...]
    logs = jnp.dot(parts, picker, preferred_element_type=f32).reshape(TILES, ROWS, 128)
    values = parts.astype(f32).reshape(TILES, ROWS, 128)
    peak = jnp.max(logs, 0)
    weights = jnp.exp(logs - peak[None])
    merged = jnp.sum(weights * values, 0) / jnp.sum(weights, 0)
    merged = jnp.where(lanes((8, 128)) < HD, merged[:8], pltpu.roll(merged[8:], HD, 1))
    out_ref[...] = slots(merged)


def probabilities(pairs, tab_ref, table, held_ref, fetches, prob_ref):
    chunk = N // len(fetches)
    matrix = turn_matrix()
    table.wait()
    ones = jnp.ones((AGENTS, 128), bf16)
    owns = []
    for head in range(LOCAL_HEADS):
        own = pairs[head // 2]
        owns.append(jnp.where(half_mask(own.shape, head % 2), own, jnp.zeros_like(own)))
    tables = split_tables(tab_ref[0], tab_ref[1])
    for c, fetch in enumerate(fetches):
        rows = pl.ds(c * chunk, chunk)
        cosine, sine = cell_tables(tables, c * (chunk // TC), chunk // TC)
        fetch.wait()
        queries = turned(held_ref[rows, :], matrix, cosine, sine)
        for head in range(LOCAL_HEADS):
            scores = lax.dot_general(
                queries[:, head // 2 * 128 : head // 2 * 128 + 128],
                owns[head],
                (((1,), (1,)), ((), ())),
                preferred_element_type=f32,
            )
            weights = jnp.exp(scores - jnp.max(scores, 1, keepdims=True))
            total = jnp.dot(weights.astype(bf16), ones, preferred_element_type=f32)
            scale = 1.0 / total
            scale = jnp.concatenate([scale, scale], axis=1)
            prob_ref[rows, pl.ds(head * AGENTS, AGENTS)] = (weights * scale).astype(bf16)


def line_kernel(v_ref, near_ref, far_ref, mate_ref, rest_ref, top_ref, bottom_ref, sems):
    copies = [
        pltpu.make_async_copy(v_ref.at[0], top_ref, sems.at[0]),
        pltpu.make_async_copy(v_ref.at[TR - 1], bottom_ref, sems.at[1]),
    ]
    for copy in copies:
        copy.start()
    for copy in copies:
        copy.wait()
    lines = []
    for row, line_ref in ((0, top_ref), (TR - 1, bottom_ref)):
        mate = near_ref[row : row + 1, :].astype(f32)
        rest = far_ref[row : row + 1, :].astype(f32)
        left = jnp.where(even_core(), rest, mate)
        right = jnp.where(even_core(), mate, rest)
        tail = jnp.concatenate([left, right, jnp.zeros((14, CH), f32)], axis=0)
        lines.append(jnp.concatenate([line_ref[...].astype(f32), tail], axis=0))
    mate_ref[...] = jnp.where(even_row(), lines[1], lines[0]).astype(bf16)
    rest_ref[...] = jnp.where(even_row(), lines[0], lines[1]).astype(bf16)


def local_kernel(
    agents_ref,
    tab_hbm_ref,
    q_ref,
    v_hbm_ref,
    near_ref,
    far_ref,
    mate_ref,
    rest_ref,
    w_ref,
    prob_ref,
    out_hbm_ref,
    wide_ref,
    tab_ref,
    held_ref,
    v_ref,
    above_ref,
    below_ref,
    l_ref,
    r_ref,
    out_ref,
    sems,
):
    v_fetches = []
    for half in range(2):
        cols = pl.ds(half * 128, 128)
        v_fetches.append(
            pltpu.make_async_copy(v_hbm_ref.at[:, :, cols], v_ref.at[:, :, cols], sems.at[half])
        )
    table = pltpu.make_async_copy(tab_hbm_ref, tab_ref, sems.at[2])
    q_fetches = []
    for c in range(3):
        part = pl.ds(c * (N // 3), N // 3)
        q_fetches.append(
            pltpu.make_async_copy(q_ref.at[part, :], held_ref.at[part, :], sems.at[3 + c])
        )
    for copy in v_fetches + [table] + q_fetches:
        copy.start()
    pairs = agent_pairs(agents_ref, wide_ref, 1.0 / math.sqrt(HD))
    outs = []
    for half in range(2):
        cols = pl.ds(half * 128, 128)
        outs.append(
            pltpu.make_async_copy(
                out_ref.at[:, cols], out_hbm_ref.at[:, cols], sems.at[6 + half]
            )
        )
    mate, rest = mate_ref[...].astype(f32), rest_ref[...].astype(f32)
    above_ref[...] = jnp.where(even_row(), rest, mate)
    below_ref[...] = jnp.where(even_row(), mate, rest)
    mate, rest = near_ref[...].astype(f32), far_ref[...].astype(f32)
    l_ref[...] = jnp.where(even_core(), rest, mate)
    r_ref[...] = jnp.where(even_core(), mate, rest)
    for half in range(2):
        cols = pl.ds(half * 128, 128)
        v_fetches[half].wait()

        def put(at, total):
            out_ref[pl.ds(at, TC), cols] = total

        w = [jnp.broadcast_to(w_ref[t : t + 1, cols], (TC, 128)) for t in range(9)]
        column = lax.broadcasted_iota(jnp.int32, (TC, 128), 0)

        def taps(row, left, right):
            row = row.astype(f32)
            before = jnp.where(column == 0, left, pltpu.roll(row, 1, 0))
            after = jnp.where(column == TC - 1, right, pltpu.roll(row, TC - 1, 0))
            return [before * w[3 * d] + row * w[3 * d + 1] + after * w[3 * d + 2] for d in range(3)]

        tail = above_ref[pl.ds(TC, 8), cols]
        t0 = taps(above_ref[pl.ds(0, TC), cols], tail[0:1], tail[1:2])

        def group(start, carry):
            a, b = carry
            lefts, rights = l_ref[pl.ds(start, 8), cols], r_ref[pl.ds(start, 8), cols]
            for k in range(8):
                t = taps(v_ref[start + k, :, cols], lefts[k : k + 1], rights[k : k + 1])
                if a is not None:
                    at = (start + k - 1) * TC
                    if not isinstance(at, int):
                        at = pl.multiple_of(at, TC)
                    put(at, a + t[2])
                a, b = b + t[1], t[0]
            return a, b

        carry = group(0, (None, t0[0]))
        a, b = lax.fori_loop(
            1, TR // 8, lambda g, c: group(pl.multiple_of(g * 8, 8), c), carry
        )
        tail = below_ref[pl.ds(TC, 8), cols]
        t = taps(below_ref[pl.ds(0, TC), cols], tail[0:1], tail[1:2])
        put((TR - 1) * TC, a + t[2])
        outs[half].start()
    probabilities(pairs, tab_ref, table, held_ref, q_fetches, prob_ref)
    for copy in outs:
        copy.wait()


def attend_kernel(av_ref, prob_ref, conv_hbm_ref, sum_ref, stat_ref, conv_ref, sems):
    step = N // AGR
    copies = []
    for c in range(AGR):
        part = pl.ds(c * step, step)
        copies.append(
            pltpu.make_async_copy(conv_hbm_ref.at[part, :], conv_ref.at[part, :], sems.at[c])
        )
        copies[c].start()
    eye = lax.broadcasted_iota(jnp.int32, (128, 128), 0) == lanes((128, 128))
    for pair in range(2):
        pieces = []
        for parity in range(2):
            part = av_ref[pl.ds((2 * pair + parity) * 128, 128), :].astype(f32)
            other = pltpu.roll(part, HD, 1)
            own = half_mask(part.shape, parity)
            for piece in (part, other) if parity == 0 else (other, part):
                pieces.append(jnp.where(own, piece, 0.0))
        agent_values = jnp.concatenate(pieces, axis=0).astype(bf16)
        for b in range(N // 512):
            rows = pl.ds(b * 512, 512)
            sum_ref[rows, pl.ds(pair * 128, 128)] = jnp.dot(
                prob_ref[rows, pl.ds(pair * 2 * AGENTS, 2 * AGENTS)],
                agent_values,
                preferred_element_type=f32,
            )
    for b in range(BLOCKS):
        if b * 128 % step == 0:
            copies[b * 128 // step].wait()
        rows = pl.ds(b * 128, 128)
        x = sum_ref[rows, :] + conv_ref[rows, :]
        sum_ref[rows, :] = x
        mean = jnp.sum(x[:, :128] + x[:, 128:], 1, keepdims=True) * (1.0 / CH)
        x = x - mean
        x = x * x
        squares = jnp.sum(x[:, :128] + x[:, 128:], 1, keepdims=True)
        stat_ref[b : b + 1, :] = jnp.sum(jnp.where(eye, mean, 0.0), 0, keepdims=True)
        stat_ref[BLOCKS + b : BLOCKS + b + 1, :] = jnp.sum(
            jnp.where(eye, squares, 0.0), 0, keepdims=True
        )


def norm_kernel(s0_ref, s1_ref, s2_ref, s3_ref, sum_ref, gain_ref, bias_ref, out_ref, done_ref, sems):
    stats = [s[...] for s in (s0_ref, s1_ref, s2_ref, s3_ref)]
    means = [s[:BLOCKS] for s in stats]
    mean = (means[0] + means[1] + means[2] + means[3]) * 0.25
    squares = sum(s[BLOCKS:] for s in stats)
    for m in means:
        squares = squares + CH * (m - mean) * (m - mean)
    scale = lax.rsqrt(squares * (1.0 / D) + epsilon)
    step = N // AGR
    copies = []
    for b in range(BLOCKS):
        rows = pl.ds(b * 128, 128)
        m = jnp.broadcast_to(mean[b : b + 1], (128, 128)).T
        s = jnp.broadcast_to(scale[b : b + 1], (128, 128)).T
        for half in range(2):
            cols = pl.ds(half * 128, 128)
            done_ref[rows, cols] = (
                (sum_ref[rows, cols] - m) * s * gain_ref[0:1, cols] + bias_ref[0:1, cols]
            ).astype(bf16)
        if (b + 1) * 128 % step == 0:
            part = pl.ds((b + 1) * 128 - step, step)
            copy = pltpu.make_async_copy(
                done_ref.at[part, :], out_ref.at[part, :], sems.at[len(copies)]
            )
            copy.start()
            copies.append(copy)
    for copy in copies:
        copy.wait()


def spread(x):
    slot = x.reshape(TILES, x.shape[0] // TILES, 128)
    return lax.all_to_all(slot, ("row", "col"), 0, 0).reshape(x.shape)


def swap(x, axis, pairs):
    return lax.ppermute(x, axis, [p for i, j in pairs for p in ((i, j), (j, i))])


def chain(axis, first):
    return [(i, i + 1) for i in range(first, lax.axis_size(axis) - 1, 2)]


def after(x, *others):
    return lax.optimization_barrier((x, *others))[0]


def shards(queries, keys, values, positions, conv_weight, norm_gain, norm_bias):
    q = queries.reshape(N, CH)
    k = keys.reshape(N, CH)
    v = values.reshape(N, CH)
    mb = 1 << 20
    wide = pltpu.VMEM((TILES * 8, 128), f32)
    packed, table = call(
        query_kernel,
        (far((TILES * 8, 128), bf16), far((2, TR + TC, 128), f32)),
        "hh",
        scratch=[
            pltpu.VMEM((N, CH), bf16),
            pltpu.VMEM((2, TC, TR), jnp.int32),
            pltpu.SemaphoreType.DMA((AGR + 1,)),
        ],
        nbytes=8 * mb,
        name="pool_queries",
    )(jnp.swapaxes(positions, 1, 2), q)
    agents = spread(packed)
    held_table = pltpu.VMEM((2, TR + TC, 128), f32)
    tk, inner, outer = call(
        key_kernel,
        (near((N, CH), bf16),) + (far((TR, CH), bf16),) * 2,
        "h h",
        scratch=[held_table, pltpu.VMEM((N, CH), bf16), pltpu.SemaphoreType.DMA((AGR + 1,))],
        nbytes=4 * mb,
        name="turn_keys",
    )(table, values, k)
    parts = call(
        partial_kernel,
        far((TILES * ROWS, 128), bf16),
        " v ",
        scratch=[pltpu.VMEM((AGENTS, N), f32), wide],
        nbytes=10 * mb,
        name="partials",
    )(agents, tk, v)
    inner = swap(inner, "col", chain("col", 0))
    outer = swap(outer, "col", chain("col", 1))
    parts, inner, outer = lax.optimization_barrier((parts, inner, outer))
    received = spread(parts)
    mate, rest = call(
        line_kernel,
        (near((TC + 16, CH), bf16),) * 2,
        "hvv",
        scratch=[pltpu.VMEM((TC, CH), bf16)] * 2 + [pltpu.SemaphoreType.DMA((2,))],
        nbytes=mb // 4,
        name="lines",
    )(values, inner, outer)
    received = after(received, mate, rest)
    mate = swap(mate, "row", chain("row", 0))
    rest = swap(rest, "row", chain("row", 1))
    merged = call(merge_kernel, far((TILES * 8, 128), bf16), " ", nbytes=2 * mb, name="merge")(
        received
    )
    merged = after(merged, mate, rest)
    agent_values = spread(merged)
    prob, convolved = call(
        local_kernel,
        (near((N, LOCAL_HEADS * AGENTS), bf16), far((N, CH), f32)),
        " hhhvvvv ",
        scratch=[
            wide,
            held_table,
            pltpu.VMEM((N, CH), bf16),
            pltpu.VMEM((TR, TC, CH), bf16),
            pltpu.VMEM((TC + 16, CH), f32),
            pltpu.VMEM((TC + 16, CH), f32),
            pltpu.VMEM((TR, CH), f32),
            pltpu.VMEM((TR, CH), f32),
            pltpu.VMEM((N, CH), f32),
            pltpu.SemaphoreType.DMA((8,)),
        ],
        nbytes=20 * mb,
        out_spaces=" h",
        name="conv_and_probabilities",
    )(after(agents, merged), table, q, values, inner, outer, mate, rest, conv_weight)
    summed, stats = call(
        attend_kernel,
        (near((N, CH), f32), near((2 * BLOCKS, 128), f32)),
        " vh",
        scratch=[pltpu.VMEM((N, CH), f32), pltpu.SemaphoreType.DMA((AGR,))],
        nbytes=4 * mb,
        name="attend",
    )(agent_values, prob, convolved)
    heads = lax.axis_size("head")
    others = [
        lax.ppermute(stats, "head", [(i, i ^ d) for i in range(heads)]) for d in range(1, heads)
    ]
    normed = call(
        norm_kernel,
        (shape((N, CH), bf16),),
        "v   v  ",
        scratch=[pltpu.VMEM((N, CH), bf16), pltpu.SemaphoreType.DMA((AGR,))],
        nbytes=4 * mb,
        out_spaces="h",
        name="norm",
    )(
        stats, *others, summed, norm_gain.reshape(1, CH), norm_bias.reshape(1, CH)
    )[0]
    return normed.reshape(TR, TC, CH)


def solution(mesh):
    in_specs = (
        P("row", "col", "head"),
        P("row", "col", "head"),
        P("row", "col", "head"),
        P(None, "row", "col"),
        P(None, "head"),
        P("head"),
        P("head"),
    )
    out_specs = P("row", "col", "head")
    return jax.shard_map(shards, mesh=mesh, in_specs=in_specs, out_specs=out_specs, check_vma=False)
```

```python
import math

import jax
import jax.numpy as jnp
from jax import lax
from jax.experimental import pallas as pl
from jax.experimental.pallas import tpu as pltpu
from jax.sharding import PartitionSpec as P

HD = 64
D = 1024
AGR = 4
TR = 48
TC = 32
CH = 256
N = TR * TC
AGENTS = 256
TILES = 64
LOCAL_HEADS = 4
PEERS = TILES // 2
PIECES = 4
BLOCKS = N // 128

f32 = jnp.float32
bf16 = jnp.bfloat16
epsilon = 1e-05

VMEM_SPEC = pl.BlockSpec(memory_space=pltpu.VMEM)
HBM_SPEC = pl.BlockSpec(memory_space=pltpu.HBM)


def call(kernel, outs, in_spaces, scratch=(), nbytes=0, name=None, out_spaces=None):
    fn = pl.pallas_call(
        kernel,
        out_shape=outs,
        in_specs=[HBM_SPEC if c == "h" else VMEM_SPEC for c in in_spaces],
        out_specs=(
            tuple(HBM_SPEC if c == "h" else VMEM_SPEC for c in out_spaces or " " * len(outs))
            if isinstance(outs, tuple)
            else VMEM_SPEC
        ),
        scratch_shapes=list(scratch),
        compiler_params=pltpu.CompilerParams(vmem_limit_bytes=20 * 1024 * 1024),
        cost_estimate=pl.CostEstimate(flops=0, bytes_accessed=nbytes, transcendentals=0),
        name=name,
    )

    def run(*args):
        spaces = {"h": pltpu.HBM, "v": pltpu.VMEM}
        return fn(
            *[
                pltpu.with_memory_space_constraint(x, spaces[c]) if c in spaces else x
                for x, c in zip(args, in_spaces, strict=True)
            ]
        )

    return run


def shape(dims, dtype):
    return jax.ShapeDtypeStruct(dims, dtype)


def near(dims, dtype):
    return pltpu.VMEM(dims, dtype)


def far(dims, dtype):
    return pltpu.HBM(dims, dtype)


def lanes(dims):
    return lax.broadcasted_iota(jnp.int32, dims, len(dims) - 1)


def turn_matrix():
    source = lax.broadcasted_iota(jnp.int32, (CH, CH), 0)
    target = lax.broadcasted_iota(jnp.int32, (CH, CH), 1)
    low = (target & 31) < 16
    minus = jnp.where(low & (source == target + 16), -1.0, 0.0)
    plus = jnp.where((~low) & (source == target - 16), 1.0, 0.0)
    return (minus + plus).astype(bf16)


def sin_cos(angle):
    return jnp.sin(angle), jnp.cos(angle)


def turned(x, matrix, cosine, sine):
    swapped = jnp.dot(x, matrix, preferred_element_type=f32)
    return (x.astype(f32) * cosine + swapped * sine).astype(bf16)


def split_tables(cosines, sines):
    cosines = jnp.concatenate([cosines, cosines], axis=1)
    sines = jnp.concatenate([sines, sines], axis=1)
    return cosines[:TR], sines[:TR], cosines[TR:], sines[TR:]


def cell_tables(tables, first, rows):
    cos_r, sin_r, cos_c, sin_c = tables
    cosine = jnp.concatenate(
        [cos_r[first + i : first + i + 1, :] * cos_c for i in range(rows)], axis=0
    )
    sine = jnp.concatenate(
        [sin_r[first + i : first + i + 1, :] + sin_c for i in range(rows)], axis=0
    )
    return cosine, sine


def slots(block):
    twice = jnp.concatenate([block, block], axis=0).astype(bf16)
    return jnp.broadcast_to(twice[None], (TILES // 2, 16, 128)).reshape(TILES * 8, 128)


def query_kernel(
    pos_ref,
    q_ref,
    agents_ref,
    tab_ref,
    held_ref,
    spot_ref,
    sems,
):
    step = N // AGR
    place = pltpu.make_async_copy(pos_ref, spot_ref, sems.at[AGR])
    place.start()
    copies = []
    for cell in range(AGR):
        part = pl.ds(cell * step, step)
        copy = pltpu.make_async_copy(q_ref.at[part, :], held_ref.at[part, :], sems.at[cell])
        copy.start()
        copies.append(copy)
    matrix = turn_matrix()
    lane = lanes((1, 128)) % HD
    power = jnp.exp((lane % 16).astype(f32) * f32(-math.log(100.0) / 16))
    freq_r = jnp.where(lane < 32, power, 0.0)
    freq_c = jnp.where(lane < 32, 0.0, power)
    place.wait()
    row_line = spot_ref[0][0:1, :].astype(f32)
    col_pos = spot_ref[1][:, 0:1].astype(f32)
    eye = lax.broadcasted_iota(jnp.int32, (TR, TR), 0) == lax.broadcasted_iota(
        jnp.int32, (TR, TR), 1
    )
    row_pos = jnp.sum(jnp.where(eye, jnp.broadcast_to(row_line, (TR, TR)), 0.0), 1, keepdims=True)
    angles = jnp.concatenate([row_pos * freq_r, col_pos * freq_c], axis=0)
    sines, cosines = sin_cos(angles)
    tab_ref[0] = cosines
    tab_ref[1] = sines
    tables = split_tables(cosines, sines)
    means = []
    for cell in range(AGR):
        cosine, sine = cell_tables(tables, cell * (TR // AGR), TR // AGR)
        copies[cell].wait()
        rotated = turned(held_ref[pl.ds(cell * step, step), :], matrix, cosine, sine)
        mean = jnp.sum(rotated.astype(f32), 0, keepdims=True) / step
        means.append(mean.astype(bf16).astype(f32))
    packed = jnp.concatenate([m[:, :128] for m in means] + [m[:, 128:] for m in means], axis=0)
    agents_ref[...] = slots(packed)


def even_core():
    return lax.axis_index("core") == 0


def even_row():
    return lax.rem(lax.axis_index("row"), 2) == 0


def key_kernel(
    tab_hbm_ref,
    v_ref,
    k_ref,
    tk_ref,
    *refs,
):
    sends, (near_ref, far_ref, tab_ref, held_ref, sems) = refs[:PIECES], refs[PIECES:]
    step = N // AGR
    table = pltpu.make_async_copy(tab_hbm_ref, tab_ref, sems.at[AGR])
    table.start()
    copies = []
    for cell in range(AGR):
        part = pl.ds(cell * step, step)
        copies.append(
            pltpu.make_async_copy(k_ref.at[part, :], held_ref.at[part, :], sems.at[cell])
        )
        copies[cell].start()
    first, last = v_ref[:, 0, :], v_ref[:, TC - 1, :]
    even = even_core()
    near_ref[...] = jnp.where(even, last, first)
    far_ref[...] = jnp.where(even, first, last)
    other = jnp.where(even, v_ref[:, :, 128:], v_ref[:, :, :128])
    other = other.reshape(N, 128)
    size = 2 * N // PIECES
    for i in range(PIECES // 2):
        sends[PIECES // 2 + i][...] = other[i * size : (i + 1) * size]
    matrix = turn_matrix()
    table.wait()
    tables = split_tables(tab_ref[0], tab_ref[1])
    for cell in range(AGR):
        part = pl.ds(cell * step, step)
        cosine, sine = cell_tables(tables, cell * (TR // AGR), TR // AGR)
        copies[cell].wait()
        keys = turned(held_ref[part, :], matrix, cosine, sine)
        tk_ref[part, :] = jnp.where(even, keys[:, :128], keys[:, 128:])
        keys = jnp.where(even, keys[:, 128:], keys[:, :128])
        span = math.gcd(size, step)
        for at in range(0, step, span):
            to = cell * step + at
            sends[to // size][pl.ds(to % size, span), :] = keys[at : at + span]


def agent_pairs(agents_ref, wide_ref, scale):
    wide_ref[...] = agents_ref[...].astype(f32) * scale
    pairs = []
    for pair in range(2):
        parts = [wide_ref[pl.ds(4 * pair + k, TILES, stride=8), :] for k in range(AGR)]
        pairs.append(jnp.concatenate(parts, axis=0).astype(bf16))
    return pairs


def half_mask(dims, parity):
    return (lanes(dims) // HD) == parity


def partial_kernel(agents_ref, tk_ref, v_ref, *refs):
    got, (out_ref, score_ref, wide_ref) = refs[:PIECES], refs[PIECES:]
    size = 2 * N // PIECES
    pairs = agent_pairs(agents_ref, wide_ref, 1.0 / math.sqrt(HD))
    mine = jnp.where(even_core(), pairs[0], pairs[1])
    offset = pl.multiple_of(lax.axis_index("core") * 128, 128)
    chunk = 512 if size % 512 == 0 else 384

    def part(c, which):
        at = c * chunk % N
        if c * chunk >= N:
            at = at + which * N
            return got[at // size][pl.ds(at % size, chunk), :]
        if which == 0:
            return tk_ref[pl.ds(at, chunk), :]
        return v_ref[pl.ds(at, chunk), pl.ds(offset, 128)]

    for parity in range(2):
        own = mine
        own = jnp.where(half_mask(own.shape, parity), own, jnp.zeros_like(own))
        peak = None
        for c in range(2 * N // chunk):
            scores = lax.dot_general(
                own,
                part(c, 0),
                (((1,), (1,)), ((), ())),
                preferred_element_type=f32,
            )
            score_ref[:, pl.ds(c * chunk, chunk)] = scores
            for s in range(chunk // 128):
                piece = scores[:, s * 128 : (s + 1) * 128]
                peak = piece if peak is None else jnp.maximum(peak, piece)
        peak = jnp.max(peak, 1, keepdims=True)
        acc = jnp.zeros((AGENTS, 128), f32)
        for c in range(2 * N // chunk):
            weights = jnp.exp(score_ref[:, pl.ds(c * chunk, chunk)] - peak).astype(bf16)
            block = part(c, 1)
            block = jnp.where(half_mask(block.shape, parity), block, jnp.ones_like(block))
            acc = acc + jnp.dot(weights, block, preferred_element_type=f32)
        other = pltpu.roll(acc, HD, 1)
        numer, total = (acc, other) if parity == 0 else (other, acc)
        logs = peak + jnp.log(total)
        values = numer / total
        logs = jnp.max(jnp.where(half_mask(logs.shape, 0), logs, -3e38), 1, keepdims=True)
        first = logs.astype(bf16).astype(f32)
        second = (logs - first).astype(bf16).astype(f32)
        third = logs - first - second
        lane = lanes((AGENTS, 128))
        packed = jnp.where(
            lane < HD,
            values,
            jnp.where(
                lane == HD,
                first,
                jnp.where(lane == HD + 1, second, jnp.where(lane == HD + 2, third, 0.0)),
            ),
        )
        groups = packed.reshape(2, AGENTS // 16, 8, 128)
        groups = jnp.concatenate([groups[0], groups[1]], 1).reshape(AGENTS, 128)
        out_ref[pl.ds(parity * AGENTS, AGENTS), :] = groups.astype(bf16)


def merge_kernel(parts_ref, out_ref):
    source = lax.broadcasted_iota(jnp.int32, (128, 128), 0)
    picker = jnp.where((source >= HD) & (source < HD + 3), 1.0, 0.0).astype(bf16)
    parts = parts_ref[...]
    logs = jnp.dot(parts, picker, preferred_element_type=f32).reshape(PEERS, 16, 128)
    values = parts.astype(f32).reshape(PEERS, 16, 128)
    peak = jnp.max(logs, 0)
    weights = jnp.exp(logs - peak[None])
    merged = jnp.sum(weights * values, 0) / jnp.sum(weights, 0)
    merged = jnp.where(lanes((8, 128)) < HD, merged[:8], pltpu.roll(merged[8:], HD, 1))
    out_ref[...] = slots(merged)


def probabilities(pairs, tab_ref, table, held_ref, fetches, prob_ref):
    chunk = N // len(fetches)
    matrix = turn_matrix()
    table.wait()
    ones = jnp.ones((AGENTS, 128), bf16)
    owns = []
    for head in range(LOCAL_HEADS):
        own = pairs[head // 2]
        owns.append(jnp.where(half_mask(own.shape, head % 2), own, jnp.zeros_like(own)))
    tables = split_tables(tab_ref[0], tab_ref[1])
    for c, fetch in enumerate(fetches):
        rows = pl.ds(c * chunk, chunk)
        cosine, sine = cell_tables(tables, c * (chunk // TC), chunk // TC)
        fetch.wait()
        queries = turned(held_ref[rows, :], matrix, cosine, sine)
        for head in range(LOCAL_HEADS):
            scores = lax.dot_general(
                queries[:, head // 2 * 128 : head // 2 * 128 + 128],
                owns[head],
                (((1,), (1,)), ((), ())),
                preferred_element_type=f32,
            )
            weights = jnp.exp(scores - jnp.max(scores, 1, keepdims=True))
            total = jnp.dot(weights.astype(bf16), ones, preferred_element_type=f32)
            scale = 1.0 / total
            scale = jnp.concatenate([scale, scale], axis=1)
            prob_ref[rows, pl.ds(head * AGENTS, AGENTS)] = (weights * scale).astype(bf16)


def line_kernel(v_ref, near_ref, far_ref, mate_ref, rest_ref, top_ref, bottom_ref, sems):
    copies = [
        pltpu.make_async_copy(v_ref.at[0], top_ref, sems.at[0]),
        pltpu.make_async_copy(v_ref.at[TR - 1], bottom_ref, sems.at[1]),
    ]
    for copy in copies:
        copy.start()
    for copy in copies:
        copy.wait()
    lines = []
    for row, line_ref in ((0, top_ref), (TR - 1, bottom_ref)):
        mate = near_ref[row : row + 1, :].astype(f32)
        rest = far_ref[row : row + 1, :].astype(f32)
        left = jnp.where(even_core(), rest, mate)
        right = jnp.where(even_core(), mate, rest)
        tail = jnp.concatenate([left, right, jnp.zeros((14, CH), f32)], axis=0)
        lines.append(jnp.concatenate([line_ref[...].astype(f32), tail], axis=0))
    mate_ref[...] = jnp.where(even_row(), lines[1], lines[0]).astype(bf16)
    rest_ref[...] = jnp.where(even_row(), lines[0], lines[1]).astype(bf16)


def local_kernel(
    agents_ref,
    tab_hbm_ref,
    q_ref,
    v_hbm_ref,
    near_ref,
    far_ref,
    mate_ref,
    rest_ref,
    w_ref,
    prob_ref,
    out_hbm_ref,
    wide_ref,
    tab_ref,
    held_ref,
    v_ref,
    above_ref,
    below_ref,
    l_ref,
    r_ref,
    out_ref,
    sems,
):
    v_fetches = []
    for half in range(2):
        cols = pl.ds(half * 128, 128)
        v_fetches.append(
            pltpu.make_async_copy(v_hbm_ref.at[:, :, cols], v_ref.at[:, :, cols], sems.at[half])
        )
    table = pltpu.make_async_copy(tab_hbm_ref, tab_ref, sems.at[2])
    q_fetches = []
    for c in range(3):
        part = pl.ds(c * (N // 3), N // 3)
        q_fetches.append(
            pltpu.make_async_copy(q_ref.at[part, :], held_ref.at[part, :], sems.at[3 + c])
        )
    for copy in v_fetches + [table] + q_fetches:
        copy.start()
    pairs = agent_pairs(agents_ref, wide_ref, 1.0 / math.sqrt(HD))
    outs = []
    for half in range(2):
        cols = pl.ds(half * 128, 128)
        outs.append(
            pltpu.make_async_copy(
                out_ref.at[:, cols], out_hbm_ref.at[:, cols], sems.at[6 + half]
            )
        )
    mate, rest = mate_ref[...].astype(f32), rest_ref[...].astype(f32)
    above_ref[...] = jnp.where(even_row(), rest, mate)
    below_ref[...] = jnp.where(even_row(), mate, rest)
    mate, rest = near_ref[...].astype(f32), far_ref[...].astype(f32)
    l_ref[...] = jnp.where(even_core(), rest, mate)
    r_ref[...] = jnp.where(even_core(), mate, rest)
    for half in range(2):
        cols = pl.ds(half * 128, 128)
        v_fetches[half].wait()

        def put(at, total):
            out_ref[pl.ds(at, TC), cols] = total

        w = [jnp.broadcast_to(w_ref[t : t + 1, cols], (TC, 128)) for t in range(9)]
        column = lax.broadcasted_iota(jnp.int32, (TC, 128), 0)

        def taps(row, left, right):
            row = row.astype(f32)
            before = jnp.where(column == 0, left, pltpu.roll(row, 1, 0))
            after = jnp.where(column == TC - 1, right, pltpu.roll(row, TC - 1, 0))
            return [before * w[3 * d] + row * w[3 * d + 1] + after * w[3 * d + 2] for d in range(3)]

        tail = above_ref[pl.ds(TC, 8), cols]
        t0 = taps(above_ref[pl.ds(0, TC), cols], tail[0:1], tail[1:2])

        def group(start, carry):
            a, b = carry
            lefts, rights = l_ref[pl.ds(start, 8), cols], r_ref[pl.ds(start, 8), cols]
            for k in range(8):
                t = taps(v_ref[start + k, :, cols], lefts[k : k + 1], rights[k : k + 1])
                if a is not None:
                    at = (start + k - 1) * TC
                    if not isinstance(at, int):
                        at = pl.multiple_of(at, TC)
                    put(at, a + t[2])
                a, b = b + t[1], t[0]
            return a, b

        carry = group(0, (None, t0[0]))
        a, b = lax.fori_loop(
            1, TR // 8, lambda g, c: group(pl.multiple_of(g * 8, 8), c), carry
        )
        tail = below_ref[pl.ds(TC, 8), cols]
        t = taps(below_ref[pl.ds(0, TC), cols], tail[0:1], tail[1:2])
        put((TR - 1) * TC, a + t[2])
        outs[half].start()
    probabilities(pairs, tab_ref, table, held_ref, q_fetches, prob_ref)
    for copy in outs:
        copy.wait()


def attend_kernel(av_ref, prob_ref, conv_hbm_ref, sum_ref, stat_ref, conv_ref, sems):
    step = N // AGR
    copies = []
    for c in range(AGR):
        part = pl.ds(c * step, step)
        copies.append(
            pltpu.make_async_copy(conv_hbm_ref.at[part, :], conv_ref.at[part, :], sems.at[c])
        )
        copies[c].start()
    eye = lax.broadcasted_iota(jnp.int32, (128, 128), 0) == lanes((128, 128))
    av = av_ref[...].astype(f32).reshape(2, AGENTS // 16, 2, 8, 128)
    for pair in range(2):
        pieces = []
        for parity in range(2):
            part = av[parity, :, pair].reshape(128, 128)
            other = pltpu.roll(part, HD, 1)
            own = half_mask(part.shape, parity)
            for piece in (part, other) if parity == 0 else (other, part):
                pieces.append(jnp.where(own, piece, 0.0))
        agent_values = jnp.concatenate(pieces, axis=0).astype(bf16)
        for b in range(N // 512):
            rows = pl.ds(b * 512, 512)
            sum_ref[rows, pl.ds(pair * 128, 128)] = jnp.dot(
                prob_ref[rows, pl.ds(pair * 2 * AGENTS, 2 * AGENTS)],
                agent_values,
                preferred_element_type=f32,
            )
    for b in range(BLOCKS):
        if b * 128 % step == 0:
            copies[b * 128 // step].wait()
        rows = pl.ds(b * 128, 128)
        x = sum_ref[rows, :] + conv_ref[rows, :]
        sum_ref[rows, :] = x
        mean = jnp.sum(x[:, :128] + x[:, 128:], 1, keepdims=True) * (1.0 / CH)
        x = x - mean
        x = x * x
        squares = jnp.sum(x[:, :128] + x[:, 128:], 1, keepdims=True)
        stat_ref[b : b + 1, :] = jnp.sum(jnp.where(eye, mean, 0.0), 0, keepdims=True)
        stat_ref[BLOCKS + b : BLOCKS + b + 1, :] = jnp.sum(
            jnp.where(eye, squares, 0.0), 0, keepdims=True
        )


def norm_kernel(s0_ref, s1_ref, s2_ref, s3_ref, sum_ref, gain_ref, bias_ref, out_ref, done_ref, sems):
    stats = [s[...] for s in (s0_ref, s1_ref, s2_ref, s3_ref)]
    means = [s[:BLOCKS] for s in stats]
    mean = (means[0] + means[1] + means[2] + means[3]) * 0.25
    squares = sum(s[BLOCKS:] for s in stats)
    for m in means:
        squares = squares + CH * (m - mean) * (m - mean)
    scale = lax.rsqrt(squares * (1.0 / D) + epsilon)
    step = N // AGR
    copies = []
    for b in range(BLOCKS):
        rows = pl.ds(b * 128, 128)
        m = jnp.broadcast_to(mean[b : b + 1], (128, 128)).T
        s = jnp.broadcast_to(scale[b : b + 1], (128, 128)).T
        for half in range(2):
            cols = pl.ds(half * 128, 128)
            done_ref[rows, cols] = (
                (sum_ref[rows, cols] - m) * s * gain_ref[0:1, cols] + bias_ref[0:1, cols]
            ).astype(bf16)
        if (b + 1) * 128 % step == 0:
            part = pl.ds((b + 1) * 128 - step, step)
            copy = pltpu.make_async_copy(
                done_ref.at[part, :], out_ref.at[part, :], sems.at[len(copies)]
            )
            copy.start()
            copies.append(copy)
    for copy in copies:
        copy.wait()


TILE_AXES = ("row", "z", "core")


def spread(x, axes=TILE_AXES):
    count = lax.axis_size(axes)
    slot = x.reshape(count, x.shape[0] // count, 128)
    return lax.all_to_all(slot, axes, 0, 0).reshape(x.shape)


def swap(x, axis, pairs):
    return lax.ppermute(x, axis, [p for i, j in pairs for p in ((i, j), (j, i))])


def chain(axis, first):
    return [(i, i + 1) for i in range(first, lax.axis_size(axis) - 1, 2)]


def after(x, *others):
    return lax.optimization_barrier((x, *others))[0]


def shards(queries, keys, values, positions, conv_weight, norm_gain, norm_bias):
    q = queries.reshape(N, CH)
    k = keys.reshape(N, CH)
    v = values.reshape(N, CH)
    mb = 1 << 20
    wide = pltpu.VMEM((TILES * 8, 128), f32)
    packed, table = call(
        query_kernel,
        (far((TILES * 8, 128), bf16), far((2, TR + TC, 128), f32)),
        "hh",
        scratch=[
            pltpu.VMEM((N, CH), bf16),
            pltpu.VMEM((2, TC, TR), jnp.int32),
            pltpu.SemaphoreType.DMA((AGR + 1,)),
        ],
        nbytes=8 * mb,
        name="pool_queries",
    )(jnp.swapaxes(positions, 1, 2), q)
    agents = spread(packed)
    held_table = pltpu.VMEM((2, TR + TC, 128), f32)
    tk, *sends, inner, outer = call(
        key_kernel,
        (near((N, 128), bf16),)
        + (near((2 * N // PIECES, 128), bf16),) * PIECES
        + (far((TR, CH), bf16),) * 2,
        "h h",
        scratch=[held_table, pltpu.VMEM((N, CH), bf16), pltpu.SemaphoreType.DMA((AGR + 1,))],
        nbytes=4 * mb,
        name="turn_keys",
    )(table, values, k)
    got = [swap(send, "core", chain("core", 0)) for send in sends]
    inner = swap(inner, "core", chain("core", 0))
    outer = swap(outer, ("z", "core"), chain(("z", "core"), 1))
    parts = call(
        partial_kernel,
        far((2 * AGENTS, 128), bf16),
        " v " + " " * PIECES,
        scratch=[pltpu.VMEM((AGENTS, 2 * N), f32), wide],
        nbytes=10 * mb,
        name="partials",
    )(agents, tk, v, *got)
    parts, inner, outer = lax.optimization_barrier((parts, inner, outer))
    received = spread(parts, ("row", "z"))
    mate, rest = call(
        line_kernel,
        (near((TC + 16, CH), bf16),) * 2,
        "hvv",
        scratch=[pltpu.VMEM((TC, CH), bf16)] * 2 + [pltpu.SemaphoreType.DMA((2,))],
        nbytes=mb // 4,
        name="lines",
    )(values, inner, outer)
    received = after(received, mate, rest)
    mate = swap(mate, "row", chain("row", 0))
    rest = swap(rest, "row", chain("row", 1))
    merged = call(merge_kernel, far((TILES * 8, 128), bf16), " ", nbytes=2 * mb, name="merge")(
        received
    )
    merged = after(merged, mate, rest)
    agent_values = spread(merged)
    prob, convolved = call(
        local_kernel,
        (near((N, LOCAL_HEADS * AGENTS), bf16), far((N, CH), f32)),
        " hhhvvvv ",
        scratch=[
            wide,
            held_table,
            pltpu.VMEM((N, CH), bf16),
            pltpu.VMEM((TR, TC, CH), bf16),
            pltpu.VMEM((TC + 16, CH), f32),
            pltpu.VMEM((TC + 16, CH), f32),
            pltpu.VMEM((TR, CH), f32),
            pltpu.VMEM((TR, CH), f32),
            pltpu.VMEM((N, CH), f32),
            pltpu.SemaphoreType.DMA((8,)),
        ],
        nbytes=20 * mb,
        out_spaces=" h",
        name="conv_and_probabilities",
    )(after(agents, merged), table, q, values, inner, outer, mate, rest, conv_weight)
    summed, stats = call(
        attend_kernel,
        (near((N, CH), f32), near((2 * BLOCKS, 128), f32)),
        " vh",
        scratch=[pltpu.VMEM((N, CH), f32), pltpu.SemaphoreType.DMA((AGR,))],
        nbytes=4 * mb,
        name="attend",
    )(agent_values, prob, convolved)
    heads = lax.axis_size("head")
    others = [
        lax.ppermute(stats, "head", [(i, i ^ d) for i in range(heads)]) for d in range(1, heads)
    ]
    normed = call(
        norm_kernel,
        (shape((N, CH), bf16),),
        "v   v  ",
        scratch=[pltpu.VMEM((N, CH), bf16), pltpu.SemaphoreType.DMA((AGR,))],
        nbytes=4 * mb,
        out_spaces="h",
        name="norm",
    )(
        stats, *others, summed, norm_gain.reshape(1, CH), norm_bias.reshape(1, CH)
    )[0]
    return normed.reshape(TR, TC, CH)


def solution(mesh):
    rows, cols, heads = mesh.devices.shape
    cores = jax.sharding.Mesh(
        mesh.devices.reshape(rows, cols // 2, 2, heads), ("row", "z", "core", "head")
    )
    tile = P("row", ("z", "core"), "head")
    in_specs = (tile,) * 3 + (
        P(None, "row", ("z", "core")),
        P(None, "head"),
        P("head"),
        P("head"),
    )
    return jax.shard_map(shards, mesh=cores, in_specs=in_specs, out_specs=tile, check_vma=False)
```

```python
import math

import jax
import jax.numpy as jnp
from jax import lax
from jax.experimental import pallas as pl
from jax.experimental.pallas import tpu as pltpu
from jax.sharding import PartitionSpec as P

HD = 64
D = 1024
AGR = 4
TR = 48
TC = 32
CH = 256
N = TR * TC
AGENTS = 256
TILES = 64
LOCAL_HEADS = 4
PEERS = TILES // 2
PIECES = 4
BLOCKS = N // 128

f32 = jnp.float32
bf16 = jnp.bfloat16
epsilon = 1e-05

VMEM_SPEC = pl.BlockSpec(memory_space=pltpu.VMEM)
HBM_SPEC = pl.BlockSpec(memory_space=pltpu.HBM)


def call(kernel, outs, in_spaces, scratch=(), nbytes=0, name=None, out_spaces=None):
    fn = pl.pallas_call(
        kernel,
        out_shape=outs,
        in_specs=[HBM_SPEC if c == "h" else VMEM_SPEC for c in in_spaces],
        out_specs=(
            tuple(HBM_SPEC if c == "h" else VMEM_SPEC for c in out_spaces or " " * len(outs))
            if isinstance(outs, tuple)
            else VMEM_SPEC
        ),
        scratch_shapes=list(scratch),
        compiler_params=pltpu.CompilerParams(vmem_limit_bytes=20 * 1024 * 1024),
        cost_estimate=pl.CostEstimate(flops=0, bytes_accessed=nbytes, transcendentals=0),
        name=name,
    )

    def run(*args):
        spaces = {"h": pltpu.HBM, "v": pltpu.VMEM}
        return fn(
            *[
                pltpu.with_memory_space_constraint(x, spaces[c]) if c in spaces else x
                for x, c in zip(args, in_spaces, strict=True)
            ]
        )

    return run


def shape(dims, dtype):
    return jax.ShapeDtypeStruct(dims, dtype)


def near(dims, dtype):
    return pltpu.VMEM(dims, dtype)


def far(dims, dtype):
    return pltpu.HBM(dims, dtype)


def lanes(dims):
    return lax.broadcasted_iota(jnp.int32, dims, len(dims) - 1)


def turn_matrix():
    source = lax.broadcasted_iota(jnp.int32, (CH, CH), 0)
    target = lax.broadcasted_iota(jnp.int32, (CH, CH), 1)
    low = (target & 31) < 16
    minus = jnp.where(low & (source == target + 16), -1.0, 0.0)
    plus = jnp.where((~low) & (source == target - 16), 1.0, 0.0)
    return (minus + plus).astype(bf16)


def sin_cos(angle):
    return jnp.sin(angle), jnp.cos(angle)


def turned(x, matrix, cosine, sine):
    swapped = jnp.dot(x, matrix, preferred_element_type=f32)
    return (x.astype(f32) * cosine + swapped * sine).astype(bf16)


def split_tables(cosines, sines):
    cosines = jnp.concatenate([cosines, cosines], axis=1)
    sines = jnp.concatenate([sines, sines], axis=1)
    return cosines[:TR], sines[:TR], cosines[TR:], sines[TR:]


def cell_tables(tables, first, rows):
    cos_r, sin_r, cos_c, sin_c = tables
    cosine = jnp.concatenate(
        [cos_r[first + i : first + i + 1, :] * cos_c for i in range(rows)], axis=0
    )
    sine = jnp.concatenate(
        [sin_r[first + i : first + i + 1, :] + sin_c for i in range(rows)], axis=0
    )
    return cosine, sine


def slots(block):
    twice = jnp.concatenate([block, block], axis=0).astype(bf16)
    return jnp.broadcast_to(twice[None], (TILES // 2, 16, 128)).reshape(TILES * 8, 128)


def query_kernel(
    pos_ref,
    q_ref,
    agents_ref,
    tab_ref,
    held_ref,
    spot_ref,
    sems,
):
    step = N // AGR
    place = pltpu.make_async_copy(pos_ref, spot_ref, sems.at[AGR])
    place.start()
    copies = []
    for cell in range(AGR):
        part = pl.ds(cell * step, step)
        copy = pltpu.make_async_copy(q_ref.at[part, :], held_ref.at[part, :], sems.at[cell])
        copy.start()
        copies.append(copy)
    matrix = turn_matrix()
    lane = lanes((1, 128)) % HD
    power = jnp.exp((lane % 16).astype(f32) * f32(-math.log(100.0) / 16))
    freq_r = jnp.where(lane < 32, power, 0.0)
    freq_c = jnp.where(lane < 32, 0.0, power)
    place.wait()
    row_line = spot_ref[0][0:1, :].astype(f32)
    col_pos = spot_ref[1][:, 0:1].astype(f32)
    eye = lax.broadcasted_iota(jnp.int32, (TR, TR), 0) == lax.broadcasted_iota(
        jnp.int32, (TR, TR), 1
    )
    row_pos = jnp.sum(jnp.where(eye, jnp.broadcast_to(row_line, (TR, TR)), 0.0), 1, keepdims=True)
    angles = jnp.concatenate([row_pos * freq_r, col_pos * freq_c], axis=0)
    sines, cosines = sin_cos(angles)
    tab_ref[0] = cosines
    tab_ref[1] = sines
    tables = split_tables(cosines, sines)
    means = []
    for cell in range(AGR):
        cosine, sine = cell_tables(tables, cell * (TR // AGR), TR // AGR)
        copies[cell].wait()
        rotated = turned(held_ref[pl.ds(cell * step, step), :], matrix, cosine, sine)
        mean = jnp.sum(rotated.astype(f32), 0, keepdims=True) / step
        means.append(mean.astype(bf16).astype(f32))
    packed = jnp.concatenate([m[:, :128] for m in means] + [m[:, 128:] for m in means], axis=0)
    agents_ref[...] = slots(packed)


def even_core():
    return lax.axis_index("core") == 0


def even_row():
    return lax.rem(lax.axis_index("row"), 2) == 0


def key_kernel(
    tab_hbm_ref,
    v_ref,
    k_ref,
    tk_ref,
    *refs,
):
    sends, (near_ref, far_ref, tab_ref, held_ref, sems) = refs[:PIECES], refs[PIECES:]
    step = N // AGR
    table = pltpu.make_async_copy(tab_hbm_ref, tab_ref, sems.at[AGR])
    table.start()
    copies = []
    for cell in range(AGR):
        part = pl.ds(cell * step, step)
        copies.append(
            pltpu.make_async_copy(k_ref.at[part, :], held_ref.at[part, :], sems.at[cell])
        )
        copies[cell].start()
    first, last = v_ref[:, 0, :], v_ref[:, TC - 1, :]
    even = even_core()
    near_ref[...] = jnp.where(even, last, first)
    far_ref[...] = jnp.where(even, first, last)
    other = jnp.where(even, v_ref[:, :, 128:], v_ref[:, :, :128])
    other = other.reshape(N, 128)
    size = 2 * N // PIECES
    for i in range(PIECES // 2):
        sends[PIECES // 2 + i][...] = other[i * size : (i + 1) * size]
    matrix = turn_matrix()
    table.wait()
    tables = split_tables(tab_ref[0], tab_ref[1])
    for cell in range(AGR):
        part = pl.ds(cell * step, step)
        cosine, sine = cell_tables(tables, cell * (TR // AGR), TR // AGR)
        copies[cell].wait()
        keys = turned(held_ref[part, :], matrix, cosine, sine)
        tk_ref[part, :] = jnp.where(even, keys[:, :128], keys[:, 128:])
        keys = jnp.where(even, keys[:, 128:], keys[:, :128])
        span = math.gcd(size, step)
        for at in range(0, step, span):
            to = cell * step + at
            sends[to // size][pl.ds(to % size, span), :] = keys[at : at + span]


def agent_pairs(agents_ref, wide_ref, scale):
    wide_ref[...] = agents_ref[...].astype(f32) * scale
    pairs = []
    for pair in range(2):
        parts = [wide_ref[pl.ds(4 * pair + k, TILES, stride=8), :] for k in range(AGR)]
        pairs.append(jnp.concatenate(parts, axis=0).astype(bf16))
    return pairs


def half_mask(dims, parity):
    return (lanes(dims) // HD) == parity


def partial_kernel(agents_ref, tk_ref, v_ref, *refs):
    got, (out_ref, score_ref, wide_ref) = refs[:PIECES], refs[PIECES:]
    size = 2 * N // PIECES
    pairs = agent_pairs(agents_ref, wide_ref, 1.0 / math.sqrt(HD))
    mine = jnp.where(even_core(), pairs[0], pairs[1])
    offset = pl.multiple_of(lax.axis_index("core") * 128, 128)
    chunk = 512 if size % 512 == 0 else 384

    def part(c, which):
        at = c * chunk % N
        if c * chunk >= N:
            at = at + which * N
            return got[at // size][pl.ds(at % size, chunk), :]
        if which == 0:
            return tk_ref[pl.ds(at, chunk), :]
        return v_ref[pl.ds(at, chunk), pl.ds(offset, 128)]

    for parity in range(2):
        own = mine
        own = jnp.where(half_mask(own.shape, parity), own, jnp.zeros_like(own))
        peak = None
        for c in range(2 * N // chunk):
            scores = lax.dot_general(
                own,
                part(c, 0),
                (((1,), (1,)), ((), ())),
                preferred_element_type=f32,
            )
            score_ref[:, pl.ds(c * chunk, chunk)] = scores
            for s in range(chunk // 128):
                piece = scores[:, s * 128 : (s + 1) * 128]
                peak = piece if peak is None else jnp.maximum(peak, piece)
        peak = jnp.max(peak, 1, keepdims=True)
        acc = jnp.zeros((AGENTS, 128), f32)
        for c in range(2 * N // chunk):
            weights = jnp.exp(score_ref[:, pl.ds(c * chunk, chunk)] - peak).astype(bf16)
            block = part(c, 1)
            block = jnp.where(half_mask(block.shape, parity), block, jnp.ones_like(block))
            acc = acc + jnp.dot(weights, block, preferred_element_type=f32)
        other = pltpu.roll(acc, HD, 1)
        numer, total = (acc, other) if parity == 0 else (other, acc)
        logs = peak + jnp.log(total)
        values = numer / total
        logs = jnp.max(jnp.where(half_mask(logs.shape, 0), logs, -3e38), 1, keepdims=True)
        first = logs.astype(bf16).astype(f32)
        second = (logs - first).astype(bf16).astype(f32)
        third = logs - first - second
        lane = lanes((AGENTS, 128))
        packed = jnp.where(
            lane < HD,
            values,
            jnp.where(
                lane == HD,
                first,
                jnp.where(lane == HD + 1, second, jnp.where(lane == HD + 2, third, 0.0)),
            ),
        )
        groups = packed.reshape(2, AGENTS // 16, 8, 128)
        groups = jnp.concatenate([groups[0], groups[1]], 1).reshape(AGENTS, 128)
        out_ref[pl.ds(parity * AGENTS, AGENTS), :] = groups.astype(bf16)


def merge_kernel(parts_ref, out_ref):
    source = lax.broadcasted_iota(jnp.int32, (128, 128), 0)
    picker = jnp.where((source >= HD) & (source < HD + 3), 1.0, 0.0).astype(bf16)
    parts = parts_ref[...]
    logs = jnp.dot(parts, picker, preferred_element_type=f32).reshape(PEERS, 16, 128)
    values = parts.astype(f32).reshape(PEERS, 16, 128)
    peak = jnp.max(logs, 0)
    weights = jnp.exp(logs - peak[None])
    merged = jnp.sum(weights * values, 0) / jnp.sum(weights, 0)
    merged = jnp.where(lanes((8, 128)) < HD, merged[:8], pltpu.roll(merged[8:], HD, 1))
    out_ref[...] = slots(merged)


def probabilities(pairs, tab_ref, table, held_ref, fetches, prob_ref):
    chunk = N // len(fetches)
    matrix = turn_matrix()
    table.wait()
    ones = jnp.ones((AGENTS, 128), bf16)
    owns = []
    for head in range(LOCAL_HEADS):
        own = pairs[head // 2]
        owns.append(jnp.where(half_mask(own.shape, head % 2), own, jnp.zeros_like(own)))
    tables = split_tables(tab_ref[0], tab_ref[1])
    for c, fetch in enumerate(fetches):
        rows = pl.ds(c * chunk, chunk)
        cosine, sine = cell_tables(tables, c * (chunk // TC), chunk // TC)
        fetch.wait()
        queries = turned(held_ref[rows, :], matrix, cosine, sine)
        for head in range(LOCAL_HEADS):
            scores = lax.dot_general(
                queries[:, head // 2 * 128 : head // 2 * 128 + 128],
                owns[head],
                (((1,), (1,)), ((), ())),
                preferred_element_type=f32,
            )
            weights = jnp.exp(scores - jnp.max(scores, 1, keepdims=True))
            total = jnp.dot(weights.astype(bf16), ones, preferred_element_type=f32)
            scale = 1.0 / total
            scale = jnp.concatenate([scale, scale], axis=1)
            prob_ref[rows, pl.ds(head * AGENTS, AGENTS)] = (weights * scale).astype(bf16)


def line_kernel(v_ref, near_ref, far_ref, mate_ref, rest_ref, top_ref, bottom_ref, sems):
    copies = [
        pltpu.make_async_copy(v_ref.at[0], top_ref, sems.at[0]),
        pltpu.make_async_copy(v_ref.at[TR - 1], bottom_ref, sems.at[1]),
    ]
    for copy in copies:
        copy.start()
    for copy in copies:
        copy.wait()
    lines = []
    for row, line_ref in ((0, top_ref), (TR - 1, bottom_ref)):
        mate = near_ref[row : row + 1, :].astype(f32)
        rest = far_ref[row : row + 1, :].astype(f32)
        left = jnp.where(even_core(), rest, mate)
        right = jnp.where(even_core(), mate, rest)
        tail = jnp.concatenate([left, right, jnp.zeros((14, CH), f32)], axis=0)
        lines.append(jnp.concatenate([line_ref[...].astype(f32), tail], axis=0))
    mate_ref[...] = jnp.where(even_row(), lines[1], lines[0]).astype(bf16)
    rest_ref[...] = jnp.where(even_row(), lines[0], lines[1]).astype(bf16)


def probability_kernel(
    agents_ref, tab_hbm_ref, q_ref, prob_ref, wide_ref, tab_ref, held_ref, sems
):
    table = pltpu.make_async_copy(tab_hbm_ref, tab_ref, sems.at[3])
    table.start()
    fetches = []
    for c in range(3):
        part = pl.ds(c * (N // 3), N // 3)
        fetches.append(pltpu.make_async_copy(q_ref.at[part, :], held_ref.at[part, :], sems.at[c]))
        fetches[c].start()
    pairs = agent_pairs(agents_ref, wide_ref, 1.0 / math.sqrt(HD))
    probabilities(pairs, tab_ref, table, held_ref, fetches, prob_ref)


def shifted(row, left, right):
    column = lax.broadcasted_iota(jnp.int32, row.shape, 0)
    before = jnp.where(column == 0, left, pltpu.roll(row, 1, 0))
    behind = jnp.where(column == TC - 1, right, pltpu.roll(row, TC - 1, 0))
    return before, row, behind


def conv_kernel(
    v_hbm_ref, near_ref, far_ref, w_ref, out_hbm_ref, v_ref, l_ref, r_ref, out_ref, sems
):
    fetches, outs = [], []
    for half in range(2):
        cols = pl.ds(half * 128, 128)
        fetches.append(
            pltpu.make_async_copy(v_hbm_ref.at[:, :, cols], v_ref.at[:, :, cols], sems.at[half])
        )
        fetches[half].start()
        outs.append(
            pltpu.make_async_copy(
                out_ref.at[:, cols], out_hbm_ref.at[:, cols], sems.at[2 + half]
            )
        )
    mate, rest = near_ref[...].astype(f32), far_ref[...].astype(f32)
    l_ref[...] = jnp.where(even_core(), rest, mate)
    r_ref[...] = jnp.where(even_core(), mate, rest)
    for half in range(2):
        cols = pl.ds(half * 128, 128)
        w = [jnp.broadcast_to(w_ref[t : t + 1, cols], (TC, 128)) for t in range(9)]

        def group(start, carry):
            a, b = carry
            lefts, rights = l_ref[pl.ds(start, 8), cols], r_ref[pl.ds(start, 8), cols]
            for k in range(8):
                row = v_ref[start + k, :, cols].astype(f32)
                x = shifted(row, lefts[k : k + 1], rights[k : k + 1])
                t = [sum(x[e] * w[3 * d + e] for e in range(3)) for d in range(3)]
                if a is not None:
                    at = (start + k - 1) * TC
                    if not isinstance(at, int):
                        at = pl.multiple_of(at, TC)
                    out_ref[pl.ds(at, TC), cols] = a + t[2]
                    b = b + t[1]
                else:
                    b = t[1]
                a, b = b, t[0]
            return a, b

        fetches[half].wait()
        carry = group(0, (None, None))
        a, b = lax.fori_loop(1, TR // 8, lambda g, c: group(pl.multiple_of(g * 8, 8), c), carry)
        out_ref[pl.ds((TR - 1) * TC, TC), cols] = a
        outs[half].start()
    for copy in outs:
        copy.wait()


def attend_kernel(
    av_ref,
    prob_ref,
    conv_hbm_ref,
    mate_ref,
    rest_ref,
    w_ref,
    sum_ref,
    stat_ref,
    conv_ref,
    sems,
):
    step = N // AGR
    copies = []
    for c in range(AGR):
        part = pl.ds(c * step, step)
        copies.append(
            pltpu.make_async_copy(conv_hbm_ref.at[part, :], conv_ref.at[part, :], sems.at[c])
        )
        copies[c].start()
    eye = lax.broadcasted_iota(jnp.int32, (128, 128), 0) == lanes((128, 128))
    av = av_ref[...].astype(f32).reshape(2, AGENTS // 16, 2, 8, 128)
    for pair in range(2):
        pieces = []
        for parity in range(2):
            part = av[parity, :, pair].reshape(128, 128)
            other = pltpu.roll(part, HD, 1)
            own = half_mask(part.shape, parity)
            for piece in (part, other) if parity == 0 else (other, part):
                pieces.append(jnp.where(own, piece, 0.0))
        agent_values = jnp.concatenate(pieces, axis=0).astype(bf16)
        for b in range(N // 512):
            rows = pl.ds(b * 512, 512)
            sum_ref[rows, pl.ds(pair * 128, 128)] = jnp.dot(
                prob_ref[rows, pl.ds(pair * 2 * AGENTS, 2 * AGENTS)],
                agent_values,
                preferred_element_type=f32,
            )
    mate, rest = mate_ref[...].astype(f32), rest_ref[...].astype(f32)
    above = jnp.where(even_row(), rest, mate)
    below = jnp.where(even_row(), mate, rest)
    for line, tap, at in ((above, 0, 0), (below, 6, N - TC)):
        x = shifted(line[:TC], line[TC : TC + 1], line[TC + 1 : TC + 2])
        total = sum(x[e] * w_ref[tap + e : tap + e + 1, :] for e in range(3))
        sum_ref[pl.ds(at, TC), :] = sum_ref[pl.ds(at, TC), :] + total
    for b in range(BLOCKS):
        if b * 128 % step == 0:
            copies[b * 128 // step].wait()
        rows = pl.ds(b * 128, 128)
        x = sum_ref[rows, :] + conv_ref[rows, :]
        sum_ref[rows, :] = x
        mean = jnp.sum(x[:, :128] + x[:, 128:], 1, keepdims=True) * (1.0 / CH)
        x = x - mean
        x = x * x
        squares = jnp.sum(x[:, :128] + x[:, 128:], 1, keepdims=True)
        stat_ref[b : b + 1, :] = jnp.sum(jnp.where(eye, mean, 0.0), 0, keepdims=True)
        stat_ref[BLOCKS + b : BLOCKS + b + 1, :] = jnp.sum(
            jnp.where(eye, squares, 0.0), 0, keepdims=True
        )


def norm_kernel(s0_ref, s1_ref, s2_ref, s3_ref, sum_ref, gain_ref, bias_ref, out_ref, done_ref, sems):
    stats = [s[...] for s in (s0_ref, s1_ref, s2_ref, s3_ref)]
    means = [s[:BLOCKS] for s in stats]
    mean = (means[0] + means[1] + means[2] + means[3]) * 0.25
    squares = sum(s[BLOCKS:] for s in stats)
    for m in means:
        squares = squares + CH * (m - mean) * (m - mean)
    scale = lax.rsqrt(squares * (1.0 / D) + epsilon)
    step = N // AGR
    copies = []
    for b in range(BLOCKS):
        rows = pl.ds(b * 128, 128)
        m = jnp.broadcast_to(mean[b : b + 1], (128, 128)).T
        s = jnp.broadcast_to(scale[b : b + 1], (128, 128)).T
        for half in range(2):
            cols = pl.ds(half * 128, 128)
            done_ref[rows, cols] = (
                (sum_ref[rows, cols] - m) * s * gain_ref[0:1, cols] + bias_ref[0:1, cols]
            ).astype(bf16)
        if (b + 1) * 128 % step == 0:
            part = pl.ds((b + 1) * 128 - step, step)
            copy = pltpu.make_async_copy(
                done_ref.at[part, :], out_ref.at[part, :], sems.at[len(copies)]
            )
            copy.start()
            copies.append(copy)
    for copy in copies:
        copy.wait()


TILE_AXES = ("row", "z", "core")


def spread(x, axes=TILE_AXES):
    count = lax.axis_size(axes)
    slot = x.reshape(count, x.shape[0] // count, 128)
    return lax.all_to_all(slot, axes, 0, 0).reshape(x.shape)


def swap(x, axis, pairs):
    return lax.ppermute(x, axis, [p for i, j in pairs for p in ((i, j), (j, i))])


def chain(axis, first):
    return [(i, i + 1) for i in range(first, lax.axis_size(axis) - 1, 2)]


def after(x, *others):
    return lax.optimization_barrier((x, *others))[0]


def shards(queries, keys, values, positions, conv_weight, norm_gain, norm_bias):
    q = queries.reshape(N, CH)
    k = keys.reshape(N, CH)
    v = values.reshape(N, CH)
    mb = 1 << 20
    wide = pltpu.VMEM((TILES * 8, 128), f32)
    packed, table = call(
        query_kernel,
        (far((TILES * 8, 128), bf16), far((2, TR + TC, 128), f32)),
        "hh",
        scratch=[
            pltpu.VMEM((N, CH), bf16),
            pltpu.VMEM((2, TC, TR), jnp.int32),
            pltpu.SemaphoreType.DMA((AGR + 1,)),
        ],
        nbytes=8 * mb,
        name="pool_queries",
    )(jnp.swapaxes(positions, 1, 2), q)
    agents = spread(packed)
    held_table = pltpu.VMEM((2, TR + TC, 128), f32)
    tk, *sends, inner, outer = call(
        key_kernel,
        (near((N, 128), bf16),)
        + (near((2 * N // PIECES, 128), bf16),) * PIECES
        + (far((TR, CH), bf16),) * 2,
        "h h",
        scratch=[held_table, pltpu.VMEM((N, CH), bf16), pltpu.SemaphoreType.DMA((AGR + 1,))],
        nbytes=4 * mb,
        name="turn_keys",
    )(table, values, k)
    got = [swap(send, "core", chain("core", 0)) for send in sends]
    inner = swap(inner, "core", chain("core", 0))
    outer = swap(outer, ("z", "core"), chain(("z", "core"), 1))
    parts = call(
        partial_kernel,
        far((2 * AGENTS, 128), bf16),
        " v " + " " * PIECES,
        scratch=[pltpu.VMEM((AGENTS, 2 * N), f32), wide],
        nbytes=10 * mb,
        name="partials",
    )(agents, tk, v, *got)
    parts, inner, outer = lax.optimization_barrier((parts, inner, outer))
    received = spread(parts, ("row", "z"))
    mate, rest = call(
        line_kernel,
        (near((TC + 16, CH), bf16),) * 2,
        "hvv",
        scratch=[pltpu.VMEM((TC, CH), bf16)] * 2 + [pltpu.SemaphoreType.DMA((2,))],
        nbytes=mb // 4,
        name="lines",
    )(values, inner, outer)
    prob = call(
        probability_kernel,
        near((N, LOCAL_HEADS * AGENTS), bf16),
        " hh",
        scratch=[
            wide,
            held_table,
            pltpu.VMEM((N, CH), bf16),
            pltpu.SemaphoreType.DMA((4,)),
        ],
        nbytes=20 * mb,
        name="probabilities",
    )(agents, table, q)
    received = after(received, mate, rest, prob)
    merged = call(merge_kernel, far((TILES * 8, 128), bf16), " ", nbytes=2 * mb, name="merge")(
        received
    )
    mate, rest, inner, outer, merged = lax.optimization_barrier(
        (mate, rest, inner, outer, merged)
    )
    mate = swap(mate, "row", chain("row", 0))
    rest = swap(rest, "row", chain("row", 1))
    agent_values = spread(merged)
    convolved = call(
        conv_kernel,
        (far((N, CH), f32),),
        "hvv ",
        scratch=[
            pltpu.VMEM((TR, TC, CH), bf16),
            pltpu.VMEM((TR, CH), f32),
            pltpu.VMEM((TR, CH), f32),
            pltpu.VMEM((N, CH), f32),
            pltpu.SemaphoreType.DMA((4,)),
        ],
        nbytes=8 * mb,
        out_spaces="h",
        name="conv",
    )(values, inner, outer, conv_weight)[0]
    summed, stats = call(
        attend_kernel,
        (near((N, CH), f32), near((2 * BLOCKS, 128), f32)),
        " vh   ",
        scratch=[pltpu.VMEM((N, CH), f32), pltpu.SemaphoreType.DMA((AGR,))],
        nbytes=4 * mb,
        name="attend",
    )(agent_values, prob, convolved, mate, rest, conv_weight)
    heads = lax.axis_size("head")
    others = [
        lax.ppermute(stats, "head", [(i, i ^ d) for i in range(heads)]) for d in range(1, heads)
    ]
    normed = call(
        norm_kernel,
        (shape((N, CH), bf16),),
        "v   v  ",
        scratch=[pltpu.VMEM((N, CH), bf16), pltpu.SemaphoreType.DMA((AGR,))],
        nbytes=4 * mb,
        out_spaces="h",
        name="norm",
    )(
        stats, *others, summed, norm_gain.reshape(1, CH), norm_bias.reshape(1, CH)
    )[0]
    return normed.reshape(TR, TC, CH)


def solution(mesh):
    rows, cols, heads = mesh.devices.shape
    cores = jax.sharding.Mesh(
        mesh.devices.reshape(rows, cols // 2, 2, heads), ("row", "z", "core", "head")
    )
    tile = P("row", ("z", "core"), "head")
    in_specs = (tile,) * 3 + (
        P(None, "row", ("z", "core")),
        P(None, "head"),
        P("head"),
        P("head"),
    )
    return jax.shard_map(shards, mesh=cores, in_specs=in_specs, out_specs=tile, check_vma=False)
```

```python
import math

import jax
import jax.numpy as jnp
from jax import lax
from jax.experimental import pallas as pl
from jax.experimental.pallas import tpu as pltpu
from jax.sharding import PartitionSpec as P

HD = 64
D = 1024
AGR = 4
TR = 48
TC = 32
CH = 256
N = TR * TC
AGENTS = 256
TILES = 64
LOCAL_HEADS = 4
PEERS = TILES // 2
PIECES = 4
BLOCKS = N // 128

f32 = jnp.float32
bf16 = jnp.bfloat16
epsilon = 1e-05

VMEM_SPEC = pl.BlockSpec(memory_space=pltpu.VMEM)
HBM_SPEC = pl.BlockSpec(memory_space=pltpu.HBM)


def call(kernel, outs, in_spaces, scratch=(), nbytes=0, name=None, out_spaces=None):
    fn = pl.pallas_call(
        kernel,
        out_shape=outs,
        in_specs=[HBM_SPEC if c == "h" else VMEM_SPEC for c in in_spaces],
        out_specs=(
            tuple(HBM_SPEC if c == "h" else VMEM_SPEC for c in out_spaces or " " * len(outs))
            if isinstance(outs, tuple)
            else VMEM_SPEC
        ),
        scratch_shapes=list(scratch),
        compiler_params=pltpu.CompilerParams(vmem_limit_bytes=20 * 1024 * 1024),
        cost_estimate=pl.CostEstimate(flops=0, bytes_accessed=nbytes, transcendentals=0),
        name=name,
    )

    def run(*args):
        spaces = {"h": pltpu.HBM, "v": pltpu.VMEM}
        return fn(
            *[
                pltpu.with_memory_space_constraint(x, spaces[c]) if c in spaces else x
                for x, c in zip(args, in_spaces, strict=True)
            ]
        )

    return run


def shape(dims, dtype):
    return jax.ShapeDtypeStruct(dims, dtype)


def near(dims, dtype):
    return pltpu.VMEM(dims, dtype)


def far(dims, dtype):
    return pltpu.HBM(dims, dtype)


def lanes(dims):
    return lax.broadcasted_iota(jnp.int32, dims, len(dims) - 1)


def turn_matrix():
    source = lax.broadcasted_iota(jnp.int32, (CH, CH), 0)
    target = lax.broadcasted_iota(jnp.int32, (CH, CH), 1)
    low = (target & 31) < 16
    minus = jnp.where(low & (source == target + 16), -1.0, 0.0)
    plus = jnp.where((~low) & (source == target - 16), 1.0, 0.0)
    return (minus + plus).astype(bf16)


def sin_cos(angle):
    return jnp.sin(angle), jnp.cos(angle)


def turned(x, matrix, cosine, sine):
    swapped = jnp.dot(x, matrix, preferred_element_type=f32)
    return (x.astype(f32) * cosine + swapped * sine).astype(bf16)


def split_tables(cosines, sines):
    cosines = jnp.concatenate([cosines, cosines], axis=1)
    sines = jnp.concatenate([sines, sines], axis=1)
    return cosines[:TR], sines[:TR], cosines[TR:], sines[TR:]


def cell_tables(tables, first, rows):
    cos_r, sin_r, cos_c, sin_c = tables
    cosine = jnp.concatenate(
        [cos_r[first + i : first + i + 1, :] * cos_c for i in range(rows)], axis=0
    )
    sine = jnp.concatenate(
        [sin_r[first + i : first + i + 1, :] + sin_c for i in range(rows)], axis=0
    )
    return cosine, sine


def slots(block):
    twice = jnp.concatenate([block, block], axis=0).astype(bf16)
    return jnp.broadcast_to(twice[None], (TILES // 2, 16, 128)).reshape(TILES * 8, 128)


def query_kernel(
    pos_ref,
    q_ref,
    agents_ref,
    tab_ref,
    held_ref,
    spot_ref,
    sems,
):
    step = N // AGR
    place = pltpu.make_async_copy(pos_ref, spot_ref, sems.at[AGR])
    place.start()
    copies = []
    for cell in range(AGR):
        part = pl.ds(cell * step, step)
        copy = pltpu.make_async_copy(q_ref.at[part, :], held_ref.at[part, :], sems.at[cell])
        copy.start()
        copies.append(copy)
    lane = lanes((1, 128)) % HD
    power = jnp.exp((lane % 16).astype(f32) * f32(-math.log(100.0) / 16))
    freq_r = jnp.where(lane < 32, power, 0.0)
    freq_c = jnp.where(lane < 32, 0.0, power)
    place.wait()
    row_line = spot_ref[0][0:1, :].astype(f32)
    col_pos = spot_ref[1][:, 0:1].astype(f32)
    eye = lax.broadcasted_iota(jnp.int32, (TR, TR), 0) == lax.broadcasted_iota(
        jnp.int32, (TR, TR), 1
    )
    row_pos = jnp.sum(jnp.where(eye, jnp.broadcast_to(row_line, (TR, TR)), 0.0), 1, keepdims=True)
    angles = jnp.concatenate([row_pos * freq_r, col_pos * freq_c], axis=0)
    sines, cosines = sin_cos(angles)
    tab_ref[0] = cosines
    tab_ref[1] = sines
    cos_r, sin_r, cos_c, sin_c = split_tables(cosines, sines)
    place_in = lanes((1, CH)) % (HD // 2)
    by_row = lanes((1, CH)) % HD < HD // 2
    means = []
    for cell in range(AGR):
        copies[cell].wait()
        columns = jnp.zeros((TC, CH), f32)
        row_cos = jnp.zeros((8, CH), f32)
        row_sin = jnp.zeros((8, CH), f32)
        for i in range(cell * (TR // AGR), (cell + 1) * (TR // AGR)):
            x = held_ref[pl.ds(i * TC, TC), :].astype(f32)
            columns = columns + x
            x = x[:8] + x[8:16] + x[16:24] + x[24:]
            row_cos = row_cos + x * cos_r[i : i + 1]
            row_sin = row_sin + x * sin_r[i : i + 1]
        col_cos = jnp.sum(columns * cos_c, 0, keepdims=True)
        col_sin = jnp.sum(columns * sin_c, 0, keepdims=True)
        straight = jnp.where(by_row, jnp.sum(row_cos, 0, keepdims=True), col_cos)
        crossed = jnp.where(by_row, jnp.sum(row_sin, 0, keepdims=True), col_sin)
        crossed = jnp.where(
            place_in < HD // 4, -pltpu.roll(crossed, CH - HD // 4, 1), pltpu.roll(crossed, HD // 4, 1)
        )
        mean = (straight + crossed) / step
        means.append(mean.astype(bf16).astype(f32))
    packed = jnp.concatenate([m[:, :128] for m in means] + [m[:, 128:] for m in means], axis=0)
    agents_ref[...] = slots(packed)


def even_core():
    return lax.axis_index("core") == 0


def even_row():
    return lax.rem(lax.axis_index("row"), 2) == 0


def key_kernel(
    tab_hbm_ref,
    v_ref,
    k_ref,
    tk_ref,
    *refs,
):
    sends, (near_ref, far_ref, tab_ref, held_ref, sems) = refs[:PIECES], refs[PIECES:]
    step = N // AGR
    table = pltpu.make_async_copy(tab_hbm_ref, tab_ref, sems.at[AGR])
    table.start()
    copies = []
    for cell in range(AGR):
        part = pl.ds(cell * step, step)
        copies.append(
            pltpu.make_async_copy(k_ref.at[part, :], held_ref.at[part, :], sems.at[cell])
        )
        copies[cell].start()
    first, last = v_ref[:, 0, :], v_ref[:, TC - 1, :]
    even = even_core()
    near_ref[...] = jnp.where(even, last, first)
    far_ref[...] = jnp.where(even, first, last)
    other = jnp.where(even, v_ref[:, :, 128:], v_ref[:, :, :128])
    other = other.reshape(N, 128)
    size = 2 * N // PIECES
    for i in range(PIECES // 2):
        sends[PIECES // 2 + i][...] = other[i * size : (i + 1) * size]
    matrix = turn_matrix()
    table.wait()
    tables = split_tables(tab_ref[0], tab_ref[1])
    for cell in range(AGR):
        part = pl.ds(cell * step, step)
        cosine, sine = cell_tables(tables, cell * (TR // AGR), TR // AGR)
        copies[cell].wait()
        keys = turned(held_ref[part, :], matrix, cosine, sine)
        tk_ref[part, :] = jnp.where(even, keys[:, :128], keys[:, 128:])
        keys = jnp.where(even, keys[:, 128:], keys[:, :128])
        span = math.gcd(size, step)
        for at in range(0, step, span):
            to = cell * step + at
            sends[to // size][pl.ds(to % size, span), :] = keys[at : at + span]


def agent_pairs(agents_ref, wide_ref, scale):
    wide_ref[...] = agents_ref[...].astype(f32) * scale
    pairs = []
    for pair in range(2):
        parts = [wide_ref[pl.ds(4 * pair + k, TILES, stride=8), :] for k in range(AGR)]
        pairs.append(jnp.concatenate(parts, axis=0).astype(bf16))
    return pairs


def half_mask(dims, parity):
    return (lanes(dims) // HD) == parity


def partial_kernel(agents_ref, tk_ref, v_ref, *refs):
    got, (out_ref, score_ref, wide_ref) = refs[:PIECES], refs[PIECES:]
    size = 2 * N // PIECES
    pairs = agent_pairs(agents_ref, wide_ref, 1.0 / math.sqrt(HD))
    mine = jnp.where(even_core(), pairs[0], pairs[1])
    offset = pl.multiple_of(lax.axis_index("core") * 128, 128)
    chunk = 512 if size % 512 == 0 else 384

    def part(c, which):
        at = c * chunk % N
        if c * chunk >= N:
            at = at + which * N
            return got[at // size][pl.ds(at % size, chunk), :]
        if which == 0:
            return tk_ref[pl.ds(at, chunk), :]
        return v_ref[pl.ds(at, chunk), pl.ds(offset, 128)]

    for parity in range(2):
        own = mine
        own = jnp.where(half_mask(own.shape, parity), own, jnp.zeros_like(own))
        peak = None
        for c in range(2 * N // chunk):
            scores = lax.dot_general(
                own,
                part(c, 0),
                (((1,), (1,)), ((), ())),
                preferred_element_type=f32,
            )
            score_ref[:, pl.ds(c * chunk, chunk)] = scores
            for s in range(chunk // 128):
                piece = scores[:, s * 128 : (s + 1) * 128]
                peak = piece if peak is None else jnp.maximum(peak, piece)
        peak = jnp.max(peak, 1, keepdims=True)
        acc = jnp.zeros((AGENTS, 128), f32)
        for c in range(2 * N // chunk):
            weights = jnp.exp(score_ref[:, pl.ds(c * chunk, chunk)] - peak).astype(bf16)
            block = part(c, 1)
            block = jnp.where(half_mask(block.shape, parity), block, jnp.ones_like(block))
            acc = acc + jnp.dot(weights, block, preferred_element_type=f32)
        other = pltpu.roll(acc, HD, 1)
        numer, total = (acc, other) if parity == 0 else (other, acc)
        logs = peak + jnp.log(total)
        values = numer / total
        logs = jnp.max(jnp.where(half_mask(logs.shape, 0), logs, -3e38), 1, keepdims=True)
        first = logs.astype(bf16).astype(f32)
        second = (logs - first).astype(bf16).astype(f32)
        third = logs - first - second
        lane = lanes((AGENTS, 128))
        packed = jnp.where(
            lane < HD,
            values,
            jnp.where(
                lane == HD,
                first,
                jnp.where(lane == HD + 1, second, jnp.where(lane == HD + 2, third, 0.0)),
            ),
        )
        groups = packed.reshape(2, AGENTS // 16, 8, 128)
        groups = jnp.concatenate([groups[0], groups[1]], 1).reshape(AGENTS, 128)
        out_ref[pl.ds(parity * AGENTS, AGENTS), :] = groups.astype(bf16)


def merge_kernel(parts_ref, out_ref):
    source = lax.broadcasted_iota(jnp.int32, (128, 128), 0)
    picker = jnp.where((source >= HD) & (source < HD + 3), 1.0, 0.0).astype(bf16)
    parts = parts_ref[...]
    logs = jnp.dot(parts, picker, preferred_element_type=f32).reshape(PEERS, 16, 128)
    values = parts.astype(f32).reshape(PEERS, 16, 128)
    peak = jnp.max(logs, 0)
    weights = jnp.exp(logs - peak[None])
    merged = jnp.sum(weights * values, 0) / jnp.sum(weights, 0)
    merged = jnp.where(lanes((8, 128)) < HD, merged[:8], pltpu.roll(merged[8:], HD, 1))
    out_ref[...] = slots(merged)


def probabilities(pairs, tab_ref, table, held_ref, fetches, prob_ref):
    chunk = N // len(fetches)
    matrix = turn_matrix()
    table.wait()
    ones = jnp.ones((AGENTS, 128), bf16)
    owns = []
    for head in range(LOCAL_HEADS):
        own = pairs[head // 2]
        owns.append(jnp.where(half_mask(own.shape, head % 2), own, jnp.zeros_like(own)))
    tables = split_tables(tab_ref[0], tab_ref[1])
    for c, fetch in enumerate(fetches):
        rows = pl.ds(c * chunk, chunk)
        cosine, sine = cell_tables(tables, c * (chunk // TC), chunk // TC)
        fetch.wait()
        queries = turned(held_ref[rows, :], matrix, cosine, sine)
        for head in range(LOCAL_HEADS):
            scores = lax.dot_general(
                queries[:, head // 2 * 128 : head // 2 * 128 + 128],
                owns[head],
                (((1,), (1,)), ((), ())),
                preferred_element_type=f32,
            )
            weights = jnp.exp(scores - jnp.max(scores, 1, keepdims=True))
            total = jnp.dot(weights.astype(bf16), ones, preferred_element_type=f32)
            scale = 1.0 / total
            scale = jnp.concatenate([scale, scale], axis=1)
            prob_ref[rows, pl.ds(head * AGENTS, AGENTS)] = (weights * scale).astype(bf16)


def probability_kernel(
    agents_ref,
    tab_hbm_ref,
    q_ref,
    v_ref,
    near_ref,
    far_ref,
    prob_ref,
    mate_ref,
    rest_ref,
    wide_ref,
    tab_ref,
    held_ref,
    top_ref,
    bottom_ref,
    sems,
):
    table = pltpu.make_async_copy(tab_hbm_ref, tab_ref, sems.at[3])
    table.start()
    fetches = []
    for c in range(3):
        part = pl.ds(c * (N // 3), N // 3)
        fetches.append(pltpu.make_async_copy(q_ref.at[part, :], held_ref.at[part, :], sems.at[c]))
        fetches[c].start()
    edges = [
        pltpu.make_async_copy(v_ref.at[0], top_ref, sems.at[4]),
        pltpu.make_async_copy(v_ref.at[TR - 1], bottom_ref, sems.at[5]),
    ]
    for copy in edges:
        copy.start()
    pairs = agent_pairs(agents_ref, wide_ref, 1.0 / math.sqrt(HD))
    probabilities(pairs, tab_ref, table, held_ref, fetches, prob_ref)
    for copy in edges:
        copy.wait()
    lines = []
    for row, line_ref in ((0, top_ref), (TR - 1, bottom_ref)):
        mate = near_ref[row : row + 1, :].astype(f32)
        rest = far_ref[row : row + 1, :].astype(f32)
        left = jnp.where(even_core(), rest, mate)
        right = jnp.where(even_core(), mate, rest)
        tail = jnp.concatenate([left, right, jnp.zeros((14, CH), f32)], axis=0)
        lines.append(jnp.concatenate([line_ref[...].astype(f32), tail], axis=0))
    mate_ref[...] = jnp.where(even_row(), lines[1], lines[0]).astype(bf16)
    rest_ref[...] = jnp.where(even_row(), lines[0], lines[1]).astype(bf16)


def shifted(row, left, right):
    column = lax.broadcasted_iota(jnp.int32, row.shape, 0)
    before = jnp.where(column == 0, left, pltpu.roll(row, 1, 0))
    behind = jnp.where(column == TC - 1, right, pltpu.roll(row, TC - 1, 0))
    return before, row, behind


def conv_kernel(
    v_hbm_ref, near_ref, far_ref, w_ref, out_hbm_ref, v_ref, l_ref, r_ref, out_ref, sems
):
    fetches, outs = [], []
    for half in range(2):
        cols = pl.ds(half * 128, 128)
        fetches.append(
            pltpu.make_async_copy(v_hbm_ref.at[:, :, cols], v_ref.at[:, :, cols], sems.at[half])
        )
        fetches[half].start()
        outs.append(
            pltpu.make_async_copy(
                out_ref.at[:, cols], out_hbm_ref.at[:, cols], sems.at[2 + half]
            )
        )
    mate, rest = near_ref[...].astype(f32), far_ref[...].astype(f32)
    l_ref[...] = jnp.where(even_core(), rest, mate)
    r_ref[...] = jnp.where(even_core(), mate, rest)
    for half in range(2):
        cols = pl.ds(half * 128, 128)
        w = [jnp.broadcast_to(w_ref[t : t + 1, cols], (TC, 128)) for t in range(9)]

        def group(start, carry):
            a, b = carry
            lefts, rights = l_ref[pl.ds(start, 8), cols], r_ref[pl.ds(start, 8), cols]
            for k in range(8):
                row = v_ref[start + k, :, cols].astype(f32)
                x = shifted(row, lefts[k : k + 1], rights[k : k + 1])
                t = [sum(x[e] * w[3 * d + e] for e in range(3)) for d in range(3)]
                if a is not None:
                    at = (start + k - 1) * TC
                    if not isinstance(at, int):
                        at = pl.multiple_of(at, TC)
                    out_ref[pl.ds(at, TC), cols] = a + t[2]
                    b = b + t[1]
                else:
                    b = t[1]
                a, b = b, t[0]
            return a, b

        fetches[half].wait()
        carry = group(0, (None, None))
        a, b = lax.fori_loop(1, TR // 8, lambda g, c: group(pl.multiple_of(g * 8, 8), c), carry)
        out_ref[pl.ds((TR - 1) * TC, TC), cols] = a
        outs[half].start()
    for copy in outs:
        copy.wait()


def attend_kernel(
    av_ref,
    prob_ref,
    conv_hbm_ref,
    mate_ref,
    rest_ref,
    w_ref,
    sum_ref,
    stat_ref,
    conv_ref,
    sems,
):
    step = N // AGR
    copies = []
    for c in range(AGR):
        part = pl.ds(c * step, step)
        copies.append(
            pltpu.make_async_copy(conv_hbm_ref.at[part, :], conv_ref.at[part, :], sems.at[c])
        )
        copies[c].start()
    eye = lax.broadcasted_iota(jnp.int32, (128, 128), 0) == lanes((128, 128))
    av = av_ref[...].astype(f32).reshape(2, AGENTS // 16, 2, 8, 128)
    for pair in range(2):
        pieces = []
        for parity in range(2):
            part = av[parity, :, pair].reshape(128, 128)
            other = pltpu.roll(part, HD, 1)
            own = half_mask(part.shape, parity)
            for piece in (part, other) if parity == 0 else (other, part):
                pieces.append(jnp.where(own, piece, 0.0))
        agent_values = jnp.concatenate(pieces, axis=0).astype(bf16)
        for b in range(N // 512):
            rows = pl.ds(b * 512, 512)
            sum_ref[rows, pl.ds(pair * 128, 128)] = jnp.dot(
                prob_ref[rows, pl.ds(pair * 2 * AGENTS, 2 * AGENTS)],
                agent_values,
                preferred_element_type=f32,
            )
    mate, rest = mate_ref[...].astype(f32), rest_ref[...].astype(f32)
    above = jnp.where(even_row(), rest, mate)
    below = jnp.where(even_row(), mate, rest)
    for line, tap, at in ((above, 0, 0), (below, 6, N - TC)):
        x = shifted(line[:TC], line[TC : TC + 1], line[TC + 1 : TC + 2])
        total = sum(x[e] * w_ref[tap + e : tap + e + 1, :] for e in range(3))
        sum_ref[pl.ds(at, TC), :] = sum_ref[pl.ds(at, TC), :] + total
    for b in range(BLOCKS):
        if b * 128 % step == 0:
            copies[b * 128 // step].wait()
        rows = pl.ds(b * 128, 128)
        x = sum_ref[rows, :] + conv_ref[rows, :]
        sum_ref[rows, :] = x
        mean = jnp.sum(x[:, :128] + x[:, 128:], 1, keepdims=True) * (1.0 / CH)
        x = x - mean
        x = x * x
        squares = jnp.sum(x[:, :128] + x[:, 128:], 1, keepdims=True)
        stat_ref[b : b + 1, :] = jnp.sum(jnp.where(eye, mean, 0.0), 0, keepdims=True)
        stat_ref[BLOCKS + b : BLOCKS + b + 1, :] = jnp.sum(
            jnp.where(eye, squares, 0.0), 0, keepdims=True
        )


def norm_kernel(s0_ref, s1_ref, s2_ref, s3_ref, sum_ref, gain_ref, bias_ref, out_ref, done_ref, sems):
    stats = [s[...] for s in (s0_ref, s1_ref, s2_ref, s3_ref)]
    means = [s[:BLOCKS] for s in stats]
    mean = (means[0] + means[1] + means[2] + means[3]) * 0.25
    squares = sum(s[BLOCKS:] for s in stats)
    for m in means:
        squares = squares + CH * (m - mean) * (m - mean)
    scale = lax.rsqrt(squares * (1.0 / D) + epsilon)
    step = N // AGR
    copies = []
    for b in range(BLOCKS):
        rows = pl.ds(b * 128, 128)
        m = jnp.broadcast_to(mean[b : b + 1], (128, 128)).T
        s = jnp.broadcast_to(scale[b : b + 1], (128, 128)).T
        for half in range(2):
            cols = pl.ds(half * 128, 128)
            done_ref[rows, cols] = (
                (sum_ref[rows, cols] - m) * s * gain_ref[0:1, cols] + bias_ref[0:1, cols]
            ).astype(bf16)
        if (b + 1) * 128 % step == 0:
            part = pl.ds((b + 1) * 128 - step, step)
            copy = pltpu.make_async_copy(
                done_ref.at[part, :], out_ref.at[part, :], sems.at[len(copies)]
            )
            copy.start()
            copies.append(copy)
    for copy in copies:
        copy.wait()


TILE_AXES = ("row", "z", "core")


def spread(x, axes=TILE_AXES):
    count = lax.axis_size(axes)
    slot = x.reshape(count, x.shape[0] // count, 128)
    return lax.all_to_all(slot, axes, 0, 0).reshape(x.shape)


def swap(x, axis, pairs):
    return lax.ppermute(x, axis, [p for i, j in pairs for p in ((i, j), (j, i))])


def chain(axis, first):
    return [(i, i + 1) for i in range(first, lax.axis_size(axis) - 1, 2)]


def after(x, *others):
    return lax.optimization_barrier((x, *others))[0]


def shards(queries, keys, values, positions, conv_weight, norm_gain, norm_bias):
    q = queries.reshape(N, CH)
    k = keys.reshape(N, CH)
    v = values.reshape(N, CH)
    mb = 1 << 20
    wide = pltpu.VMEM((TILES * 8, 128), f32)
    packed, table = call(
        query_kernel,
        (far((TILES * 8, 128), bf16), far((2, TR + TC, 128), f32)),
        "hh",
        scratch=[
            pltpu.VMEM((N, CH), bf16),
            pltpu.VMEM((2, TC, TR), jnp.int32),
            pltpu.SemaphoreType.DMA((AGR + 1,)),
        ],
        nbytes=8 * mb,
        name="pool_queries",
    )(jnp.swapaxes(positions, 1, 2), q)
    agents = spread(packed)
    held_table = pltpu.VMEM((2, TR + TC, 128), f32)
    tk, *sends, inner, outer = call(
        key_kernel,
        (near((N, 128), bf16),)
        + (near((2 * N // PIECES, 128), bf16),) * PIECES
        + (far((TR, CH), bf16),) * 2,
        "h h",
        scratch=[held_table, pltpu.VMEM((N, CH), bf16), pltpu.SemaphoreType.DMA((AGR + 1,))],
        nbytes=4 * mb,
        name="turn_keys",
    )(table, values, k)
    got = [swap(send, "core", chain("core", 0)) for send in sends]
    inner = swap(inner, "core", chain("core", 0))
    outer = swap(outer, ("z", "core"), chain(("z", "core"), 1))
    parts = call(
        partial_kernel,
        far((2 * AGENTS, 128), bf16),
        " v " + " " * PIECES,
        scratch=[pltpu.VMEM((AGENTS, 2 * N), f32), wide],
        nbytes=10 * mb,
        name="partials",
    )(agents, tk, v, *got)
    parts, inner, outer = lax.optimization_barrier((parts, inner, outer))
    received = spread(parts, ("row", "z"))
    prob, mate, rest = call(
        probability_kernel,
        (near((N, LOCAL_HEADS * AGENTS), bf16),) + (near((TC + 16, CH), bf16),) * 2,
        " hhhvv",
        scratch=[wide, held_table, pltpu.VMEM((N, CH), bf16)]
        + [pltpu.VMEM((TC, CH), bf16)] * 2
        + [pltpu.SemaphoreType.DMA((6,))],
        nbytes=20 * mb,
        name="probabilities",
    )(agents, table, q, values, inner, outer)
    received = after(received, mate, rest, prob)
    merged = call(merge_kernel, far((TILES * 8, 128), bf16), " ", nbytes=2 * mb, name="merge")(
        received
    )
    mate, rest, inner, outer, merged = lax.optimization_barrier(
        (mate, rest, inner, outer, merged)
    )
    mate = swap(mate, "row", chain("row", 0))
    rest = swap(rest, "row", chain("row", 1))
    agent_values = spread(merged)
    convolved = call(
        conv_kernel,
        (far((N, CH), f32),),
        "hvv ",
        scratch=[
            pltpu.VMEM((TR, TC, CH), bf16),
            pltpu.VMEM((TR, CH), f32),
            pltpu.VMEM((TR, CH), f32),
            pltpu.VMEM((N, CH), f32),
            pltpu.SemaphoreType.DMA((4,)),
        ],
        nbytes=8 * mb,
        out_spaces="h",
        name="conv",
    )(values, inner, outer, conv_weight)[0]
    summed, stats = call(
        attend_kernel,
        (near((N, CH), f32), near((2 * BLOCKS, 128), f32)),
        " vh   ",
        scratch=[pltpu.VMEM((N, CH), f32), pltpu.SemaphoreType.DMA((AGR,))],
        nbytes=4 * mb,
        name="attend",
    )(agent_values, prob, convolved, mate, rest, conv_weight)
    heads = lax.axis_size("head")
    others = [
        lax.ppermute(stats, "head", [(i, i ^ d) for i in range(heads)]) for d in range(1, heads)
    ]
    normed = call(
        norm_kernel,
        (shape((N, CH), bf16),),
        "v   v  ",
        scratch=[pltpu.VMEM((N, CH), bf16), pltpu.SemaphoreType.DMA((AGR,))],
        nbytes=4 * mb,
        out_spaces="h",
        name="norm",
    )(
        stats, *others, summed, norm_gain.reshape(1, CH), norm_bias.reshape(1, CH)
    )[0]
    return normed.reshape(TR, TC, CH)


def solution(mesh):
    rows, cols, heads = mesh.devices.shape
    cores = jax.sharding.Mesh(
        mesh.devices.reshape(rows, cols // 2, 2, heads), ("row", "z", "core", "head")
    )
    tile = P("row", ("z", "core"), "head")
    in_specs = (tile,) * 3 + (
        P(None, "row", ("z", "core")),
        P(None, "head"),
        P("head"),
        P("head"),
    )
    return jax.shard_map(shards, mesh=cores, in_specs=in_specs, out_specs=tile, check_vma=False)
```

```python
import math

import jax
import jax.numpy as jnp
from jax import lax
from jax.experimental import pallas as pl
from jax.experimental.pallas import tpu as pltpu
from jax.sharding import PartitionSpec as P

HD = 64
D = 1024
AGR = 4
TR = 48
TC = 32
CH = 256
N = TR * TC
AGENTS = 256
TILES = 64
LOCAL_HEADS = 4
PEERS = TILES // 2
PIECES = 4
BLOCKS = N // 128

f32 = jnp.float32
bf16 = jnp.bfloat16
epsilon = 1e-05

VMEM_SPEC = pl.BlockSpec(memory_space=pltpu.VMEM)
HBM_SPEC = pl.BlockSpec(memory_space=pltpu.HBM)


def call(kernel, outs, in_spaces, scratch=(), nbytes=0, name=None, out_spaces=None):
    fn = pl.pallas_call(
        kernel,
        out_shape=outs,
        in_specs=[HBM_SPEC if c == "h" else VMEM_SPEC for c in in_spaces],
        out_specs=(
            tuple(HBM_SPEC if c == "h" else VMEM_SPEC for c in out_spaces or " " * len(outs))
            if isinstance(outs, tuple)
            else VMEM_SPEC
        ),
        scratch_shapes=list(scratch),
        compiler_params=pltpu.CompilerParams(vmem_limit_bytes=20 * 1024 * 1024),
        cost_estimate=pl.CostEstimate(flops=0, bytes_accessed=nbytes, transcendentals=0),
        name=name,
    )

    def run(*args):
        spaces = {"h": pltpu.HBM, "v": pltpu.VMEM}
        return fn(
            *[
                pltpu.with_memory_space_constraint(x, spaces[c]) if c in spaces else x
                for x, c in zip(args, in_spaces, strict=True)
            ]
        )

    return run


def shape(dims, dtype):
    return jax.ShapeDtypeStruct(dims, dtype)


def near(dims, dtype):
    return pltpu.VMEM(dims, dtype)


def far(dims, dtype):
    return pltpu.HBM(dims, dtype)


def lanes(dims):
    return lax.broadcasted_iota(jnp.int32, dims, len(dims) - 1)


def turn_matrix():
    source = lax.broadcasted_iota(jnp.int32, (CH, CH), 0)
    target = lax.broadcasted_iota(jnp.int32, (CH, CH), 1)
    low = (target & 31) < 16
    minus = jnp.where(low & (source == target + 16), -1.0, 0.0)
    plus = jnp.where((~low) & (source == target - 16), 1.0, 0.0)
    return (minus + plus).astype(bf16)


def sin_cos(angle):
    return jnp.sin(angle), jnp.cos(angle)


def turned(x, matrix, cosine, sine):
    swapped = jnp.dot(x, matrix, preferred_element_type=f32)
    return (x.astype(f32) * cosine + swapped * sine).astype(bf16)


def split_tables(cosines, sines):
    cosines = jnp.concatenate([cosines, cosines], axis=1)
    sines = jnp.concatenate([sines, sines], axis=1)
    return cosines[:TR], sines[:TR], cosines[TR:], sines[TR:]


def cell_tables(tables, first, rows):
    cos_r, sin_r, cos_c, sin_c = tables
    cosine = jnp.concatenate(
        [cos_r[first + i : first + i + 1, :] * cos_c for i in range(rows)], axis=0
    )
    sine = jnp.concatenate(
        [sin_r[first + i : first + i + 1, :] + sin_c for i in range(rows)], axis=0
    )
    return cosine, sine


def slots(block):
    twice = jnp.concatenate([block, block], axis=0).astype(bf16)
    return jnp.broadcast_to(twice[None], (TILES // 2, 16, 128)).reshape(TILES * 8, 128)


def query_kernel(
    pos_ref,
    q_ref,
    agents_ref,
    tab_ref,
    held_ref,
    spot_ref,
    sems,
):
    step = N // AGR
    place = pltpu.make_async_copy(pos_ref, spot_ref, sems.at[AGR])
    place.start()
    copies = []
    for cell in range(AGR):
        part = pl.ds(cell * step, step)
        copy = pltpu.make_async_copy(q_ref.at[part, :], held_ref.at[part, :], sems.at[cell])
        copy.start()
        copies.append(copy)
    lane = lanes((1, 128)) % HD
    power = jnp.exp((lane % 16).astype(f32) * f32(-math.log(100.0) / 16))
    freq_r = jnp.where(lane < 32, power, 0.0)
    freq_c = jnp.where(lane < 32, 0.0, power)
    place.wait()
    row_line = spot_ref[0][0:1, :].astype(f32)
    col_pos = spot_ref[1][:, 0:1].astype(f32)
    eye = lax.broadcasted_iota(jnp.int32, (TR, TR), 0) == lax.broadcasted_iota(
        jnp.int32, (TR, TR), 1
    )
    row_pos = jnp.sum(jnp.where(eye, jnp.broadcast_to(row_line, (TR, TR)), 0.0), 1, keepdims=True)
    angles = jnp.concatenate([row_pos * freq_r, col_pos * freq_c], axis=0)
    sines, cosines = sin_cos(angles)
    tab_ref[0] = cosines
    tab_ref[1] = sines
    cos_r, sin_r, cos_c, sin_c = split_tables(cosines, sines)
    place_in = lanes((1, CH)) % (HD // 2)
    by_row = lanes((1, CH)) % HD < HD // 2
    means = []
    for cell in range(AGR):
        copies[cell].wait()
        columns = jnp.zeros((TC, CH), f32)
        row_cos = jnp.zeros((8, CH), f32)
        row_sin = jnp.zeros((8, CH), f32)
        for i in range(cell * (TR // AGR), (cell + 1) * (TR // AGR)):
            x = held_ref[pl.ds(i * TC, TC), :].astype(f32)
            columns = columns + x
            x = x[:8] + x[8:16] + x[16:24] + x[24:]
            row_cos = row_cos + x * cos_r[i : i + 1]
            row_sin = row_sin + x * sin_r[i : i + 1]
        col_cos = jnp.sum(columns * cos_c, 0, keepdims=True)
        col_sin = jnp.sum(columns * sin_c, 0, keepdims=True)
        straight = jnp.where(by_row, jnp.sum(row_cos, 0, keepdims=True), col_cos)
        crossed = jnp.where(by_row, jnp.sum(row_sin, 0, keepdims=True), col_sin)
        crossed = jnp.where(
            place_in < HD // 4, -pltpu.roll(crossed, CH - HD // 4, 1), pltpu.roll(crossed, HD // 4, 1)
        )
        mean = (straight + crossed) / step
        means.append(mean.astype(bf16).astype(f32))
    packed = jnp.concatenate([m[:, :128] for m in means] + [m[:, 128:] for m in means], axis=0)
    agents_ref[...] = slots(packed)


def even_core():
    return lax.axis_index("core") == 0


def even_row():
    return lax.rem(lax.axis_index("row"), 2) == 0


def key_kernel(
    tab_hbm_ref,
    v_ref,
    flat_ref,
    k_ref,
    tk_ref,
    *refs,
):
    sends, (near_ref, far_ref, tab_ref, held_ref, sems) = refs[:PIECES], refs[PIECES:]
    step = N // AGR
    size = 2 * N // PIECES
    half = PIECES // 2
    offset = pl.multiple_of((1 - lax.axis_index("core")) * 128, 128)
    table = pltpu.make_async_copy(tab_hbm_ref, tab_ref, sems.at[0])
    table.start()
    whole = pltpu.make_async_copy(v_ref, held_ref, sems.at[1])
    whole.start()
    copies = []
    for i in range(half):
        source = flat_ref.at[pl.ds(i * size, size), pl.ds(offset, 128)]
        copies.append(pltpu.make_async_copy(source, sends[half + i], sems.at[2 + i]))
        copies[i].start()
    even = even_core()
    matrix = turn_matrix()
    table.wait()
    tables = split_tables(tab_ref[0], tab_ref[1])
    for cell in range(AGR):
        part = pl.ds(cell * step, step)
        cosine, sine = cell_tables(tables, cell * (TR // AGR), TR // AGR)
        keys = turned(k_ref[part, :], matrix, cosine, sine)
        tk_ref[part, :] = jnp.where(even, keys[:, :128], keys[:, 128:])
        keys = jnp.where(even, keys[:, 128:], keys[:, :128])
        span = math.gcd(size, step)
        for at in range(0, step, span):
            to = cell * step + at
            sends[to // size][pl.ds(to % size, span), :] = keys[at : at + span]
    whole.wait()
    first, last = held_ref[:, 0, :], held_ref[:, TC - 1, :]
    near_ref[...] = jnp.where(even, last, first)
    far_ref[...] = jnp.where(even, first, last)
    for copy in copies:
        copy.wait()


def agent_pairs(agents_ref, wide_ref, scale):
    wide_ref[...] = agents_ref[...].astype(f32) * scale
    pairs = []
    for pair in range(2):
        parts = [wide_ref[pl.ds(4 * pair + k, TILES, stride=8), :] for k in range(AGR)]
        pairs.append(jnp.concatenate(parts, axis=0).astype(bf16))
    return pairs


def half_mask(dims, parity):
    return (lanes(dims) // HD) == parity


def partial_kernel(agents_ref, tk_ref, v_ref, *refs):
    got, (out_ref, score_ref, wide_ref) = refs[:PIECES], refs[PIECES:]
    size = 2 * N // PIECES
    pairs = agent_pairs(agents_ref, wide_ref, 1.0 / math.sqrt(HD))
    mine = jnp.where(even_core(), pairs[0], pairs[1])
    offset = pl.multiple_of(lax.axis_index("core") * 128, 128)
    chunk = 512 if size % 512 == 0 else 384

    def part(c, which):
        at = c * chunk % N
        if c * chunk >= N:
            at = at + which * N
            return got[at // size][pl.ds(at % size, chunk), :]
        if which == 0:
            return tk_ref[pl.ds(at, chunk), :]
        return v_ref[pl.ds(at, chunk), pl.ds(offset, 128)]

    for parity in range(2):
        own = mine
        own = jnp.where(half_mask(own.shape, parity), own, jnp.zeros_like(own))
        peak = None
        for c in range(2 * N // chunk):
            scores = lax.dot_general(
                own,
                part(c, 0),
                (((1,), (1,)), ((), ())),
                preferred_element_type=f32,
            )
            score_ref[:, pl.ds(c * chunk, chunk)] = scores
            for s in range(chunk // 128):
                piece = scores[:, s * 128 : (s + 1) * 128]
                peak = piece if peak is None else jnp.maximum(peak, piece)
        peak = jnp.max(peak, 1, keepdims=True)
        acc = jnp.zeros((AGENTS, 128), f32)
        for c in range(2 * N // chunk):
            weights = jnp.exp(score_ref[:, pl.ds(c * chunk, chunk)] - peak).astype(bf16)
            block = part(c, 1)
            block = jnp.where(half_mask(block.shape, parity), block, jnp.ones_like(block))
            acc = acc + jnp.dot(weights, block, preferred_element_type=f32)
        other = pltpu.roll(acc, HD, 1)
        numer, total = (acc, other) if parity == 0 else (other, acc)
        logs = peak + jnp.log(total)
        values = numer / total
        logs = jnp.max(jnp.where(half_mask(logs.shape, 0), logs, -3e38), 1, keepdims=True)
        first = logs.astype(bf16).astype(f32)
        second = (logs - first).astype(bf16).astype(f32)
        third = logs - first - second
        lane = lanes((AGENTS, 128))
        packed = jnp.where(
            lane < HD,
            values,
            jnp.where(
                lane == HD,
                first,
                jnp.where(lane == HD + 1, second, jnp.where(lane == HD + 2, third, 0.0)),
            ),
        )
        groups = packed.reshape(2, AGENTS // 16, 8, 128)
        groups = jnp.concatenate([groups[0], groups[1]], 1).reshape(AGENTS, 128)
        out_ref[pl.ds(parity * AGENTS, AGENTS), :] = groups.astype(bf16)


def merge_kernel(parts_ref, out_ref):
    source = lax.broadcasted_iota(jnp.int32, (128, 128), 0)
    picker = jnp.where((source >= HD) & (source < HD + 3), 1.0, 0.0).astype(bf16)
    parts = parts_ref[...]
    logs = jnp.dot(parts, picker, preferred_element_type=f32).reshape(PEERS, 16, 128)
    values = parts.astype(f32).reshape(PEERS, 16, 128)
    peak = jnp.max(logs, 0)
    weights = jnp.exp(logs - peak[None])
    merged = jnp.sum(weights * values, 0) / jnp.sum(weights, 0)
    merged = jnp.where(lanes((8, 128)) < HD, merged[:8], pltpu.roll(merged[8:], HD, 1))
    out_ref[...] = slots(merged)


def probabilities(pairs, tab_ref, table, held_ref, fetches, prob_ref):
    chunk = N // len(fetches)
    matrix = turn_matrix()
    table.wait()
    ones = jnp.ones((AGENTS, 128), bf16)
    owns = []
    for head in range(LOCAL_HEADS):
        own = pairs[head // 2]
        owns.append(jnp.where(half_mask(own.shape, head % 2), own, jnp.zeros_like(own)))
    tables = split_tables(tab_ref[0], tab_ref[1])
    for c, fetch in enumerate(fetches):
        rows = pl.ds(c * chunk, chunk)
        cosine, sine = cell_tables(tables, c * (chunk // TC), chunk // TC)
        fetch.wait()
        queries = turned(held_ref[rows, :], matrix, cosine, sine)
        for head in range(LOCAL_HEADS):
            scores = lax.dot_general(
                queries[:, head // 2 * 128 : head // 2 * 128 + 128],
                owns[head],
                (((1,), (1,)), ((), ())),
                preferred_element_type=f32,
            )
            weights = jnp.exp(scores - jnp.max(scores, 1, keepdims=True))
            total = jnp.dot(weights.astype(bf16), ones, preferred_element_type=f32)
            scale = 1.0 / total
            scale = jnp.concatenate([scale, scale], axis=1)
            prob_ref[rows, pl.ds(head * AGENTS, AGENTS)] = (weights * scale).astype(bf16)


def probability_kernel(
    agents_ref,
    tab_hbm_ref,
    q_ref,
    v_ref,
    near_ref,
    far_ref,
    prob_ref,
    mate_ref,
    rest_ref,
    wide_ref,
    tab_ref,
    held_ref,
    top_ref,
    bottom_ref,
    sems,
):
    table = pltpu.make_async_copy(tab_hbm_ref, tab_ref, sems.at[3])
    table.start()
    fetches = []
    for c in range(3):
        part = pl.ds(c * (N // 3), N // 3)
        fetches.append(pltpu.make_async_copy(q_ref.at[part, :], held_ref.at[part, :], sems.at[c]))
        fetches[c].start()
    edges = [
        pltpu.make_async_copy(v_ref.at[0], top_ref, sems.at[4]),
        pltpu.make_async_copy(v_ref.at[TR - 1], bottom_ref, sems.at[5]),
    ]
    for copy in edges:
        copy.start()
    pairs = agent_pairs(agents_ref, wide_ref, 1.0 / math.sqrt(HD))
    probabilities(pairs, tab_ref, table, held_ref, fetches, prob_ref)
    for copy in edges:
        copy.wait()
    lines = []
    for row, line_ref in ((0, top_ref), (TR - 1, bottom_ref)):
        mate = near_ref[row : row + 1, :].astype(f32)
        rest = far_ref[row : row + 1, :].astype(f32)
        left = jnp.where(even_core(), rest, mate)
        right = jnp.where(even_core(), mate, rest)
        tail = jnp.concatenate([left, right, jnp.zeros((14, CH), f32)], axis=0)
        lines.append(jnp.concatenate([line_ref[...].astype(f32), tail], axis=0))
    mate_ref[...] = jnp.where(even_row(), lines[1], lines[0]).astype(bf16)
    rest_ref[...] = jnp.where(even_row(), lines[0], lines[1]).astype(bf16)


def shifted(row, left, right):
    column = lax.broadcasted_iota(jnp.int32, row.shape, 0)
    before = jnp.where(column == 0, left, pltpu.roll(row, 1, 0))
    behind = jnp.where(column == TC - 1, right, pltpu.roll(row, TC - 1, 0))
    return before, row, behind


def conv_kernel(
    v_hbm_ref, near_ref, far_ref, w_ref, out_hbm_ref, v_ref, l_ref, r_ref, out_ref, sems
):
    fetches, outs = [], []
    for half in range(2):
        cols = pl.ds(half * 128, 128)
        fetches.append(
            pltpu.make_async_copy(v_hbm_ref.at[:, :, cols], v_ref.at[:, :, cols], sems.at[half])
        )
        fetches[half].start()
        outs.append(
            pltpu.make_async_copy(
                out_ref.at[:, cols], out_hbm_ref.at[:, cols], sems.at[2 + half]
            )
        )
    mate, rest = near_ref[...].astype(f32), far_ref[...].astype(f32)
    l_ref[...] = jnp.where(even_core(), rest, mate)
    r_ref[...] = jnp.where(even_core(), mate, rest)
    for half in range(2):
        cols = pl.ds(half * 128, 128)
        w = [jnp.broadcast_to(w_ref[t : t + 1, cols], (TC, 128)) for t in range(9)]

        def group(start, carry):
            a, b = carry
            lefts, rights = l_ref[pl.ds(start, 8), cols], r_ref[pl.ds(start, 8), cols]
            for k in range(8):
                row = v_ref[start + k, :, cols].astype(f32)
                x = shifted(row, lefts[k : k + 1], rights[k : k + 1])
                t = [sum(x[e] * w[3 * d + e] for e in range(3)) for d in range(3)]
                if a is not None:
                    at = (start + k - 1) * TC
                    if not isinstance(at, int):
                        at = pl.multiple_of(at, TC)
                    out_ref[pl.ds(at, TC), cols] = a + t[2]
                    b = b + t[1]
                else:
                    b = t[1]
                a, b = b, t[0]
            return a, b

        fetches[half].wait()
        carry = group(0, (None, None))
        a, b = lax.fori_loop(1, TR // 8, lambda g, c: group(pl.multiple_of(g * 8, 8), c), carry)
        out_ref[pl.ds((TR - 1) * TC, TC), cols] = a
        outs[half].start()
    for copy in outs:
        copy.wait()


def attend_kernel(
    av_ref,
    prob_ref,
    conv_hbm_ref,
    mate_ref,
    rest_ref,
    w_ref,
    sum_ref,
    stat_ref,
    conv_ref,
    sems,
):
    step = N // AGR
    copies = []
    for c in range(AGR):
        part = pl.ds(c * step, step)
        copies.append(
            pltpu.make_async_copy(conv_hbm_ref.at[part, :], conv_ref.at[part, :], sems.at[c])
        )
        copies[c].start()
    eye = lax.broadcasted_iota(jnp.int32, (128, 128), 0) == lanes((128, 128))
    av = av_ref[...].astype(f32).reshape(2, AGENTS // 16, 2, 8, 128)
    for pair in range(2):
        pieces = []
        for parity in range(2):
            part = av[parity, :, pair].reshape(128, 128)
            other = pltpu.roll(part, HD, 1)
            own = half_mask(part.shape, parity)
            for piece in (part, other) if parity == 0 else (other, part):
                pieces.append(jnp.where(own, piece, 0.0))
        agent_values = jnp.concatenate(pieces, axis=0).astype(bf16)
        for b in range(N // 512):
            rows = pl.ds(b * 512, 512)
            sum_ref[rows, pl.ds(pair * 128, 128)] = jnp.dot(
                prob_ref[rows, pl.ds(pair * 2 * AGENTS, 2 * AGENTS)],
                agent_values,
                preferred_element_type=f32,
            )
    mate, rest = mate_ref[...].astype(f32), rest_ref[...].astype(f32)
    above = jnp.where(even_row(), rest, mate)
    below = jnp.where(even_row(), mate, rest)
    for line, tap, at in ((above, 0, 0), (below, 6, N - TC)):
        x = shifted(line[:TC], line[TC : TC + 1], line[TC + 1 : TC + 2])
        total = sum(x[e] * w_ref[tap + e : tap + e + 1, :] for e in range(3))
        sum_ref[pl.ds(at, TC), :] = sum_ref[pl.ds(at, TC), :] + total
    for b in range(BLOCKS):
        if b * 128 % step == 0:
            copies[b * 128 // step].wait()
        rows = pl.ds(b * 128, 128)
        x = sum_ref[rows, :] + conv_ref[rows, :]
        sum_ref[rows, :] = x
        mean = jnp.sum(x[:, :128] + x[:, 128:], 1, keepdims=True) * (1.0 / CH)
        x = x - mean
        x = x * x
        squares = jnp.sum(x[:, :128] + x[:, 128:], 1, keepdims=True)
        stat_ref[b : b + 1, :] = jnp.sum(jnp.where(eye, mean, 0.0), 0, keepdims=True)
        stat_ref[BLOCKS + b : BLOCKS + b + 1, :] = jnp.sum(
            jnp.where(eye, squares, 0.0), 0, keepdims=True
        )


def norm_kernel(s0_ref, s1_ref, s2_ref, s3_ref, sum_ref, gain_ref, bias_ref, out_ref, done_ref, sems):
    stats = [s[...] for s in (s0_ref, s1_ref, s2_ref, s3_ref)]
    means = [s[:BLOCKS] for s in stats]
    mean = (means[0] + means[1] + means[2] + means[3]) * 0.25
    squares = sum(s[BLOCKS:] for s in stats)
    for m in means:
        squares = squares + CH * (m - mean) * (m - mean)
    scale = lax.rsqrt(squares * (1.0 / D) + epsilon)
    step = N // AGR
    copies = []
    for b in range(BLOCKS):
        rows = pl.ds(b * 128, 128)
        m = jnp.broadcast_to(mean[b : b + 1], (128, 128)).T
        s = jnp.broadcast_to(scale[b : b + 1], (128, 128)).T
        for half in range(2):
            cols = pl.ds(half * 128, 128)
            done_ref[rows, cols] = (
                (sum_ref[rows, cols] - m) * s * gain_ref[0:1, cols] + bias_ref[0:1, cols]
            ).astype(bf16)
        if (b + 1) * 128 % step == 0:
            part = pl.ds((b + 1) * 128 - step, step)
            copy = pltpu.make_async_copy(
                done_ref.at[part, :], out_ref.at[part, :], sems.at[len(copies)]
            )
            copy.start()
            copies.append(copy)
    for copy in copies:
        copy.wait()


TILE_AXES = ("row", "z", "core")


def spread(x, axes=TILE_AXES):
    count = lax.axis_size(axes)
    slot = x.reshape(count, x.shape[0] // count, 128)
    return lax.all_to_all(slot, axes, 0, 0).reshape(x.shape)


def swap(x, axis, pairs):
    return lax.ppermute(x, axis, [p for i, j in pairs for p in ((i, j), (j, i))])


def chain(axis, first):
    return [(i, i + 1) for i in range(first, lax.axis_size(axis) - 1, 2)]


def after(x, *others):
    return lax.optimization_barrier((x, *others))[0]


def shards(queries, keys, values, positions, conv_weight, norm_gain, norm_bias):
    q = queries.reshape(N, CH)
    k = keys.reshape(N, CH)
    v = values.reshape(N, CH)
    mb = 1 << 20
    wide = pltpu.VMEM((TILES * 8, 128), f32)
    packed, table = call(
        query_kernel,
        (far((TILES * 8, 128), bf16), far((2, TR + TC, 128), f32)),
        "hh",
        scratch=[
            pltpu.VMEM((N, CH), bf16),
            pltpu.VMEM((2, TC, TR), jnp.int32),
            pltpu.SemaphoreType.DMA((AGR + 1,)),
        ],
        nbytes=8 * mb,
        name="pool_queries",
    )(jnp.swapaxes(positions, 1, 2), q)
    agents = spread(packed)
    held_table = pltpu.VMEM((2, TR + TC, 128), f32)
    tk, *sends, inner, outer = call(
        key_kernel,
        (near((N, 128), bf16),)
        + (near((2 * N // PIECES, 128), bf16),) * PIECES
        + (near((TR, CH), bf16),) * 2,
        "hhh ",
        scratch=[
            held_table,
            pltpu.VMEM((TR, TC, CH), bf16),
            pltpu.SemaphoreType.DMA((2 + PIECES // 2,)),
        ],
        nbytes=4 * mb,
        name="turn_keys",
    )(table, values, v, k)
    got = [swap(send, "core", chain("core", 0)) for send in sends]
    inner = swap(inner, "core", chain("core", 0))
    outer = swap(outer, ("z", "core"), chain(("z", "core"), 1))
    parts = call(
        partial_kernel,
        far((2 * AGENTS, 128), bf16),
        " v " + " " * PIECES,
        scratch=[pltpu.VMEM((AGENTS, 2 * N), f32), wide],
        nbytes=10 * mb,
        name="partials",
    )(agents, tk, v, *got)
    parts, inner, outer = lax.optimization_barrier((parts, inner, outer))
    received = spread(parts, ("row", "z"))
    prob, mate, rest = call(
        probability_kernel,
        (near((N, LOCAL_HEADS * AGENTS), bf16),) + (near((TC + 16, CH), bf16),) * 2,
        " hhhvv",
        scratch=[wide, held_table, pltpu.VMEM((N, CH), bf16)]
        + [pltpu.VMEM((TC, CH), bf16)] * 2
        + [pltpu.SemaphoreType.DMA((6,))],
        nbytes=20 * mb,
        name="probabilities",
    )(agents, table, q, values, inner, outer)
    received = after(received, mate, rest, prob)
    merged = call(merge_kernel, far((TILES * 8, 128), bf16), " ", nbytes=2 * mb, name="merge")(
        received
    )
    mate, rest, inner, outer, merged = lax.optimization_barrier(
        (mate, rest, inner, outer, merged)
    )
    mate = swap(mate, "row", chain("row", 0))
    rest = swap(rest, "row", chain("row", 1))
    agent_values = spread(merged)
    convolved = call(
        conv_kernel,
        (far((N, CH), f32),),
        "hvv ",
        scratch=[
            pltpu.VMEM((TR, TC, CH), bf16),
            pltpu.VMEM((TR, CH), f32),
            pltpu.VMEM((TR, CH), f32),
            pltpu.VMEM((N, CH), f32),
            pltpu.SemaphoreType.DMA((4,)),
        ],
        nbytes=8 * mb,
        out_spaces="h",
        name="conv",
    )(values, inner, outer, conv_weight)[0]
    summed, stats = call(
        attend_kernel,
        (near((N, CH), f32), near((2 * BLOCKS, 128), f32)),
        " vh   ",
        scratch=[pltpu.VMEM((N, CH), f32), pltpu.SemaphoreType.DMA((AGR,))],
        nbytes=4 * mb,
        name="attend",
    )(agent_values, prob, convolved, mate, rest, conv_weight)
    heads = lax.axis_size("head")
    others = [
        lax.ppermute(stats, "head", [(i, i ^ d) for i in range(heads)]) for d in range(1, heads)
    ]
    normed = call(
        norm_kernel,
        (shape((N, CH), bf16),),
        "v   v  ",
        scratch=[pltpu.VMEM((N, CH), bf16), pltpu.SemaphoreType.DMA((AGR,))],
        nbytes=4 * mb,
        out_spaces="h",
        name="norm",
    )(
        stats, *others, summed, norm_gain.reshape(1, CH), norm_bias.reshape(1, CH)
    )[0]
    return normed.reshape(TR, TC, CH)


def solution(mesh):
    rows, cols, heads = mesh.devices.shape
    cores = jax.sharding.Mesh(
        mesh.devices.reshape(rows, cols // 2, 2, heads), ("row", "z", "core", "head")
    )
    tile = P("row", ("z", "core"), "head")
    in_specs = (tile,) * 3 + (
        P(None, "row", ("z", "core")),
        P(None, "head"),
        P("head"),
        P("head"),
    )
    return jax.shard_map(shards, mesh=cores, in_specs=in_specs, out_specs=tile, check_vma=False)
```

```python
import math

import jax
import jax.numpy as jnp
from jax import lax
from jax.experimental import pallas as pl
from jax.experimental.pallas import tpu as pltpu
from jax.sharding import PartitionSpec as P

HD = 64
D = 1024
AGR = 4
TR = 48
TC = 32
CH = 256
N = TR * TC
AGENTS = 256
TILES = 64
LOCAL_HEADS = 4
PEERS = TILES // 2
PIECES = 4
BLOCKS = N // 128

f32 = jnp.float32
bf16 = jnp.bfloat16
epsilon = 1e-05

VMEM_SPEC = pl.BlockSpec(memory_space=pltpu.VMEM)
HBM_SPEC = pl.BlockSpec(memory_space=pltpu.HBM)


def call(kernel, outs, in_spaces, scratch=(), nbytes=0, name=None, out_spaces=None):
    fn = pl.pallas_call(
        kernel,
        out_shape=outs,
        in_specs=[HBM_SPEC if c == "h" else VMEM_SPEC for c in in_spaces],
        out_specs=(
            tuple(HBM_SPEC if c == "h" else VMEM_SPEC for c in out_spaces or " " * len(outs))
            if isinstance(outs, tuple)
            else VMEM_SPEC
        ),
        scratch_shapes=list(scratch),
        compiler_params=pltpu.CompilerParams(vmem_limit_bytes=20 * 1024 * 1024),
        cost_estimate=pl.CostEstimate(flops=0, bytes_accessed=nbytes, transcendentals=0),
        name=name,
    )

    def run(*args):
        spaces = {"h": pltpu.HBM, "v": pltpu.VMEM}
        return fn(
            *[
                pltpu.with_memory_space_constraint(x, spaces[c]) if c in spaces else x
                for x, c in zip(args, in_spaces, strict=True)
            ]
        )

    return run


def shape(dims, dtype):
    return jax.ShapeDtypeStruct(dims, dtype)


def near(dims, dtype):
    return pltpu.VMEM(dims, dtype)


def far(dims, dtype):
    return pltpu.HBM(dims, dtype)


def lanes(dims):
    return lax.broadcasted_iota(jnp.int32, dims, len(dims) - 1)


def turn_matrix():
    source = lax.broadcasted_iota(jnp.int32, (CH, CH), 0)
    target = lax.broadcasted_iota(jnp.int32, (CH, CH), 1)
    low = (target & 31) < 16
    minus = jnp.where(low & (source == target + 16), -1.0, 0.0)
    plus = jnp.where((~low) & (source == target - 16), 1.0, 0.0)
    return (minus + plus).astype(bf16)


def sin_cos(angle):
    return jnp.sin(angle), jnp.cos(angle)


def turned(x, matrix, cosine, sine):
    swapped = jnp.dot(x, matrix, preferred_element_type=f32)
    return (x.astype(f32) * cosine + swapped * sine).astype(bf16)


def split_tables(cosines, sines):
    cosines = jnp.concatenate([cosines, cosines], axis=1)
    sines = jnp.concatenate([sines, sines], axis=1)
    return cosines[:TR], sines[:TR], cosines[TR:], sines[TR:]


def cell_tables(tables, first, rows):
    cos_r, sin_r, cos_c, sin_c = tables
    cosine = jnp.concatenate(
        [cos_r[first + i : first + i + 1, :] * cos_c for i in range(rows)], axis=0
    )
    sine = jnp.concatenate(
        [sin_r[first + i : first + i + 1, :] + sin_c for i in range(rows)], axis=0
    )
    return cosine, sine


def slots(block):
    twice = jnp.concatenate([block, block], axis=0).astype(bf16)
    return jnp.broadcast_to(twice[None], (TILES // 2, 16, 128)).reshape(TILES * 8, 128)


def query_kernel(
    pos_ref,
    q_ref,
    agents_ref,
    tab_ref,
    held_ref,
    spot_ref,
    sems,
):
    step = N // AGR
    place = pltpu.make_async_copy(pos_ref, spot_ref, sems.at[AGR])
    place.start()
    copies = []
    for cell in range(AGR):
        part = pl.ds(cell * step, step)
        copy = pltpu.make_async_copy(q_ref.at[part, :], held_ref.at[part, :], sems.at[cell])
        copy.start()
        copies.append(copy)
    lane = lanes((1, 128)) % HD
    power = jnp.exp((lane % 16).astype(f32) * f32(-math.log(100.0) / 16))
    freq_r = jnp.where(lane < 32, power, 0.0)
    freq_c = jnp.where(lane < 32, 0.0, power)
    place.wait()
    row_line = spot_ref[0][0:1, :].astype(f32)
    col_pos = spot_ref[1][:, 0:1].astype(f32)
    eye = lax.broadcasted_iota(jnp.int32, (TR, TR), 0) == lax.broadcasted_iota(
        jnp.int32, (TR, TR), 1
    )
    row_pos = jnp.sum(jnp.where(eye, jnp.broadcast_to(row_line, (TR, TR)), 0.0), 1, keepdims=True)
    angles = jnp.concatenate([row_pos * freq_r, col_pos * freq_c], axis=0)
    sines, cosines = sin_cos(angles)
    tab_ref[0] = cosines
    tab_ref[1] = sines
    cos_r, sin_r, cos_c, sin_c = split_tables(cosines, sines)
    place_in = lanes((1, CH)) % (HD // 2)
    by_row = lanes((1, CH)) % HD < HD // 2
    means = []
    for cell in range(AGR):
        copies[cell].wait()
        columns = jnp.zeros((TC, CH), f32)
        row_cos = jnp.zeros((8, CH), f32)
        row_sin = jnp.zeros((8, CH), f32)
        for i in range(cell * (TR // AGR), (cell + 1) * (TR // AGR)):
            x = held_ref[pl.ds(i * TC, TC), :].astype(f32)
            columns = columns + x
            x = x[:8] + x[8:16] + x[16:24] + x[24:]
            row_cos = row_cos + x * cos_r[i : i + 1]
            row_sin = row_sin + x * sin_r[i : i + 1]
        col_cos = jnp.sum(columns * cos_c, 0, keepdims=True)
        col_sin = jnp.sum(columns * sin_c, 0, keepdims=True)
        straight = jnp.where(by_row, jnp.sum(row_cos, 0, keepdims=True), col_cos)
        crossed = jnp.where(by_row, jnp.sum(row_sin, 0, keepdims=True), col_sin)
        crossed = jnp.where(
            place_in < HD // 4, -pltpu.roll(crossed, CH - HD // 4, 1), pltpu.roll(crossed, HD // 4, 1)
        )
        mean = (straight + crossed) / step
        means.append(mean.astype(bf16).astype(f32))
    packed = jnp.concatenate([m[:, :128] for m in means] + [m[:, 128:] for m in means], axis=0)
    agents_ref[...] = slots(packed)


def even_core():
    return lax.axis_index("core") == 0


def even_row():
    return lax.rem(lax.axis_index("row"), 2) == 0


def key_kernel(
    tab_hbm_ref,
    v_ref,
    flat_ref,
    k_ref,
    tk_ref,
    *refs,
):
    sends, (near_ref, far_ref, tab_ref, held_ref, sems) = refs[:PIECES], refs[PIECES:]
    step = N // AGR
    size = 2 * N // PIECES
    half = PIECES // 2
    offset = pl.multiple_of((1 - lax.axis_index("core")) * 128, 128)
    table = pltpu.make_async_copy(tab_hbm_ref, tab_ref, sems.at[0])
    table.start()
    whole = pltpu.make_async_copy(v_ref, held_ref, sems.at[1])
    whole.start()
    copies = []
    for i in range(half):
        source = flat_ref.at[pl.ds(i * size, size), pl.ds(offset, 128)]
        copies.append(pltpu.make_async_copy(source, sends[half + i], sems.at[2 + i]))
        copies[i].start()
    even = even_core()
    matrix = turn_matrix()
    table.wait()
    tables = split_tables(tab_ref[0], tab_ref[1])
    for cell in range(AGR):
        part = pl.ds(cell * step, step)
        cosine, sine = cell_tables(tables, cell * (TR // AGR), TR // AGR)
        keys = turned(k_ref[part, :], matrix, cosine, sine)
        tk_ref[part, :] = jnp.where(even, keys[:, :128], keys[:, 128:])
        keys = jnp.where(even, keys[:, 128:], keys[:, :128])
        span = math.gcd(size, step)
        for at in range(0, step, span):
            to = cell * step + at
            sends[to // size][pl.ds(to % size, span), :] = keys[at : at + span]
    whole.wait()
    first, last = held_ref[:, 0, :], held_ref[:, TC - 1, :]
    near_ref[...] = jnp.where(even, last, first)
    far_ref[...] = jnp.where(even, first, last)
    for copy in copies:
        copy.wait()


def agent_pairs(agents_ref, wide_ref, scale):
    wide_ref[...] = agents_ref[...].astype(f32) * scale
    pairs = []
    for pair in range(2):
        parts = [wide_ref[pl.ds(4 * pair + k, TILES, stride=8), :] for k in range(AGR)]
        pairs.append(jnp.concatenate(parts, axis=0).astype(bf16))
    return pairs


def half_mask(dims, parity):
    return (lanes(dims) // HD) == parity


def partial_kernel(agents_ref, tk_ref, v_ref, *refs):
    got, (out_ref, score_ref, wide_ref) = refs[:PIECES], refs[PIECES:]
    size = 2 * N // PIECES
    pairs = agent_pairs(agents_ref, wide_ref, 1.0 / math.sqrt(HD))
    mine = jnp.where(even_core(), pairs[0], pairs[1])
    offset = pl.multiple_of(lax.axis_index("core") * 128, 128)
    chunk = 512 if size % 512 == 0 else 384

    def part(c, which):
        at = c * chunk % N
        if c * chunk >= N:
            at = at + which * N
            return got[at // size][pl.ds(at % size, chunk), :]
        if which == 0:
            return tk_ref[pl.ds(at, chunk), :]
        return v_ref[pl.ds(at, chunk), pl.ds(offset, 128)]

    peaks = []
    for parity in range(2):
        own = jnp.where(half_mask(mine.shape, parity), mine, jnp.zeros_like(mine))
        peak = None
        for c in range(2 * N // chunk):
            scores = lax.dot_general(
                own,
                part(c, 0),
                (((1,), (1,)), ((), ())),
                preferred_element_type=f32,
            )
            score_ref[parity, :, pl.ds(c * chunk, chunk)] = scores
            for s in range(chunk // 128):
                piece = scores[:, s * 128 : (s + 1) * 128]
                peak = piece if peak is None else jnp.maximum(peak, piece)
        peaks.append(jnp.max(peak, 1, keepdims=True))
    for parity in range(2):
        peak = peaks[parity]
        acc = jnp.zeros((AGENTS, 128), f32)
        for c in range(2 * N // chunk):
            weights = jnp.exp(score_ref[parity, :, pl.ds(c * chunk, chunk)] - peak).astype(bf16)
            block = part(c, 1)
            block = jnp.where(half_mask(block.shape, parity), block, jnp.ones_like(block))
            acc = acc + jnp.dot(weights, block, preferred_element_type=f32)
        other = pltpu.roll(acc, HD, 1)
        numer, total = (acc, other) if parity == 0 else (other, acc)
        logs = peak + jnp.log(total)
        values = numer / total
        logs = jnp.max(jnp.where(half_mask(logs.shape, 0), logs, -3e38), 1, keepdims=True)
        first = logs.astype(bf16).astype(f32)
        second = (logs - first).astype(bf16).astype(f32)
        third = logs - first - second
        lane = lanes((AGENTS, 128))
        packed = jnp.where(
            lane < HD,
            values,
            jnp.where(
                lane == HD,
                first,
                jnp.where(lane == HD + 1, second, jnp.where(lane == HD + 2, third, 0.0)),
            ),
        )
        groups = packed.reshape(2, AGENTS // 16, 8, 128)
        groups = jnp.concatenate([groups[0], groups[1]], 1).reshape(AGENTS, 128)
        out_ref[pl.ds(parity * AGENTS, AGENTS), :] = groups.astype(bf16)


def merge_kernel(parts_ref, out_ref):
    source = lax.broadcasted_iota(jnp.int32, (128, 128), 0)
    picker = jnp.where((source >= HD) & (source < HD + 3), 1.0, 0.0).astype(bf16)
    parts = parts_ref[...]
    logs = jnp.dot(parts, picker, preferred_element_type=f32).reshape(PEERS, 16, 128)
    values = parts.astype(f32).reshape(PEERS, 16, 128)
    peak = jnp.max(logs, 0)
    weights = jnp.exp(logs - peak[None])
    merged = jnp.sum(weights * values, 0) / jnp.sum(weights, 0)
    merged = jnp.where(lanes((8, 128)) < HD, merged[:8], pltpu.roll(merged[8:], HD, 1))
    out_ref[...] = slots(merged)


def probabilities(pairs, tab_ref, table, held_ref, fetches, prob_ref):
    chunk = N // len(fetches)
    matrix = turn_matrix()
    table.wait()
    ones = jnp.ones((AGENTS, 128), bf16)
    owns = []
    for head in range(LOCAL_HEADS):
        own = pairs[head // 2]
        owns.append(jnp.where(half_mask(own.shape, head % 2), own, jnp.zeros_like(own)))
    tables = split_tables(tab_ref[0], tab_ref[1])
    for c, fetch in enumerate(fetches):
        rows = pl.ds(c * chunk, chunk)
        cosine, sine = cell_tables(tables, c * (chunk // TC), chunk // TC)
        fetch.wait()
        queries = turned(held_ref[rows, :], matrix, cosine, sine)
        for head in range(LOCAL_HEADS):
            scores = lax.dot_general(
                queries[:, head // 2 * 128 : head // 2 * 128 + 128],
                owns[head],
                (((1,), (1,)), ((), ())),
                preferred_element_type=f32,
            )
            weights = jnp.exp(scores - jnp.max(scores, 1, keepdims=True))
            total = jnp.dot(weights.astype(bf16), ones, preferred_element_type=f32)
            scale = 1.0 / total
            scale = jnp.concatenate([scale, scale], axis=1)
            prob_ref[rows, pl.ds(head * AGENTS, AGENTS)] = (weights * scale).astype(bf16)


def probability_kernel(
    agents_ref,
    tab_hbm_ref,
    q_ref,
    v_ref,
    near_ref,
    far_ref,
    prob_ref,
    mate_ref,
    rest_ref,
    wide_ref,
    tab_ref,
    held_ref,
    top_ref,
    bottom_ref,
    sems,
):
    table = pltpu.make_async_copy(tab_hbm_ref, tab_ref, sems.at[3])
    table.start()
    fetches = []
    for c in range(3):
        part = pl.ds(c * (N // 3), N // 3)
        fetches.append(pltpu.make_async_copy(q_ref.at[part, :], held_ref.at[part, :], sems.at[c]))
        fetches[c].start()
    edges = [
        pltpu.make_async_copy(v_ref.at[0], top_ref, sems.at[4]),
        pltpu.make_async_copy(v_ref.at[TR - 1], bottom_ref, sems.at[5]),
    ]
    for copy in edges:
        copy.start()
    pairs = agent_pairs(agents_ref, wide_ref, 1.0 / math.sqrt(HD))
    probabilities(pairs, tab_ref, table, held_ref, fetches, prob_ref)
    for copy in edges:
        copy.wait()
    lines = []
    for row, line_ref in ((0, top_ref), (TR - 1, bottom_ref)):
        mate = near_ref[row : row + 1, :].astype(f32)
        rest = far_ref[row : row + 1, :].astype(f32)
        left = jnp.where(even_core(), rest, mate)
        right = jnp.where(even_core(), mate, rest)
        tail = jnp.concatenate([left, right, jnp.zeros((14, CH), f32)], axis=0)
        lines.append(jnp.concatenate([line_ref[...].astype(f32), tail], axis=0))
    mate_ref[...] = jnp.where(even_row(), lines[1], lines[0]).astype(bf16)
    rest_ref[...] = jnp.where(even_row(), lines[0], lines[1]).astype(bf16)


def shifted(row, left, right):
    column = lax.broadcasted_iota(jnp.int32, row.shape, 0)
    before = jnp.where(column == 0, left, pltpu.roll(row, 1, 0))
    behind = jnp.where(column == TC - 1, right, pltpu.roll(row, TC - 1, 0))
    return before, row, behind


def conv_kernel(
    v_hbm_ref, near_ref, far_ref, w_ref, out_hbm_ref, v_ref, l_ref, r_ref, out_ref, sems
):
    fetches, outs = [], []
    for half in range(2):
        cols = pl.ds(half * 128, 128)
        fetches.append(
            pltpu.make_async_copy(v_hbm_ref.at[:, :, cols], v_ref.at[:, :, cols], sems.at[half])
        )
        fetches[half].start()
        outs.append(
            pltpu.make_async_copy(
                out_ref.at[:, cols], out_hbm_ref.at[:, cols], sems.at[2 + half]
            )
        )
    mate, rest = near_ref[...].astype(f32), far_ref[...].astype(f32)
    l_ref[...] = jnp.where(even_core(), rest, mate)
    r_ref[...] = jnp.where(even_core(), mate, rest)
    for half in range(2):
        cols = pl.ds(half * 128, 128)
        w = [jnp.broadcast_to(w_ref[t : t + 1, cols], (TC, 128)) for t in range(9)]

        def group(start, carry):
            a, b = carry
            lefts, rights = l_ref[pl.ds(start, 8), cols], r_ref[pl.ds(start, 8), cols]
            for k in range(8):
                row = v_ref[start + k, :, cols].astype(f32)
                x = shifted(row, lefts[k : k + 1], rights[k : k + 1])
                t = [sum(x[e] * w[3 * d + e] for e in range(3)) for d in range(3)]
                if a is not None:
                    at = (start + k - 1) * TC
                    if not isinstance(at, int):
                        at = pl.multiple_of(at, TC)
                    out_ref[pl.ds(at, TC), cols] = a + t[2]
                    b = b + t[1]
                else:
                    b = t[1]
                a, b = b, t[0]
            return a, b

        fetches[half].wait()
        carry = group(0, (None, None))
        a, b = lax.fori_loop(1, TR // 8, lambda g, c: group(pl.multiple_of(g * 8, 8), c), carry)
        out_ref[pl.ds((TR - 1) * TC, TC), cols] = a
        outs[half].start()
    for copy in outs:
        copy.wait()


def attend_kernel(
    av_ref,
    prob_ref,
    conv_hbm_ref,
    mate_ref,
    rest_ref,
    w_ref,
    sum_ref,
    stat_ref,
    conv_ref,
    sems,
):
    step = N // AGR
    copies = []
    for c in range(AGR):
        part = pl.ds(c * step, step)
        copies.append(
            pltpu.make_async_copy(conv_hbm_ref.at[part, :], conv_ref.at[part, :], sems.at[c])
        )
        copies[c].start()
    eye = lax.broadcasted_iota(jnp.int32, (128, 128), 0) == lanes((128, 128))
    av = av_ref[...].astype(f32).reshape(2, AGENTS // 16, 2, 8, 128)
    for pair in range(2):
        pieces = []
        for parity in range(2):
            part = av[parity, :, pair].reshape(128, 128)
            other = pltpu.roll(part, HD, 1)
            own = half_mask(part.shape, parity)
            for piece in (part, other) if parity == 0 else (other, part):
                pieces.append(jnp.where(own, piece, 0.0))
        agent_values = jnp.concatenate(pieces, axis=0).astype(bf16)
        for b in range(N // 512):
            rows = pl.ds(b * 512, 512)
            sum_ref[rows, pl.ds(pair * 128, 128)] = jnp.dot(
                prob_ref[rows, pl.ds(pair * 2 * AGENTS, 2 * AGENTS)],
                agent_values,
                preferred_element_type=f32,
            )
    mate, rest = mate_ref[...].astype(f32), rest_ref[...].astype(f32)
    above = jnp.where(even_row(), rest, mate)
    below = jnp.where(even_row(), mate, rest)
    for line, tap, at in ((above, 0, 0), (below, 6, N - TC)):
        x = shifted(line[:TC], line[TC : TC + 1], line[TC + 1 : TC + 2])
        total = sum(x[e] * w_ref[tap + e : tap + e + 1, :] for e in range(3))
        sum_ref[pl.ds(at, TC), :] = sum_ref[pl.ds(at, TC), :] + total
    for b in range(BLOCKS):
        if b * 128 % step == 0:
            copies[b * 128 // step].wait()
        rows = pl.ds(b * 128, 128)
        x = sum_ref[rows, :] + conv_ref[rows, :]
        sum_ref[rows, :] = x
        mean = jnp.sum(x[:, :128] + x[:, 128:], 1, keepdims=True) * (1.0 / CH)
        x = x - mean
        x = x * x
        squares = jnp.sum(x[:, :128] + x[:, 128:], 1, keepdims=True)
        stat_ref[b : b + 1, :] = jnp.sum(jnp.where(eye, mean, 0.0), 0, keepdims=True)
        stat_ref[BLOCKS + b : BLOCKS + b + 1, :] = jnp.sum(
            jnp.where(eye, squares, 0.0), 0, keepdims=True
        )


def norm_kernel(s0_ref, s1_ref, s2_ref, s3_ref, sum_ref, gain_ref, bias_ref, out_ref, done_ref, sems):
    stats = [s[...] for s in (s0_ref, s1_ref, s2_ref, s3_ref)]
    means = [s[:BLOCKS] for s in stats]
    mean = (means[0] + means[1] + means[2] + means[3]) * 0.25
    squares = sum(s[BLOCKS:] for s in stats)
    for m in means:
        squares = squares + CH * (m - mean) * (m - mean)
    scale = lax.rsqrt(squares * (1.0 / D) + epsilon)
    step = N // AGR
    copies = []
    for b in range(BLOCKS):
        rows = pl.ds(b * 128, 128)
        m = jnp.broadcast_to(mean[b : b + 1], (128, 128)).T
        s = jnp.broadcast_to(scale[b : b + 1], (128, 128)).T
        for half in range(2):
            cols = pl.ds(half * 128, 128)
            done_ref[rows, cols] = (
                (sum_ref[rows, cols] - m) * s * gain_ref[0:1, cols] + bias_ref[0:1, cols]
            ).astype(bf16)
        if (b + 1) * 128 % step == 0:
            part = pl.ds((b + 1) * 128 - step, step)
            copy = pltpu.make_async_copy(
                done_ref.at[part, :], out_ref.at[part, :], sems.at[len(copies)]
            )
            copy.start()
            copies.append(copy)
    for copy in copies:
        copy.wait()


TILE_AXES = ("row", "z", "core")


def spread(x, axes=TILE_AXES):
    count = lax.axis_size(axes)
    slot = x.reshape(count, x.shape[0] // count, 128)
    return lax.all_to_all(slot, axes, 0, 0).reshape(x.shape)


def swap(x, axis, pairs):
    return lax.ppermute(x, axis, [p for i, j in pairs for p in ((i, j), (j, i))])


def chain(axis, first):
    return [(i, i + 1) for i in range(first, lax.axis_size(axis) - 1, 2)]


def after(x, *others):
    return lax.optimization_barrier((x, *others))[0]


def shards(queries, keys, values, positions, conv_weight, norm_gain, norm_bias):
    q = queries.reshape(N, CH)
    k = keys.reshape(N, CH)
    v = values.reshape(N, CH)
    mb = 1 << 20
    wide = pltpu.VMEM((TILES * 8, 128), f32)
    packed, table = call(
        query_kernel,
        (far((TILES * 8, 128), bf16), far((2, TR + TC, 128), f32)),
        "hh",
        scratch=[
            pltpu.VMEM((N, CH), bf16),
            pltpu.VMEM((2, TC, TR), jnp.int32),
            pltpu.SemaphoreType.DMA((AGR + 1,)),
        ],
        nbytes=8 * mb,
        name="pool_queries",
    )(jnp.swapaxes(positions, 1, 2), q)
    agents = spread(packed)
    held_table = pltpu.VMEM((2, TR + TC, 128), f32)
    tk, *sends, inner, outer = call(
        key_kernel,
        (near((N, 128), bf16),)
        + (near((2 * N // PIECES, 128), bf16),) * PIECES
        + (near((TR, CH), bf16),) * 2,
        "hhh ",
        scratch=[
            held_table,
            pltpu.VMEM((TR, TC, CH), bf16),
            pltpu.SemaphoreType.DMA((2 + PIECES // 2,)),
        ],
        nbytes=4 * mb,
        name="turn_keys",
    )(table, values, v, k)
    got = [swap(send, "core", chain("core", 0)) for send in sends]
    inner = swap(inner, "core", chain("core", 0))
    outer = swap(outer, ("z", "core"), chain(("z", "core"), 1))
    parts = call(
        partial_kernel,
        far((2 * AGENTS, 128), bf16),
        " v " + " " * PIECES,
        scratch=[pltpu.VMEM((2, AGENTS, 2 * N), f32), wide],
        nbytes=10 * mb,
        name="partials",
    )(agents, tk, v, *got)
    parts, inner, outer = lax.optimization_barrier((parts, inner, outer))
    received = spread(parts, ("row", "z"))
    prob, mate, rest = call(
        probability_kernel,
        (near((N, LOCAL_HEADS * AGENTS), bf16),) + (near((TC + 16, CH), bf16),) * 2,
        " hhhvv",
        scratch=[wide, held_table, pltpu.VMEM((N, CH), bf16)]
        + [pltpu.VMEM((TC, CH), bf16)] * 2
        + [pltpu.SemaphoreType.DMA((6,))],
        nbytes=20 * mb,
        name="probabilities",
    )(agents, table, q, values, inner, outer)
    received = after(received, mate, rest, prob)
    merged = call(merge_kernel, far((TILES * 8, 128), bf16), " ", nbytes=2 * mb, name="merge")(
        received
    )
    mate, rest, inner, outer, merged = lax.optimization_barrier(
        (mate, rest, inner, outer, merged)
    )
    mate = swap(mate, "row", chain("row", 0))
    rest = swap(rest, "row", chain("row", 1))
    agent_values = spread(merged)
    convolved = call(
        conv_kernel,
        (far((N, CH), f32),),
        "hvv ",
        scratch=[
            pltpu.VMEM((TR, TC, CH), bf16),
            pltpu.VMEM((TR, CH), f32),
            pltpu.VMEM((TR, CH), f32),
            pltpu.VMEM((N, CH), f32),
            pltpu.SemaphoreType.DMA((4,)),
        ],
        nbytes=8 * mb,
        out_spaces="h",
        name="conv",
    )(values, inner, outer, conv_weight)[0]
    summed, stats = call(
        attend_kernel,
        (near((N, CH), f32), near((2 * BLOCKS, 128), f32)),
        " vh   ",
        scratch=[pltpu.VMEM((N, CH), f32), pltpu.SemaphoreType.DMA((AGR,))],
        nbytes=4 * mb,
        name="attend",
    )(agent_values, prob, convolved, mate, rest, conv_weight)
    heads = lax.axis_size("head")
    others = [
        lax.ppermute(stats, "head", [(i, i ^ d) for i in range(heads)]) for d in range(1, heads)
    ]
    normed = call(
        norm_kernel,
        (shape((N, CH), bf16),),
        "v   v  ",
        scratch=[pltpu.VMEM((N, CH), bf16), pltpu.SemaphoreType.DMA((AGR,))],
        nbytes=4 * mb,
        out_spaces="h",
        name="norm",
    )(
        stats, *others, summed, norm_gain.reshape(1, CH), norm_bias.reshape(1, CH)
    )[0]
    return normed.reshape(TR, TC, CH)


def solution(mesh):
    rows, cols, heads = mesh.devices.shape
    cores = jax.sharding.Mesh(
        mesh.devices.reshape(rows, cols // 2, 2, heads), ("row", "z", "core", "head")
    )
    tile = P("row", ("z", "core"), "head")
    in_specs = (tile,) * 3 + (
        P(None, "row", ("z", "core")),
        P(None, "head"),
        P("head"),
        P("head"),
    )
    return jax.shard_map(shards, mesh=cores, in_specs=in_specs, out_specs=tile, check_vma=False)
```

```python
import math

import jax
import jax.numpy as jnp
from jax import lax
from jax.experimental import pallas as pl
from jax.experimental.pallas import tpu as pltpu
from jax.sharding import PartitionSpec as P

HD = 64
D = 1024
AGR = 4
TR = 48
TC = 32
CH = 256
N = TR * TC
AGENTS = 256
TILES = 64
LOCAL_HEADS = 4
PEERS = TILES // 2
PIECES = 4
BLOCKS = N // 128

f32 = jnp.float32
bf16 = jnp.bfloat16
epsilon = 1e-05

VMEM_SPEC = pl.BlockSpec(memory_space=pltpu.VMEM)
HBM_SPEC = pl.BlockSpec(memory_space=pltpu.HBM)


def call(kernel, outs, in_spaces, scratch=(), nbytes=0, name=None, out_spaces=None):
    fn = pl.pallas_call(
        kernel,
        out_shape=outs,
        in_specs=[HBM_SPEC if c == "h" else VMEM_SPEC for c in in_spaces],
        out_specs=(
            tuple(HBM_SPEC if c == "h" else VMEM_SPEC for c in out_spaces or " " * len(outs))
            if isinstance(outs, tuple)
            else VMEM_SPEC
        ),
        scratch_shapes=list(scratch),
        compiler_params=pltpu.CompilerParams(vmem_limit_bytes=20 * 1024 * 1024),
        cost_estimate=pl.CostEstimate(flops=0, bytes_accessed=nbytes, transcendentals=0),
        name=name,
    )

    def run(*args):
        spaces = {"h": pltpu.HBM, "v": pltpu.VMEM}
        return fn(
            *[
                pltpu.with_memory_space_constraint(x, spaces[c]) if c in spaces else x
                for x, c in zip(args, in_spaces, strict=True)
            ]
        )

    return run


def shape(dims, dtype):
    return jax.ShapeDtypeStruct(dims, dtype)


def near(dims, dtype):
    return pltpu.VMEM(dims, dtype)


def far(dims, dtype):
    return pltpu.HBM(dims, dtype)


def lanes(dims):
    return lax.broadcasted_iota(jnp.int32, dims, len(dims) - 1)


def turn_matrix():
    source = lax.broadcasted_iota(jnp.int32, (CH, CH), 0)
    target = lax.broadcasted_iota(jnp.int32, (CH, CH), 1)
    low = (target & 31) < 16
    minus = jnp.where(low & (source == target + 16), -1.0, 0.0)
    plus = jnp.where((~low) & (source == target - 16), 1.0, 0.0)
    return (minus + plus).astype(bf16)


def sin_cos(angle):
    return jnp.sin(angle), jnp.cos(angle)


def turned(x, matrix, cosine, sine):
    swapped = jnp.dot(x, matrix, preferred_element_type=f32)
    return (x.astype(f32) * cosine + swapped * sine).astype(bf16)


def split_tables(cosines, sines):
    cosines = jnp.concatenate([cosines, cosines], axis=1)
    sines = jnp.concatenate([sines, sines], axis=1)
    return cosines[:TR], sines[:TR], cosines[TR:], sines[TR:]


def cell_tables(tables, first, rows):
    cos_r, sin_r, cos_c, sin_c = tables
    cosine = jnp.concatenate(
        [cos_r[first + i : first + i + 1, :] * cos_c for i in range(rows)], axis=0
    )
    sine = jnp.concatenate(
        [sin_r[first + i : first + i + 1, :] + sin_c for i in range(rows)], axis=0
    )
    return cosine, sine


def slots(block):
    twice = jnp.concatenate([block, block], axis=0).astype(bf16)
    return jnp.broadcast_to(twice[None], (TILES // 2, 16, 128)).reshape(TILES * 8, 128)


def query_kernel(
    pos_ref,
    q_ref,
    agents_ref,
    tab_ref,
    held_ref,
    spot_ref,
    sems,
):
    step = N // AGR
    place = pltpu.make_async_copy(pos_ref, spot_ref, sems.at[AGR])
    place.start()
    copies = []
    for cell in range(AGR):
        part = pl.ds(cell * step, step)
        copy = pltpu.make_async_copy(q_ref.at[part, :], held_ref.at[part, :], sems.at[cell])
        copy.start()
        copies.append(copy)
    lane = lanes((1, 128)) % HD
    power = jnp.exp((lane % 16).astype(f32) * f32(-math.log(100.0) / 16))
    freq_r = jnp.where(lane < 32, power, 0.0)
    freq_c = jnp.where(lane < 32, 0.0, power)
    place.wait()
    row_line = spot_ref[0][0:1, :].astype(f32)
    col_pos = spot_ref[1][:, 0:1].astype(f32)
    eye = lax.broadcasted_iota(jnp.int32, (TR, TR), 0) == lax.broadcasted_iota(
        jnp.int32, (TR, TR), 1
    )
    row_pos = jnp.sum(jnp.where(eye, jnp.broadcast_to(row_line, (TR, TR)), 0.0), 1, keepdims=True)
    angles = jnp.concatenate([row_pos * freq_r, col_pos * freq_c], axis=0)
    sines, cosines = sin_cos(angles)
    tab_ref[0] = cosines
    tab_ref[1] = sines
    cos_r, sin_r, cos_c, sin_c = split_tables(cosines, sines)
    place_in = lanes((1, CH)) % (HD // 2)
    by_row = lanes((1, CH)) % HD < HD // 2
    means = []
    for cell in range(AGR):
        copies[cell].wait()
        columns = jnp.zeros((TC, CH), f32)
        row_cos = jnp.zeros((8, CH), f32)
        row_sin = jnp.zeros((8, CH), f32)
        for i in range(cell * (TR // AGR), (cell + 1) * (TR // AGR)):
            x = held_ref[pl.ds(i * TC, TC), :].astype(f32)
            columns = columns + x
            x = x[:8] + x[8:16] + x[16:24] + x[24:]
            row_cos = row_cos + x * cos_r[i : i + 1]
            row_sin = row_sin + x * sin_r[i : i + 1]
        col_cos = jnp.sum(columns * cos_c, 0, keepdims=True)
        col_sin = jnp.sum(columns * sin_c, 0, keepdims=True)
        straight = jnp.where(by_row, jnp.sum(row_cos, 0, keepdims=True), col_cos)
        crossed = jnp.where(by_row, jnp.sum(row_sin, 0, keepdims=True), col_sin)
        crossed = jnp.where(
            place_in < HD // 4, -pltpu.roll(crossed, CH - HD // 4, 1), pltpu.roll(crossed, HD // 4, 1)
        )
        mean = (straight + crossed) / step
        means.append(mean.astype(bf16).astype(f32))
    packed = jnp.concatenate([m[:, :128] for m in means] + [m[:, 128:] for m in means], axis=0)
    agents_ref[...] = slots(packed)


def even_core():
    return lax.axis_index("core") == 0


def even_row():
    return lax.rem(lax.axis_index("row"), 2) == 0


def key_kernel(
    tab_hbm_ref,
    v_ref,
    flat_ref,
    k_ref,
    tk_ref,
    *refs,
):
    sends, (near_ref, far_ref, tab_ref, held_ref, sems) = refs[:PIECES], refs[PIECES:]
    step = N // AGR
    size = 2 * N // PIECES
    half = PIECES // 2
    offset = pl.multiple_of((1 - lax.axis_index("core")) * 128, 128)
    table = pltpu.make_async_copy(tab_hbm_ref, tab_ref, sems.at[0])
    table.start()
    whole = pltpu.make_async_copy(v_ref, held_ref, sems.at[1])
    whole.start()
    copies = []
    for i in range(half):
        source = flat_ref.at[pl.ds(i * size, size), pl.ds(offset, 128)]
        copies.append(pltpu.make_async_copy(source, sends[half + i], sems.at[2 + i]))
        copies[i].start()
    even = even_core()
    matrix = turn_matrix()
    table.wait()
    tables = split_tables(tab_ref[0], tab_ref[1])
    for cell in range(AGR):
        part = pl.ds(cell * step, step)
        cosine, sine = cell_tables(tables, cell * (TR // AGR), TR // AGR)
        keys = turned(k_ref[part, :], matrix, cosine, sine)
        tk_ref[part, :] = jnp.where(even, keys[:, :128], keys[:, 128:])
        keys = jnp.where(even, keys[:, 128:], keys[:, :128])
        span = math.gcd(size, step)
        for at in range(0, step, span):
            to = cell * step + at
            sends[to // size][pl.ds(to % size, span), :] = keys[at : at + span]
    whole.wait()
    first, last = held_ref[:, 0, :], held_ref[:, TC - 1, :]
    near_ref[...] = jnp.where(even, last, first)
    far_ref[...] = jnp.where(even, first, last)
    for copy in copies:
        copy.wait()


def agent_pairs(agents_ref, wide_ref, scale):
    wide_ref[...] = agents_ref[...].astype(f32) * scale
    pairs = []
    for pair in range(2):
        parts = [wide_ref[pl.ds(4 * pair + k, TILES, stride=8), :] for k in range(AGR)]
        pairs.append(jnp.concatenate(parts, axis=0).astype(bf16))
    return pairs


def half_mask(dims, parity):
    return (lanes(dims) // HD) == parity


def partial_kernel(agents_ref, tk_ref, v_ref, *refs):
    got, (out_ref, score_ref, wide_ref, done_ref, sems) = refs[:PIECES], refs[PIECES:]
    outs = []
    size = 2 * N // PIECES
    pairs = agent_pairs(agents_ref, wide_ref, 1.0 / math.sqrt(HD))
    mine = jnp.where(even_core(), pairs[0], pairs[1])
    offset = pl.multiple_of(lax.axis_index("core") * 128, 128)
    chunk = 512 if size % 512 == 0 else 384

    def part(c, which):
        at = c * chunk % N
        if c * chunk >= N:
            at = at + which * N
            return got[at // size][pl.ds(at % size, chunk), :]
        if which == 0:
            return tk_ref[pl.ds(at, chunk), :]
        return v_ref[pl.ds(at, chunk), pl.ds(offset, 128)]

    peaks = []
    for parity in range(2):
        own = jnp.where(half_mask(mine.shape, parity), mine, jnp.zeros_like(mine))
        peak = None
        for c in range(2 * N // chunk):
            scores = lax.dot_general(
                own,
                part(c, 0),
                (((1,), (1,)), ((), ())),
                preferred_element_type=f32,
            )
            score_ref[parity, :, pl.ds(c * chunk, chunk)] = scores
            for s in range(chunk // 128):
                piece = scores[:, s * 128 : (s + 1) * 128]
                peak = piece if peak is None else jnp.maximum(peak, piece)
        peaks.append(jnp.max(peak, 1, keepdims=True))
    for parity in range(2):
        peak = peaks[parity]
        acc = jnp.zeros((AGENTS, 128), f32)
        for c in range(2 * N // chunk):
            weights = jnp.exp(score_ref[parity, :, pl.ds(c * chunk, chunk)] - peak).astype(bf16)
            block = part(c, 1)
            block = jnp.where(half_mask(block.shape, parity), block, jnp.ones_like(block))
            acc = acc + jnp.dot(weights, block, preferred_element_type=f32)
        other = pltpu.roll(acc, HD, 1)
        numer, total = (acc, other) if parity == 0 else (other, acc)
        logs = peak + jnp.log(total)
        values = numer / total
        logs = jnp.max(jnp.where(half_mask(logs.shape, 0), logs, -3e38), 1, keepdims=True)
        first = logs.astype(bf16).astype(f32)
        second = (logs - first).astype(bf16).astype(f32)
        third = logs - first - second
        lane = lanes((AGENTS, 128))
        packed = jnp.where(
            lane < HD,
            values,
            jnp.where(
                lane == HD,
                first,
                jnp.where(lane == HD + 1, second, jnp.where(lane == HD + 2, third, 0.0)),
            ),
        )
        groups = packed.reshape(2, AGENTS // 16, 8, 128)
        groups = jnp.concatenate([groups[0], groups[1]], 1).reshape(AGENTS, 128)
        rows = pl.ds(parity * AGENTS, AGENTS)
        done_ref[rows, :] = groups.astype(bf16)
        outs.append(
            pltpu.make_async_copy(done_ref.at[rows, :], out_ref.at[rows, :], sems.at[parity])
        )
        outs[parity].start()
    for copy in outs:
        copy.wait()


def merge_kernel(parts_ref, out_ref):
    source = lax.broadcasted_iota(jnp.int32, (128, 128), 0)
    picker = jnp.where((source >= HD) & (source < HD + 3), 1.0, 0.0).astype(bf16)
    parts = parts_ref[...]
    logs = jnp.dot(parts, picker, preferred_element_type=f32).reshape(PEERS, 16, 128)
    values = parts.astype(f32).reshape(PEERS, 16, 128)
    peak = jnp.max(logs, 0)
    weights = jnp.exp(logs - peak[None])
    merged = jnp.sum(weights * values, 0) / jnp.sum(weights, 0)
    merged = jnp.where(lanes((8, 128)) < HD, merged[:8], pltpu.roll(merged[8:], HD, 1))
    out_ref[...] = slots(merged)


def probabilities(pairs, tab_ref, table, held_ref, fetches, prob_ref):
    chunk = N // len(fetches)
    matrix = turn_matrix()
    table.wait()
    ones = jnp.ones((AGENTS, 128), bf16)
    owns = []
    for head in range(LOCAL_HEADS):
        own = pairs[head // 2]
        owns.append(jnp.where(half_mask(own.shape, head % 2), own, jnp.zeros_like(own)))
    tables = split_tables(tab_ref[0], tab_ref[1])
    for c, fetch in enumerate(fetches):
        rows = pl.ds(c * chunk, chunk)
        cosine, sine = cell_tables(tables, c * (chunk // TC), chunk // TC)
        fetch.wait()
        queries = turned(held_ref[rows, :], matrix, cosine, sine)
        for head in range(LOCAL_HEADS):
            scores = lax.dot_general(
                queries[:, head // 2 * 128 : head // 2 * 128 + 128],
                owns[head],
                (((1,), (1,)), ((), ())),
                preferred_element_type=f32,
            )
            weights = jnp.exp(scores - jnp.max(scores, 1, keepdims=True))
            total = jnp.dot(weights.astype(bf16), ones, preferred_element_type=f32)
            scale = 1.0 / total
            scale = jnp.concatenate([scale, scale], axis=1)
            prob_ref[rows, pl.ds(head * AGENTS, AGENTS)] = (weights * scale).astype(bf16)


def probability_kernel(
    agents_ref,
    tab_hbm_ref,
    q_ref,
    v_ref,
    near_ref,
    far_ref,
    prob_ref,
    mate_ref,
    rest_ref,
    wide_ref,
    tab_ref,
    held_ref,
    top_ref,
    bottom_ref,
    sems,
):
    table = pltpu.make_async_copy(tab_hbm_ref, tab_ref, sems.at[3])
    table.start()
    fetches = []
    for c in range(3):
        part = pl.ds(c * (N // 3), N // 3)
        fetches.append(pltpu.make_async_copy(q_ref.at[part, :], held_ref.at[part, :], sems.at[c]))
        fetches[c].start()
    edges = [
        pltpu.make_async_copy(v_ref.at[0], top_ref, sems.at[4]),
        pltpu.make_async_copy(v_ref.at[TR - 1], bottom_ref, sems.at[5]),
    ]
    for copy in edges:
        copy.start()
    pairs = agent_pairs(agents_ref, wide_ref, 1.0 / math.sqrt(HD))
    probabilities(pairs, tab_ref, table, held_ref, fetches, prob_ref)
    for copy in edges:
        copy.wait()
    lines = []
    for row, line_ref in ((0, top_ref), (TR - 1, bottom_ref)):
        mate = near_ref[row : row + 1, :].astype(f32)
        rest = far_ref[row : row + 1, :].astype(f32)
        left = jnp.where(even_core(), rest, mate)
        right = jnp.where(even_core(), mate, rest)
        tail = jnp.concatenate([left, right, jnp.zeros((14, CH), f32)], axis=0)
        lines.append(jnp.concatenate([line_ref[...].astype(f32), tail], axis=0))
    mate_ref[...] = jnp.where(even_row(), lines[1], lines[0]).astype(bf16)
    rest_ref[...] = jnp.where(even_row(), lines[0], lines[1]).astype(bf16)


def shifted(row, left, right):
    column = lax.broadcasted_iota(jnp.int32, row.shape, 0)
    before = jnp.where(column == 0, left, pltpu.roll(row, 1, 0))
    behind = jnp.where(column == TC - 1, right, pltpu.roll(row, TC - 1, 0))
    return before, row, behind


def conv_kernel(
    v_hbm_ref, near_ref, far_ref, w_ref, out_hbm_ref, v_ref, l_ref, r_ref, out_ref, sems
):
    fetches, outs = [], []
    for half in range(2):
        cols = pl.ds(half * 128, 128)
        fetches.append(
            pltpu.make_async_copy(v_hbm_ref.at[:, :, cols], v_ref.at[:, :, cols], sems.at[half])
        )
        fetches[half].start()
        outs.append(
            pltpu.make_async_copy(
                out_ref.at[:, cols], out_hbm_ref.at[:, cols], sems.at[2 + half]
            )
        )
    mate, rest = near_ref[...].astype(f32), far_ref[...].astype(f32)
    l_ref[...] = jnp.where(even_core(), rest, mate)
    r_ref[...] = jnp.where(even_core(), mate, rest)
    for half in range(2):
        cols = pl.ds(half * 128, 128)
        w = [jnp.broadcast_to(w_ref[t : t + 1, cols], (TC, 128)) for t in range(9)]

        def group(start, carry):
            a, b = carry
            lefts, rights = l_ref[pl.ds(start, 8), cols], r_ref[pl.ds(start, 8), cols]
            for k in range(8):
                row = v_ref[start + k, :, cols].astype(f32)
                x = shifted(row, lefts[k : k + 1], rights[k : k + 1])
                t = [sum(x[e] * w[3 * d + e] for e in range(3)) for d in range(3)]
                if a is not None:
                    at = (start + k - 1) * TC
                    if not isinstance(at, int):
                        at = pl.multiple_of(at, TC)
                    out_ref[pl.ds(at, TC), cols] = a + t[2]
                    b = b + t[1]
                else:
                    b = t[1]
                a, b = b, t[0]
            return a, b

        fetches[half].wait()
        carry = group(0, (None, None))
        a, b = lax.fori_loop(1, TR // 8, lambda g, c: group(pl.multiple_of(g * 8, 8), c), carry)
        out_ref[pl.ds((TR - 1) * TC, TC), cols] = a
        outs[half].start()
    for copy in outs:
        copy.wait()


def attend_kernel(
    av_ref,
    prob_ref,
    conv_hbm_ref,
    mate_ref,
    rest_ref,
    w_ref,
    sum_ref,
    stat_ref,
    conv_ref,
    sems,
):
    step = N // AGR
    copies = []
    for c in range(AGR):
        part = pl.ds(c * step, step)
        copies.append(
            pltpu.make_async_copy(conv_hbm_ref.at[part, :], conv_ref.at[part, :], sems.at[c])
        )
        copies[c].start()
    eye = lax.broadcasted_iota(jnp.int32, (128, 128), 0) == lanes((128, 128))
    av = av_ref[...].astype(f32).reshape(2, AGENTS // 16, 2, 8, 128)
    for pair in range(2):
        pieces = []
        for parity in range(2):
            part = av[parity, :, pair].reshape(128, 128)
            other = pltpu.roll(part, HD, 1)
            own = half_mask(part.shape, parity)
            for piece in (part, other) if parity == 0 else (other, part):
                pieces.append(jnp.where(own, piece, 0.0))
        agent_values = jnp.concatenate(pieces, axis=0).astype(bf16)
        for b in range(N // 512):
            rows = pl.ds(b * 512, 512)
            sum_ref[rows, pl.ds(pair * 128, 128)] = jnp.dot(
                prob_ref[rows, pl.ds(pair * 2 * AGENTS, 2 * AGENTS)],
                agent_values,
                preferred_element_type=f32,
            )
    mate, rest = mate_ref[...].astype(f32), rest_ref[...].astype(f32)
    above = jnp.where(even_row(), rest, mate)
    below = jnp.where(even_row(), mate, rest)
    for line, tap, at in ((above, 0, 0), (below, 6, N - TC)):
        x = shifted(line[:TC], line[TC : TC + 1], line[TC + 1 : TC + 2])
        total = sum(x[e] * w_ref[tap + e : tap + e + 1, :] for e in range(3))
        sum_ref[pl.ds(at, TC), :] = sum_ref[pl.ds(at, TC), :] + total
    for b in range(BLOCKS):
        if b * 128 % step == 0:
            copies[b * 128 // step].wait()
        rows = pl.ds(b * 128, 128)
        x = sum_ref[rows, :] + conv_ref[rows, :]
        sum_ref[rows, :] = x
        mean = jnp.sum(x[:, :128] + x[:, 128:], 1, keepdims=True) * (1.0 / CH)
        x = x - mean
        x = x * x
        squares = jnp.sum(x[:, :128] + x[:, 128:], 1, keepdims=True)
        stat_ref[b : b + 1, :] = jnp.sum(jnp.where(eye, mean, 0.0), 0, keepdims=True)
        stat_ref[BLOCKS + b : BLOCKS + b + 1, :] = jnp.sum(
            jnp.where(eye, squares, 0.0), 0, keepdims=True
        )


def norm_kernel(s0_ref, s1_ref, s2_ref, s3_ref, sum_ref, gain_ref, bias_ref, out_ref, done_ref, sems):
    stats = [s[...] for s in (s0_ref, s1_ref, s2_ref, s3_ref)]
    means = [s[:BLOCKS] for s in stats]
    mean = (means[0] + means[1] + means[2] + means[3]) * 0.25
    squares = sum(s[BLOCKS:] for s in stats)
    for m in means:
        squares = squares + CH * (m - mean) * (m - mean)
    scale = lax.rsqrt(squares * (1.0 / D) + epsilon)
    step = N // AGR
    copies = []
    for b in range(BLOCKS):
        rows = pl.ds(b * 128, 128)
        m = jnp.broadcast_to(mean[b : b + 1], (128, 128)).T
        s = jnp.broadcast_to(scale[b : b + 1], (128, 128)).T
        for half in range(2):
            cols = pl.ds(half * 128, 128)
            done_ref[rows, cols] = (
                (sum_ref[rows, cols] - m) * s * gain_ref[0:1, cols] + bias_ref[0:1, cols]
            ).astype(bf16)
        if (b + 1) * 128 % step == 0:
            part = pl.ds((b + 1) * 128 - step, step)
            copy = pltpu.make_async_copy(
                done_ref.at[part, :], out_ref.at[part, :], sems.at[len(copies)]
            )
            copy.start()
            copies.append(copy)
    for copy in copies:
        copy.wait()


TILE_AXES = ("row", "z", "core")


def spread(x, axes=TILE_AXES):
    count = lax.axis_size(axes)
    slot = x.reshape(count, x.shape[0] // count, 128)
    return lax.all_to_all(slot, axes, 0, 0).reshape(x.shape)


def swap(x, axis, pairs):
    return lax.ppermute(x, axis, [p for i, j in pairs for p in ((i, j), (j, i))])


def chain(axis, first):
    return [(i, i + 1) for i in range(first, lax.axis_size(axis) - 1, 2)]


def after(x, *others):
    return lax.optimization_barrier((x, *others))[0]


def shards(queries, keys, values, positions, conv_weight, norm_gain, norm_bias):
    q = queries.reshape(N, CH)
    k = keys.reshape(N, CH)
    v = values.reshape(N, CH)
    mb = 1 << 20
    wide = pltpu.VMEM((TILES * 8, 128), f32)
    packed, table = call(
        query_kernel,
        (far((TILES * 8, 128), bf16), far((2, TR + TC, 128), f32)),
        "hh",
        scratch=[
            pltpu.VMEM((N, CH), bf16),
            pltpu.VMEM((2, TC, TR), jnp.int32),
            pltpu.SemaphoreType.DMA((AGR + 1,)),
        ],
        nbytes=8 * mb,
        name="pool_queries",
    )(jnp.swapaxes(positions, 1, 2), q)
    agents = spread(packed)
    held_table = pltpu.VMEM((2, TR + TC, 128), f32)
    tk, *sends, inner, outer = call(
        key_kernel,
        (near((N, 128), bf16),)
        + (near((2 * N // PIECES, 128), bf16),) * PIECES
        + (near((TR, CH), bf16),) * 2,
        "hhh ",
        scratch=[
            held_table,
            pltpu.VMEM((TR, TC, CH), bf16),
            pltpu.SemaphoreType.DMA((2 + PIECES // 2,)),
        ],
        nbytes=4 * mb,
        name="turn_keys",
    )(table, values, v, k)
    got = [swap(send, "core", chain("core", 0)) for send in sends]
    inner = swap(inner, "core", chain("core", 0))
    outer = swap(outer, ("z", "core"), chain(("z", "core"), 1))
    parts = call(
        partial_kernel,
        (far((2 * AGENTS, 128), bf16),),
        " v " + " " * PIECES,
        scratch=[
            pltpu.VMEM((2, AGENTS, 2 * N), f32),
            wide,
            pltpu.VMEM((2 * AGENTS, 128), bf16),
            pltpu.SemaphoreType.DMA((2,)),
        ],
        out_spaces="h",
        nbytes=10 * mb,
        name="partials",
    )(agents, tk, v, *got)[0]
    parts, inner, outer = lax.optimization_barrier((parts, inner, outer))
    received = spread(parts, ("row", "z"))
    prob, mate, rest = call(
        probability_kernel,
        (near((N, LOCAL_HEADS * AGENTS), bf16),) + (near((TC + 16, CH), bf16),) * 2,
        " hhhvv",
        scratch=[wide, held_table, pltpu.VMEM((N, CH), bf16)]
        + [pltpu.VMEM((TC, CH), bf16)] * 2
        + [pltpu.SemaphoreType.DMA((6,))],
        nbytes=20 * mb,
        name="probabilities",
    )(agents, table, q, values, inner, outer)
    received = after(received, mate, rest, prob)
    merged = call(merge_kernel, far((TILES * 8, 128), bf16), " ", nbytes=2 * mb, name="merge")(
        received
    )
    mate, rest, inner, outer, merged = lax.optimization_barrier(
        (mate, rest, inner, outer, merged)
    )
    mate = swap(mate, "row", chain("row", 0))
    rest = swap(rest, "row", chain("row", 1))
    agent_values = spread(merged)
    convolved = call(
        conv_kernel,
        (far((N, CH), f32),),
        "hvv ",
        scratch=[
            pltpu.VMEM((TR, TC, CH), bf16),
            pltpu.VMEM((TR, CH), f32),
            pltpu.VMEM((TR, CH), f32),
            pltpu.VMEM((N, CH), f32),
            pltpu.SemaphoreType.DMA((4,)),
        ],
        nbytes=8 * mb,
        out_spaces="h",
        name="conv",
    )(values, inner, outer, conv_weight)[0]
    summed, stats = call(
        attend_kernel,
        (near((N, CH), f32), near((2 * BLOCKS, 128), f32)),
        " vh   ",
        scratch=[pltpu.VMEM((N, CH), f32), pltpu.SemaphoreType.DMA((AGR,))],
        nbytes=4 * mb,
        name="attend",
    )(agent_values, prob, convolved, mate, rest, conv_weight)
    heads = lax.axis_size("head")
    others = [
        lax.ppermute(stats, "head", [(i, i ^ d) for i in range(heads)]) for d in range(1, heads)
    ]
    normed = call(
        norm_kernel,
        (shape((N, CH), bf16),),
        "v   v  ",
        scratch=[pltpu.VMEM((N, CH), bf16), pltpu.SemaphoreType.DMA((AGR,))],
        nbytes=4 * mb,
        out_spaces="h",
        name="norm",
    )(
        stats, *others, summed, norm_gain.reshape(1, CH), norm_bias.reshape(1, CH)
    )[0]
    return normed.reshape(TR, TC, CH)


def solution(mesh):
    rows, cols, heads = mesh.devices.shape
    cores = jax.sharding.Mesh(
        mesh.devices.reshape(rows, cols // 2, 2, heads), ("row", "z", "core", "head")
    )
    tile = P("row", ("z", "core"), "head")
    in_specs = (tile,) * 3 + (
        P(None, "row", ("z", "core")),
        P(None, "head"),
        P("head"),
        P("head"),
    )
    return jax.shard_map(shards, mesh=cores, in_specs=in_specs, out_specs=tile, check_vma=False)
```
